32 devices in a mesh: dp: 4 (over y, x), blk: 8 (over z, core).
Axes of the slice: x: 2, y: 2, z: 4, core: 2. Of those that a mesh axis runs over, the one named last changes fastest.
Arguments:
- tokens: bfloat16 [8, 1024, 768], P('dp', 'blk'), may hold values from -6 to 6
- segment_ids: int32 [8, 1024], P('dp', 'blk'), may hold values from 0 to 5, never falling along the last dimension, each value on 1 to 512 neighbouring positions
- gain_attn: bfloat16 [768], replicated, may hold values from 0.5 to 1.5
- w_query: bfloat16 [768, 768], replicated, may hold values from -0.109375 to 0.109375
- w_key: bfloat16 [768, 768], replicated, may hold values from -0.109375 to 0.109375
- w_value: bfloat16 [768, 768], replicated, may hold values from -0.21875 to 0.21875
- w_out: bfloat16 [768, 768], replicated, may hold values from -0.875 to 0.875
- gain_ffn: bfloat16 [768], replicated, may hold values from 0.5 to 1.5
- w_in: bfloat16 [768, 3072], replicated, may hold values from -0.21875 to 0.21875
- w_down: bfloat16 [3072, 768], replicated, may hold values from -0.15625 to 0.15625
- rel_table: bfloat16 [32, 12], replicated, may hold values from -4 to 4
- cotangent: bfloat16 [8, 1024, 768], P('dp', 'blk'), may hold values from -6 to 6
Outputs:
- output: bfloat16 [8, 1024, 768], P('dp', 'blk')
- grad_tokens: bfloat16 [8, 1024, 768], P('dp', 'blk')
- grad_gain_attn: float32 [768], P('blk')
- grad_w_query: float32 [768, 768], P('blk')
- grad_w_key: float32 [768, 768], P('blk')
- grad_w_value: float32 [768, 768], P('blk')
- grad_w_out: float32 [768, 768], P('blk')
- grad_gain_ffn: float32 [768], P('blk')
- grad_w_in: float32 [768, 3072], P('blk')
- grad_w_down: float32 [3072, 768], P('blk')
- grad_rel_table: float32 [32, 12], P('blk')
The draws below stay inside these ranges and needn't reach their ends.
Inputs may be any that keep to these rules, and one draw needn't show every extreme that they name: `segment_ids`: along each row of 1024 positions the ids never fall, so each id covers one contiguous run of tokens, a sequence of at most 512 tokens; a token attends only to tokens of its row with its id.
All inputs are finite; a program needn't handle non-finite values.
Results may differ from the reference program's by a relative error of at most 0.014.
The reference program's roundings to bfloat16 on the way count: a program that leaves them out, or rounds other values in their place, can miss the bound.
Values may be sent and summed in bfloat16 or wider, within the bound.
A program may use at most 192 MiB of HBM per device.

```python
import math
import jax
import jax.numpy as jnp
import numpy as np
from jax import lax

D = 768
H = 12
DH = 64
FF = 3072
NB = 32
ROW_LEN = 1024
SEGS = 6
ROWS = 8
HD = 768


def steps_of(key, extent, split, smallest, top_value):
    level, own = 1.0, jax.random.fold_in(key, 6)
    for dim, blocks in split:
        draws = jnp.exp(jax.random.uniform(jax.random.fold_in(own, dim), (blocks,), jnp.float32, smallest / len(split), top_value / len(split)))
        level = level * jnp.repeat(draws, extent[dim] // blocks).reshape([-1 if axis == dim else 1 for axis in range(len(extent))])
    return level


def length_profile(number_of, total, reach, lean):
    weights = [(1 << 20) // math.isqrt(rank ** lean) + 1 for rank in range(2, number_of + 1)]
    spare, holding = total - reach - (number_of - 1), [1] * (number_of - 1)
    while spare > 0:
        free = [i for i in range(number_of - 1) if holding[i] < reach]
        whole, left = sum([weights[i] for i in free]), spare
        for i in free:
            addition = min(reach - holding[i], max(1, left * weights[i] // whole), spare)
            holding[i] = holding[i] + addition
            spare = spare - addition
    return np.array([reach] + holding)


def ragged(own_key, number_of, total, bound, lean):
    if number_of == 2:
        one = jax.random.randint(own_key, (), max(1, total - bound), min(bound, total - 1) + 1)
        return jnp.stack([one, total - one])
    tallies = jnp.asarray(length_profile(number_of, total, bound, lean), jnp.int32)
    couples = (number_of - 1) // 2
    giver, receiver = tallies[1:1 + 2 * couples:2], tallies[2:2 + 2 * couples:2]
    room = jnp.minimum(giver - 1, bound - receiver)
    passed = jax.random.randint(jax.random.fold_in(own_key, 1), (couples,), 0, 1 << 20) % (room + 1)
    tallies = tallies.at[1:1 + 2 * couples:2].set(giver - passed).at[2:2 + 2 * couples:2].set(receiver + passed)
    return tallies[jax.random.permutation(jax.random.fold_in(own_key, 2), number_of)]


def gaussian(own_key, extent, deviation, bound, split=(), kind=jnp.bfloat16):
    values = jax.random.normal(own_key, extent, jnp.float32) * deviation
    if len(split) > 0:
        values = steps_of(own_key, extent, split, -0.22, 0.18) * values
    return jnp.clip(values, min=-bound, max=bound).astype(kind)


def setup_inputs(seed: int = 0) -> dict:
    streams_of = jax.random.split(jax.random.key(seed), 13)
    tokens = gaussian(streams_of[0], (ROWS, ROW_LEN, D), 1.0, 6.0, ((0, 4), (1, 8)))
    segment_ids = jax.vmap(lambda own: jnp.searchsorted(jnp.cumsum(ragged(own, SEGS, ROW_LEN, ROW_LEN // 2, 1)), jnp.arange(ROW_LEN), side="right"))(jax.random.split(streams_of[1], ROWS)).reshape((ROWS, ROW_LEN)).astype(jnp.int32)
    gain_attn = jnp.clip(1.0 + 0.1 * jax.random.normal(streams_of[2], (D,), jnp.float32), 0.5, 1.5).astype(jnp.bfloat16)
    w_query = gaussian(streams_of[3], (D, HD), (4 * D) ** -0.5, 0.109375)
    w_key = gaussian(streams_of[4], (D, HD), (4 * D) ** -0.5, 0.109375)
    w_value = gaussian(streams_of[5], (D, HD), D ** -0.5, 0.21875)
    w_out = gaussian(streams_of[6], (HD, D), (HD // 16) ** -0.5, 0.875)
    gain_ffn = jnp.clip(1.0 + 0.1 * jax.random.normal(streams_of[7], (D,), jnp.float32), 0.5, 1.5).astype(jnp.bfloat16)
    w_in = gaussian(streams_of[8], (D, FF), D ** -0.5, 0.21875)
    w_down = gaussian(streams_of[9], (FF, D), (FF // 2) ** -0.5, 0.15625)
    rel_table = gaussian(streams_of[10], (NB, H), 1.0, 4.0)
    cotangent = gaussian(streams_of[11], (ROWS, ROW_LEN, D), 1.0, 6.0, ((0, 4), (1, 8)))
    return dict(tokens=tokens, segment_ids=segment_ids, gain_attn=gain_attn, w_query=w_query, w_key=w_key, w_value=w_value, w_out=w_out, gain_ffn=gain_ffn, w_in=w_in, w_down=w_down, rel_table=rel_table, cotangent=cotangent)


EPS = 1e-06
NEG = -1e+30
EDGES = (12, 16, 23, 32, 46, 64, 91)

@jax.custom_vjp
def low(v):
    return lax.optimization_barrier(v.astype(jnp.bfloat16)).astype(jnp.float32)

@jax.custom_vjp
def low_back(v):
    return v

def low_keep(v):
    return (low(v), None)

def low_pass(kept, grad):
    return (grad,)

def back_keep(v):
    return (v, None)

def back_low(kept, grad):
    return (low(grad),)
low.defvjp(low_keep, low_pass)
low_back.defvjp(back_keep, back_low)

def bucket_of(offset):
    distance = jnp.abs(offset)
    far_part = 8 + sum(((distance >= edge).astype(jnp.int32) for edge in EDGES))
    return jnp.where(offset > 0, 16, 0) + jnp.where(distance < 8, distance, far_part)

def matmul(left, right):
    return jnp.dot(left, right, preferred_element_type=jnp.float32, precision=lax.Precision.HIGHEST)

def rms(values, gain):
    return values * lax.rsqrt(lax.optimization_barrier(jnp.mean(values * values, axis=-1, keepdims=True)) + EPS) * gain

def layer(x, seg, gain_attn, w_query, w_key, w_value, w_out, gain_ffn, w_in, w_down, table):
    count = x.shape[0]
    flat = x.reshape(-1, D)
    norm_one = low(rms(flat, gain_attn))

    def project(weight):
        return low(low_back(matmul(norm_one, weight))).reshape(count, ROW_LEN, H, DH)
    query, keys, values = (project(w_query), project(w_key), project(w_value))
    places = jnp.arange(ROW_LEN, dtype=jnp.int32)
    bias = jnp.transpose(table[bucket_of(places[None, :] - places[:, None])], (2, 0, 1))

    def one_row(parts):
        row_q, row_k, row_v, row_s = parts
        scores = jnp.einsum('qhd,khd->hqk', row_q, row_k, precision=lax.Precision.HIGHEST) + bias
        scores = low_back(scores)
        same = row_s[:, None] == row_s[None, :]
        scores = jnp.where(same[None], scores, NEG)
        probs = jax.nn.softmax(scores, axis=-1)
        return jnp.einsum('hqk,khd->qhd', low(probs), row_v, precision=lax.Precision.HIGHEST)
    attended = lax.map(jax.checkpoint(one_row), (query, keys, values, seg))
    attended = low(low_back(attended.reshape(-1, H * DH)))
    hidden = flat + low_back(matmul(attended, w_out))
    norm_two = low(rms(hidden, gain_ffn))
    pre = low_back(matmul(norm_two, w_in))
    active = low(jax.nn.gelu(pre, approximate=True))
    result = hidden + matmul(active, w_down)
    return result.reshape(count, ROW_LEN, D)

def reference(tokens, segment_ids, gain_attn, w_query, w_key, w_value, w_out, gain_ffn, w_in, w_down, rel_table, cotangent):
    weights = tuple((w.astype(jnp.float32) for w in (gain_attn, w_query, w_key, w_value, w_out, gain_ffn, w_in, w_down, rel_table)))
    group = math.gcd(ROWS, 4)
    x_groups = tokens.astype(jnp.float32).reshape(ROWS // group, group, ROW_LEN, D)
    seg_groups = segment_ids.reshape(ROWS // group, group, ROW_LEN)
    dy_groups = cotangent.astype(jnp.float32).reshape(ROWS // group, group, ROW_LEN, D)

    def one_group(totals, parts):
        x_part, seg_part, dy_part = parts

        def forward(x_in, *params):
            return layer(x_in, seg_part, *params)
        result, pull = jax.vjp(forward, x_part, *weights)
        grads = pull(dy_part)
        return (tuple((a + b for a, b in zip(totals, grads[1:]))), (result, grads[0]))
    start = tuple((jnp.zeros_like(w) for w in weights))
    totals, (results, dxs) = lax.scan(one_group, start, (x_groups, seg_groups, dy_groups))
    output = results.reshape(ROWS, ROW_LEN, D).astype(jnp.bfloat16)
    grad_tokens = dxs.reshape(ROWS, ROW_LEN, D).astype(jnp.bfloat16)
    return (output, grad_tokens, totals[0], totals[1], totals[2], totals[3], totals[4], totals[5], totals[6], totals[7], totals[8])
```

```python
import functools
import math

import jax
import jax.numpy as jnp
from jax import lax
from jax.experimental import pallas as pl
from jax.experimental.pallas import tpu as pltpu
from jax.sharding import PartitionSpec as P

EPS = 1e-06
NEG = -1e30
EDGES = (12, 16, 23, 32, 46, 64, 91)
ROOT_TWO_PI = 0.7978845608028654
CUBIC = 0.044715


def bucket_of(offset):
    distance = jnp.abs(offset)
    far_part = 8 + sum(((distance >= edge).astype(jnp.int32) for edge in EDGES))
    return jnp.where(offset > 0, 16, 0) + jnp.where(distance < 8, distance, far_part)


def gelu_both(values):
    inner_arg = ROOT_TWO_PI * (values + CUBIC * values * values * values)
    tangent = jnp.tanh(inner_arg)
    result = 0.5 * values * (1.0 + tangent)
    slope = 0.5 * (1.0 + tangent) + 0.5 * values * (1.0 - tangent * tangent) * ROOT_TWO_PI * (
        1.0 + 3.0 * CUBIC * values * values
    )
    return (result, slope)


def rms_forward(values, gain):
    scale = lax.rsqrt(jnp.mean(values * values, axis=-1, keepdims=True) + EPS)
    normed = values * scale
    return (normed, scale, (normed * gain).astype(jnp.bfloat16))


def rms_backward(grad, normed, scale, gain):
    gain_grad = jnp.sum(grad * normed, axis=0)
    inner_grad = grad * gain
    back = scale * (inner_grad - normed * jnp.mean(inner_grad * normed, axis=-1, keepdims=True))
    return (back, gain_grad)


def outer_sum(left, right):
    return jnp.einsum("td,tf->df", left, right, preferred_element_type=jnp.float32)


def times_t(left, right):
    return jnp.einsum("tf,df->td", left, right, preferred_element_type=jnp.float32)


def masked_scores(query, keys, bias, seg_query, seg_keys):
    raw = (
        jnp.einsum("bqhd,bkhd->bhqk", query, keys, preferred_element_type=jnp.float32) + bias[None]
    )
    same = seg_query[:, None, :, None] == seg_keys[:, None, None, :]
    return jnp.where(same, raw, NEG)


def score_grads(q_part, k_part, v_part, bias, sq_part, sk_part, total, d_mixed):
    scores = masked_scores(q_part, k_part, bias, sq_part, sk_part)
    probs = jnp.exp(scores - total[..., None])
    grad_probs = jnp.einsum("bqhd,bkhd->bhqk", d_mixed, v_part, preferred_element_type=jnp.float32)
    return (probs, grad_probs)


def on_device(
    tokens,
    segment_ids,
    gain_attn,
    w_query,
    w_key,
    w_value,
    w_out,
    gain_ffn,
    w_in,
    w_down,
    rel_table,
    cotangent,
):
    rows, block, width = tokens.shape
    buckets, heads = rel_table.shape
    inner = w_query.shape[1]
    head_dim = inner // heads
    length = block * lax.axis_size("blk")
    group = math.gcd(rows, max(1, 512 // block))
    blocks = rows // group
    gain_one = gain_attn.astype(jnp.float32)
    gain_two = gain_ffn.astype(jnp.float32)
    table_f = rel_table.astype(jnp.float32)
    flat = tokens.reshape(rows * block, width).astype(jnp.float32)
    normed_one, scale_one, low_one = rms_forward(flat, gain_one)

    def project(weight):
        return (
            jnp.dot(low_one, weight, preferred_element_type=jnp.float32)
            .astype(jnp.bfloat16)
            .reshape(rows, block, inner)
        )

    query, keys, values = (project(w_query), project(w_key), project(w_value))
    key_all, value_all, seg_all = (
        lax.all_gather(keys, "blk", axis=1, tiled=True),
        lax.all_gather(values, "blk", axis=1, tiled=True),
        lax.all_gather(segment_ids, "blk", axis=1, tiled=True),
    )
    places = lax.axis_index("blk") * block + jnp.arange(block, dtype=jnp.int32)
    offsets = jnp.arange(length, dtype=jnp.int32)[None, :] - places[:, None]
    onehot = (
        bucket_of(offsets)[None] == jnp.arange(buckets, dtype=jnp.int32)[:, None, None]
    ).astype(jnp.float32)
    bias = jnp.einsum("nqk,nh->hqk", onehot, table_f, precision=lax.Precision.HIGHEST)
    q_groups = query.reshape(blocks, group, block, heads, head_dim)
    seg_query = segment_ids.reshape(blocks, group, block)

    def key_groups(key_rows, value_rows, seg_rows):
        return (
            key_rows.reshape(blocks, group, length, heads, head_dim),
            value_rows.reshape(blocks, group, length, heads, head_dim),
            seg_rows.reshape(blocks, group, length),
        )

    k_groups, v_groups, seg_keys = key_groups(key_all, value_all, seg_all)

    def attend(parts):
        q_part, k_part, v_part, sq_part, sk_part = parts
        scores = masked_scores(q_part, k_part, bias, sq_part, sk_part)
        top = jnp.max(scores, axis=-1, keepdims=True)
        total = jnp.log(jnp.sum(jnp.exp(scores - top), axis=-1, keepdims=True)) + top
        probs = jnp.exp(scores - total).astype(jnp.bfloat16)
        mixed = jnp.einsum("bhqk,bkhd->bqhd", probs, v_part, preferred_element_type=jnp.float32)
        return (mixed.astype(jnp.bfloat16), total[..., 0])

    attended, log_totals = lax.map(attend, (q_groups, k_groups, v_groups, seg_query, seg_keys))
    attended_flat = attended.reshape(rows * block, inner)
    hidden = flat + jnp.dot(attended_flat, w_out, preferred_element_type=jnp.float32)
    normed_two, scale_two, low_two = rms_forward(hidden, gain_two)
    pre = jnp.dot(low_two, w_in, preferred_element_type=jnp.float32)
    gelu_value, gelu_slope = gelu_both(pre)
    active = gelu_value.astype(jnp.bfloat16)
    output = (hidden + jnp.dot(active, w_down, preferred_element_type=jnp.float32)).astype(
        jnp.bfloat16
    )
    grad_out = cotangent.reshape(rows * block, width)
    grad_down = outer_sum(active, grad_out)
    grad_pre = (times_t(grad_out, w_down) * gelu_slope).astype(jnp.bfloat16)
    grad_in = outer_sum(low_two, grad_pre)
    back_two, grad_gain_two = rms_backward(times_t(grad_pre, w_in), normed_two, scale_two, gain_two)
    grad_hidden = grad_out.astype(jnp.float32) + back_two
    grad_proj = grad_hidden.astype(jnp.bfloat16)
    grad_wout = outer_sum(attended_flat, grad_proj)
    grad_att = (
        times_t(grad_proj, w_out)
        .astype(jnp.bfloat16)
        .reshape(blocks, group, block, heads, head_dim)
    )
    key_back, value_back, seg_back = (
        lax.all_gather(keys, "blk", axis=1, tiled=True),
        lax.all_gather(values, "blk", axis=1, tiled=True),
        lax.all_gather(segment_ids, "blk", axis=1, tiled=True),
    )
    k_back, v_back, sk_back = key_groups(key_back, value_back, seg_back)
    start = jnp.zeros((heads, block, length), jnp.float32)

    def attend_back(carry, parts):
        q_part, k_part, v_part, sq_part, sk_part, total, d_mixed = parts
        probs, grad_probs = score_grads(
            q_part, k_part, v_part, bias, sq_part, sk_part, total, d_mixed
        )
        center = jnp.sum(probs * grad_probs, axis=-1, keepdims=True)
        grad_scores = (probs * (grad_probs - center)).astype(jnp.bfloat16)
        grad_q = jnp.einsum(
            "bhqk,bkhd->bqhd", grad_scores, k_part, preferred_element_type=jnp.float32
        ).astype(jnp.bfloat16)
        grad_k = jnp.einsum(
            "bhqk,bqhd->bkhd", grad_scores, q_part, preferred_element_type=jnp.float32
        )
        grad_v = jnp.einsum(
            "bhqk,bqhd->bkhd",
            probs.astype(jnp.bfloat16),
            d_mixed,
            preferred_element_type=jnp.float32,
        )
        paired = jnp.stack([grad_k, grad_v], axis=2).reshape(group, length, 2, inner)
        return (carry + jnp.sum(grad_scores.astype(jnp.float32), axis=0), (grad_q, paired))

    bias_grad, (grad_query, paired) = lax.scan(
        attend_back, start, (q_groups, k_back, v_back, seg_query, sk_back, log_totals, grad_att)
    )
    paired = paired.reshape(rows, length, 2, inner)
    kv_grad = lax.psum_scatter(paired, "blk", scatter_dimension=1, tiled=True).astype(jnp.bfloat16)
    grad_key = kv_grad[:, :, 0].reshape(rows * block, inner)
    grad_value = kv_grad[:, :, 1].reshape(rows * block, inner)
    grad_query = grad_query.reshape(rows * block, inner)
    grad_wq = outer_sum(low_one, grad_query)
    grad_wk = outer_sum(low_one, grad_key)
    grad_wv = outer_sum(low_one, grad_value)
    grad_low_one = (
        times_t(grad_query, w_query) + times_t(grad_key, w_key) + times_t(grad_value, w_value)
    )
    back_one, grad_gain_one = rms_backward(grad_low_one, normed_one, scale_one, gain_one)
    grad_tokens = (grad_hidden + back_one).astype(jnp.bfloat16).reshape(rows, block, width)
    grad_table = jnp.einsum("hqk,nqk->nh", bias_grad, onehot, precision=lax.Precision.HIGHEST)
    grads = (
        grad_gain_one,
        grad_wq,
        grad_wk,
        grad_wv,
        grad_wout,
        grad_gain_two,
        grad_in,
        grad_down,
        grad_table,
    )
    pieces = (
        lax.psum_scatter(grads[0], "blk", scatter_dimension=0, tiled=True),
        lax.psum_scatter(grads[1], "blk", scatter_dimension=0, tiled=True),
        lax.psum_scatter(grads[2], "blk", scatter_dimension=0, tiled=True),
        lax.psum_scatter(grads[3], "blk", scatter_dimension=0, tiled=True),
        lax.psum_scatter(grads[4], "blk", scatter_dimension=0, tiled=True),
        lax.psum_scatter(grads[5], "blk", scatter_dimension=0, tiled=True),
        lax.psum_scatter(grads[6], "blk", scatter_dimension=0, tiled=True),
        lax.psum_scatter(grads[7], "blk", scatter_dimension=0, tiled=True),
        lax.psum_scatter(grads[8], "blk", scatter_dimension=0, tiled=True),
    )
    shares = lax.psum(
        (
            pieces[0],
            pieces[1],
            pieces[2],
            pieces[3],
            pieces[4],
            pieces[5],
            pieces[6],
            pieces[7],
            pieces[8],
        ),
        "dp",
    )
    return (
        output.reshape(rows, block, width),
        grad_tokens,
        shares[0],
        shares[1],
        shares[2],
        shares[3],
        shares[4],
        shares[5],
        shares[6],
        shares[7],
        shares[8],
    )


BF = jnp.bfloat16
F32 = jnp.float32
MESH = pl.DeviceIdType.MESH
VLIMIT = 60 * 1024 * 1024
TILE = 128
REACH = 511


def mm(a, b):
    return lax.dot_general(a, b, (((1,), (0,)), ((), ())), preferred_element_type=F32)


def mm_nt(a, b):
    return lax.dot_general(a, b, (((1,), (1,)), ((), ())), preferred_element_type=F32)


def mm_tn(a, b):
    return lax.dot_general(a, b, (((0,), (0,)), ((), ())), preferred_element_type=F32)


def iota(shape, dim):
    return lax.broadcasted_iota(jnp.int32, shape, dim)


def spot():
    blk = lax.axis_index("blk")
    return lax.axis_index("dp"), blk // 2, blk % 2


def gather_kernel(nz, tok, dy, seg, xrow, dyrow, segall, zero, segbuf, s_sem, r_sem, l_sem):
    dp, z, c = spot()
    blk = 2 * z + c
    block = tok.shape[1]
    nb = 2 * nz
    barrier = pltpu.get_barrier_semaphore()
    for k in range(1, nb):
        pl.semaphore_signal(
            barrier, inc=1, device_id=(dp, lax.rem(blk + k, nb)), device_id_type=MESH
        )
    pl.semaphore_wait(barrier, nb - 1)

    def copy(src, dst, send, recv, zz, cc):
        return pltpu.make_async_remote_copy(
            src, dst, s_sem.at[send], r_sem.at[recv], device_id=(dp, 2 * zz + cc), device_id_type=MESH
        )

    mine = xrow.at[blk]
    for hop, dz in ((0, 1), (1, -1)):

        @pl.when((z + dz >= 0) & (z + dz < nz))
        def _():
            copy(tok.at[1 - c], mine, 2 * hop, blk, z + dz, 1 - c).start()
            copy(tok.at[c], mine, 2 * hop + 1, blk, z + dz, c).start()

    copy(tok.at[1 - c], mine, 4, blk, z, 1 - c).start()
    copy(dy.at[1 - c], dyrow.at[c], 5, nb, z, 1 - c).start()
    segbuf[...] = jnp.zeros_like(segbuf)
    segbuf[0:2, :] = seg[...]
    for k in range(1, nb):
        to = lax.rem(blk + k, nb)
        pltpu.make_async_remote_copy(
            segbuf,
            segall.at[blk],
            s_sem.at[10 + k],
            r_sem.at[nb + 1 + blk],
            device_id=(dp, to),
            device_id_type=MESH,
        ).start()
    segall[blk] = segbuf[...]
    own = pltpu.make_async_copy(tok.at[c], mine, l_sem.at[0])
    own.start()
    own_dy = pltpu.make_async_copy(dy.at[c], dyrow.at[c], l_sem.at[1])
    own_dy.start()

    reach = -(-REACH // (2 * block))
    for b in range(nb):

        @pl.when(jnp.abs(b // 2 - z) > reach)
        def _():
            xrow[b] = jnp.zeros(xrow.shape[1:], xrow.dtype)

    def arrived(b):
        copy(tok.at[0], xrow.at[b], 0, b, z, 1 - c).wait_recv()

    for far in range(1, reach + 1):
        for way, dz in ((0, 1), (1, -1)):
            src = z - dz * far

            @pl.when((src >= 0) & (src < nz))
            def _():
                for h in range(2):
                    arrived(2 * src + h)
                    if far < reach:

                        @pl.when((z + dz >= 0) & (z + dz < nz))
                        def _():
                            copy(
                                xrow.at[2 * src + h],
                                xrow.at[2 * src + h],
                                6 + 2 * way + h,
                                2 * src + h,
                                z + dz,
                                c,
                            ).start()

    arrived(2 * z + 1 - c)
    copy(dy.at[0], dyrow.at[1 - c], 0, nb, z, 1 - c).wait_recv()
    for k in range(1, nb):
        frm = lax.rem(blk + nb - k, nb)
        copy(segbuf, segall.at[frm], 0, nb + 1 + frm, z, 1 - c).wait_recv()
    own.wait()
    own_dy.wait()
    for hop, dz in ((0, 1), (1, -1)):

        @pl.when((z + dz >= 0) & (z + dz < nz))
        def _():
            copy(tok.at[0], mine, 2 * hop, blk, z, 1 - c).wait_send()
            copy(tok.at[0], mine, 2 * hop + 1, blk, z, 1 - c).wait_send()

        for far in range(1, reach):
            src = z - dz * far

            @pl.when((src >= 0) & (src < nz) & (z + dz >= 0) & (z + dz < nz))
            def _():
                for h in range(2):
                    copy(tok.at[0], mine, 6 + 2 * hop + h, blk, z, 1 - c).wait_send()

    copy(tok.at[0], mine, 4, blk, z, 1 - c).wait_send()
    copy(dy.at[0], dyrow.at[0], 5, nb, z, 1 - c).wait_send()
    for k in range(1, nb):
        copy(segbuf, segall.at[0], 10 + k, nb + 1, z, 1 - c).wait_send()


def gather(nz, tok, dy, seg):
    _, block, width = tok.shape
    nb = 2 * nz
    vm = pl.BlockSpec(memory_space=pltpu.VMEM)
    return pl.pallas_call(
        functools.partial(gather_kernel, nz),
        out_shape=(
            jax.ShapeDtypeStruct((nb, block, width), BF),
            jax.ShapeDtypeStruct((2, block, width), BF),
            jax.ShapeDtypeStruct((nb, 8, block), jnp.int32),
        ),
        in_specs=[vm] * 3,
        out_specs=(vm, vm, vm),
        scratch_shapes=[
            pltpu.VMEM((8, 128), F32),
            pltpu.VMEM((8, block), jnp.int32),
            pltpu.SemaphoreType.DMA((10 + nb,)),
            pltpu.SemaphoreType.DMA((2 * nb + 2,)),
            pltpu.SemaphoreType.DMA((2,)),
        ],
        compiler_params=pltpu.CompilerParams(
            collective_id=1, has_side_effects=True, vmem_limit_bytes=VLIMIT
        ),
    )(tok, dy, seg)


def norm_rows(x, gain):
    x = x.astype(F32)
    scale = lax.rsqrt(jnp.mean(x * x, axis=-1, keepdims=True) + EPS)
    normed = x * scale
    return normed, scale, (normed * gain).astype(BF)


def prepare_bias(table_ref, near, heads):
    buckets = table_ref.shape[0]
    for d in range(3):
        lane = iota((buckets, 2 * TILE), 1)
        back = jnp.where(lane < TILE, lane, lane - 2 * TILE)
        hot = (bucket_of((d - 1) * TILE - back) == iota((buckets, 2 * TILE), 0)).astype(BF)
        strip = mm_tn(table_ref[...], hot)
        for h in range(heads):
            row = jnp.broadcast_to(strip[h : h + 1, :], (TILE, 2 * TILE))
            near[h, d] = pltpu.roll(row, 0, 1, stride=1, stride_axis=0)[:, :TILE]


def prepare_masks(segall, kaug, qseg, qright, qleft, z, c, tq):
    nkb = kaug.shape[0] // TILE
    for b in range(nkb):
        row = segall[b, pl.ds(c, 1), :]
        r = iota((TILE, TILE), 0)
        hot = jnp.where((r == row) | (r == 8 + b), 1.0, 0.0).astype(F32)
        kaug[b * TILE : (b + 1) * TILE, :] = hot.T.astype(BF)
    for i in range(tq // TILE):
        qb = (tq // TILE) * z + i
        row = segall[qb, pl.ds(c, 1), :]
        r = iota((TILE, TILE), 0)
        lost = jnp.where((r < 8) & (r != row), NEG, 0.0).astype(F32)
        qseg[i * TILE : (i + 1) * TILE, :] = lost.T
        col = iota((TILE, TILE), 1) - 8
        ok = (col >= 0) & (col < nkb)
        qright[i * TILE : (i + 1) * TILE, :] = jnp.where(ok & (col >= qb + 2), 1.0, 0.0)
        qleft[i * TILE : (i + 1) * TILE, :] = jnp.where(ok & (col <= qb - 2), 1.0, 0.0)


def stacked(ref, cols, dst, tq):
    part = ref[:, cols].astype(F32)
    low = iota((tq, TILE), 1) < TILE // 2
    dst[0:tq, 0:TILE] = jnp.where(low, part, 0.0).astype(BF)
    dst[tq : 2 * tq, 0:TILE] = jnp.where(low, 0.0, part).astype(BF)


def attn_forward_pair(p, z, q, k, v, kaug, qseg, qright, qleft, near, ts, probs, att, qa, s):
    tq = q.shape[0]
    length = k.shape[0]
    nkb = length // TILE
    cols = pl.ds(pl.multiple_of(p * TILE, TILE), TILE)
    stacked(q, cols, qa, tq)
    for hh in range(2):
        far = ts[31, 2 * p + hh] * qright[...] + ts[15, 2 * p + hh] * qleft[...] + qseg[...]
        qa[hh * tq : (hh + 1) * tq, TILE:] = far.astype(BF)

    def score(rb, carry):
        rows = pl.ds(pl.multiple_of(rb * TILE, TILE), TILE)
        left = jnp.concatenate([k[rows, cols], kaug[rows, :]], axis=1)
        s[pl.ds(pl.multiple_of((rb + 1) * TILE, TILE), TILE), :] = mm_nt(left, qa[...])
        return carry

    lax.fori_loop(0, nkb, score, 0)
    for i in range(tq // TILE):
        for d in range(3):
            row = ((tq // TILE) * z + i + d) * TILE
            rows = pl.ds(pl.multiple_of(row, TILE), TILE)
            for hh in range(2):
                at = hh * tq + i * TILE
                s[rows, at : at + TILE] = s[rows, at : at + TILE] + near[2 * p + hh, d]

    def top(rb, best):
        rows = pl.ds(pl.multiple_of((rb + 1) * TILE, TILE), TILE)
        return jnp.maximum(best, jnp.max(s[rows, :].reshape(TILE // 8, 8, 2 * tq), axis=0))

    best = lax.fori_loop(0, nkb, top, jnp.full((8, 2 * tq), -3e38, F32))
    best = jnp.max(best, axis=0, keepdims=True)

    def expo(rb, total):
        rows = pl.ds(pl.multiple_of((rb + 1) * TILE, TILE), TILE)
        e = jnp.exp(s[rows, :] - best)
        s[rows, :] = e
        return total + jnp.sum(e.reshape(TILE // 8, 8, 2 * tq), axis=0)

    total = lax.fori_loop(0, nkb, expo, jnp.zeros((8, 2 * tq), F32))
    inverse = 1.0 / jnp.sum(total, axis=0, keepdims=True)

    def finish(rb, carry):
        rows = pl.ds(pl.multiple_of(rb * TILE, TILE), TILE)
        at = pl.ds(pl.multiple_of((rb + 1) * TILE, TILE), TILE)
        probs[p, rows, :] = (s[at, :] * inverse).astype(BF)
        return carry

    lax.fori_loop(0, nkb, finish, 0)
    mixed = mm_tn(v[:, cols], probs[p])
    both = jnp.concatenate([mixed[: TILE // 2, :tq], mixed[TILE // 2 :, tq:]], axis=0)
    att[:, cols] = both.T.astype(BF)


def forward_kernel(
    xrow, segall, gain, wq, wk, wv, table, ts, n1, k, v, q, probs, att,
    kaug, qseg, qright, qleft, near, qa, s,
):
    _, z, c = spot()
    nb, block, _ = xrow.shape
    tq = 2 * block
    g = gain[...].astype(F32)
    prepare_bias(table, near, 2 * probs.shape[0])
    prepare_masks(segall, kaug, qseg, qright, qleft, z, c, tq)
    for b in range(nb // 2):
        rows = slice(b * tq, (b + 1) * tq)
        part = xrow[2 * b : 2 * b + 2].reshape(tq, xrow.shape[2])
        n1[rows, :] = norm_rows(part, g)[2]
        k[rows, :] = mm(n1[rows, :], wk[...]).astype(BF)
        v[rows, :] = mm(n1[rows, :], wv[...]).astype(BF)
    own = n1[pl.ds(pl.multiple_of(z * tq, tq), tq), :]
    q[...] = mm(own, wq[...]).astype(BF)
    s[0:TILE, :] = jnp.zeros((TILE, s.shape[1]), F32)
    s[s.shape[0] - TILE :, :] = jnp.zeros((TILE, s.shape[1]), F32)

    def pair(p, carry):
        attn_forward_pair(p, z, q, k, v, kaug, qseg, qright, qleft, near, ts, probs, att, qa, s)
        return carry

    lax.fori_loop(0, probs.shape[0], pair, 0)


def forward(xrow, segall, gain, wq, wk, wv, table):
    nb, block, width = xrow.shape
    length, tq = nb * block, 2 * block
    inner = wq.shape[1]
    heads = table.shape[1]
    pairs = heads // 2
    vm = pl.BlockSpec(memory_space=pltpu.VMEM)
    sm = pl.BlockSpec(memory_space=pltpu.SMEM)
    return pl.pallas_call(
        forward_kernel,
        out_shape=(
            jax.ShapeDtypeStruct((length, width), BF),
            jax.ShapeDtypeStruct((length, inner), BF),
            jax.ShapeDtypeStruct((length, inner), BF),
            jax.ShapeDtypeStruct((tq, inner), BF),
            jax.ShapeDtypeStruct((pairs, length, 2 * tq), BF),
            jax.ShapeDtypeStruct((tq, inner), BF),
        ),
        in_specs=[vm] * 7 + [sm],
        out_specs=(vm,) * 6,
        scratch_shapes=[
            pltpu.VMEM((length, TILE), BF),
            pltpu.VMEM((tq, TILE), F32),
            pltpu.VMEM((tq, TILE), F32),
            pltpu.VMEM((tq, TILE), F32),
            pltpu.VMEM((heads, 3, TILE, TILE), F32),
            pltpu.VMEM((2 * tq, 2 * TILE), BF),
            pltpu.VMEM((length + 2 * TILE, 2 * tq), F32),
        ],
        compiler_params=pltpu.CompilerParams(vmem_limit_bytes=VLIMIT),
    )(xrow, segall, gain, wq, wk, wv, table, table.astype(F32))


def ffn_kernel(
    xown, att, dy, gain, wout, win, wdown, out, dh, datt, pdown, pin, pout, gfin,
    n2, act, slope,
):
    tq, width = att.shape[0], wout.shape[1]
    inner = win.shape[1]
    nb = pdown.shape[0]
    wide = width
    steps = inner // wide
    g = gain[...].astype(F32)
    h = xown[...].reshape(tq, width).astype(F32) + mm(att[...], wout[...])
    normed, scale, low = norm_rows(h, g)
    n2[...] = low
    d = dy[...].reshape(tq, width)
    total = h
    for j in range(steps):
        cols = slice(j * wide, (j + 1) * wide)
        value, slant = gelu_both(mm(n2[...], win[:, cols]))
        act[:, cols] = value.astype(BF)
        slope[:, cols] = slant
        total = total + mm(act[:, cols], wdown[cols, :])
    out[...] = total.astype(BF).reshape(out.shape)
    per = inner // nb
    quarters = pdown.shape[1]
    for j in range(steps):
        cols = slice(j * wide, (j + 1) * wide)
        grad = mm_tn(act[:, cols], d).astype(BF)
        count = wide // per
        pdown[j * count : (j + 1) * count] = grad.reshape(count, quarters, per // quarters, width)
    dn2 = jnp.zeros((tq, width), F32)
    for j in range(steps):
        cols = slice(j * wide, (j + 1) * wide)
        dpre = (mm_nt(d, wdown[cols, :]) * slope[:, cols]).astype(BF)
        pin[:, j] = mm_tn(n2[...], dpre).astype(BF).reshape(nb, width // nb, wide)
        dn2 = dn2 + mm_nt(dpre, win[:, cols])
    back, gain_grad = rms_backward(dn2, normed, scale, g)
    gfin[...] = gain_grad[None]
    dhid = d.astype(F32) + back
    dh[...] = dhid
    dhl = dhid.astype(BF)
    pout[...] = mm_tn(att[...], dhl).astype(BF).reshape(nb, width // nb, width)
    datt[...] = mm_nt(dhl, wout[...]).astype(BF)


def ffn(xown, att, dy, gain, wout, win, wdown, nb, quarters):
    tq, width = att.shape[0], wout.shape[1]
    inner = win.shape[1]
    vm = pl.BlockSpec(memory_space=pltpu.VMEM)
    return pl.pallas_call(
        ffn_kernel,
        out_shape=(
            jax.ShapeDtypeStruct((2, tq // 2, width), BF),
            jax.ShapeDtypeStruct((tq, width), F32),
            jax.ShapeDtypeStruct((tq, att.shape[1]), BF),
            jax.ShapeDtypeStruct((nb, quarters, inner // nb // quarters, width), BF),
            jax.ShapeDtypeStruct((nb, quarters, width // nb, inner // quarters), BF),
            jax.ShapeDtypeStruct((nb, width // nb, width), BF),
            jax.ShapeDtypeStruct((1, width), F32),
        ),
        in_specs=[vm] * 7,
        out_specs=(vm,) * 7,
        scratch_shapes=[
            pltpu.VMEM((tq, width), BF),
            pltpu.VMEM((tq, inner), BF),
            pltpu.VMEM((tq, inner), F32),
        ],
        compiler_params=pltpu.CompilerParams(vmem_limit_bytes=VLIMIT),
    )(xown, att, dy, gain, wout, win, wdown)


def attn_backward_pair(p, z, q, k, v, kaug, datt, probs, dk, dv, dq, near, far, qm, dm, dprob, ds):
    tq = q.shape[0]
    length = k.shape[0]
    nkb = length // TILE
    cols = pl.ds(pl.multiple_of(p * TILE, TILE), TILE)
    stacked(q, cols, qm, tq)
    stacked(datt, cols, dm, tq)

    def first(rb, total):
        rows = pl.ds(pl.multiple_of(rb * TILE, TILE), TILE)
        part = mm_nt(v[rows, cols], dm[...])
        dprob[rows, :] = part
        mixed = part * probs[p, rows, :].astype(F32)
        dv[rows, cols] = mm(probs[p, rows, :], dm[...]).astype(BF)
        return total + jnp.sum(mixed.reshape(TILE // 8, 8, 2 * tq), axis=0)

    total = lax.fori_loop(0, nkb, first, jnp.zeros((8, 2 * tq), F32))
    center = jnp.sum(total, axis=0, keepdims=True)

    def second(rb, carry):
        rows = pl.ds(pl.multiple_of(rb * TILE, TILE), TILE)
        at = pl.ds(pl.multiple_of((rb + 1) * TILE, TILE), TILE)
        part = (probs[p, rows, :].astype(F32) * (dprob[rows, :] - center)).astype(BF)
        ds[at, :] = part
        dk[rows, cols] = mm(part, qm[...]).astype(BF)
        return carry

    lax.fori_loop(0, nkb, second, 0)
    left = jnp.concatenate([k[:, cols], kaug[...]], axis=1)
    back = mm_tn(left, ds[TILE : TILE + length, :])
    both = jnp.concatenate([back[: TILE // 2, :tq], back[TILE // 2 : TILE, tq:]], axis=0)
    dq[:, cols] = both.T.astype(BF)
    sums = back[TILE + 8 : TILE + 8 + nkb, :]
    kb = iota((nkb, 2 * tq), 0)
    lane = iota((nkb, 2 * tq), 1)
    qb = (tq // TILE) * z + (lane % tq) // TILE
    far[0, pl.ds(p, 1), :] = jnp.sum(jnp.where(kb >= qb + 2, sums, 0.0), axis=0, keepdims=True)
    far[1, pl.ds(p, 1), :] = jnp.sum(jnp.where(kb <= qb - 2, sums, 0.0), axis=0, keepdims=True)
    for hh in range(2):
        for d in range(3):
            acc = jnp.zeros((TILE, TILE), F32)
            for i in range(tq // TILE):
                row = ((tq // TILE) * z + i + d) * TILE
                at = hh * tq + i * TILE
                acc = acc + ds[pl.ds(pl.multiple_of(row, TILE), TILE), at : at + TILE].astype(F32)
            near[2 * p + hh, d] = acc


def table_sums(near, far, rows, small, first_row, tq):
    heads = near.shape[0]
    rows[...] = jnp.zeros_like(rows)
    for d in range(3):
        offset = (d - 1) * TILE + iota((TILE, TILE), 0) - iota((TILE, TILE), 1)
        bucket = bucket_of(offset)
        for b in range(32):
            if (d == 0 and b >= 16) or (d == 2 and b < 16):
                continue
            hit = bucket == b

            def one(h, carry):
                part = jnp.where(hit, near[h, d], 0.0)
                part = jnp.sum(part.reshape(TILE // 8, 8, TILE), axis=0)
                rows[pl.ds(h, 1), b, :] = rows[pl.ds(h, 1), b, :] + jnp.sum(part, axis=0, keepdims=True)
                return carry

            lax.fori_loop(0, heads, one, 0)
    for h in range(heads):
        p, hh = h // 2, h % 2
        for side, b in ((0, 31), (1, 15)):
            line = far[side, p : p + 1, hh * tq : (hh + 1) * tq]
            for i in range(tq // TILE):
                rows[h, b : b + 1, :] = rows[h, b : b + 1, :] + line[:, i * TILE : (i + 1) * TILE]
    for part in range(heads * 32 // TILE):
        per = TILE // 32
        square = rows[part * per : (part + 1) * per].reshape(TILE, TILE)
        small[first_row + part : first_row + part + 1, :] = jnp.sum(square.T, axis=0, keepdims=True)


def backward_kernel(
    xrow, segall, gain, wq, wk, wv, n1, q, k, v, probs, datt, gfin, dpart, dqpart, pqkv, small,
    kaug, dk, dv, dq, near, far, qm, dm, dprob, ds, rows,
):
    _, z, c = spot()
    tq = q.shape[0]
    length = k.shape[0]
    width = n1.shape[1]
    nkb = length // TILE
    nb = pqkv.shape[0]
    for b in range(nkb):
        lane = iota((TILE, TILE), 1)
        kaug[b * TILE : (b + 1) * TILE, :] = jnp.where(lane == 8 + b, 1.0, 0.0).astype(BF)
    ds[0:TILE, :] = jnp.zeros((TILE, ds.shape[1]), BF)
    ds[ds.shape[0] - TILE :, :] = jnp.zeros((TILE, ds.shape[1]), BF)

    def pair(p, carry):
        attn_backward_pair(
            p, z, q, k, v, kaug, datt, probs, dk, dv, dq, near, far, qm, dm, dprob, ds
        )
        return carry

    lax.fori_loop(0, probs.shape[0], pair, 0)
    g = gain[...].astype(F32)
    for i, (left, right) in enumerate(
        ((n1[pl.ds(pl.multiple_of(z * tq, tq), tq), :], dq), (n1[...], dk), (n1[...], dv))
    ):
        pqkv[:, i] = mm_tn(left, right[...]).astype(BF).reshape(nb, width // nb, right.shape[1])
    gain_sum = jnp.zeros((1, width), F32)
    for b in range(length // tq):
        rows_b = slice(b * tq, (b + 1) * tq)
        part = mm_nt(dk[rows_b, :], wk[...]) + mm_nt(dv[rows_b, :], wv[...])
        dpart[b] = part.astype(BF)
        normed = norm_rows(xrow[2 * b : 2 * b + 2].reshape(tq, width), g)[0]
        gain_sum = gain_sum + jnp.sum(part * normed, axis=0, keepdims=True)

        @pl.when(b == z)
        def _():
            dqpart[...] = part

    own = mm_nt(dq[...], wq[...])
    dqpart[...] = dqpart[...] + own
    normed = norm_rows(xrow[pl.ds(2 * z, 2)].reshape(tq, width), g)[0]
    gain_sum = gain_sum + jnp.sum(own * normed, axis=0, keepdims=True)
    small[...] = jnp.zeros_like(small)
    lines = width // TILE
    for i in range(lines):
        small[i : i + 1, :] = gain_sum[:, i * TILE : (i + 1) * TILE]
        small[lines + i : lines + i + 1, :] = gfin[:, i * TILE : (i + 1) * TILE]
    table_sums(near, far, rows, small, 2 * lines, tq)


def backward(xrow, segall, gain, wq, wk, wv, n1, q, k, v, probs, datt, gfin):
    nb, block, width = xrow.shape
    length, tq = nb * block, 2 * block
    inner = wq.shape[1]
    pairs = probs.shape[0]
    vm = pl.BlockSpec(memory_space=pltpu.VMEM)
    return pl.pallas_call(
        backward_kernel,
        out_shape=(
            jax.ShapeDtypeStruct((length // tq, tq, width), BF),
            jax.ShapeDtypeStruct((tq, width), F32),
            jax.ShapeDtypeStruct((nb, 3, width // nb, inner), BF),
            jax.ShapeDtypeStruct((16, TILE), F32),
        ),
        in_specs=[vm] * 13,
        out_specs=(vm,) * 4,
        scratch_shapes=[
            pltpu.VMEM((length, TILE), BF),
            pltpu.VMEM((length, inner), BF),
            pltpu.VMEM((length, inner), BF),
            pltpu.VMEM((tq, inner), BF),
            pltpu.VMEM((2 * pairs, 3, TILE, TILE), F32),
            pltpu.VMEM((2, 8, 2 * tq), F32),
            pltpu.VMEM((2 * tq, TILE), BF),
            pltpu.VMEM((2 * tq, TILE), BF),
            pltpu.VMEM((length, 2 * tq), F32),
            pltpu.VMEM((length + 2 * TILE, 2 * tq), BF),
            pltpu.VMEM((2 * pairs, 32, TILE), F32),
        ],
        compiler_params=pltpu.CompilerParams(vmem_limit_bytes=VLIMIT),
    )(xrow, segall, gain, wq, wk, wv, n1, q, k, v, probs, datt, gfin)


def fast_device(
    nz, tokens, segment_ids, gain_attn, w_query, w_key, w_value, w_out, gain_ffn, w_in, w_down,
    rel_table, cotangent,
):
    rows, block, width = tokens.shape
    nb, quarters = 2 * nz, 4
    tq = 2 * block
    z, c = lax.axis_index("blk") // 2, lax.axis_index("blk") % 2
    xrow, dyrow, segall = gather(nz, tokens, cotangent, segment_ids)
    g1, g2 = gain_attn.reshape(1, width), gain_ffn.reshape(1, width)
    n1, k, v, q, probs, att = forward(xrow, segall, g1, w_query, w_key, w_value, rel_table)
    xown = lax.dynamic_slice_in_dim(xrow, 2 * z, 2, 0)
    out, dh, datt, pdown, pin, pout, gfin = ffn(
        xown, att, dyrow, g2, w_out, w_in, w_down, nb, quarters
    )
    dpart, dqpart, pqkv, small = backward(
        xrow, segall, g1, w_query, w_key, w_value, n1, q, k, v, probs, datt, gfin
    )
    def scatter(part):
        return lax.psum(lax.psum_scatter(part.astype(F32), "blk", tiled=True), "dp")[0]

    gdown = scatter(pdown).reshape(-1, width)
    gin = jnp.transpose(scatter(pin), (1, 0, 2)).reshape(width // nb, -1)
    gqkv = scatter(pqkv)
    gout = scatter(pout)
    flat = lax.psum(small, ("dp", "blk")).reshape(-1)
    b = lax.axis_index("blk")
    share = width // nb
    ga = lax.dynamic_slice_in_dim(flat[:width], b * share, share)
    gf = lax.dynamic_slice_in_dim(flat[width : 2 * width], b * share, share)
    heads = rel_table.shape[1]
    gt = flat[2 * width : 2 * width + 32 * heads].reshape(heads, 32).T
    gt = lax.dynamic_slice_in_dim(gt, b * (32 // nb), 32 // nb)
    every = lax.all_gather(dpart, "blk", axis=0).reshape(nz, 2, nz, tq, width)
    mine = every[:, c][:, z].astype(F32)
    keep = (jnp.arange(nz) != z)[:, None, None]
    dn1 = dqpart + jnp.sum(jnp.where(keep, mine, 0.0), axis=0)
    x = xown.reshape(tq, width).astype(F32)
    normed, scale, _ = rms_forward(x, gain_attn.astype(F32))
    back, _ = rms_backward(dn1, normed, scale, gain_attn.astype(F32))
    grad_tokens = (dh + back).astype(BF).reshape(2, block, width)

    def home(own):
        pairs = [(i, i ^ 1) for i in range(nb)]
        other = lax.ppermute(lax.dynamic_index_in_dim(own, 1 - c, 0, False), "blk", pairs)
        kept = lax.dynamic_index_in_dim(own, c, 0, False)
        return jnp.where(c == 0, jnp.stack([kept, other]), jnp.stack([other, kept]))

    return (
        home(out), home(grad_tokens), ga, gqkv[0], gqkv[1], gqkv[2], gout, gf, gin, gdown, gt,
    )


def pick(mesh):
    if mesh.shape["dp"] == 4 and mesh.shape["blk"] == 8:
        return functools.partial(fast_device, mesh.shape["blk"] // 2)
    return on_device


def solution(mesh):
    placed = (
        P("dp", "blk", None),
        P("dp", "blk"),
        P(),
        P(),
        P(),
        P(),
        P(),
        P(),
        P(),
        P(),
        P(),
        P("dp", "blk", None),
    )
    return jax.shard_map(
        pick(mesh),
        mesh=mesh,
        in_specs=placed,
        out_specs=(
            P("dp", "blk", None),
            P("dp", "blk", None),
            P("blk"),
            P("blk", None),
            P("blk", None),
            P("blk", None),
            P("blk", None),
            P("blk"),
            P("blk", None),
            P("blk", None),
            P("blk", None),
        ),
        check_vma=False,
    )
```

```python
import functools
import math

import jax
import jax.numpy as jnp
from jax import lax
from jax.experimental import pallas as pl
from jax.experimental.pallas import tpu as pltpu
from jax.sharding import PartitionSpec as P

EPS = 1e-06
NEG = -1e30
EDGES = (12, 16, 23, 32, 46, 64, 91)
ROOT_TWO_PI = 0.7978845608028654
CUBIC = 0.044715


def bucket_of(offset):
    distance = jnp.abs(offset)
    far_part = 8 + sum(((distance >= edge).astype(jnp.int32) for edge in EDGES))
    return jnp.where(offset > 0, 16, 0) + jnp.where(distance < 8, distance, far_part)


def gelu_both(values):
    inner_arg = ROOT_TWO_PI * (values + CUBIC * values * values * values)
    tangent = jnp.tanh(inner_arg)
    result = 0.5 * values * (1.0 + tangent)
    slope = 0.5 * (1.0 + tangent) + 0.5 * values * (1.0 - tangent * tangent) * ROOT_TWO_PI * (
        1.0 + 3.0 * CUBIC * values * values
    )
    return (result, slope)


def rms_forward(values, gain):
    scale = lax.rsqrt(jnp.mean(values * values, axis=-1, keepdims=True) + EPS)
    normed = values * scale
    return (normed, scale, (normed * gain).astype(jnp.bfloat16))


def rms_backward(grad, normed, scale, gain):
    gain_grad = jnp.sum(grad * normed, axis=0)
    inner_grad = grad * gain
    back = scale * (inner_grad - normed * jnp.mean(inner_grad * normed, axis=-1, keepdims=True))
    return (back, gain_grad)


def outer_sum(left, right):
    return jnp.einsum("td,tf->df", left, right, preferred_element_type=jnp.float32)


def times_t(left, right):
    return jnp.einsum("tf,df->td", left, right, preferred_element_type=jnp.float32)


def masked_scores(query, keys, bias, seg_query, seg_keys):
    raw = (
        jnp.einsum("bqhd,bkhd->bhqk", query, keys, preferred_element_type=jnp.float32) + bias[None]
    )
    same = seg_query[:, None, :, None] == seg_keys[:, None, None, :]
    return jnp.where(same, raw, NEG)


def score_grads(q_part, k_part, v_part, bias, sq_part, sk_part, total, d_mixed):
    scores = masked_scores(q_part, k_part, bias, sq_part, sk_part)
    probs = jnp.exp(scores - total[..., None])
    grad_probs = jnp.einsum("bqhd,bkhd->bhqk", d_mixed, v_part, preferred_element_type=jnp.float32)
    return (probs, grad_probs)


def on_device(
    tokens,
    segment_ids,
    gain_attn,
    w_query,
    w_key,
    w_value,
    w_out,
    gain_ffn,
    w_in,
    w_down,
    rel_table,
    cotangent,
):
    rows, block, width = tokens.shape
    buckets, heads = rel_table.shape
    inner = w_query.shape[1]
    head_dim = inner // heads
    length = block * lax.axis_size("blk")
    group = math.gcd(rows, max(1, 512 // block))
    blocks = rows // group
    gain_one = gain_attn.astype(jnp.float32)
    gain_two = gain_ffn.astype(jnp.float32)
    table_f = rel_table.astype(jnp.float32)
    flat = tokens.reshape(rows * block, width).astype(jnp.float32)
    normed_one, scale_one, low_one = rms_forward(flat, gain_one)

    def project(weight):
        return (
            jnp.dot(low_one, weight, preferred_element_type=jnp.float32)
            .astype(jnp.bfloat16)
            .reshape(rows, block, inner)
        )

    query, keys, values = (project(w_query), project(w_key), project(w_value))
    key_all, value_all, seg_all = (
        lax.all_gather(keys, "blk", axis=1, tiled=True),
        lax.all_gather(values, "blk", axis=1, tiled=True),
        lax.all_gather(segment_ids, "blk", axis=1, tiled=True),
    )
    places = lax.axis_index("blk") * block + jnp.arange(block, dtype=jnp.int32)
    offsets = jnp.arange(length, dtype=jnp.int32)[None, :] - places[:, None]
    onehot = (
        bucket_of(offsets)[None] == jnp.arange(buckets, dtype=jnp.int32)[:, None, None]
    ).astype(jnp.float32)
    bias = jnp.einsum("nqk,nh->hqk", onehot, table_f, precision=lax.Precision.HIGHEST)
    q_groups = query.reshape(blocks, group, block, heads, head_dim)
    seg_query = segment_ids.reshape(blocks, group, block)

    def key_groups(key_rows, value_rows, seg_rows):
        return (
            key_rows.reshape(blocks, group, length, heads, head_dim),
            value_rows.reshape(blocks, group, length, heads, head_dim),
            seg_rows.reshape(blocks, group, length),
        )

    k_groups, v_groups, seg_keys = key_groups(key_all, value_all, seg_all)

    def attend(parts):
        q_part, k_part, v_part, sq_part, sk_part = parts
        scores = masked_scores(q_part, k_part, bias, sq_part, sk_part)
        top = jnp.max(scores, axis=-1, keepdims=True)
        total = jnp.log(jnp.sum(jnp.exp(scores - top), axis=-1, keepdims=True)) + top
        probs = jnp.exp(scores - total).astype(jnp.bfloat16)
        mixed = jnp.einsum("bhqk,bkhd->bqhd", probs, v_part, preferred_element_type=jnp.float32)
        return (mixed.astype(jnp.bfloat16), total[..., 0])

    attended, log_totals = lax.map(attend, (q_groups, k_groups, v_groups, seg_query, seg_keys))
    attended_flat = attended.reshape(rows * block, inner)
    hidden = flat + jnp.dot(attended_flat, w_out, preferred_element_type=jnp.float32)
    normed_two, scale_two, low_two = rms_forward(hidden, gain_two)
    pre = jnp.dot(low_two, w_in, preferred_element_type=jnp.float32)
    gelu_value, gelu_slope = gelu_both(pre)
    active = gelu_value.astype(jnp.bfloat16)
    output = (hidden + jnp.dot(active, w_down, preferred_element_type=jnp.float32)).astype(
        jnp.bfloat16
    )
    grad_out = cotangent.reshape(rows * block, width)
    grad_down = outer_sum(active, grad_out)
    grad_pre = (times_t(grad_out, w_down) * gelu_slope).astype(jnp.bfloat16)
    grad_in = outer_sum(low_two, grad_pre)
    back_two, grad_gain_two = rms_backward(times_t(grad_pre, w_in), normed_two, scale_two, gain_two)
    grad_hidden = grad_out.astype(jnp.float32) + back_two
    grad_proj = grad_hidden.astype(jnp.bfloat16)
    grad_wout = outer_sum(attended_flat, grad_proj)
    grad_att = (
        times_t(grad_proj, w_out)
        .astype(jnp.bfloat16)
        .reshape(blocks, group, block, heads, head_dim)
    )
    key_back, value_back, seg_back = (
        lax.all_gather(keys, "blk", axis=1, tiled=True),
        lax.all_gather(values, "blk", axis=1, tiled=True),
        lax.all_gather(segment_ids, "blk", axis=1, tiled=True),
    )
    k_back, v_back, sk_back = key_groups(key_back, value_back, seg_back)
    start = jnp.zeros((heads, block, length), jnp.float32)

    def attend_back(carry, parts):
        q_part, k_part, v_part, sq_part, sk_part, total, d_mixed = parts
        probs, grad_probs = score_grads(
            q_part, k_part, v_part, bias, sq_part, sk_part, total, d_mixed
        )
        center = jnp.sum(probs * grad_probs, axis=-1, keepdims=True)
        grad_scores = (probs * (grad_probs - center)).astype(jnp.bfloat16)
        grad_q = jnp.einsum(
            "bhqk,bkhd->bqhd", grad_scores, k_part, preferred_element_type=jnp.float32
        ).astype(jnp.bfloat16)
        grad_k = jnp.einsum(
            "bhqk,bqhd->bkhd", grad_scores, q_part, preferred_element_type=jnp.float32
        )
        grad_v = jnp.einsum(
            "bhqk,bqhd->bkhd",
            probs.astype(jnp.bfloat16),
            d_mixed,
            preferred_element_type=jnp.float32,
        )
        paired = jnp.stack([grad_k, grad_v], axis=2).reshape(group, length, 2, inner)
        return (carry + jnp.sum(grad_scores.astype(jnp.float32), axis=0), (grad_q, paired))

    bias_grad, (grad_query, paired) = lax.scan(
        attend_back, start, (q_groups, k_back, v_back, seg_query, sk_back, log_totals, grad_att)
    )
    paired = paired.reshape(rows, length, 2, inner)
    kv_grad = lax.psum_scatter(paired, "blk", scatter_dimension=1, tiled=True).astype(jnp.bfloat16)
    grad_key = kv_grad[:, :, 0].reshape(rows * block, inner)
    grad_value = kv_grad[:, :, 1].reshape(rows * block, inner)
    grad_query = grad_query.reshape(rows * block, inner)
    grad_wq = outer_sum(low_one, grad_query)
    grad_wk = outer_sum(low_one, grad_key)
    grad_wv = outer_sum(low_one, grad_value)
    grad_low_one = (
        times_t(grad_query, w_query) + times_t(grad_key, w_key) + times_t(grad_value, w_value)
    )
    back_one, grad_gain_one = rms_backward(grad_low_one, normed_one, scale_one, gain_one)
    grad_tokens = (grad_hidden + back_one).astype(jnp.bfloat16).reshape(rows, block, width)
    grad_table = jnp.einsum("hqk,nqk->nh", bias_grad, onehot, precision=lax.Precision.HIGHEST)
    grads = (
        grad_gain_one,
        grad_wq,
        grad_wk,
        grad_wv,
        grad_wout,
        grad_gain_two,
        grad_in,
        grad_down,
        grad_table,
    )
    pieces = (
        lax.psum_scatter(grads[0], "blk", scatter_dimension=0, tiled=True),
        lax.psum_scatter(grads[1], "blk", scatter_dimension=0, tiled=True),
        lax.psum_scatter(grads[2], "blk", scatter_dimension=0, tiled=True),
        lax.psum_scatter(grads[3], "blk", scatter_dimension=0, tiled=True),
        lax.psum_scatter(grads[4], "blk", scatter_dimension=0, tiled=True),
        lax.psum_scatter(grads[5], "blk", scatter_dimension=0, tiled=True),
        lax.psum_scatter(grads[6], "blk", scatter_dimension=0, tiled=True),
        lax.psum_scatter(grads[7], "blk", scatter_dimension=0, tiled=True),
        lax.psum_scatter(grads[8], "blk", scatter_dimension=0, tiled=True),
    )
    shares = lax.psum(
        (
            pieces[0],
            pieces[1],
            pieces[2],
            pieces[3],
            pieces[4],
            pieces[5],
            pieces[6],
            pieces[7],
            pieces[8],
        ),
        "dp",
    )
    return (
        output.reshape(rows, block, width),
        grad_tokens,
        shares[0],
        shares[1],
        shares[2],
        shares[3],
        shares[4],
        shares[5],
        shares[6],
        shares[7],
        shares[8],
    )


BF = jnp.bfloat16
F32 = jnp.float32
MESH = pl.DeviceIdType.MESH
VLIMIT = 60 * 1024 * 1024
TILE = 128
REACH = 511


def mm(a, b):
    return lax.dot_general(a, b, (((1,), (0,)), ((), ())), preferred_element_type=F32)


def mm_nt(a, b):
    return lax.dot_general(a, b, (((1,), (1,)), ((), ())), preferred_element_type=F32)


def mm_tn(a, b):
    return lax.dot_general(a, b, (((0,), (0,)), ((), ())), preferred_element_type=F32)


def iota(shape, dim):
    return lax.broadcasted_iota(jnp.int32, shape, dim)


def spot():
    blk = lax.axis_index("blk")
    return lax.axis_index("dp"), blk // 2, blk % 2


def gather_kernel(nz, tok, dy, seg, xrow, dyrow, segall, zero, segbuf, s_sem, r_sem, l_sem):
    dp, z, c = spot()
    blk = 2 * z + c
    block = tok.shape[1]
    nb = 2 * nz
    barrier = pltpu.get_barrier_semaphore()
    for k in range(1, nb):
        pl.semaphore_signal(
            barrier, inc=1, device_id=(dp, lax.rem(blk + k, nb)), device_id_type=MESH
        )
    pl.semaphore_wait(barrier, nb - 1)

    def copy(src, dst, send, recv, zz, cc):
        return pltpu.make_async_remote_copy(
            src, dst, s_sem.at[send], r_sem.at[recv], device_id=(dp, 2 * zz + cc), device_id_type=MESH
        )

    mine = xrow.at[blk]
    for hop, dz in ((0, 1), (1, -1)):

        @pl.when((z + dz >= 0) & (z + dz < nz))
        def _():
            copy(tok.at[1 - c], mine, 2 * hop, blk, z + dz, 1 - c).start()
            copy(tok.at[c], mine, 2 * hop + 1, blk, z + dz, c).start()

    copy(tok.at[1 - c], mine, 4, blk, z, 1 - c).start()
    copy(dy.at[1 - c], dyrow.at[c], 5, nb, z, 1 - c).start()
    segbuf[...] = jnp.zeros_like(segbuf)
    segbuf[0:2, :] = seg[...]
    for k in range(1, nb):
        to = lax.rem(blk + k, nb)
        pltpu.make_async_remote_copy(
            segbuf,
            segall.at[blk],
            s_sem.at[10 + k],
            r_sem.at[nb + 1 + blk],
            device_id=(dp, to),
            device_id_type=MESH,
        ).start()
    segall[blk] = segbuf[...]
    own = pltpu.make_async_copy(tok.at[c], mine, l_sem.at[0])
    own.start()
    own_dy = pltpu.make_async_copy(dy.at[c], dyrow.at[c], l_sem.at[1])
    own_dy.start()

    reach = -(-REACH // (2 * block))
    for b in range(nb):

        @pl.when(jnp.abs(b // 2 - z) > reach)
        def _():
            xrow[b] = jnp.zeros(xrow.shape[1:], xrow.dtype)

    def arrived(b):
        copy(tok.at[0], xrow.at[b], 0, b, z, 1 - c).wait_recv()

    for far in range(1, reach + 1):
        for way, dz in ((0, 1), (1, -1)):
            src = z - dz * far

            @pl.when((src >= 0) & (src < nz))
            def _():
                for h in range(2):
                    arrived(2 * src + h)
                    if far < reach:

                        @pl.when((z + dz >= 0) & (z + dz < nz))
                        def _():
                            copy(
                                xrow.at[2 * src + h],
                                xrow.at[2 * src + h],
                                6 + 2 * way + h,
                                2 * src + h,
                                z + dz,
                                c,
                            ).start()

    arrived(2 * z + 1 - c)
    copy(dy.at[0], dyrow.at[1 - c], 0, nb, z, 1 - c).wait_recv()
    for k in range(1, nb):
        frm = lax.rem(blk + nb - k, nb)
        copy(segbuf, segall.at[frm], 0, nb + 1 + frm, z, 1 - c).wait_recv()
    own.wait()
    own_dy.wait()
    for hop, dz in ((0, 1), (1, -1)):

        @pl.when((z + dz >= 0) & (z + dz < nz))
        def _():
            copy(tok.at[0], mine, 2 * hop, blk, z, 1 - c).wait_send()
            copy(tok.at[0], mine, 2 * hop + 1, blk, z, 1 - c).wait_send()

        for far in range(1, reach):
            src = z - dz * far

            @pl.when((src >= 0) & (src < nz) & (z + dz >= 0) & (z + dz < nz))
            def _():
                for h in range(2):
                    copy(tok.at[0], mine, 6 + 2 * hop + h, blk, z, 1 - c).wait_send()

    copy(tok.at[0], mine, 4, blk, z, 1 - c).wait_send()
    copy(dy.at[0], dyrow.at[0], 5, nb, z, 1 - c).wait_send()
    for k in range(1, nb):
        copy(segbuf, segall.at[0], 10 + k, nb + 1, z, 1 - c).wait_send()


def gather(nz, tok, dy, seg):
    _, block, width = tok.shape
    nb = 2 * nz
    vm = pl.BlockSpec(memory_space=pltpu.VMEM)
    return pl.pallas_call(
        functools.partial(gather_kernel, nz),
        out_shape=(
            jax.ShapeDtypeStruct((nb, block, width), BF),
            jax.ShapeDtypeStruct((2, block, width), BF),
            jax.ShapeDtypeStruct((nb, 8, block), jnp.int32),
        ),
        in_specs=[vm] * 3,
        out_specs=(vm, vm, vm),
        scratch_shapes=[
            pltpu.VMEM((8, 128), F32),
            pltpu.VMEM((8, block), jnp.int32),
            pltpu.SemaphoreType.DMA((10 + nb,)),
            pltpu.SemaphoreType.DMA((2 * nb + 2,)),
            pltpu.SemaphoreType.DMA((2,)),
        ],
        compiler_params=pltpu.CompilerParams(
            collective_id=1, has_side_effects=True, vmem_limit_bytes=VLIMIT
        ),
    )(tok, dy, seg)


def norm_rows(x, gain):
    x = x.astype(F32)
    scale = lax.rsqrt(jnp.mean(x * x, axis=-1, keepdims=True) + EPS)
    normed = x * scale
    return normed, scale, (normed * gain).astype(BF)


def prepare_bias(table_ref, near, heads):
    buckets = table_ref.shape[0]
    for d in range(3):
        lane = iota((buckets, 2 * TILE), 1)
        back = jnp.where(lane < TILE, lane, lane - 2 * TILE)
        hot = (bucket_of((d - 1) * TILE - back) == iota((buckets, 2 * TILE), 0)).astype(BF)
        strip = mm_tn(table_ref[...], hot)
        for h in range(heads):
            row = jnp.broadcast_to(strip[h : h + 1, :], (TILE, 2 * TILE))
            near[h, d] = pltpu.roll(row, 0, 1, stride=1, stride_axis=0)[:, :TILE]


def prepare_masks(segall, kaug, qseg, qright, qleft, z, c, tq):
    nkb = kaug.shape[0] // TILE
    for b in range(nkb):
        row = segall[b, pl.ds(c, 1), :]
        r = iota((TILE, TILE), 0)
        hot = jnp.where((r == row) | (r == 8 + b), 1.0, 0.0).astype(F32)
        kaug[b * TILE : (b + 1) * TILE, :] = hot.T.astype(BF)
    for i in range(tq // TILE):
        qb = (tq // TILE) * z + i
        row = segall[qb, pl.ds(c, 1), :]
        r = iota((TILE, TILE), 0)
        lost = jnp.where((r < 8) & (r != row), NEG, 0.0).astype(F32)
        qseg[i * TILE : (i + 1) * TILE, :] = lost.T
        col = iota((TILE, TILE), 1) - 8
        ok = (col >= 0) & (col < nkb)
        qright[i * TILE : (i + 1) * TILE, :] = jnp.where(ok & (col >= qb + 2), 1.0, 0.0)
        qleft[i * TILE : (i + 1) * TILE, :] = jnp.where(ok & (col <= qb - 2), 1.0, 0.0)


def stacked(ref, cols, dst, tq):
    part = ref[:, cols].astype(F32)
    low = iota((tq, TILE), 1) < TILE // 2
    dst[0:tq, 0:TILE] = jnp.where(low, part, 0.0).astype(BF)
    dst[tq : 2 * tq, 0:TILE] = jnp.where(low, 0.0, part).astype(BF)


def attn_forward_pair(p, z, q, k, v, kaug, qseg, qright, qleft, near, ts, probs, att, qa, s):
    tq = q.shape[0]
    length = k.shape[0]
    nkb = length // TILE
    cols = pl.ds(pl.multiple_of(p * TILE, TILE), TILE)
    stacked(q, cols, qa, tq)
    for hh in range(2):
        far = ts[31, 2 * p + hh] * qright[...] + ts[15, 2 * p + hh] * qleft[...] + qseg[...]
        qa[hh * tq : (hh + 1) * tq, TILE:] = far.astype(BF)

    def score(rb, carry):
        rows = pl.ds(pl.multiple_of(rb * TILE, TILE), TILE)
        left = jnp.concatenate([k[rows, cols], kaug[rows, :]], axis=1)
        s[pl.ds(pl.multiple_of((rb + 1) * TILE, TILE), TILE), :] = mm_nt(left, qa[...])
        return carry

    lax.fori_loop(0, nkb, score, 0)
    for i in range(tq // TILE):
        for d in range(3):
            row = ((tq // TILE) * z + i + d) * TILE
            rows = pl.ds(pl.multiple_of(row, TILE), TILE)
            for hh in range(2):
                at = hh * tq + i * TILE
                s[rows, at : at + TILE] = s[rows, at : at + TILE] + near[2 * p + hh, d]

    def top(rb, best):
        rows = pl.ds(pl.multiple_of((rb + 1) * TILE, TILE), TILE)
        return jnp.maximum(best, jnp.max(s[rows, :].reshape(TILE // 8, 8, 2 * tq), axis=0))

    best = lax.fori_loop(0, nkb, top, jnp.full((8, 2 * tq), -3e38, F32))
    best = jnp.max(best, axis=0, keepdims=True)

    def expo(rb, total):
        rows = pl.ds(pl.multiple_of((rb + 1) * TILE, TILE), TILE)
        e = jnp.exp(s[rows, :] - best)
        s[rows, :] = e
        return total + jnp.sum(e.reshape(TILE // 8, 8, 2 * tq), axis=0)

    total = lax.fori_loop(0, nkb, expo, jnp.zeros((8, 2 * tq), F32))
    inverse = 1.0 / jnp.sum(total, axis=0, keepdims=True)

    def finish(rb, carry):
        rows = pl.ds(pl.multiple_of(rb * TILE, TILE), TILE)
        at = pl.ds(pl.multiple_of((rb + 1) * TILE, TILE), TILE)
        probs[p, rows, :] = (s[at, :] * inverse).astype(BF)
        return carry

    lax.fori_loop(0, nkb, finish, 0)
    mixed = mm_tn(v[:, cols], probs[p])
    both = jnp.concatenate([mixed[: TILE // 2, :tq], mixed[TILE // 2 :, tq:]], axis=0)
    att[:, cols] = both.T.astype(BF)


def forward_kernel(
    xrow, segall, gain, wq, wk, wv, table, ts, n1, k, v, q, probs, att,
    kaug, qseg, qright, qleft, near, qa, s,
):
    _, z, c = spot()
    nb, block, _ = xrow.shape
    tq = 2 * block
    g = gain[...].astype(F32)
    prepare_bias(table, near, 2 * probs.shape[0])
    prepare_masks(segall, kaug, qseg, qright, qleft, z, c, tq)
    for b in range(nb // 2):
        rows = slice(b * tq, (b + 1) * tq)
        part = xrow[2 * b : 2 * b + 2].reshape(tq, xrow.shape[2])
        n1[rows, :] = norm_rows(part, g)[2]
        k[rows, :] = mm(n1[rows, :], wk[...]).astype(BF)
        v[rows, :] = mm(n1[rows, :], wv[...]).astype(BF)
    own = n1[pl.ds(pl.multiple_of(z * tq, tq), tq), :]
    q[...] = mm(own, wq[...]).astype(BF)
    s[0:TILE, :] = jnp.zeros((TILE, s.shape[1]), F32)
    s[s.shape[0] - TILE :, :] = jnp.zeros((TILE, s.shape[1]), F32)

    def pair(p, carry):
        attn_forward_pair(p, z, q, k, v, kaug, qseg, qright, qleft, near, ts, probs, att, qa, s)
        return carry

    lax.fori_loop(0, probs.shape[0], pair, 0)


def forward(xrow, segall, gain, wq, wk, wv, table):
    nb, block, width = xrow.shape
    length, tq = nb * block, 2 * block
    inner = wq.shape[1]
    heads = table.shape[1]
    pairs = heads // 2
    vm = pl.BlockSpec(memory_space=pltpu.VMEM)
    sm = pl.BlockSpec(memory_space=pltpu.SMEM)
    return pl.pallas_call(
        forward_kernel,
        out_shape=(
            jax.ShapeDtypeStruct((length, width), BF),
            jax.ShapeDtypeStruct((length, inner), BF),
            jax.ShapeDtypeStruct((length, inner), BF),
            jax.ShapeDtypeStruct((tq, inner), BF),
            jax.ShapeDtypeStruct((pairs, length, 2 * tq), BF),
            jax.ShapeDtypeStruct((tq, inner), BF),
        ),
        in_specs=[vm] * 7 + [sm],
        out_specs=(vm,) * 6,
        scratch_shapes=[
            pltpu.VMEM((length, TILE), BF),
            pltpu.VMEM((tq, TILE), F32),
            pltpu.VMEM((tq, TILE), F32),
            pltpu.VMEM((tq, TILE), F32),
            pltpu.VMEM((heads, 3, TILE, TILE), F32),
            pltpu.VMEM((2 * tq, 2 * TILE), BF),
            pltpu.VMEM((length + 2 * TILE, 2 * tq), F32),
        ],
        compiler_params=pltpu.CompilerParams(vmem_limit_bytes=VLIMIT),
    )(xrow, segall, gain, wq, wk, wv, table, table.astype(F32))


def ffn_kernel(
    xown, att, dy, gain, wout, win, wdown, out, dh, datt, pdown, pin, pout, gfin,
    n2, act, slope,
):
    tq, width = att.shape[0], wout.shape[1]
    inner = win.shape[1]
    nb = pdown.shape[0]
    wide = width
    steps = inner // wide
    g = gain[...].astype(F32)
    h = xown[...].reshape(tq, width).astype(F32) + mm(att[...], wout[...])
    normed, scale, low = norm_rows(h, g)
    n2[...] = low
    d = dy[...].reshape(tq, width)
    total = h
    for j in range(steps):
        cols = slice(j * wide, (j + 1) * wide)
        value, slant = gelu_both(mm(n2[...], win[:, cols]))
        act[:, cols] = value.astype(BF)
        slope[:, cols] = slant
        total = total + mm(act[:, cols], wdown[cols, :])
    out[...] = total.astype(BF).reshape(out.shape)
    per = inner // nb
    quarters = pdown.shape[1]
    for j in range(steps):
        cols = slice(j * wide, (j + 1) * wide)
        grad = mm_tn(act[:, cols], d).astype(BF)
        count = wide // per
        pdown[j * count : (j + 1) * count] = grad.reshape(count, quarters, per // quarters, width)
    dn2 = jnp.zeros((tq, width), F32)
    for j in range(steps):
        cols = slice(j * wide, (j + 1) * wide)
        dpre = (mm_nt(d, wdown[cols, :]) * slope[:, cols]).astype(BF)
        pin[:, j] = mm_tn(n2[...], dpre).astype(BF).reshape(nb, width // nb, wide)
        dn2 = dn2 + mm_nt(dpre, win[:, cols])
    back, gain_grad = rms_backward(dn2, normed, scale, g)
    gfin[...] = gain_grad[None]
    dhid = d.astype(F32) + back
    dh[...] = dhid
    dhl = dhid.astype(BF)
    pout[...] = mm_tn(att[...], dhl).astype(BF).reshape(nb, width // nb, width)
    datt[...] = mm_nt(dhl, wout[...]).astype(BF)


def ffn(xown, att, dy, gain, wout, win, wdown, nb, quarters):
    tq, width = att.shape[0], wout.shape[1]
    inner = win.shape[1]
    vm = pl.BlockSpec(memory_space=pltpu.VMEM)
    return pl.pallas_call(
        ffn_kernel,
        out_shape=(
            jax.ShapeDtypeStruct((2, tq // 2, width), BF),
            jax.ShapeDtypeStruct((tq, width), F32),
            jax.ShapeDtypeStruct((tq, att.shape[1]), BF),
            jax.ShapeDtypeStruct((nb, quarters, inner // nb // quarters, width), BF),
            jax.ShapeDtypeStruct((nb, quarters, width // nb, inner // quarters), BF),
            jax.ShapeDtypeStruct((nb, width // nb, width), BF),
            jax.ShapeDtypeStruct((1, width), F32),
        ),
        in_specs=[vm] * 7,
        out_specs=(vm,) * 7,
        scratch_shapes=[
            pltpu.VMEM((tq, width), BF),
            pltpu.VMEM((tq, inner), BF),
            pltpu.VMEM((tq, inner), F32),
        ],
        compiler_params=pltpu.CompilerParams(vmem_limit_bytes=VLIMIT),
    )(xown, att, dy, gain, wout, win, wdown)


def attn_backward_pair(p, z, q, k, v, kaug, datt, probs, dk, dv, dq, near, far, qm, dm, dprob, ds):
    tq = q.shape[0]
    length = k.shape[0]
    nkb = length // TILE
    cols = pl.ds(pl.multiple_of(p * TILE, TILE), TILE)
    stacked(q, cols, qm, tq)
    stacked(datt, cols, dm, tq)

    def first(rb, total):
        rows = pl.ds(pl.multiple_of(rb * TILE, TILE), TILE)
        part = mm_nt(v[rows, cols], dm[...])
        dprob[rows, :] = part
        mixed = part * probs[p, rows, :].astype(F32)
        dv[rows, cols] = mm(probs[p, rows, :], dm[...]).astype(BF)
        return total + jnp.sum(mixed.reshape(TILE // 8, 8, 2 * tq), axis=0)

    total = lax.fori_loop(0, nkb, first, jnp.zeros((8, 2 * tq), F32))
    center = jnp.sum(total, axis=0, keepdims=True)

    def second(rb, carry):
        rows = pl.ds(pl.multiple_of(rb * TILE, TILE), TILE)
        at = pl.ds(pl.multiple_of((rb + 1) * TILE, TILE), TILE)
        part = (probs[p, rows, :].astype(F32) * (dprob[rows, :] - center)).astype(BF)
        ds[at, :] = part
        dk[rows, cols] = mm(part, qm[...]).astype(BF)
        return carry

    lax.fori_loop(0, nkb, second, 0)
    left = jnp.concatenate([k[:, cols], kaug[...]], axis=1)
    back = mm_tn(left, ds[TILE : TILE + length, :])
    both = jnp.concatenate([back[: TILE // 2, :tq], back[TILE // 2 : TILE, tq:]], axis=0)
    dq[:, cols] = both.T.astype(BF)
    sums = back[TILE + 8 : TILE + 8 + nkb, :]
    kb = iota((nkb, 2 * tq), 0)
    lane = iota((nkb, 2 * tq), 1)
    qb = (tq // TILE) * z + (lane % tq) // TILE
    far[0, pl.ds(p, 1), :] = jnp.sum(jnp.where(kb >= qb + 2, sums, 0.0), axis=0, keepdims=True)
    far[1, pl.ds(p, 1), :] = jnp.sum(jnp.where(kb <= qb - 2, sums, 0.0), axis=0, keepdims=True)
    for hh in range(2):
        for d in range(3):
            acc = jnp.zeros((TILE, TILE), F32)
            for i in range(tq // TILE):
                row = ((tq // TILE) * z + i + d) * TILE
                at = hh * tq + i * TILE
                acc = acc + ds[pl.ds(pl.multiple_of(row, TILE), TILE), at : at + TILE].astype(F32)
            near[2 * p + hh, d] = acc


def table_sums(near, far, rows, small, first_row, tq):
    heads = near.shape[0]
    rows[...] = jnp.zeros_like(rows)
    for d in range(3):
        offset = (d - 1) * TILE + iota((TILE, TILE), 0) - iota((TILE, TILE), 1)
        bucket = bucket_of(offset)
        for b in range(32):
            if (d == 0 and b >= 16) or (d == 2 and b < 16):
                continue
            hit = bucket == b

            def one(h, carry):
                part = jnp.where(hit, near[h, d], 0.0)
                part = jnp.sum(part.reshape(TILE // 8, 8, TILE), axis=0)
                rows[pl.ds(h, 1), b, :] = rows[pl.ds(h, 1), b, :] + jnp.sum(part, axis=0, keepdims=True)
                return carry

            lax.fori_loop(0, heads, one, 0)
    for h in range(heads):
        p, hh = h // 2, h % 2
        for side, b in ((0, 31), (1, 15)):
            line = far[side, p : p + 1, hh * tq : (hh + 1) * tq]
            for i in range(tq // TILE):
                rows[h, b : b + 1, :] = rows[h, b : b + 1, :] + line[:, i * TILE : (i + 1) * TILE]
    for part in range(heads * 32 // TILE):
        per = TILE // 32
        square = rows[part * per : (part + 1) * per].reshape(TILE, TILE)
        small[first_row + part : first_row + part + 1, :] = jnp.sum(square.T, axis=0, keepdims=True)


def backward_kernel(
    xrow, segall, gain, wq, wk, wv, n1, q, k, v, probs, datt, gfin, pout, dpart, dqpart, pqkv, small,
    kaug, dk, dv, dq, near, far, qm, dm, dprob, ds, rows,
):
    _, z, c = spot()
    tq = q.shape[0]
    length = k.shape[0]
    width = n1.shape[1]
    nkb = length // TILE
    nb = pqkv.shape[0]
    for b in range(nkb):
        lane = iota((TILE, TILE), 1)
        kaug[b * TILE : (b + 1) * TILE, :] = jnp.where(lane == 8 + b, 1.0, 0.0).astype(BF)
    ds[0:TILE, :] = jnp.zeros((TILE, ds.shape[1]), BF)
    ds[ds.shape[0] - TILE :, :] = jnp.zeros((TILE, ds.shape[1]), BF)

    def pair(p, carry):
        attn_backward_pair(
            p, z, q, k, v, kaug, datt, probs, dk, dv, dq, near, far, qm, dm, dprob, ds
        )
        return carry

    lax.fori_loop(0, probs.shape[0], pair, 0)
    g = gain[...].astype(F32)
    pqkv[:, 3] = pout[...]
    for i, (left, right) in enumerate(
        ((n1[pl.ds(pl.multiple_of(z * tq, tq), tq), :], dq), (n1[...], dk), (n1[...], dv))
    ):
        pqkv[:, i] = mm_tn(left, right[...]).astype(BF).reshape(nb, width // nb, right.shape[1])
    gain_sum = jnp.zeros((1, width), F32)
    for b in range(length // tq):
        rows_b = slice(b * tq, (b + 1) * tq)
        part = mm_nt(dk[rows_b, :], wk[...]) + mm_nt(dv[rows_b, :], wv[...])
        dpart[b] = part.astype(BF)
        normed = norm_rows(xrow[2 * b : 2 * b + 2].reshape(tq, width), g)[0]
        gain_sum = gain_sum + jnp.sum(part * normed, axis=0, keepdims=True)

        @pl.when(b == z)
        def _():
            dqpart[...] = part

    own = mm_nt(dq[...], wq[...])
    dqpart[...] = dqpart[...] + own
    normed = norm_rows(xrow[pl.ds(2 * z, 2)].reshape(tq, width), g)[0]
    gain_sum = gain_sum + jnp.sum(own * normed, axis=0, keepdims=True)
    small[...] = jnp.zeros_like(small)
    lines = width // TILE
    for i in range(lines):
        small[i : i + 1, :] = gain_sum[:, i * TILE : (i + 1) * TILE]
        small[lines + i : lines + i + 1, :] = gfin[:, i * TILE : (i + 1) * TILE]
    table_sums(near, far, rows, small, 2 * lines, tq)


def backward(xrow, segall, gain, wq, wk, wv, n1, q, k, v, probs, datt, gfin, pout):
    nb, block, width = xrow.shape
    length, tq = nb * block, 2 * block
    inner = wq.shape[1]
    pairs = probs.shape[0]
    vm = pl.BlockSpec(memory_space=pltpu.VMEM)
    return pl.pallas_call(
        backward_kernel,
        out_shape=(
            jax.ShapeDtypeStruct((length // tq, tq, width), BF),
            jax.ShapeDtypeStruct((tq, width), F32),
            jax.ShapeDtypeStruct((nb, 4, width // nb, inner), BF),
            jax.ShapeDtypeStruct((16, TILE), F32),
        ),
        in_specs=[vm] * 14,
        out_specs=(vm,) * 4,
        scratch_shapes=[
            pltpu.VMEM((length, TILE), BF),
            pltpu.VMEM((length, inner), BF),
            pltpu.VMEM((length, inner), BF),
            pltpu.VMEM((tq, inner), BF),
            pltpu.VMEM((2 * pairs, 3, TILE, TILE), F32),
            pltpu.VMEM((2, 8, 2 * tq), F32),
            pltpu.VMEM((2 * tq, TILE), BF),
            pltpu.VMEM((2 * tq, TILE), BF),
            pltpu.VMEM((length, 2 * tq), F32),
            pltpu.VMEM((length + 2 * TILE, 2 * tq), BF),
            pltpu.VMEM((2 * pairs, 32, TILE), F32),
        ],
        compiler_params=pltpu.CompilerParams(vmem_limit_bytes=VLIMIT),
    )(xrow, segall, gain, wq, wk, wv, n1, q, k, v, probs, datt, gfin, pout)


class Sums:
    UNITS = ("down", "in", "attn")

    def __init__(self, nz, bufs, s_sem, r_sem):
        self.nz = nz
        self.dp, self.z, self.c = spot()
        self.bufs, self.s_sem, self.r_sem = bufs, s_sem, r_sem
        x, y = self.dp % 2, self.dp // 2
        c = self.c
        self.f, self.g = 1 + c, 2 - c
        self.s1 = (1 - c) * x + c * y
        self.s2 = (1 - c) * y + c * x
        self.peer1 = self.dp + self.f * (1 - 2 * self.s1)
        self.peer2 = self.dp + self.g * (1 - 2 * self.s2)
        self.count = 0
        self.table = {}
        self.pending = []

    def sem(self, key):
        if key not in self.table:
            self.table[key] = self.count
            self.count += 1
        return self.table[key]

    def copy(self, src, dst, key, dp=None, z=None, c=None):
        n = self.sem(key)
        dp = self.dp if dp is None else dp
        z = self.z if z is None else z
        c = self.c if c is None else c
        return pltpu.make_async_remote_copy(
            src, dst, self.s_sem.at[n], self.r_sem.at[n], device_id=(dp, 2 * z + c), device_id_type=MESH
        )

    def start(self, src, dst, key, **to):
        op = self.copy(src, dst, key, **to)
        op.start()
        self.pending.append(op)

    def drain(self):
        for op in self.pending:
            op.wait_send()
        self.pending = []

    def q(self, i1, i2):
        return i1 * self.f + i2 * self.g

    def a_start(self, u, zs=None):
        b = self.bufs[u]
        for zz in range(self.nz) if zs is None else zs:
            self.start(b["pb"].at[2 * zz + 1 - self.c], b["ra"].at[zz], (u, "a", zz), c=1 - self.c)

    def a_finish(self, u, zz):
        b = self.bufs[u]
        self.copy(b["pb"].at[0], b["ra"].at[zz], (u, "a", zz), c=1 - self.c).wait_recv()

        def one(q, carry):
            b["ra"][zz, q] = (b["ra"][zz, q].astype(F32) + b["pb"][2 * zz + self.c, q].astype(F32)).astype(BF)
            return carry

        lax.fori_loop(0, 4, one, 0)

    def first_start(self, u, zz):
        b = self.bufs[u]
        for i2 in range(2):
            self.start(
                b["ra"].at[zz, self.q(1 - self.s1, i2)], b["r1"].at[zz, i2], (u, "1", zz, i2), dp=self.peer1
            )

    def first_finish(self, u, zz):
        b = self.bufs[u]
        for i2 in range(2):
            self.copy(b["ra"].at[0, 0], b["r1"].at[zz, i2], (u, "1", zz, i2)).wait_recv()
            b["r1"][zz, i2] = (
                b["r1"][zz, i2].astype(F32) + b["ra"][zz, self.q(self.s1, i2)].astype(F32)
            ).astype(BF)

    def second_start(self, u, zz):
        b = self.bufs[u]
        self.start(b["r1"].at[zz, 1 - self.s2], b["r2"].at[zz], (u, "2", zz), dp=self.peer2)

    def second_finish(self, u, zz):
        b = self.bufs[u]
        self.copy(b["r1"].at[0, 0], b["r2"].at[zz], (u, "2", zz)).wait_recv()
        b["r2"][zz] = (b["r2"][zz].astype(F32) + b["r1"][zz, self.s2].astype(F32)).astype(BF)

    def z_start(self, u, name):
        b = self.bufs[u]
        for dz in range(1, self.nz):
            to = lax.rem(self.z + dz, self.nz)
            self.start(b[name].at[to], b["rz"].at[self.nz - 1 - dz], (u, "z", self.nz - 1 - dz), z=to)

    def z_wait(self, u, name):
        b = self.bufs[u]
        for slot in range(self.nz - 1):
            self.copy(b[name].at[0], b["rz"].at[slot], (u, "z", slot)).wait_recv()

    def z_finish_last(self, u):
        self.z_wait(u, "r2")
        b = self.bufs[u]
        total = b["r2"][self.z].astype(F32)
        for slot in range(self.nz - 1):
            total = total + b["rz"][slot].astype(F32)
        b["g"][self.dp] = total.astype(BF)

    def z_finish_mid(self, u):
        self.z_wait(u, "r1")
        b = self.bufs[u]
        for i2 in range(2):
            total = b["r1"][self.z, i2].astype(F32)
            for slot in range(self.nz - 1):
                total = total + b["rz"][slot, i2].astype(F32)
            b["r1"][self.z, i2] = total.astype(BF)

    def second_last_start(self, u):
        b = self.bufs[u]
        self.start(b["r1"].at[self.z, 1 - self.s2], b["r2"].at[0], (u, "2", 0), dp=self.peer2)

    def second_last_finish(self, u):
        b = self.bufs[u]
        self.copy(b["r1"].at[0, 0], b["r2"].at[0], (u, "2", 0)).wait_recv()
        total = b["r2"][0].astype(F32) + b["r1"][self.z, self.s2].astype(F32)
        b["g"][self.dp] = total.astype(BF)

    def spread_start(self, u):
        b = self.bufs[u]
        for k in range(1, 4):
            self.start(
                b["g"].at[self.dp], b["g"].at[self.dp], (u, "g", 3 - k), dp=lax.rem(self.dp + k, 4)
            )

    def spread_finish(self, u):
        b = self.bufs[u]
        for k in range(1, 4):
            self.copy(b["g"].at[0], b["g"].at[lax.rem(self.dp + k, 4)], (u, "g", 3 - (4 - k))).wait_recv()


def unit_scratch(nz, share, width, order):
    block = (share, width)
    return {
        "ra": pltpu.VMEM((nz, 4) + block, BF),
        "r1": pltpu.VMEM((nz, 2) + block, BF),
        "r2": pltpu.VMEM(((nz,) if order == "xyz" else (1,)) + block, BF),
        "rz": pltpu.VMEM((nz - 1,) + (() if order == "xyz" else (2,)) + block, BF),
        "g": pltpu.VMEM((4,) + block, BF),
    }


def reduce_kernel(nz, names, *refs):
    pdown, pin, pattn, small, dpart, dqpart, xown, dh, gain, out_own = refs[:10]
    o_out, o_gt, o_down, o_in, o_q, o_k, o_v, o_o, o_small = refs[10:19]
    scr = list(refs[19:])
    bufs = {}
    for u, part in (("down", pdown), ("in", pin), ("attn", pattn)):
        bufs[u] = {"pb": part}
        for name in names:
            bufs[u][name] = scr.pop(0)
    rd, gt, sm, smr, s_sem, r_sem, l_sem = scr
    eng = Sums(nz, bufs, s_sem, r_sem)
    dp, z, c = eng.dp, eng.z, eng.c
    barrier = pltpu.get_barrier_semaphore()
    peers = [(dp, 2 * z + 1 - c)]
    peers += [(lax.rem(dp + k, 4), 2 * z + c) for k in range(1, 4)]
    peers += [(dp, 2 * lax.rem(z + k, nz) + c) for k in range(1, nz)]
    for peer in peers:
        pl.semaphore_signal(barrier, inc=1, device_id=peer, device_id_type=MESH)
    pl.semaphore_wait(barrier, len(peers))

    for u in Sums.UNITS:
        eng.a_start(u)
    tq, width = dqpart.shape
    reach = -(-REACH // tq)

    def near(other):
        return jnp.abs(other - z) <= reach

    for dz in range(1, nz):
        to = lax.rem(z + dz, nz)
        op = eng.copy(dpart.at[to], rd.at[nz - 1 - dz], ("d", nz - 1 - dz), z=to)

        @pl.when(near(to))
        def _():
            op.start()

    eng.start(out_own.at[1 - c], o_out.at[c], ("out",), c=1 - c)
    kept = pltpu.make_async_copy(out_own.at[c], o_out.at[c], l_sem.at[0])
    kept.start()

    hops = (dict(c=1 - c), dict(dp=dp + 1 - 2 * (dp % 2)), dict(dp=dp + 2 - 4 * (dp // 2)),
            dict(z=z + 1 - 2 * (z % 2)), dict(z=z + 2 - 4 * (z // 2)))
    sm[0] = small[...]

    def small_start(i):
        eng.start(sm.at[i], smr.at[i], ("s", i), **hops[i])

    def small_finish(i):
        eng.copy(sm.at[i], smr.at[i], ("s", i), **hops[i]).wait_recv()
        sm[i + 1] = sm[i] + smr[i]

    small_start(0)
    for zz in range(nz):
        eng.a_finish("down", zz)
        eng.first_start("down", zz)
    small_finish(0)
    small_start(1)
    for zz in range(nz):
        eng.a_finish("in", zz)
        eng.first_start("in", zz)
    for zz in range(nz):
        eng.a_finish("attn", zz)
        eng.first_start("attn", zz)
    small_finish(1)
    small_start(2)
    for zz in range(nz):
        eng.first_finish("down", zz)
    eng.z_start("down", "r1")
    for zz in range(nz):
        eng.first_finish("in", zz)
        eng.second_start("in", zz)
    small_finish(2)
    small_start(3)
    for zz in range(nz):
        eng.first_finish("attn", zz)
        eng.second_start("attn", zz)
    eng.z_finish_mid("down")
    eng.second_last_start("down")
    for zz in range(nz):
        eng.second_finish("in", zz)
    eng.z_start("in", "r2")
    small_finish(3)
    small_start(4)
    eng.second_last_finish("down")
    eng.spread_start("down")
    for zz in range(nz):
        eng.second_finish("attn", zz)
    eng.z_start("attn", "r2")
    eng.z_finish_last("in")
    eng.spread_start("in")

    for slot in range(nz - 1):
        src = lax.rem(z + slot + 1, nz)

        @pl.when(near(src))
        def _():
            eng.copy(dpart.at[0], rd.at[slot], ("d", slot)).wait_recv()

        @pl.when(jnp.logical_not(near(src)))
        def _():
            rd[slot] = jnp.zeros((tq, width), BF)

    g = gain[...].astype(F32)
    dn1 = dqpart[...]
    for slot in range(nz - 1):
        dn1 = dn1 + rd[slot].astype(F32)
    normed, scale, _ = norm_rows(xown[...].reshape(tq, width), g)
    back, _ = rms_backward(dn1, normed, scale, g)
    gt[...] = (dh[...] + back).astype(BF).reshape(gt.shape)
    eng.start(gt.at[1 - c], o_gt.at[c], ("gt",), c=1 - c)
    kept_gt = pltpu.make_async_copy(gt.at[c], o_gt.at[c], l_sem.at[1])
    kept_gt.start()

    eng.z_finish_last("attn")
    eng.spread_start("attn")
    small_finish(4)
    o_small[...] = sm[5]
    eng.spread_finish("down")
    o_down[...] = bufs["down"]["g"][...].astype(F32)
    eng.spread_finish("in")
    for j in range(4):
        o_in[:, j * width : (j + 1) * width] = bufs["in"]["g"][j].astype(F32)
    eng.spread_finish("attn")
    for j, ref in enumerate((o_q, o_k, o_v, o_o)):
        ref[...] = bufs["attn"]["g"][j].astype(F32)
    eng.copy(out_own.at[0], o_out.at[1 - c], ("out",)).wait_recv()
    eng.copy(gt.at[0], o_gt.at[1 - c], ("gt",)).wait_recv()
    kept.wait()
    kept_gt.wait()
    eng.drain()
    for dz in range(1, nz):
        to = lax.rem(z + dz, nz)

        @pl.when(near(to))
        def _():
            eng.copy(dpart.at[to], rd.at[nz - 1 - dz], ("d", nz - 1 - dz), z=to).wait_send()


def reduce(nz, pdown, pin, pattn, small, dpart, dqpart, xown, dh, gain, out_own):
    nb, _, share, width = pattn.shape
    tq = dqpart.shape[0]
    names = ("ra", "r1", "r2", "rz", "g")
    scratch = []
    for u in Sums.UNITS:
        bufs = unit_scratch(nz, share, width, "xzy" if u == "down" else "xyz")
        scratch += [bufs[name] for name in names]
    vm = pl.BlockSpec(memory_space=pltpu.VMEM)
    home = jax.ShapeDtypeStruct((2, tq // 2, width), BF)
    one = jax.ShapeDtypeStruct((share, width), F32)
    return pl.pallas_call(
        functools.partial(reduce_kernel, nz, names),
        out_shape=(
            home,
            home,
            jax.ShapeDtypeStruct((4, share, width), F32),
            jax.ShapeDtypeStruct((share, 4 * width), F32),
            one, one, one, one,
            jax.ShapeDtypeStruct(small.shape, F32),
        ),
        in_specs=[vm] * 10,
        out_specs=(vm,) * 9,
        scratch_shapes=scratch
        + [
            pltpu.VMEM((nz - 1, tq, width), BF),
            pltpu.VMEM((2, tq // 2, width), BF),
            pltpu.VMEM((6,) + small.shape, F32),
            pltpu.VMEM((5,) + small.shape, F32),
            pltpu.SemaphoreType.DMA((96,)),
            pltpu.SemaphoreType.DMA((96,)),
            pltpu.SemaphoreType.DMA((2,)),
        ],
        compiler_params=pltpu.CompilerParams(
            collective_id=2, has_side_effects=True, vmem_limit_bytes=VLIMIT
        ),
    )(pdown, pin, pattn, small, dpart, dqpart, xown, dh, gain, out_own)


def fast_device(
    nz, tokens, segment_ids, gain_attn, w_query, w_key, w_value, w_out, gain_ffn, w_in, w_down,
    rel_table, cotangent,
):
    rows, block, width = tokens.shape
    nb, quarters = 2 * nz, 4
    z, c = lax.axis_index("blk") // 2, lax.axis_index("blk") % 2
    xrow, dyrow, segall = gather(nz, tokens, cotangent, segment_ids)
    g1, g2 = gain_attn.reshape(1, width), gain_ffn.reshape(1, width)
    n1, k, v, q, probs, att = forward(xrow, segall, g1, w_query, w_key, w_value, rel_table)
    xown = lax.dynamic_slice_in_dim(xrow, 2 * z, 2, 0)
    out, dh, datt, pdown, pin, pout, gfin = ffn(
        xown, att, dyrow, g2, w_out, w_in, w_down, nb, quarters
    )
    dpart, dqpart, pattn, small = backward(
        xrow, segall, g1, w_query, w_key, w_value, n1, q, k, v, probs, datt, gfin, pout
    )
    out, grad_tokens, gdown, gin, gq, gk, gv, go, small = reduce(
        nz, pdown, pin, pattn, small, dpart, dqpart, xown, dh, g1, out
    )
    flat = small.reshape(-1)
    b = lax.axis_index("blk")
    share = width // nb
    ga = lax.dynamic_slice_in_dim(flat[:width], b * share, share)
    gf = lax.dynamic_slice_in_dim(flat[width : 2 * width], b * share, share)
    heads = rel_table.shape[1]
    gt = flat[2 * width : 2 * width + 32 * heads].reshape(heads, 32).T
    gt = lax.dynamic_slice_in_dim(gt, b * (32 // nb), 32 // nb)
    return (out, grad_tokens, ga, gq, gk, gv, go, gf, gin, gdown.reshape(-1, width), gt)


def pick(mesh):
    if mesh.shape["dp"] == 4 and mesh.shape["blk"] == 8:
        return functools.partial(fast_device, mesh.shape["blk"] // 2)
    return on_device


def solution(mesh):
    placed = (
        P("dp", "blk", None),
        P("dp", "blk"),
        P(),
        P(),
        P(),
        P(),
        P(),
        P(),
        P(),
        P(),
        P(),
        P("dp", "blk", None),
    )
    return jax.shard_map(
        pick(mesh),
        mesh=mesh,
        in_specs=placed,
        out_specs=(
            P("dp", "blk", None),
            P("dp", "blk", None),
            P("blk"),
            P("blk", None),
            P("blk", None),
            P("blk", None),
            P("blk", None),
            P("blk"),
            P("blk", None),
            P("blk", None),
            P("blk", None),
        ),
        check_vma=False,
    )
```

```python
import functools
import math

import jax
import jax.numpy as jnp
from jax import lax
from jax.experimental import pallas as pl
from jax.experimental.pallas import tpu as pltpu
from jax.sharding import PartitionSpec as P

EPS = 1e-06
NEG = -1e30
EDGES = (12, 16, 23, 32, 46, 64, 91)
ROOT_TWO_PI = 0.7978845608028654
CUBIC = 0.044715


def bucket_of(offset):
    distance = jnp.abs(offset)
    far_part = 8 + sum(((distance >= edge).astype(jnp.int32) for edge in EDGES))
    return jnp.where(offset > 0, 16, 0) + jnp.where(distance < 8, distance, far_part)


def gelu_both(values):
    inner_arg = ROOT_TWO_PI * (values + CUBIC * values * values * values)
    tangent = jnp.tanh(inner_arg)
    result = 0.5 * values * (1.0 + tangent)
    slope = 0.5 * (1.0 + tangent) + 0.5 * values * (1.0 - tangent * tangent) * ROOT_TWO_PI * (
        1.0 + 3.0 * CUBIC * values * values
    )
    return (result, slope)


def rms_forward(values, gain):
    scale = lax.rsqrt(jnp.mean(values * values, axis=-1, keepdims=True) + EPS)
    normed = values * scale
    return (normed, scale, (normed * gain).astype(jnp.bfloat16))


def rms_backward(grad, normed, scale, gain):
    gain_grad = jnp.sum(grad * normed, axis=0)
    inner_grad = grad * gain
    back = scale * (inner_grad - normed * jnp.mean(inner_grad * normed, axis=-1, keepdims=True))
    return (back, gain_grad)


def outer_sum(left, right):
    return jnp.einsum("td,tf->df", left, right, preferred_element_type=jnp.float32)


def times_t(left, right):
    return jnp.einsum("tf,df->td", left, right, preferred_element_type=jnp.float32)


def masked_scores(query, keys, bias, seg_query, seg_keys):
    raw = (
        jnp.einsum("bqhd,bkhd->bhqk", query, keys, preferred_element_type=jnp.float32) + bias[None]
    )
    same = seg_query[:, None, :, None] == seg_keys[:, None, None, :]
    return jnp.where(same, raw, NEG)


def score_grads(q_part, k_part, v_part, bias, sq_part, sk_part, total, d_mixed):
    scores = masked_scores(q_part, k_part, bias, sq_part, sk_part)
    probs = jnp.exp(scores - total[..., None])
    grad_probs = jnp.einsum("bqhd,bkhd->bhqk", d_mixed, v_part, preferred_element_type=jnp.float32)
    return (probs, grad_probs)


def on_device(
    tokens,
    segment_ids,
    gain_attn,
    w_query,
    w_key,
    w_value,
    w_out,
    gain_ffn,
    w_in,
    w_down,
    rel_table,
    cotangent,
):
    rows, block, width = tokens.shape
    buckets, heads = rel_table.shape
    inner = w_query.shape[1]
    head_dim = inner // heads
    length = block * lax.axis_size("blk")
    group = math.gcd(rows, max(1, 512 // block))
    blocks = rows // group
    gain_one = gain_attn.astype(jnp.float32)
    gain_two = gain_ffn.astype(jnp.float32)
    table_f = rel_table.astype(jnp.float32)
    flat = tokens.reshape(rows * block, width).astype(jnp.float32)
    normed_one, scale_one, low_one = rms_forward(flat, gain_one)

    def project(weight):
        return (
            jnp.dot(low_one, weight, preferred_element_type=jnp.float32)
            .astype(jnp.bfloat16)
            .reshape(rows, block, inner)
        )

    query, keys, values = (project(w_query), project(w_key), project(w_value))
    key_all, value_all, seg_all = (
        lax.all_gather(keys, "blk", axis=1, tiled=True),
        lax.all_gather(values, "blk", axis=1, tiled=True),
        lax.all_gather(segment_ids, "blk", axis=1, tiled=True),
    )
    places = lax.axis_index("blk") * block + jnp.arange(block, dtype=jnp.int32)
    offsets = jnp.arange(length, dtype=jnp.int32)[None, :] - places[:, None]
    onehot = (
        bucket_of(offsets)[None] == jnp.arange(buckets, dtype=jnp.int32)[:, None, None]
    ).astype(jnp.float32)
    bias = jnp.einsum("nqk,nh->hqk", onehot, table_f, precision=lax.Precision.HIGHEST)
    q_groups = query.reshape(blocks, group, block, heads, head_dim)
    seg_query = segment_ids.reshape(blocks, group, block)

    def key_groups(key_rows, value_rows, seg_rows):
        return (
            key_rows.reshape(blocks, group, length, heads, head_dim),
            value_rows.reshape(blocks, group, length, heads, head_dim),
            seg_rows.reshape(blocks, group, length),
        )

    k_groups, v_groups, seg_keys = key_groups(key_all, value_all, seg_all)

    def attend(parts):
        q_part, k_part, v_part, sq_part, sk_part = parts
        scores = masked_scores(q_part, k_part, bias, sq_part, sk_part)
        top = jnp.max(scores, axis=-1, keepdims=True)
        total = jnp.log(jnp.sum(jnp.exp(scores - top), axis=-1, keepdims=True)) + top
        probs = jnp.exp(scores - total).astype(jnp.bfloat16)
        mixed = jnp.einsum("bhqk,bkhd->bqhd", probs, v_part, preferred_element_type=jnp.float32)
        return (mixed.astype(jnp.bfloat16), total[..., 0])

    attended, log_totals = lax.map(attend, (q_groups, k_groups, v_groups, seg_query, seg_keys))
    attended_flat = attended.reshape(rows * block, inner)
    hidden = flat + jnp.dot(attended_flat, w_out, preferred_element_type=jnp.float32)
    normed_two, scale_two, low_two = rms_forward(hidden, gain_two)
    pre = jnp.dot(low_two, w_in, preferred_element_type=jnp.float32)
    gelu_value, gelu_slope = gelu_both(pre)
    active = gelu_value.astype(jnp.bfloat16)
    output = (hidden + jnp.dot(active, w_down, preferred_element_type=jnp.float32)).astype(
        jnp.bfloat16
    )
    grad_out = cotangent.reshape(rows * block, width)
    grad_down = outer_sum(active, grad_out)
    grad_pre = (times_t(grad_out, w_down) * gelu_slope).astype(jnp.bfloat16)
    grad_in = outer_sum(low_two, grad_pre)
    back_two, grad_gain_two = rms_backward(times_t(grad_pre, w_in), normed_two, scale_two, gain_two)
    grad_hidden = grad_out.astype(jnp.float32) + back_two
    grad_proj = grad_hidden.astype(jnp.bfloat16)
    grad_wout = outer_sum(attended_flat, grad_proj)
    grad_att = (
        times_t(grad_proj, w_out)
        .astype(jnp.bfloat16)
        .reshape(blocks, group, block, heads, head_dim)
    )
    key_back, value_back, seg_back = (
        lax.all_gather(keys, "blk", axis=1, tiled=True),
        lax.all_gather(values, "blk", axis=1, tiled=True),
        lax.all_gather(segment_ids, "blk", axis=1, tiled=True),
    )
    k_back, v_back, sk_back = key_groups(key_back, value_back, seg_back)
    start = jnp.zeros((heads, block, length), jnp.float32)

    def attend_back(carry, parts):
        q_part, k_part, v_part, sq_part, sk_part, total, d_mixed = parts
        probs, grad_probs = score_grads(
            q_part, k_part, v_part, bias, sq_part, sk_part, total, d_mixed
        )
        center = jnp.sum(probs * grad_probs, axis=-1, keepdims=True)
        grad_scores = (probs * (grad_probs - center)).astype(jnp.bfloat16)
        grad_q = jnp.einsum(
            "bhqk,bkhd->bqhd", grad_scores, k_part, preferred_element_type=jnp.float32
        ).astype(jnp.bfloat16)
        grad_k = jnp.einsum(
            "bhqk,bqhd->bkhd", grad_scores, q_part, preferred_element_type=jnp.float32
        )
        grad_v = jnp.einsum(
            "bhqk,bqhd->bkhd",
            probs.astype(jnp.bfloat16),
            d_mixed,
            preferred_element_type=jnp.float32,
        )
        paired = jnp.stack([grad_k, grad_v], axis=2).reshape(group, length, 2, inner)
        return (carry + jnp.sum(grad_scores.astype(jnp.float32), axis=0), (grad_q, paired))

    bias_grad, (grad_query, paired) = lax.scan(
        attend_back, start, (q_groups, k_back, v_back, seg_query, sk_back, log_totals, grad_att)
    )
    paired = paired.reshape(rows, length, 2, inner)
    kv_grad = lax.psum_scatter(paired, "blk", scatter_dimension=1, tiled=True).astype(jnp.bfloat16)
    grad_key = kv_grad[:, :, 0].reshape(rows * block, inner)
    grad_value = kv_grad[:, :, 1].reshape(rows * block, inner)
    grad_query = grad_query.reshape(rows * block, inner)
    grad_wq = outer_sum(low_one, grad_query)
    grad_wk = outer_sum(low_one, grad_key)
    grad_wv = outer_sum(low_one, grad_value)
    grad_low_one = (
        times_t(grad_query, w_query) + times_t(grad_key, w_key) + times_t(grad_value, w_value)
    )
    back_one, grad_gain_one = rms_backward(grad_low_one, normed_one, scale_one, gain_one)
    grad_tokens = (grad_hidden + back_one).astype(jnp.bfloat16).reshape(rows, block, width)
    grad_table = jnp.einsum("hqk,nqk->nh", bias_grad, onehot, precision=lax.Precision.HIGHEST)
    grads = (
        grad_gain_one,
        grad_wq,
        grad_wk,
        grad_wv,
        grad_wout,
        grad_gain_two,
        grad_in,
        grad_down,
        grad_table,
    )
    pieces = (
        lax.psum_scatter(grads[0], "blk", scatter_dimension=0, tiled=True),
        lax.psum_scatter(grads[1], "blk", scatter_dimension=0, tiled=True),
        lax.psum_scatter(grads[2], "blk", scatter_dimension=0, tiled=True),
        lax.psum_scatter(grads[3], "blk", scatter_dimension=0, tiled=True),
        lax.psum_scatter(grads[4], "blk", scatter_dimension=0, tiled=True),
        lax.psum_scatter(grads[5], "blk", scatter_dimension=0, tiled=True),
        lax.psum_scatter(grads[6], "blk", scatter_dimension=0, tiled=True),
        lax.psum_scatter(grads[7], "blk", scatter_dimension=0, tiled=True),
        lax.psum_scatter(grads[8], "blk", scatter_dimension=0, tiled=True),
    )
    shares = lax.psum(
        (
            pieces[0],
            pieces[1],
            pieces[2],
            pieces[3],
            pieces[4],
            pieces[5],
            pieces[6],
            pieces[7],
            pieces[8],
        ),
        "dp",
    )
    return (
        output.reshape(rows, block, width),
        grad_tokens,
        shares[0],
        shares[1],
        shares[2],
        shares[3],
        shares[4],
        shares[5],
        shares[6],
        shares[7],
        shares[8],
    )


BF = jnp.bfloat16
F32 = jnp.float32
MESH = pl.DeviceIdType.MESH
VLIMIT = 60 * 1024 * 1024
TILE = 128
REACH = 511


def mm(a, b):
    return lax.dot_general(a, b, (((1,), (0,)), ((), ())), preferred_element_type=F32)


def mm_nt(a, b):
    return lax.dot_general(a, b, (((1,), (1,)), ((), ())), preferred_element_type=F32)


def mm_tn(a, b):
    return lax.dot_general(a, b, (((0,), (0,)), ((), ())), preferred_element_type=F32)


def iota(shape, dim):
    return lax.broadcasted_iota(jnp.int32, shape, dim)


def spot():
    blk = lax.axis_index("blk")
    return lax.axis_index("dp"), blk // 2, blk % 2


def gather_kernel(nz, tok, dy, seg, xrow, dyrow, segall, zero, segbuf, s_sem, r_sem, l_sem):
    dp, z, c = spot()
    blk = 2 * z + c
    block = tok.shape[1]
    nb = 2 * nz
    barrier = pltpu.get_barrier_semaphore()
    for k in range(1, nb):
        pl.semaphore_signal(
            barrier, inc=1, device_id=(dp, lax.rem(blk + k, nb)), device_id_type=MESH
        )
    pl.semaphore_wait(barrier, nb - 1)

    def copy(src, dst, send, recv, zz, cc):
        return pltpu.make_async_remote_copy(
            src, dst, s_sem.at[send], r_sem.at[recv], device_id=(dp, 2 * zz + cc), device_id_type=MESH
        )

    mine = xrow.at[blk]
    for hop, dz in ((0, 1), (1, -1)):

        @pl.when((z + dz >= 0) & (z + dz < nz))
        def _():
            copy(tok.at[1 - c], mine, 2 * hop, blk, z + dz, 1 - c).start()
            copy(tok.at[c], mine, 2 * hop + 1, blk, z + dz, c).start()

    copy(tok.at[1 - c], mine, 4, blk, z, 1 - c).start()
    copy(dy.at[1 - c], dyrow.at[c], 5, nb, z, 1 - c).start()
    segbuf[...] = jnp.zeros_like(segbuf)
    segbuf[0:2, :] = seg[...]
    for k in range(1, nb):
        to = lax.rem(blk + k, nb)
        pltpu.make_async_remote_copy(
            segbuf,
            segall.at[blk],
            s_sem.at[10 + k],
            r_sem.at[nb + 1 + blk],
            device_id=(dp, to),
            device_id_type=MESH,
        ).start()
    segall[blk] = segbuf[...]
    own = pltpu.make_async_copy(tok.at[c], mine, l_sem.at[0])
    own.start()
    own_dy = pltpu.make_async_copy(dy.at[c], dyrow.at[c], l_sem.at[1])
    own_dy.start()

    reach = -(-REACH // (2 * block))
    for b in range(nb):

        @pl.when(jnp.abs(b // 2 - z) > reach)
        def _():
            xrow[b] = jnp.zeros(xrow.shape[1:], xrow.dtype)

    def arrived(b):
        copy(tok.at[0], xrow.at[b], 0, b, z, 1 - c).wait_recv()

    for far in range(1, reach + 1):
        for way, dz in ((0, 1), (1, -1)):
            src = z - dz * far

            @pl.when((src >= 0) & (src < nz))
            def _():
                for h in range(2):
                    arrived(2 * src + h)
                    if far < reach:

                        @pl.when((z + dz >= 0) & (z + dz < nz))
                        def _():
                            copy(
                                xrow.at[2 * src + h],
                                xrow.at[2 * src + h],
                                6 + 2 * way + h,
                                2 * src + h,
                                z + dz,
                                c,
                            ).start()

    arrived(2 * z + 1 - c)
    copy(dy.at[0], dyrow.at[1 - c], 0, nb, z, 1 - c).wait_recv()
    for k in range(1, nb):
        frm = lax.rem(blk + nb - k, nb)
        copy(segbuf, segall.at[frm], 0, nb + 1 + frm, z, 1 - c).wait_recv()
    own.wait()
    own_dy.wait()
    for hop, dz in ((0, 1), (1, -1)):

        @pl.when((z + dz >= 0) & (z + dz < nz))
        def _():
            copy(tok.at[0], mine, 2 * hop, blk, z, 1 - c).wait_send()
            copy(tok.at[0], mine, 2 * hop + 1, blk, z, 1 - c).wait_send()

        for far in range(1, reach):
            src = z - dz * far

            @pl.when((src >= 0) & (src < nz) & (z + dz >= 0) & (z + dz < nz))
            def _():
                for h in range(2):
                    copy(tok.at[0], mine, 6 + 2 * hop + h, blk, z, 1 - c).wait_send()

    copy(tok.at[0], mine, 4, blk, z, 1 - c).wait_send()
    copy(dy.at[0], dyrow.at[0], 5, nb, z, 1 - c).wait_send()
    for k in range(1, nb):
        copy(segbuf, segall.at[0], 10 + k, nb + 1, z, 1 - c).wait_send()


def gather(nz, tok, dy, seg):
    _, block, width = tok.shape
    nb = 2 * nz
    vm = pl.BlockSpec(memory_space=pltpu.VMEM)
    return pl.pallas_call(
        functools.partial(gather_kernel, nz),
        out_shape=(
            jax.ShapeDtypeStruct((nb, block, width), BF),
            jax.ShapeDtypeStruct((2, block, width), BF),
            jax.ShapeDtypeStruct((nb, 8, block), jnp.int32),
        ),
        in_specs=[vm] * 3,
        out_specs=(vm, vm, vm),
        scratch_shapes=[
            pltpu.VMEM((8, 128), F32),
            pltpu.VMEM((8, block), jnp.int32),
            pltpu.SemaphoreType.DMA((10 + nb,)),
            pltpu.SemaphoreType.DMA((2 * nb + 2,)),
            pltpu.SemaphoreType.DMA((2,)),
        ],
        compiler_params=pltpu.CompilerParams(
            collective_id=1, has_side_effects=True, vmem_limit_bytes=VLIMIT
        ),
    )(tok, dy, seg)


def norm_rows(x, gain):
    x = x.astype(F32)
    scale = lax.rsqrt(jnp.mean(x * x, axis=-1, keepdims=True) + EPS)
    normed = x * scale
    return normed, scale, (normed * gain).astype(BF)


def flip():
    return (iota((TILE, TILE), 0) + iota((TILE, TILE), 1) == TILE - 1).astype(BF)


def flipped(x):
    turn = flip()
    parts = [mm(turn, x[i : i + TILE, :]).astype(BF) for i in range(0, x.shape[0], TILE)]
    return jnp.concatenate(parts, axis=0)


def prepare_bias(table_ref, near, heads):
    buckets = table_ref.shape[0]
    turn = flip()
    for d in range(3):
        lane = iota((buckets, 2 * TILE), 1)
        back = jnp.where(lane < TILE, lane, lane - 2 * TILE)
        hot = (bucket_of((d - 1) * TILE - back) == iota((buckets, 2 * TILE), 0)).astype(BF)
        strip = mm_tn(table_ref[...], hot)
        for h in range(heads):
            row = jnp.broadcast_to(strip[h : h + 1, :], (TILE, 2 * TILE))
            line = pltpu.roll(row, 0, 1, stride=1, stride_axis=0)[:, :TILE]
            near[h, d] = mm(line.astype(BF), turn)


def prepare_masks(segall, kaug, qseg, qright, qleft, z, c, tq):
    nkb = kaug.shape[0] // TILE
    for b in range(nkb):
        row = segall[b, pl.ds(c, 1), :]
        r = iota((TILE, TILE), 0)
        hot = jnp.where((r == row) | (r == 8 + b), 1.0, 0.0).astype(F32)
        kaug[b * TILE : (b + 1) * TILE, :] = hot.T.astype(BF)
    for i in range(tq // TILE):
        qb = (tq // TILE) * z + i
        row = segall[qb, pl.ds(c, 1), :]
        r = iota((TILE, TILE), 0)
        lost = jnp.where((r < 8) & (r != row), NEG, 0.0).astype(F32)
        qseg[i * TILE : (i + 1) * TILE, :] = mm(flip(), lost.T.astype(BF))
        col = iota((TILE, TILE), 1) - 8
        ok = (col >= 0) & (col < nkb)
        qright[i * TILE : (i + 1) * TILE, :] = jnp.where(ok & (col >= qb + 2), 1.0, 0.0)
        qleft[i * TILE : (i + 1) * TILE, :] = jnp.where(ok & (col <= qb - 2), 1.0, 0.0)


def stacked(ref, cols, dst, tq):
    part = ref[:, cols].astype(F32)
    low = iota((tq, TILE), 1) < TILE // 2
    dst[0:tq, 0:TILE] = jnp.where(low, part, 0.0).astype(BF)
    dst[tq : 2 * tq, 0:TILE] = jnp.where(low, 0.0, part).astype(BF)


def attn_forward_pair(p, z, q, k, v, kaug, qseg, qright, qleft, near, ts, probs, att, qa, s):
    tq = q.shape[0]
    length = k.shape[0]
    nkb = length // TILE
    cols = pl.ds(pl.multiple_of(p * TILE, TILE), TILE)
    stacked(q, cols, qa, tq)
    for hh in range(2):
        far = ts[31, 2 * p + hh] * qright[...] + ts[15, 2 * p + hh] * qleft[...] + qseg[...]
        qa[hh * tq : (hh + 1) * tq, TILE:] = far.astype(BF)

    def score(rb, carry):
        rows = pl.ds(pl.multiple_of(rb * TILE, TILE), TILE)
        left = jnp.concatenate([k[rows, cols], kaug[rows, :]], axis=1)
        s[pl.ds(pl.multiple_of((rb + 1) * TILE, TILE), TILE), :] = mm_nt(left, qa[...])
        return carry

    lax.fori_loop(0, nkb, score, 0)
    for i in range(tq // TILE):
        for d in range(3):
            row = ((tq // TILE) * z + i + d) * TILE
            rows = pl.ds(pl.multiple_of(row, TILE), TILE)
            for hh in range(2):
                at = hh * tq + i * TILE
                s[rows, at : at + TILE] = s[rows, at : at + TILE] + near[2 * p + hh, d]

    def top(rb, best):
        rows = pl.ds(pl.multiple_of((rb + 1) * TILE, TILE), TILE)
        return jnp.maximum(best, jnp.max(s[rows, :].reshape(TILE // 8, 8, 2 * tq), axis=0))

    best = lax.fori_loop(0, nkb, top, jnp.full((8, 2 * tq), -3e38, F32))
    best = jnp.max(best, axis=0, keepdims=True)

    def expo(rb, total):
        rows = pl.ds(pl.multiple_of((rb + 1) * TILE, TILE), TILE)
        e = jnp.exp(s[rows, :] - best)
        s[rows, :] = e
        return total + jnp.sum(e.reshape(TILE // 8, 8, 2 * tq), axis=0)

    total = lax.fori_loop(0, nkb, expo, jnp.zeros((8, 2 * tq), F32))
    inverse = 1.0 / jnp.sum(total, axis=0, keepdims=True)

    def finish(rb, carry):
        rows = pl.ds(pl.multiple_of(rb * TILE, TILE), TILE)
        at = pl.ds(pl.multiple_of((rb + 1) * TILE, TILE), TILE)
        probs[p, rows, :] = (s[at, :] * inverse).astype(BF)
        return carry

    lax.fori_loop(0, nkb, finish, 0)
    mixed = mm_tn(v[:, cols], probs[p])
    both = jnp.concatenate([mixed[: TILE // 2, :tq], mixed[TILE // 2 :, tq:]], axis=0)
    att[:, cols] = both.T.astype(BF)


def forward_kernel(
    xrow, segall, gain, wq, wk, wv, table, ts, n1, k, v, q, probs, att,
    kaug, qseg, qright, qleft, near, qa, s,
):
    _, z, c = spot()
    nb, block, _ = xrow.shape
    tq = 2 * block
    g = gain[...].astype(F32)
    prepare_bias(table, near, 2 * probs.shape[0])
    prepare_masks(segall, kaug, qseg, qright, qleft, z, c, tq)
    for b in range(nb // 2):
        rows = slice(b * tq, (b + 1) * tq)
        part = xrow[2 * b : 2 * b + 2].reshape(tq, xrow.shape[2])
        n1[rows, :] = norm_rows(part, g)[2]
        k[rows, :] = mm(n1[rows, :], wk[...]).astype(BF)
        v[rows, :] = mm(n1[rows, :], wv[...]).astype(BF)
    own = n1[pl.ds(pl.multiple_of(z * tq, tq), tq), :]
    q[...] = mm(flipped(own), wq[...]).astype(BF)
    s[0:TILE, :] = jnp.zeros((TILE, s.shape[1]), F32)
    s[s.shape[0] - TILE :, :] = jnp.zeros((TILE, s.shape[1]), F32)

    def pair(p, carry):
        attn_forward_pair(p, z, q, k, v, kaug, qseg, qright, qleft, near, ts, probs, att, qa, s)
        return carry

    lax.fori_loop(0, probs.shape[0], pair, 0)
    att[...] = flipped(att[...])


def forward(xrow, segall, gain, wq, wk, wv, table):
    nb, block, width = xrow.shape
    length, tq = nb * block, 2 * block
    inner = wq.shape[1]
    heads = table.shape[1]
    pairs = heads // 2
    vm = pl.BlockSpec(memory_space=pltpu.VMEM)
    sm = pl.BlockSpec(memory_space=pltpu.SMEM)
    return pl.pallas_call(
        forward_kernel,
        out_shape=(
            jax.ShapeDtypeStruct((length, width), BF),
            jax.ShapeDtypeStruct((length, inner), BF),
            jax.ShapeDtypeStruct((length, inner), BF),
            jax.ShapeDtypeStruct((tq, inner), BF),
            jax.ShapeDtypeStruct((pairs, length, 2 * tq), BF),
            jax.ShapeDtypeStruct((tq, inner), BF),
        ),
        in_specs=[vm] * 7 + [sm],
        out_specs=(vm,) * 6,
        scratch_shapes=[
            pltpu.VMEM((length, TILE), BF),
            pltpu.VMEM((tq, TILE), F32),
            pltpu.VMEM((tq, TILE), F32),
            pltpu.VMEM((tq, TILE), F32),
            pltpu.VMEM((heads, 3, TILE, TILE), F32),
            pltpu.VMEM((2 * tq, 2 * TILE), BF),
            pltpu.VMEM((length + 2 * TILE, 2 * tq), F32),
        ],
        compiler_params=pltpu.CompilerParams(vmem_limit_bytes=VLIMIT),
    )(xrow, segall, gain, wq, wk, wv, table, table.astype(F32))


class Sums:
    def __init__(self, nz, bufs, s_sem, r_sem):
        self.nz = nz
        self.dp, self.z, self.c = spot()
        self.bufs, self.s_sem, self.r_sem = bufs, s_sem, r_sem
        x, y = self.dp % 2, self.dp // 2
        c = self.c
        self.f, self.g = 1 + c, 2 - c
        self.s1 = (1 - c) * x + c * y
        self.s2 = (1 - c) * y + c * x
        self.peer1 = self.dp + self.f * (1 - 2 * self.s1)
        self.peer2 = self.dp + self.g * (1 - 2 * self.s2)
        self.bit, self.high = self.z % 2, self.z // 2
        self.near_z = self.z + 1 - 2 * self.bit
        self.far_z = self.z + 2 - 4 * self.high
        self.table = {}
        self.pending = []

    def copy(self, src, dst, key, dp=None, z=None, c=None):
        n = self.table.setdefault(key, len(self.table))
        dp = self.dp if dp is None else dp
        z = self.z if z is None else z
        c = self.c if c is None else c
        return pltpu.make_async_remote_copy(
            src, dst, self.s_sem.at[n], self.r_sem.at[n], device_id=(dp, 2 * z + c), device_id_type=MESH
        )

    def start(self, src, dst, key, **to):
        op = self.copy(src, dst, key, **to)
        op.start()
        self.pending.append(op)

    def drain(self):
        for op in self.pending:
            op.wait_send()
        self.pending = []

    def q(self, i1, i2):
        return i1 * self.f + i2 * self.g

    def a_start(self, u, zz, q):
        b = self.bufs[u]
        self.start(
            b["pb"].at[2 * zz + 1 - self.c, q], b["ra"].at[zz, q], (u, "a", zz, q), c=1 - self.c
        )

    def a_finish(self, u, zz):
        b = self.bufs[u]
        for q in range(4):
            self.copy(b["pb"].at[0, 0], b["ra"].at[zz, q], (u, "a", zz, q), c=1 - self.c).wait_recv()

        def one(q, carry):
            b["ra"][zz, q] = (b["ra"][zz, q].astype(F32) + b["pb"][2 * zz + self.c, q].astype(F32)).astype(BF)
            return carry

        lax.fori_loop(0, 4, one, 0)

    def first_start(self, u, zz):
        b = self.bufs[u]
        for i2 in range(2):
            self.start(
                b["ra"].at[zz, self.q(1 - self.s1, i2)], b["r1"].at[zz, i2], (u, "1", zz, i2), dp=self.peer1
            )

    def first_finish(self, u, zz):
        b = self.bufs[u]
        for i2 in range(2):
            self.copy(b["ra"].at[0, 0], b["r1"].at[zz, i2], (u, "1", zz, i2)).wait_recv()

        def one(i2, carry):
            b["r1"][zz, i2] = (
                b["r1"][zz, i2].astype(F32) + b["ra"][zz, self.q(self.s1, i2)].astype(F32)
            ).astype(BF)
            return carry

        lax.fori_loop(0, 2, one, 0)

    def second_start(self, u, zz):
        b = self.bufs[u]
        self.start(b["r1"].at[zz, 1 - self.s2], b["r2"].at[zz], (u, "2", zz), dp=self.peer2)

    def second_finish(self, u, zz):
        b = self.bufs[u]
        self.copy(b["r1"].at[0, 0], b["r2"].at[zz], (u, "2", zz)).wait_recv()
        b["r2"][zz] = (b["r2"][zz].astype(F32) + b["r1"][zz, self.s2].astype(F32)).astype(BF)

    def near_start(self, u, name):
        b = self.bufs[u]
        for i in range(2):
            self.start(
                b[name].at[2 * i + 1 - self.bit], b["rz"].at[i], (u, "z", i), z=self.near_z
            )

    def add(self, dst, a, b, last=None):
        total = a[...].astype(F32) + b[...].astype(F32)
        dst[...] = total.astype(BF)

    def near_finish(self, u, name):
        b = self.bufs[u]
        for i in range(2):
            self.copy(b[name].at[0], b["rz"].at[i], (u, "z", i)).wait_recv()
        mine = b[name].at[2 * (1 - self.high) + self.bit]
        self.add(b["rz"].at[1 - self.high], b["rz"].at[1 - self.high], mine)
        self.start(b["rz"].at[1 - self.high], b["rz"].at[2], (u, "z", 2), z=self.far_z)
        mine = b[name].at[self.z]
        self.add(b["rz"].at[self.high], b["rz"].at[self.high], mine)

    def far_finish(self, u):
        b = self.bufs[u]
        self.copy(b["rz"].at[0], b["rz"].at[2], (u, "z", 2)).wait_recv()

    def far_last(self, u):
        self.far_finish(u)
        b = self.bufs[u]
        self.add(b["g"].at[self.dp], b["rz"].at[self.high], b["rz"].at[2])

    def far_mid(self, u):
        self.far_finish(u)
        b = self.bufs[u]
        self.add(b["rz"].at[2], b["rz"].at[self.high], b["rz"].at[2])
        self.start(b["rz"].at[2, 1 - self.s2], b["r2"].at[0], (u, "2", 0), dp=self.peer2)

    def second_last_finish(self, u):
        b = self.bufs[u]
        self.copy(b["rz"].at[0, 0], b["r2"].at[0], (u, "2", 0)).wait_recv()
        self.add(b["g"].at[self.dp], b["r2"].at[0], b["rz"].at[2, self.s2])

    def spread_two_start(self, u):
        b = self.bufs[u]
        for dp, key in ((self.peer2, "g0"), (self.peer1, "g1")):
            self.start(b["g"].at[self.dp], b["g"].at[self.dp], (u, key), dp=dp)

    def spread_two_mid(self, u):
        b = self.bufs[u]
        self.copy(b["g"].at[0], b["g"].at[self.peer2], (u, "g0")).wait_recv()
        self.start(b["g"].at[self.peer2], b["g"].at[self.peer2], (u, "g2"), dp=self.peer1)

    def spread_two_finish(self, u):
        b = self.bufs[u]
        self.copy(b["g"].at[0], b["g"].at[self.peer1], (u, "g1")).wait_recv()
        across = self.peer1 + self.peer2 - self.dp
        self.copy(b["g"].at[0], b["g"].at[across], (u, "g2")).wait_recv()

    def spread_start(self, u):
        b = self.bufs[u]
        for k in range(1, 4):
            self.start(
                b["g"].at[self.dp], b["g"].at[self.dp], (u, "g", 3 - k), dp=lax.rem(self.dp + k, 4)
            )

    def spread_finish(self, u):
        b = self.bufs[u]
        for k in range(1, 4):
            self.copy(b["g"].at[0], b["g"].at[lax.rem(self.dp + k, 4)], (u, "g", k - 1)).wait_recv()


def attn_backward_pair(p, z, q, k, v, kaug, datt, probs, dk, dv, dq, diag, far, qm, dm, dprob, ds):
    tq = q.shape[0]
    length = k.shape[0]
    nkb = length // TILE
    cols = slice(p * TILE, (p + 1) * TILE)
    stacked(q, cols, qm, tq)
    stacked(datt, cols, dm, tq)
    dprob[...] = mm_nt(v[:, cols], dm[...])

    def first(rb, total):
        rows = pl.ds(pl.multiple_of(rb * TILE, TILE), TILE)
        mixed = dprob[rows, :] * probs[rows, :].astype(F32)
        return total + jnp.sum(mixed.reshape(TILE // 8, 8, 2 * tq), axis=0)

    total = lax.fori_loop(0, nkb, first, jnp.zeros((8, 2 * tq), F32))
    center = jnp.sum(total, axis=0, keepdims=True)
    dv[:, cols] = mm(probs[...], dm[...]).astype(BF)

    def second(rb, carry):
        rows = pl.ds(pl.multiple_of(rb * TILE, TILE), TILE)
        at = pl.ds(pl.multiple_of((rb + 1) * TILE, TILE), TILE)
        ds[at, :] = (probs[rows, :].astype(F32) * (dprob[rows, :] - center)).astype(BF)
        return carry

    lax.fori_loop(0, nkb, second, 0)
    dk[:, cols] = mm(ds[TILE : TILE + length, :], qm[...]).astype(BF)
    left = jnp.concatenate([k[:, cols], kaug[...]], axis=1)
    back = mm_tn(left, ds[TILE : TILE + length, :])
    both = jnp.concatenate([back[: TILE // 2, :tq], back[TILE // 2 : TILE, tq:]], axis=0)
    dq[:, cols] = both.T.astype(BF)
    sums = back[TILE + 8 : TILE + 8 + nkb, :]
    kb = iota((nkb, 2 * tq), 0)
    lane = iota((nkb, 2 * tq), 1)
    qb = (tq // TILE) * z + (lane % tq) // TILE
    right = jnp.sum(jnp.where(kb >= qb + 2, sums, 0.0), axis=0, keepdims=True)
    left = jnp.sum(jnp.where(kb <= qb - 2, sums, 0.0), axis=0, keepdims=True)
    for hh in range(2):
        h = 2 * p + hh
        far[0, h : h + 1, :] = right[:, hh * tq : (hh + 1) * tq]
        far[1, h : h + 1, :] = left[:, hh * tq : (hh + 1) * tq]
        for d in range(3):
            acc = jnp.zeros((TILE, TILE), F32)
            for i in range(tq // TILE):
                row = ((tq // TILE) * z + i + d) * TILE
                at = hh * tq + i * TILE
                acc = acc + ds[pl.ds(pl.multiple_of(row, TILE), TILE), at : at + TILE].astype(F32)
            wide = jnp.concatenate([acc, jnp.zeros((TILE, TILE), F32)], axis=1)
            wide = pltpu.roll(wide, 0, 1, stride=1, stride_axis=0)
            diag[d, h : h + 1, :] = jnp.sum(wide, axis=0, keepdims=True)


def table_sums(diag, far, heads):
    rows = diag.shape[1]
    total = jnp.zeros((rows, TILE), F32)
    for d in range(3):
        offset = (d - 1) * TILE + iota((2 * TILE, TILE), 0) - (TILE - 1)
        hot = (bucket_of(offset) == iota((2 * TILE, TILE), 1)).astype(F32)
        total = total + lax.dot_general(
            diag[d], hot, (((1,), (0,)), ((), ())),
            preferred_element_type=F32, precision=lax.Precision.HIGHEST,
        )
    lane = iota((rows, TILE), 1)
    for side, b in ((0, 31), (1, 15)):
        total = total + jnp.where(lane == b, jnp.sum(far[side], axis=1, keepdims=True), 0.0)
    return jnp.where(iota((rows, TILE), 0) < heads, total, 0.0)


def back_kernel(nz, *refs):
    (att_h, xrow_h, dy_h, n1_h, q_h, k_h, v_h, probs_h, wout_h, win_h, wdown_h, wq_h, wk_h, wv_h, g1, g2) = refs[:16]
    o_out, o_gt, g_down, g_in, g_attn, o_small = refs[16:22]
    (
        buf_a, buf_b, pdown, pin, att, xown, dy, q, k, v, probs, wout, wqkv,
        ra_d, r1_d, r2_d, rz_d, ra_i, r1_i, r2_i, rz_i, ra_a, r1_a, r2_a, rz_a,
        n2, dh, dhl, datt, dk, dv, dq, kaug, diag, far, qm, dm, dprob, ds,
        own_dn1, rd, relay, outb, sm, smr, s_sem, r_sem, l_sem,
    ) = refs[22:]
    bufs = {
        "down": dict(pb=pdown, ra=ra_d, r1=r1_d, r2=r2_d, rz=rz_d, g=g_down),
        "in": dict(pb=pin, ra=ra_i, r1=r1_i, r2=r2_i, rz=rz_i, g=g_in),
        "attn": dict(pb=buf_a, ra=ra_a, r1=r1_a, r2=r2_a, rz=rz_a, g=g_attn),
    }
    eng = Sums(nz, bufs, s_sem, r_sem)
    dp, z, c = eng.dp, eng.z, eng.c
    barrier = pltpu.get_barrier_semaphore()
    peers = [(dp, 2 * z + 1 - c), (eng.peer1, 2 * z + c), (eng.peer2, 2 * z + c)]
    peers += [(eng.peer1 + eng.peer2 - dp, 2 * z + c)]
    peers += [(dp, 2 * lax.rem(z + k, nz) + c) for k in range(1, nz)]
    for peer in peers:
        pl.semaphore_signal(barrier, inc=1, device_id=peer, device_id_type=MESH)

    tq, width = n2.shape
    nb = pdown.shape[0]
    share = width // nb
    length = k.shape[0]
    steps = buf_b.shape[0]
    loads = {}

    def load(name, src, dst):
        loads[name] = pltpu.make_async_copy(src, dst, l_sem.at[len(loads)])
        loads[name].start()

    def ready(*names):
        for name in names:
            loads[name].wait()

    load("att", att_h, att)
    load("wout", wout_h, wout)
    load("xown", xrow_h.at[pl.ds(2 * z, 2)], xown)
    load("dy", dy_h, dy)
    per = nb // steps
    for j in range(steps):
        load(("win", j), win_h.at[:, j * width : (j + 1) * width], buf_b.at[j])
        load(("wdown", j), wdown_h.at[j * per : (j + 1) * per], buf_a.at[j * per : (j + 1) * per])
    load("v", v_h, v)
    load("q", q_h, q)
    load("p0", probs_h.at[0], probs.at[0])
    load("p1", probs_h.at[1], probs.at[1])
    load("k", k_h, k)
    load("wq", wq_h, wqkv.at[0])
    load("wk", wk_h, wqkv.at[1])
    load("wv", wv_h, wqkv.at[2])

    for b in range(length // TILE):
        lane = iota((TILE, TILE), 1)
        kaug[b * TILE : (b + 1) * TILE, :] = jnp.where(lane == 8 + b, 1.0, 0.0).astype(BF)
    ds[0:TILE, :] = jnp.zeros((TILE, ds.shape[1]), BF)
    ds[ds.shape[0] - TILE :, :] = jnp.zeros((TILE, ds.shape[1]), BF)
    diag[...] = jnp.zeros_like(diag)
    far[...] = jnp.zeros_like(far)

    gain2 = g2[...].astype(F32)
    ready("att", "wout", "xown")
    dh[...] = xown[...].reshape(tq, width).astype(F32) + mm(att[...], wout[...])
    n2[...] = norm_rows(dh[...], gain2)[2]
    ready("dy")
    total = own_dn1
    for j in range(steps):
        ready(("win", j), ("wdown", j))
        value, slant = gelu_both(mm(n2[...], buf_b[j]))
        act = value.astype(BF)
        down = buf_a[j * per : (j + 1) * per].reshape(width, width)
        d = dy[...].reshape(tq, width)
        pdown[j * per : (j + 1) * per] = mm_tn(act, d).astype(BF).reshape(per, 4, share, width)
        if j == 0:
            pl.semaphore_wait(barrier, len(peers))
        for qq in range(4):
            eng.a_start("down", j, qq)
        dpre = (mm_nt(d, down) * slant).astype(BF)
        pin[:, j] = mm_tn(n2[...], dpre).astype(BF).reshape(nb, share, width)
        for zz in range(nz):
            eng.a_start("in", zz, j)
        if j == 0:
            total[...] = mm(act, down)
            rd_sum = mm_nt(dpre, buf_b[j])
        else:
            total[...] += mm(act, down)
            rd_sum = rd_sum + mm_nt(dpre, buf_b[j])
        if j > 0:
            eng.a_finish("down", j - 1)
            eng.first_start("down", j - 1)
    dn2 = rd_sum
    h = dh[...]
    outb[...] = (h + total[...]).astype(BF).reshape(outb.shape)
    eng.a_finish("down", steps - 1)
    eng.first_start("down", steps - 1)
    normed, scale, _ = norm_rows(h, gain2)
    back, gain_grad = rms_backward(dn2, normed, scale, gain2)
    lines = width // TILE
    sm[0] = jnp.zeros(sm.shape[1:], F32)
    for i in range(lines):
        sm[0, lines + i : lines + i + 1, :] = gain_grad[None, i * TILE : (i + 1) * TILE]
    dh[...] = dy[...].reshape(tq, width).astype(F32) + back
    dhl[...] = dh[...].astype(BF)
    datt[...] = flipped(mm_nt(dhl[...], wout[...]).astype(BF))
    for zz in range(nz):
        eng.a_finish("in", zz)
        eng.first_start("in", zz)
    eng.start(outb.at[1 - c], o_out.at[c], ("out",), c=1 - c)
    kept = pltpu.make_async_copy(outb.at[c], o_out.at[c], l_sem.at[len(loads)])
    kept.start()
    loads["kept"] = kept
    for b in range(nz):
        load(("n1", b), n1_h.at[b * tq : (b + 1) * tq], buf_b.at[b, 0:tq])
        for i in range(2):
            load(("x", b, i), xrow_h.at[2 * b + i], buf_b.at[b, tq + i * (tq // 2) : tq + (i + 1) * (tq // 2)])
    buf_a[:, 3] = mm_tn(att[...], dhl[...]).astype(BF).reshape(nb, share, width)
    for zz in range(nz):
        eng.a_start("attn", zz, 3)

    ready("v", "q", "k")
    pairs = q.shape[1] // TILE
    for p in range(pairs):
        ready("p%d" % p)
        attn_backward_pair(
            p, z, q, k, v, kaug, datt, probs.at[p % 2], dk, dv, dq, diag, far, qm, dm, dprob, ds
        )
        if p + 2 < pairs:
            load("p%d" % (p + 2), probs_h.at[p + 2], probs.at[p % 2])
        if p == 1:
            for zz in range(nz):
                eng.first_finish("down", zz)
            eng.near_start("down", "r1")
        if p == 4:
            eng.near_finish("down", "r1")
        if p == 5:
            for zz in range(nz):
                eng.first_finish("in", zz)
                eng.second_start("in", zz)

    ready("wq", "wk", "wv")
    for b in range(nz):
        ready(("n1", b), ("x", b, 0), ("x", b, 1))

    def weight(i, right):
        acc = mm_tn(buf_b[0, 0:tq], right[0:tq, :])
        for b in range(1, nz):
            acc = acc + mm_tn(buf_b[b, 0:tq], right[b * tq : (b + 1) * tq, :])
        buf_a[:, i] = acc.astype(BF).reshape(nb, share, width)
        for zz in range(nz):
            eng.a_start("attn", zz, i)

    weight(1, dk)
    weight(2, dv)
    eng.far_mid("down")
    dq[...] = flipped(dq[...])
    buf_a[:, 0] = mm_tn(buf_b[z, 0:tq], dq[...]).astype(BF).reshape(nb, share, width)
    for zz in range(nz):
        eng.a_start("attn", zz, 0)

    gain1 = g1[...].astype(F32)
    for b in range(nz):
        rows_b = slice(b * tq, (b + 1) * tq)
        part = mm_nt(dk[rows_b, :], wqkv[1]) + mm_nt(dv[rows_b, :], wqkv[2])
        buf_b[b, 2 * tq : 3 * tq] = part.astype(BF)

    def inside(other):
        return (other >= 0) & (other < nz)

    ways = ((0, 1), (1, -1))
    for way, dz in ways:

        @pl.when(inside(z + 2 * dz))
        def _():
            eng.copy(
                buf_b.at[z + 2 * dz, 2 * tq : 3 * tq], relay.at[way], ("d1", way), z=z + dz
            ).start()

    for zz in range(nz):
        eng.a_finish("attn", zz)
        eng.first_start("attn", zz)
    eng.second_last_finish("down")
    eng.spread_two_start("down")
    for zz in range(nz):
        eng.second_finish("in", zz)
    eng.near_start("in", "r2")

    for way, dz in ways:

        @pl.when(inside(z - dz) & inside(z + dz))
        def _():
            eng.copy(relay.at[way], relay.at[way], ("d1", way)).wait_recv()
            buf_b[z + dz, 2 * tq : 3 * tq] = (
                buf_b[z + dz, 2 * tq : 3 * tq].astype(F32) + relay[way].astype(F32)
            ).astype(BF)

        @pl.when(inside(z + dz))
        def _():
            eng.copy(buf_b.at[z + dz, 2 * tq : 3 * tq], rd.at[way], ("d2", way), z=z + dz).start()

    mine = pl.ds(pl.multiple_of(z * tq, tq), tq)
    own_dn1[...] = (
        mm_nt(dk[mine, :], wqkv[1]) + mm_nt(dv[mine, :], wqkv[2]) + mm_nt(dq[...], wqkv[0])
    )
    gain_sum = jnp.zeros((1, width), F32)
    for b in range(nz):
        rows_b = slice(b * tq, (b + 1) * tq)
        normed = norm_rows(buf_b[b, tq : 2 * tq], gain1)[0]
        part = mm_nt(dk[rows_b, :], wqkv[1]) + mm_nt(dv[rows_b, :], wqkv[2])
        gain_sum = gain_sum + jnp.sum(part * normed, axis=0, keepdims=True)
    normed = norm_rows(xown[...].reshape(tq, width), gain1)[0]
    gain_sum = gain_sum + jnp.sum(mm_nt(dq[...], wqkv[0]) * normed, axis=0, keepdims=True)
    for i in range(lines):
        sm[0, i : i + 1, :] = gain_sum[:, i * TILE : (i + 1) * TILE]
    sm[0, 2 * lines :, :] = table_sums(diag, far, 2 * pairs)[: sm.shape[1] - 2 * lines]
    hops = (
        dict(c=1 - c), dict(dp=dp + 1 - 2 * (dp % 2)), dict(dp=dp + 2 - 4 * (dp // 2)),
        dict(z=eng.near_z), dict(z=eng.far_z),
    )

    def small_start(i):
        eng.start(sm.at[i], smr.at[i], ("s", i), **hops[i])

    def small_finish(i):
        eng.copy(sm.at[i], smr.at[i], ("s", i), **hops[i]).wait_recv()
        sm[i + 1] = sm[i] + smr[i]

    small_start(0)
    eng.near_finish("in", "r2")
    eng.spread_two_mid("down")
    small_finish(0)
    small_start(1)
    for zz in range(nz):
        eng.first_finish("attn", zz)
        eng.second_start("attn", zz)
    small_finish(1)
    small_start(2)
    eng.far_last("in")
    eng.spread_two_start("in")

    dn1 = own_dn1
    for way, dz in ways:

        @pl.when(inside(z - dz))
        def _():
            eng.copy(rd.at[way], rd.at[way], ("d2", way)).wait_recv()
            dn1[...] += rd[way].astype(F32)

    normed, scale, _ = norm_rows(xown[...].reshape(tq, width), gain1)
    back, _ = rms_backward(dn1[...], normed, scale, gain1)
    xown[...] = (dh[...] + back).astype(BF).reshape(xown.shape)
    eng.start(xown.at[1 - c], o_gt.at[c], ("gt",), c=1 - c)
    kept_gt = pltpu.make_async_copy(xown.at[c], o_gt.at[c], l_sem.at[len(loads)])
    kept_gt.start()

    small_finish(2)
    small_start(3)
    eng.spread_two_mid("in")
    for zz in range(nz):
        eng.second_finish("attn", zz)
    eng.near_start("attn", "r2")
    small_finish(3)
    small_start(4)
    eng.near_finish("attn", "r2")
    small_finish(4)
    o_small[...] = sm[5]
    eng.far_last("attn")
    eng.spread_start("attn")
    eng.copy(outb.at[0], o_out.at[1 - c], ("out",)).wait_recv()
    eng.copy(xown.at[0], o_gt.at[1 - c], ("gt",)).wait_recv()
    kept.wait()
    kept_gt.wait()
    eng.spread_two_finish("down")
    eng.spread_two_finish("in")
    eng.spread_finish("attn")
    eng.drain()
    for way, dz in ways:

        @pl.when(inside(z + 2 * dz))
        def _():
            eng.copy(buf_b.at[0, 0:tq], relay.at[way], ("d1", way)).wait_send()

        @pl.when(inside(z + dz))
        def _():
            eng.copy(buf_b.at[0, 0:tq], rd.at[way], ("d2", way)).wait_send()


def back(nz, att, xrow, dy, n1, q, k, v, probs, wout, win, wdown, wq, wk, wv, g1, g2):
    nb, block, width = xrow.shape
    length, tq = nb * block, 2 * block
    share = width // nb
    pairs = probs.shape[0]
    steps = win.shape[1] // width
    vm = pl.BlockSpec(memory_space=pltpu.VMEM)
    hbm = pl.BlockSpec(memory_space=pl.ANY)
    home = jax.ShapeDtypeStruct((2, block, width), BF)
    quarters = jax.ShapeDtypeStruct((4, share, width), BF)
    whole = pltpu.VMEM((nb, 4, share, width), BF)
    rows = pltpu.VMEM((tq, width), BF)
    one = (share, width)
    long = pltpu.VMEM((length, width), BF)
    scratch = [
        whole, pltpu.VMEM((steps, width, width), BF), whole, whole,
        rows, pltpu.VMEM((2, block, width), BF), pltpu.VMEM((2, block, width), BF), rows, long, long,
        pltpu.VMEM((2, length, 2 * tq), BF), pltpu.VMEM((width, width), BF), pltpu.VMEM((3, width, width), BF),
    ]
    for order in ("xzy", "xyz", "xyz"):
        scratch += [
            pltpu.VMEM((nz, 4) + one, BF),
            pltpu.VMEM((nz, 2) + one, BF),
            pltpu.VMEM((nz if order == "xyz" else 1,) + one, BF),
            pltpu.VMEM(((3,) if order == "xyz" else (3, 2)) + one, BF),
        ]
    small = (24, TILE)
    scratch += [
        rows, pltpu.VMEM((tq, width), F32), rows, rows, long, long, rows,
        pltpu.VMEM((length, TILE), BF),
        pltpu.VMEM((3, 16, 2 * TILE), F32),
        pltpu.VMEM((2, 16, tq), F32),
        pltpu.VMEM((2 * tq, TILE), BF),
        pltpu.VMEM((2 * tq, TILE), BF),
        pltpu.VMEM((length, 2 * tq), F32),
        pltpu.VMEM((length + 2 * TILE, 2 * tq), BF),
        pltpu.VMEM((tq, width), F32),
        pltpu.VMEM((2, tq, width), BF),
        pltpu.VMEM((2, tq, width), BF),
        pltpu.VMEM((2, block, width), BF),
        pltpu.VMEM((6,) + small, F32),
        pltpu.VMEM((5,) + small, F32),
        pltpu.SemaphoreType.DMA((140,)),
        pltpu.SemaphoreType.DMA((140,)),
        pltpu.SemaphoreType.DMA((48,)),
    ]
    return pl.pallas_call(
        functools.partial(back_kernel, nz),
        out_shape=(home, home, quarters, quarters, quarters, jax.ShapeDtypeStruct(small, F32)),
        in_specs=[hbm] * 14 + [vm] * 2,
        out_specs=(vm,) * 6,
        scratch_shapes=scratch,
        compiler_params=pltpu.CompilerParams(
            collective_id=2, has_side_effects=True, vmem_limit_bytes=64 * 1024 * 1024
        ),
    )(att, xrow, dy, n1, q, k, v, probs, wout, win, wdown, wq, wk, wv, g1, g2)


def fast_device(
    nz, tokens, segment_ids, gain_attn, w_query, w_key, w_value, w_out, gain_ffn, w_in, w_down,
    rel_table, cotangent,
):
    rows, block, width = tokens.shape
    nb = 2 * nz
    share = width // nb
    xrow, dyrow, segall = gather(nz, tokens, cotangent, segment_ids)
    g1, g2 = gain_attn.reshape(1, width), gain_ffn.reshape(1, width)
    n1, k, v, q, probs, att = forward(xrow, segall, g1, w_query, w_key, w_value, rel_table)
    out, grad_tokens, gdown, gin, gattn, small = back(
        nz, att, xrow, dyrow, n1, q, k, v, probs, w_out, w_in,
        w_down.reshape(nb, 4, w_down.shape[0] // nb // 4, width), w_query, w_key, w_value, g1, g2,
    )
    b = lax.axis_index("blk")
    lines = width // TILE
    ga = lax.dynamic_slice_in_dim(small[:lines].reshape(-1), b * share, share)
    gf = lax.dynamic_slice_in_dim(small[lines : 2 * lines].reshape(-1), b * share, share)
    heads = rel_table.shape[1]
    gt = lax.dynamic_slice(small, (2 * lines, b * (32 // nb)), (heads, 32 // nb)).T
    gin = jnp.transpose(gin, (1, 0, 2)).reshape(share, -1).astype(F32)
    gattn = gattn.astype(F32)
    return (
        out, grad_tokens, ga, gattn[0], gattn[1], gattn[2], gattn[3], gf, gin,
        gdown.reshape(-1, width).astype(F32), gt,
    )


def pick(mesh):
    if mesh.shape["dp"] == 4 and mesh.shape["blk"] == 8:
        return functools.partial(fast_device, mesh.shape["blk"] // 2)
    return on_device


def solution(mesh):
    placed = (
        P("dp", "blk", None),
        P("dp", "blk"),
        P(),
        P(),
        P(),
        P(),
        P(),
        P(),
        P(),
        P(),
        P(),
        P("dp", "blk", None),
    )
    return jax.shard_map(
        pick(mesh),
        mesh=mesh,
        in_specs=placed,
        out_specs=(
            P("dp", "blk", None),
            P("dp", "blk", None),
            P("blk"),
            P("blk", None),
            P("blk", None),
            P("blk", None),
            P("blk", None),
            P("blk"),
            P("blk", None),
            P("blk", None),
            P("blk", None),
        ),
        check_vma=False,
    )
```

```python
import functools
import math

import jax
import jax.numpy as jnp
from jax import lax
from jax.experimental import pallas as pl
from jax.experimental.pallas import tpu as pltpu
from jax.sharding import PartitionSpec as P

EPS = 1e-06
NEG = -1e30
EDGES = (12, 16, 23, 32, 46, 64, 91)
ROOT_TWO_PI = 0.7978845608028654
CUBIC = 0.044715


def bucket_of(offset):
    distance = jnp.abs(offset)
    far_part = 8 + sum(((distance >= edge).astype(jnp.int32) for edge in EDGES))
    return jnp.where(offset > 0, 16, 0) + jnp.where(distance < 8, distance, far_part)


def gelu_both(values):
    inner_arg = ROOT_TWO_PI * (values + CUBIC * values * values * values)
    tangent = jnp.tanh(inner_arg)
    result = 0.5 * values * (1.0 + tangent)
    slope = 0.5 * (1.0 + tangent) + 0.5 * values * (1.0 - tangent * tangent) * ROOT_TWO_PI * (
        1.0 + 3.0 * CUBIC * values * values
    )
    return (result, slope)


def rms_forward(values, gain):
    scale = lax.rsqrt(jnp.mean(values * values, axis=-1, keepdims=True) + EPS)
    normed = values * scale
    return (normed, scale, (normed * gain).astype(jnp.bfloat16))


def rms_backward(grad, normed, scale, gain):
    gain_grad = jnp.sum(grad * normed, axis=0)
    inner_grad = grad * gain
    back = scale * (inner_grad - normed * jnp.mean(inner_grad * normed, axis=-1, keepdims=True))
    return (back, gain_grad)


def outer_sum(left, right):
    return jnp.einsum("td,tf->df", left, right, preferred_element_type=jnp.float32)


def times_t(left, right):
    return jnp.einsum("tf,df->td", left, right, preferred_element_type=jnp.float32)


def masked_scores(query, keys, bias, seg_query, seg_keys):
    raw = (
        jnp.einsum("bqhd,bkhd->bhqk", query, keys, preferred_element_type=jnp.float32) + bias[None]
    )
    same = seg_query[:, None, :, None] == seg_keys[:, None, None, :]
    return jnp.where(same, raw, NEG)


def score_grads(q_part, k_part, v_part, bias, sq_part, sk_part, total, d_mixed):
    scores = masked_scores(q_part, k_part, bias, sq_part, sk_part)
    probs = jnp.exp(scores - total[..., None])
    grad_probs = jnp.einsum("bqhd,bkhd->bhqk", d_mixed, v_part, preferred_element_type=jnp.float32)
    return (probs, grad_probs)


def on_device(
    tokens,
    segment_ids,
    gain_attn,
    w_query,
    w_key,
    w_value,
    w_out,
    gain_ffn,
    w_in,
    w_down,
    rel_table,
    cotangent,
):
    rows, block, width = tokens.shape
    buckets, heads = rel_table.shape
    inner = w_query.shape[1]
    head_dim = inner // heads
    length = block * lax.axis_size("blk")
    group = math.gcd(rows, max(1, 512 // block))
    blocks = rows // group
    gain_one = gain_attn.astype(jnp.float32)
    gain_two = gain_ffn.astype(jnp.float32)
    table_f = rel_table.astype(jnp.float32)
    flat = tokens.reshape(rows * block, width).astype(jnp.float32)
    normed_one, scale_one, low_one = rms_forward(flat, gain_one)

    def project(weight):
        return (
            jnp.dot(low_one, weight, preferred_element_type=jnp.float32)
            .astype(jnp.bfloat16)
            .reshape(rows, block, inner)
        )

    query, keys, values = (project(w_query), project(w_key), project(w_value))
    key_all, value_all, seg_all = (
        lax.all_gather(keys, "blk", axis=1, tiled=True),
        lax.all_gather(values, "blk", axis=1, tiled=True),
        lax.all_gather(segment_ids, "blk", axis=1, tiled=True),
    )
    places = lax.axis_index("blk") * block + jnp.arange(block, dtype=jnp.int32)
    offsets = jnp.arange(length, dtype=jnp.int32)[None, :] - places[:, None]
    onehot = (
        bucket_of(offsets)[None] == jnp.arange(buckets, dtype=jnp.int32)[:, None, None]
    ).astype(jnp.float32)
    bias = jnp.einsum("nqk,nh->hqk", onehot, table_f, precision=lax.Precision.HIGHEST)
    q_groups = query.reshape(blocks, group, block, heads, head_dim)
    seg_query = segment_ids.reshape(blocks, group, block)

    def key_groups(key_rows, value_rows, seg_rows):
        return (
            key_rows.reshape(blocks, group, length, heads, head_dim),
            value_rows.reshape(blocks, group, length, heads, head_dim),
            seg_rows.reshape(blocks, group, length),
        )

    k_groups, v_groups, seg_keys = key_groups(key_all, value_all, seg_all)

    def attend(parts):
        q_part, k_part, v_part, sq_part, sk_part = parts
        scores = masked_scores(q_part, k_part, bias, sq_part, sk_part)
        top = jnp.max(scores, axis=-1, keepdims=True)
        total = jnp.log(jnp.sum(jnp.exp(scores - top), axis=-1, keepdims=True)) + top
        probs = jnp.exp(scores - total).astype(jnp.bfloat16)
        mixed = jnp.einsum("bhqk,bkhd->bqhd", probs, v_part, preferred_element_type=jnp.float32)
        return (mixed.astype(jnp.bfloat16), total[..., 0])

    attended, log_totals = lax.map(attend, (q_groups, k_groups, v_groups, seg_query, seg_keys))
    attended_flat = attended.reshape(rows * block, inner)
    hidden = flat + jnp.dot(attended_flat, w_out, preferred_element_type=jnp.float32)
    normed_two, scale_two, low_two = rms_forward(hidden, gain_two)
    pre = jnp.dot(low_two, w_in, preferred_element_type=jnp.float32)
    gelu_value, gelu_slope = gelu_both(pre)
    active = gelu_value.astype(jnp.bfloat16)
    output = (hidden + jnp.dot(active, w_down, preferred_element_type=jnp.float32)).astype(
        jnp.bfloat16
    )
    grad_out = cotangent.reshape(rows * block, width)
    grad_down = outer_sum(active, grad_out)
    grad_pre = (times_t(grad_out, w_down) * gelu_slope).astype(jnp.bfloat16)
    grad_in = outer_sum(low_two, grad_pre)
    back_two, grad_gain_two = rms_backward(times_t(grad_pre, w_in), normed_two, scale_two, gain_two)
    grad_hidden = grad_out.astype(jnp.float32) + back_two
    grad_proj = grad_hidden.astype(jnp.bfloat16)
    grad_wout = outer_sum(attended_flat, grad_proj)
    grad_att = (
        times_t(grad_proj, w_out)
        .astype(jnp.bfloat16)
        .reshape(blocks, group, block, heads, head_dim)
    )
    key_back, value_back, seg_back = (
        lax.all_gather(keys, "blk", axis=1, tiled=True),
        lax.all_gather(values, "blk", axis=1, tiled=True),
        lax.all_gather(segment_ids, "blk", axis=1, tiled=True),
    )
    k_back, v_back, sk_back = key_groups(key_back, value_back, seg_back)
    start = jnp.zeros((heads, block, length), jnp.float32)

    def attend_back(carry, parts):
        q_part, k_part, v_part, sq_part, sk_part, total, d_mixed = parts
        probs, grad_probs = score_grads(
            q_part, k_part, v_part, bias, sq_part, sk_part, total, d_mixed
        )
        center = jnp.sum(probs * grad_probs, axis=-1, keepdims=True)
        grad_scores = (probs * (grad_probs - center)).astype(jnp.bfloat16)
        grad_q = jnp.einsum(
            "bhqk,bkhd->bqhd", grad_scores, k_part, preferred_element_type=jnp.float32
        ).astype(jnp.bfloat16)
        grad_k = jnp.einsum(
            "bhqk,bqhd->bkhd", grad_scores, q_part, preferred_element_type=jnp.float32
        )
        grad_v = jnp.einsum(
            "bhqk,bqhd->bkhd",
            probs.astype(jnp.bfloat16),
            d_mixed,
            preferred_element_type=jnp.float32,
        )
        paired = jnp.stack([grad_k, grad_v], axis=2).reshape(group, length, 2, inner)
        return (carry + jnp.sum(grad_scores.astype(jnp.float32), axis=0), (grad_q, paired))

    bias_grad, (grad_query, paired) = lax.scan(
        attend_back, start, (q_groups, k_back, v_back, seg_query, sk_back, log_totals, grad_att)
    )
    paired = paired.reshape(rows, length, 2, inner)
    kv_grad = lax.psum_scatter(paired, "blk", scatter_dimension=1, tiled=True).astype(jnp.bfloat16)
    grad_key = kv_grad[:, :, 0].reshape(rows * block, inner)
    grad_value = kv_grad[:, :, 1].reshape(rows * block, inner)
    grad_query = grad_query.reshape(rows * block, inner)
    grad_wq = outer_sum(low_one, grad_query)
    grad_wk = outer_sum(low_one, grad_key)
    grad_wv = outer_sum(low_one, grad_value)
    grad_low_one = (
        times_t(grad_query, w_query) + times_t(grad_key, w_key) + times_t(grad_value, w_value)
    )
    back_one, grad_gain_one = rms_backward(grad_low_one, normed_one, scale_one, gain_one)
    grad_tokens = (grad_hidden + back_one).astype(jnp.bfloat16).reshape(rows, block, width)
    grad_table = jnp.einsum("hqk,nqk->nh", bias_grad, onehot, precision=lax.Precision.HIGHEST)
    grads = (
        grad_gain_one,
        grad_wq,
        grad_wk,
        grad_wv,
        grad_wout,
        grad_gain_two,
        grad_in,
        grad_down,
        grad_table,
    )
    pieces = (
        lax.psum_scatter(grads[0], "blk", scatter_dimension=0, tiled=True),
        lax.psum_scatter(grads[1], "blk", scatter_dimension=0, tiled=True),
        lax.psum_scatter(grads[2], "blk", scatter_dimension=0, tiled=True),
        lax.psum_scatter(grads[3], "blk", scatter_dimension=0, tiled=True),
        lax.psum_scatter(grads[4], "blk", scatter_dimension=0, tiled=True),
        lax.psum_scatter(grads[5], "blk", scatter_dimension=0, tiled=True),
        lax.psum_scatter(grads[6], "blk", scatter_dimension=0, tiled=True),
        lax.psum_scatter(grads[7], "blk", scatter_dimension=0, tiled=True),
        lax.psum_scatter(grads[8], "blk", scatter_dimension=0, tiled=True),
    )
    shares = lax.psum(
        (
            pieces[0],
            pieces[1],
            pieces[2],
            pieces[3],
            pieces[4],
            pieces[5],
            pieces[6],
            pieces[7],
            pieces[8],
        ),
        "dp",
    )
    return (
        output.reshape(rows, block, width),
        grad_tokens,
        shares[0],
        shares[1],
        shares[2],
        shares[3],
        shares[4],
        shares[5],
        shares[6],
        shares[7],
        shares[8],
    )


BF = jnp.bfloat16
F32 = jnp.float32
MESH = pl.DeviceIdType.MESH
VLIMIT = 60 * 1024 * 1024
TILE = 128
REACH = 511


def mm(a, b):
    return lax.dot_general(a, b, (((1,), (0,)), ((), ())), preferred_element_type=F32)


def mm_nt(a, b):
    return lax.dot_general(a, b, (((1,), (1,)), ((), ())), preferred_element_type=F32)


def mm_tn(a, b):
    return lax.dot_general(a, b, (((0,), (0,)), ((), ())), preferred_element_type=F32)


def iota(shape, dim):
    return lax.broadcasted_iota(jnp.int32, shape, dim)


def spot():
    blk = lax.axis_index("blk")
    return lax.axis_index("dp"), blk // 2, blk % 2


def norm_rows(x, gain):
    x = x.astype(F32)
    scale = lax.rsqrt(jnp.mean(x * x, axis=-1, keepdims=True) + EPS)
    normed = x * scale
    return normed, scale, (normed * gain).astype(BF)


def flip():
    return (iota((TILE, TILE), 0) + iota((TILE, TILE), 1) == TILE - 1).astype(BF)


def flipped(x):
    turn = flip()
    parts = [mm(turn, x[i : i + TILE, :]).astype(BF) for i in range(0, x.shape[0], TILE)]
    return jnp.concatenate(parts, axis=0)


def near_rows(h, d):
    return pl.ds(pl.multiple_of((3 * h + d) * TILE, TILE), TILE)


def prepare_bias(table_ref, near, heads):
    buckets = table_ref.shape[0]
    turn = flip()
    for d in range(3):
        lane = iota((buckets, 2 * TILE), 1)
        back = jnp.where(lane < TILE, lane, lane - 2 * TILE)
        hot = (bucket_of((d - 1) * TILE - back) == iota((buckets, 2 * TILE), 0)).astype(BF)
        strip = mm_tn(table_ref[...], hot)
        for h in range(heads):
            row = jnp.broadcast_to(strip[h : h + 1, :], (TILE, 2 * TILE))
            line = pltpu.roll(row, 0, 1, stride=1, stride_axis=0)[:, :TILE]
            near[near_rows(h, d), :] = mm(line.astype(BF), turn).astype(BF)


class Sums:
    def __init__(self, nz, bufs, s_sem, r_sem):
        self.nz = nz
        self.dp, self.z, self.c = spot()
        self.bufs, self.s_sem, self.r_sem = bufs, s_sem, r_sem
        x, y = self.dp % 2, self.dp // 2
        c = self.c
        self.f, self.g = 1 + c, 2 - c
        self.s1 = (1 - c) * x + c * y
        self.s2 = (1 - c) * y + c * x
        self.peer1 = self.dp + self.f * (1 - 2 * self.s1)
        self.peer2 = self.dp + self.g * (1 - 2 * self.s2)
        self.bit, self.high = self.z % 2, self.z // 2
        self.near_z = self.z + 1 - 2 * self.bit
        self.far_z = self.z + 2 - 4 * self.high
        self.table = {}
        self.pending = []

    def copy(self, src, dst, key, dp=None, z=None, c=None):
        n = self.table.setdefault(key, len(self.table))
        dp = self.dp if dp is None else dp
        z = self.z if z is None else z
        c = self.c if c is None else c
        return pltpu.make_async_remote_copy(
            src, dst, self.s_sem.at[n], self.r_sem.at[n], device_id=(dp, 2 * z + c), device_id_type=MESH
        )

    def start(self, src, dst, key, **to):
        op = self.copy(src, dst, key, **to)
        op.start()
        self.pending.append((key, op))

    def drain(self, *head):
        left = []
        for key, op in self.pending:
            if key[: len(head)] == head:
                op.wait_send()
            else:
                left.append((key, op))
        self.pending = left

    def q(self, i1, i2):
        return i1 * self.f + i2 * self.g

    def a_start(self, u, zz, q):
        b = self.bufs[u]
        self.start(
            b["pb"].at[2 * zz + 1 - self.c, q], b["ra"].at[zz, q], (u, "a", zz, q), c=1 - self.c
        )

    def a_finish(self, u, zz):
        b = self.bufs[u]
        for q in range(4):
            self.copy(b["pb"].at[0, 0], b["ra"].at[zz, q], (u, "a", zz, q), c=1 - self.c).wait_recv()

        def one(q, carry):
            b["ra"][zz, q] = (b["ra"][zz, q].astype(F32) + b["pb"][2 * zz + self.c, q].astype(F32)).astype(BF)
            return carry

        lax.fori_loop(0, 4, one, 0)

    def first_start(self, u, zz):
        b = self.bufs[u]
        for i2 in range(2):
            self.start(
                b["ra"].at[zz, self.q(1 - self.s1, i2)], b["r1"].at[zz, i2], (u, "1", zz, i2), dp=self.peer1
            )

    def first_finish(self, u, zz):
        b = self.bufs[u]
        for i2 in range(2):
            self.copy(b["ra"].at[0, 0], b["r1"].at[zz, i2], (u, "1", zz, i2)).wait_recv()

        def one(i2, carry):
            b["r1"][zz, i2] = (
                b["r1"][zz, i2].astype(F32) + b["ra"][zz, self.q(self.s1, i2)].astype(F32)
            ).astype(BF)
            return carry

        lax.fori_loop(0, 2, one, 0)

    def second_start(self, u, zz):
        b = self.bufs[u]
        self.start(b["r1"].at[zz, 1 - self.s2], b["r2"].at[zz], (u, "2", zz), dp=self.peer2)

    def second_finish(self, u, zz):
        b = self.bufs[u]
        self.copy(b["r1"].at[0, 0], b["r2"].at[zz], (u, "2", zz)).wait_recv()
        b["r2"][zz] = (b["r2"][zz].astype(F32) + b["r1"][zz, self.s2].astype(F32)).astype(BF)

    def near_start(self, u, name, i):
        b = self.bufs[u]
        self.start(b[name].at[2 * i + 1 - self.bit], b["rz"].at[i], (u, "z", i), z=self.near_z)

    def add(self, dst, a, b, last=None):
        total = a[...].astype(F32) + b[...].astype(F32)
        dst[...] = total.astype(BF)

    def near_finish(self, u, name):
        b = self.bufs[u]
        for i in range(2):
            self.copy(b[name].at[0], b["rz"].at[i], (u, "z", i)).wait_recv()
        mine = b[name].at[2 * (1 - self.high) + self.bit]
        self.add(b["rz"].at[1 - self.high], b["rz"].at[1 - self.high], mine)
        self.start(b["rz"].at[1 - self.high], b["rz"].at[2], (u, "z", 2), z=self.far_z)
        mine = b[name].at[self.z]
        self.add(b["rz"].at[self.high], b["rz"].at[self.high], mine)

    def far_finish(self, u):
        b = self.bufs[u]
        self.copy(b["rz"].at[0], b["rz"].at[2], (u, "z", 2)).wait_recv()

    def far_last(self, u):
        self.far_finish(u)
        b = self.bufs[u]
        self.add(b["g"].at[self.dp], b["rz"].at[self.high], b["rz"].at[2])

    def far_mid(self, u):
        self.far_finish(u)
        b = self.bufs[u]
        self.add(b["rz"].at[2], b["rz"].at[self.high], b["rz"].at[2])
        self.start(b["rz"].at[2, 1 - self.s2], b["r2"].at[0], (u, "2", 0), dp=self.peer2)

    def second_last_finish(self, u):
        b = self.bufs[u]
        self.copy(b["rz"].at[0, 0], b["r2"].at[0], (u, "2", 0)).wait_recv()
        self.add(b["g"].at[self.dp], b["r2"].at[0], b["rz"].at[2, self.s2])

    def spread_two_start(self, u):
        b = self.bufs[u]
        for dp, key in ((self.peer2, "g0"), (self.peer1, "g1")):
            self.start(b["g"].at[self.dp], b["g"].at[self.dp], (u, key), dp=dp)

    def spread_two_mid(self, u):
        b = self.bufs[u]
        self.copy(b["g"].at[0], b["g"].at[self.peer2], (u, "g0")).wait_recv()
        self.start(b["g"].at[self.peer2], b["g"].at[self.peer2], (u, "g2"), dp=self.peer1)

    def spread_two_finish(self, u):
        b = self.bufs[u]
        self.copy(b["g"].at[0], b["g"].at[self.peer1], (u, "g1")).wait_recv()
        across = self.peer1 + self.peer2 - self.dp
        self.copy(b["g"].at[0], b["g"].at[across], (u, "g2")).wait_recv()

    def spread_start(self, u):
        b = self.bufs[u]
        for k in range(1, 4):
            self.start(
                b["g"].at[self.dp], b["g"].at[self.dp], (u, "g", 3 - k), dp=lax.rem(self.dp + k, 4)
            )

    def spread_finish(self, u):
        b = self.bufs[u]
        for k in range(1, 4):
            self.copy(b["g"].at[0], b["g"].at[lax.rem(self.dp + k, 4)], (u, "g", k - 1)).wait_recv()


def table_sums(diag, far, heads):
    rows = diag.shape[1]
    total = jnp.zeros((rows, TILE), F32)
    for d in range(3):
        offset = (d - 1) * TILE + iota((2 * TILE, TILE), 0) - (TILE - 1)
        hot = (bucket_of(offset) == iota((2 * TILE, TILE), 1)).astype(F32)
        total = total + lax.dot_general(
            diag[d], hot, (((1,), (0,)), ((), ())),
            preferred_element_type=F32, precision=lax.Precision.HIGHEST,
        )
    lane = iota((rows, TILE), 1)
    for side, b in ((0, 31), (1, 15)):
        total = total + jnp.where(lane == b, jnp.sum(far[side], axis=1, keepdims=True), 0.0)
    return jnp.where(iota((rows, TILE), 0) < heads, total, 0.0)


def key_masks(segall, kaug, zz, c, nkb):
    for h in range(2):
        b = 2 * zz + h
        row = segall[b, pl.ds(c, 1), :]
        r = iota((TILE, TILE), 0)
        hot = jnp.where((r == row) | (r == 8 + b), 1.0, 0.0).astype(F32)
        kaug[pl.ds(pl.multiple_of(b * TILE, TILE), TILE), :] = hot.T.astype(BF)


def query_side(q, segall, table, qa, z, c, nkb):
    tq = q.shape[0]
    lost, right, left = [], [], []
    for i in range(tq // TILE):
        qb = (tq // TILE) * z + i
        row = segall[qb, pl.ds(c, 1), :]
        r = iota((TILE, TILE), 0)
        one = jnp.where((r < 8) & (r != row), NEG, 0.0).astype(F32)
        lost.append(mm(flip(), one.T.astype(BF)))
        col = iota((TILE, TILE), 1) - 8
        ok = (col >= 0) & (col < nkb)
        right.append(jnp.where(ok & (col >= qb + 2), 1.0, 0.0))
        left.append(jnp.where(ok & (col <= qb - 2), 1.0, 0.0))
    low = iota((tq, TILE), 1) < TILE // 2
    for p in range(qa.shape[0]):
        part = q[:, p * TILE : (p + 1) * TILE]
        for hh in range(2):
            h = 2 * p + hh
            rows = slice(hh * tq, (hh + 1) * tq)
            qa[p, rows, 0:TILE] = jnp.where(low if hh == 0 else jnp.logical_not(low), part, 0.0).astype(BF)
            far_r = table[31:32, h : h + 1].astype(F32)
            far_l = table[15:16, h : h + 1].astype(F32)
            for i in range(tq // TILE):
                at = hh * tq + i * TILE
                qa[p, at : at + TILE, TILE:] = (lost[i] + far_r * right[i] + far_l * left[i]).astype(BF)


def attend_step(i, zz, z, k, v, kaug, qa, near, probs, stat, s, acc, tq):
    rows = pl.ds(pl.multiple_of(zz * tq, tq), tq)
    blocks = tq // TILE

    def pair(p, carry):
        cols = pl.ds(pl.multiple_of(p * TILE, TILE), TILE)
        s[...] = mm_nt(jnp.concatenate([k[rows, cols], kaug[rows, :]], axis=1), qa[p])
        if i == 0:
            for kk in range(blocks):
                for qq in range(blocks):
                    for hh in range(2):
                        at = hh * tq + qq * TILE
                        spot_ = (slice(kk * TILE, (kk + 1) * TILE), slice(at, at + TILE))
                        s[spot_] = s[spot_] + near[near_rows(2 * p + hh, kk - qq + 1), :].astype(F32)
        else:

            @pl.when(jnp.abs(zz - z) == 1)
            def _():
                after = (zz - z + 1) // 2
                kr = pl.ds(pl.multiple_of((1 - after) * (tq - TILE), TILE), TILE)
                for hh in range(2):
                    qc = pl.ds(pl.multiple_of(hh * tq + after * (tq - TILE), TILE), TILE)
                    s[kr, qc] = s[kr, qc] + near[near_rows(2 * p + hh, 2 * after), :].astype(F32)

        top = jnp.max(s[...], axis=0, keepdims=True)
        if i > 0:
            old = stat[p, 0:1, :]
            top = jnp.maximum(old, top)
        e = jnp.exp(s[...] - top)
        probs[p, rows, :] = e.astype(BF)
        total = jnp.sum(e, axis=0, keepdims=True)
        mixed = mm_tn(v[rows, cols], probs[p, rows, :])
        arows = pl.ds(pl.multiple_of(p * TILE, TILE), TILE)
        if i > 0:
            fade = jnp.exp(old - top)
            total = total + stat[p, 1:2, :] * fade
            mixed = mixed + acc[arows, :] * fade
        acc[arows, :] = mixed
        stat[p, 0:1, :] = top
        stat[p, 1:2, :] = total
        stat[p, 2 + i : 3 + i, :] = top
        return carry

    lax.fori_loop(0, probs.shape[0], pair, 0)


def attn_backward_pair(p, z, nz, qa, k, v, kaug, datt, probs, scale, dq, diag, far, dm, dprob, ds):
    tq = dq.shape[0]
    length = k.shape[0]
    nkb = length // TILE
    cols = slice(p * TILE, (p + 1) * TILE)
    part = datt[p * tq : (p + 1) * tq, :].astype(F32)
    low = iota((tq, TILE), 1) < TILE // 2
    both = jnp.concatenate([jnp.where(low, part, 0.0), jnp.where(low, 0.0, part)], axis=0)
    column = scale[p].T
    total = jnp.zeros((8, 2 * tq), F32)
    for b in range(nz):
        rows = slice(b * tq, (b + 1) * tq)
        scaled = (both * column[:, b : b + 1]).astype(BF)
        dm[b * 2 * tq : (b + 1) * 2 * tq, :] = scaled
        dprob[rows, :] = mm_nt(v[rows, cols], scaled)
        mixed = dprob[rows, :] * probs[p, rows, :].astype(F32)
        total = total + jnp.sum(mixed.reshape(tq // 8, 8, 2 * tq), axis=0)
    center = jnp.sum(total, axis=0, keepdims=True)
    for b in range(nz):
        rows = slice(b * tq, (b + 1) * tq)
        v[rows, cols] = mm(probs[p, rows, :], dm[b * 2 * tq : (b + 1) * 2 * tq, :]).astype(BF)
        shift = center * scale[p, b : b + 1, :]
        ds[TILE + b * tq : TILE + (b + 1) * tq, :] = (
            probs[p, rows, :].astype(F32) * (dprob[rows, :] - shift)
        ).astype(BF)
    left = jnp.concatenate([k[:, cols], kaug[...]], axis=1)
    back = mm_tn(left, ds[TILE : TILE + length, :])
    k[:, cols] = mm(ds[TILE : TILE + length, :], qa[p, :, 0:TILE]).astype(BF)
    both = jnp.concatenate([back[: TILE // 2, :tq], back[TILE // 2 : TILE, tq:]], axis=0)
    dq[:, cols] = both.T.astype(BF)
    sums = back[TILE + 8 : TILE + 8 + nkb, :]
    kb = iota((nkb, 2 * tq), 0)
    lane = iota((nkb, 2 * tq), 1)
    qb = (tq // TILE) * z + (lane % tq) // TILE
    right = jnp.sum(jnp.where(kb >= qb + 2, sums, 0.0), axis=0, keepdims=True)
    left = jnp.sum(jnp.where(kb <= qb - 2, sums, 0.0), axis=0, keepdims=True)
    for hh in range(2):
        h = 2 * p + hh
        far[0, h : h + 1, :] = right[:, hh * tq : (hh + 1) * tq]
        far[1, h : h + 1, :] = left[:, hh * tq : (hh + 1) * tq]
        for d in range(3):
            near_sum = jnp.zeros((TILE, TILE), F32)
            for i in range(tq // TILE):
                row = ((tq // TILE) * z + i + d) * TILE
                at = hh * tq + i * TILE
                near_sum = near_sum + ds[pl.ds(pl.multiple_of(row, TILE), TILE), at : at + TILE].astype(F32)
            wide = jnp.concatenate([near_sum, jnp.zeros((TILE, TILE), F32)], axis=1)
            wide = pltpu.roll(wide, 0, 1, stride=1, stride_axis=0)
            diag[d, h : h + 1, :] = jnp.sum(wide, axis=0, keepdims=True)


def layer_kernel(nz, *refs):
    (tok_h, dy_h, seg, wq_h, wk_h, wv_h, wout_h, win_h, wdown_h, gains, table) = refs[:11]
    o_out, o_gt, g_down, g_in, g_attn, o_small = refs[11:17]
    (
        x, k, v, qa, probs, att, dy, wqkv, wout, buf_a, buf_b, pdown, pin,
        ra_d, ra_i, r1_d, r2_d, rz_d, r1_i, r2_i, rz_i, r2_a, rz_a,
        n2, dh, dhl, own_dn1, dprob, ds, near, kaug, diag, far, stat, scale,
        rd, relay, segall, segbuf, sm, smr, s_sem, r_sem, l_sem, gs_sem, gr_sem, credit, credit1,
    ) = refs[17:]
    bufs = {
        "down": dict(pb=pdown, ra=ra_d, r1=r1_d, r2=r2_d, rz=rz_d, g=g_down),
        "in": dict(pb=pin, ra=ra_i, r1=r1_i, r2=r2_i, rz=rz_i, g=g_in),
        "attn": dict(pb=buf_a, ra=ra_d, r1=r1_d, r2=r2_a, rz=rz_a, g=g_attn),
    }
    eng = Sums(nz, bufs, s_sem, r_sem)
    dp, z, c = eng.dp, eng.z, eng.c
    blk = 2 * z + c
    nb, block, width = x.shape
    tq = 2 * block
    length = nb * block
    nkb = length // TILE
    share = width // nb
    steps = buf_b.shape[0]
    per = nb // steps
    pairs = probs.shape[0]
    heads = 2 * pairs
    barrier = pltpu.get_barrier_semaphore()
    peers = [(dp, lax.rem(blk + i, nb)) for i in range(1, nb)]
    peers += [(eng.peer1, blk), (eng.peer2, blk), (eng.peer1 + eng.peer2 - dp, blk)]
    for peer in peers:
        pl.semaphore_signal(barrier, inc=1, device_id=peer, device_id_type=MESH)

    loads = {}

    def load(name, src, dst):
        loads[name] = pltpu.make_async_copy(src, dst, l_sem.at[len(loads)])
        loads[name].start()

    def ready(*names):
        for name in names:
            loads[name].wait()

    load("x", tok_h.at[c], x.at[blk])
    load("wk", wk_h, wqkv.at[1])
    load("wv", wv_h, wqkv.at[2])
    load("wq", wq_h, wqkv.at[0])

    def gcopy(src, dst, send, recv, zz, cc):
        return pltpu.make_async_remote_copy(
            src, dst, gs_sem.at[send], gr_sem.at[recv], device_id=(dp, 2 * zz + cc), device_id_type=MESH
        )

    def inside(other):
        return (other >= 0) & (other < nz)

    segbuf[...] = jnp.zeros_like(segbuf)
    segbuf[0:2, :] = seg[...]
    segall[blk] = segbuf[...]
    pl.semaphore_wait(barrier, len(peers))

    ways = ((0, 1), (1, -1))
    mine = x.at[blk]
    gcopy(tok_h.at[1 - c], mine, 4, blk, z, 1 - c).start()
    for i in range(1, nb):
        pltpu.make_async_remote_copy(
            segbuf, segall.at[blk], gs_sem.at[10 + i], gr_sem.at[nb + 1 + blk],
            device_id=(dp, lax.rem(blk + i, nb)), device_id_type=MESH,
        ).start()
    for way, dz in ways:

        @pl.when(inside(z + dz))
        def _():
            gcopy(tok_h.at[1 - c], mine, 2 * way, blk, z + dz, 1 - c).start()
            gcopy(tok_h.at[c], mine, 2 * way + 1, blk, z + dz, c).start()

    gcopy(dy_h.at[1 - c], dy.at[c], 5, nb, z, 1 - c).start()
    load("dy", dy_h.at[c], dy.at[c])
    load("wout", wout_h, wout)
    for j in range(steps):
        load(("win", j), win_h.at[:, j * width : (j + 1) * width], buf_b.at[j])
        load(("wdown", j), wdown_h.at[j * per : (j + 1) * per], buf_a.at[j * per : (j + 1) * per])

    prepare_bias(table, near, heads)
    reach = -(-REACH // tq)
    for zz in range(nz):

        @pl.when(jnp.abs(zz - z) > reach)
        def _():
            rows = slice(zz * tq, (zz + 1) * tq)
            x[2 * zz : 2 * zz + 2] = jnp.zeros((2, block, width), BF)
            for ref in (k, v):
                ref[rows, :] = jnp.zeros((tq, width), BF)
            kaug[rows, :] = jnp.zeros((tq, TILE), BF)
            for p in range(pairs):
                probs[p, rows, :] = jnp.zeros((tq, 2 * tq), BF)

    ds[0:TILE, :] = jnp.zeros((TILE, ds.shape[1]), BF)
    ds[ds.shape[0] - TILE :, :] = jnp.zeros((TILE, ds.shape[1]), BF)
    diag[...] = jnp.zeros_like(diag)
    far[...] = jnp.zeros_like(far)
    scale[...] = jnp.zeros_like(scale)
    sm[0] = jnp.zeros(sm.shape[1:], F32)
    gain1 = gains[0:1, :].astype(F32)
    gain2 = gains[1:2, :].astype(F32)

    def x_arrived(b):
        gcopy(x.at[b], x.at[b], 0, b, z, 1 - c).wait_recv()

    def seg_arrived(b):
        gcopy(segbuf, segall.at[b], 0, nb + 1 + b, z, 1 - c).wait_recv()

    def keys_of(zz):
        rows = pl.ds(pl.multiple_of(zz * tq, tq), tq)
        key_masks(segall, kaug, zz, c, nkb)
        n1 = norm_rows(x[pl.ds(2 * zz, 2)].reshape(tq, width), gain1)[2]
        k[rows, :] = mm(n1, wqkv[1]).astype(BF)
        v[rows, :] = mm(n1, wqkv[2]).astype(BF)
        return n1

    s_blk, acc = dprob.at[0:tq], dprob.at[tq : tq + pairs * TILE]
    ready("x", "wk", "wv", "wq")
    x_arrived(2 * z + 1 - c)
    seg_arrived(2 * z + 1 - c)
    q_rev = mm(flipped(keys_of(z)), wqkv[0]).astype(BF).astype(F32)
    query_side(q_rev, segall, table, qa, z, c, nkb)
    order = (z, eng.near_z, 2 - eng.high, 3 - 3 * eng.high)
    attend_step(0, order[0], z, k, v, kaug, qa, near, probs, stat, s_blk, acc, tq)
    for way, dz in ways:
        src = z - dz

        @pl.when(inside(src))
        def _():
            for h in range(2):
                x_arrived(2 * src + h)

                @pl.when(inside(z + dz))
                def _():
                    gcopy(
                        x.at[2 * src + h], x.at[2 * src + h], 6 + 2 * way + h, 2 * src + h, z + dz, c
                    ).start()

    for i in range(1, nb):
        other = lax.rem(blk + i, nb)

        @pl.when(other // 2 != z)
        def _():
            seg_arrived(other)

    for i in range(1, 4):
        zz = order[i]

        @pl.when(jnp.abs(zz - z) <= reach)
        def _():
            @pl.when(jnp.abs(zz - z) == 2)
            def _():
                for h in range(2):
                    x_arrived(2 * zz + h)

            keys_of(zz)
            attend_step(i, zz, z, k, v, kaug, qa, near, probs, stat, s_blk, acc, tq)

    for p in range(pairs):
        inverse = 1.0 / stat[p, 1:2, :]
        top = stat[p, 0:1, :]
        for i in range(4):

            @pl.when(jnp.abs(order[i] - z) <= reach)
            def _():
                scale[p, pl.ds(order[i], 1), :] = jnp.exp(stat[p, 2 + i : 3 + i, :] - top) * inverse

        mixed = acc[p * TILE : (p + 1) * TILE, :] * inverse
        both = jnp.concatenate([mixed[: TILE // 2, :tq], mixed[TILE // 2 :, tq:]], axis=0)
        att[:, p * TILE : (p + 1) * TILE] = both.T.astype(BF)
    att[...] = flipped(att[...])

    ready("wout")
    x_own = x.at[pl.ds(2 * z, 2)]
    dh[...] = x_own[...].reshape(tq, width).astype(F32) + mm(att[...], wout[...])
    n2[...] = norm_rows(dh[...], gain2)[2]
    ready("dy")
    gcopy(dy.at[0], dy.at[1 - c], 0, nb, z, 1 - c).wait_recv()
    total = own_dn1
    for j in range(steps):
        ready(("win", j), ("wdown", j))
        value, slant = gelu_both(mm(n2[...], buf_b[j]))
        act = value.astype(BF)
        down = buf_a[j * per : (j + 1) * per].reshape(width, width)
        d = dy[...].reshape(tq, width)
        pdown[j * per : (j + 1) * per] = mm_tn(act, d).astype(BF).reshape(per, 4, share, width)
        for qq in range(4):
            eng.a_start("down", j, qq)
        dpre = (mm_nt(d, down) * slant).astype(BF)
        pin[:, j] = mm_tn(n2[...], dpre).astype(BF).reshape(nb, share, width)
        for zz in range(nz):
            eng.a_start("in", zz, j)
        if j == 0:
            total[...] = mm(act, down)
            dn2 = mm_nt(dpre, buf_b[j])
        else:
            total[...] += mm(act, down)
            dn2 = dn2 + mm_nt(dpre, buf_b[j])
        if j > 0:
            eng.a_finish("down", j - 1)
            eng.first_start("down", j - 1)
    h = dh[...]
    n2[...] = (h + total[...]).astype(BF)
    eng.a_finish("down", steps - 1)
    eng.first_start("down", steps - 1)
    normed, r2, _ = norm_rows(h, gain2)
    back, gain_grad = rms_backward(dn2, normed, r2, gain2)
    lines = width // TILE
    for i in range(lines):
        sm[0, lines + i : lines + i + 1, :] = gain_grad[None, i * TILE : (i + 1) * TILE]
    dh[...] = dy[...].reshape(tq, width).astype(F32) + back
    dhl[...] = dh[...].astype(BF)
    back = flipped(mm_nt(dhl[...], wout[...]).astype(BF))
    datt, dm = near.at[0 : pairs * tq], near.at[pairs * tq : pairs * tq + nz * 2 * tq]
    for p in range(pairs):
        datt[p * tq : (p + 1) * tq, :] = back[:, p * TILE : (p + 1) * TILE]
    for zz in range(nz):
        eng.a_finish("in", zz)
        eng.first_start("in", zz)
    out_half = [n2.at[pl.ds(pl.multiple_of(i * block, block), block)] for i in (c, 1 - c)]
    eng.start(out_half[1], o_out.at[c], ("out",), c=1 - c)
    load("kept", out_half[0], o_out.at[c])
    buf_a[:, 3] = mm_tn(att[...], dhl[...]).astype(BF).reshape(nb, share, width)

    dq = dhl
    for b in range(nz):
        buf_b[b, tq : 2 * tq] = norm_rows(x[2 * b : 2 * b + 2].reshape(tq, width), gain1)[2]

    def first_near(u, i):
        for zz in (2 * i, 2 * i + 1):
            eng.first_finish(u, zz)
        eng.near_start(u, "r1", i)

    def first_second(u, i):
        for zz in (2 * i, 2 * i + 1):
            eng.first_finish(u, zz)
            eng.second_start(u, zz)

    def second_near(u, i):
        for zz in (2 * i, 2 * i + 1):
            eng.second_finish(u, zz)
        eng.near_start(u, "r2", i)

    for p in range(pairs):
        attn_backward_pair(
            p, z, nz, qa, k, v, kaug, datt, probs, scale, dq, diag, far, dm, dprob, ds
        )
        if p < 2:
            first_near("down", p)
        if p == 2:
            eng.drain("down", "1")
            pl.semaphore_signal(credit, inc=1, device_id=(dp, 2 * z + 1 - c), device_id_type=MESH)
        if p == 3:
            eng.near_finish("down", "r1")
            eng.drain("down", "z", 0)
            eng.drain("down", "z", 1)
            pl.semaphore_signal(credit1, inc=1, device_id=(eng.peer1, blk), device_id_type=MESH)
            pl.semaphore_wait(credit, 1)
            for zz in range(nz):
                eng.a_start("attn", zz, 3)
        if p >= 4:
            first_second("in", p - 4)

    def weight(i, parts):
        grad = sum(mm_tn(left, right) for left, right in parts)
        buf_a[:, i] = grad.astype(BF).reshape(nb, share, width)
        for zz in range(nz):
            eng.a_start("attn", zz, i)

    for i, ref in ((1, k), (2, v)):
        weight(i, [(buf_b[b, tq : 2 * tq], ref[b * tq : (b + 1) * tq, :]) for b in range(nz)])
    eng.far_mid("down")
    dq[...] = flipped(dq[...])
    weight(0, [(buf_b[z, tq : 2 * tq], dq[...])])
    second_near("in", 0)

    own_dn1[...] = mm_nt(dq[...], wqkv[0])
    own_normed = norm_rows(x_own[...].reshape(tq, width), gain1)[0]
    gain_sum = jnp.sum(own_dn1[...] * own_normed, axis=0, keepdims=True)
    for b in range(nz):
        rows = slice(b * tq, (b + 1) * tq)
        part = mm_nt(k[rows, :], wqkv[1]) + mm_nt(v[rows, :], wqkv[2])
        buf_b[b, 0:tq] = part.astype(BF)
        normed = norm_rows(x[2 * b : 2 * b + 2].reshape(tq, width), gain1)[0]
        gain_sum = gain_sum + jnp.sum(part * normed, axis=0, keepdims=True)

        @pl.when(z == b)
        def _():
            own_dn1[...] += part

    for way, dz in ways:

        @pl.when(inside(z + 2 * dz))
        def _():
            eng.copy(buf_b.at[z + 2 * dz, 0:tq], relay.at[way], ("d1", way), z=z + dz).start()

    pl.semaphore_wait(credit1, 1)
    for zz in range(nz):
        eng.a_finish("attn", zz)
        eng.first_start("attn", zz)
    second_near("in", 1)
    eng.second_last_finish("down")
    eng.spread_two_start("down")
    for i in range(lines):
        sm[0, i : i + 1, :] = gain_sum[:, i * TILE : (i + 1) * TILE]
    sm[0, 2 * lines :, :] = table_sums(diag, far, heads)[: sm.shape[1] - 2 * lines]
    hops = (
        dict(c=1 - c), dict(dp=dp + 1 - 2 * (dp % 2)), dict(dp=dp + 2 - 4 * (dp // 2)),
        dict(z=eng.near_z), dict(z=eng.far_z),
    )

    def small_start(i):
        eng.start(sm.at[i], smr.at[i], ("s", i), **hops[i])

    def small_finish(i):
        eng.copy(sm.at[i], smr.at[i], ("s", i), **hops[i]).wait_recv()
        sm[i + 1] = sm[i] + smr[i]

    small_start(0)
    eng.near_finish("in", "r2")
    first_second("attn", 0)
    small_finish(0)
    small_start(1)
    for way, dz in ways:

        @pl.when(inside(z - dz) & inside(z + dz))
        def _():
            eng.copy(relay.at[way], relay.at[way], ("d1", way)).wait_recv()
            buf_b[z + dz, 0:tq] = (buf_b[z + dz, 0:tq].astype(F32) + relay[way].astype(F32)).astype(BF)

        @pl.when(inside(z + dz))
        def _():
            eng.copy(buf_b.at[z + dz, 0:tq], rd.at[way], ("d2", way), z=z + dz).start()

    eng.spread_two_mid("down")
    first_second("attn", 1)
    small_finish(1)
    small_start(2)
    eng.far_last("in")
    eng.spread_two_start("in")
    second_near("attn", 0)
    small_finish(2)
    small_start(3)
    second_near("attn", 1)
    eng.spread_two_mid("in")
    small_finish(3)
    small_start(4)
    eng.near_finish("attn", "r2")

    dn1 = own_dn1
    for way, dz in ways:

        @pl.when(inside(z - dz))
        def _():
            eng.copy(rd.at[way], rd.at[way], ("d2", way)).wait_recv()
            dn1[...] += rd[way].astype(F32)

    normed, r1, _ = norm_rows(x_own[...].reshape(tq, width), gain1)
    back, _ = rms_backward(dn1[...], normed, r1, gain1)
    dy[...] = (dh[...] + back).astype(BF).reshape(dy.shape)
    eng.start(dy.at[1 - c], o_gt.at[c], ("gt",), c=1 - c)
    load("kept_gt", dy.at[c], o_gt.at[c])

    small_finish(4)
    o_small[...] = sm[5]
    eng.far_last("attn")
    eng.spread_start("attn")
    eng.copy(dy.at[0], o_out.at[1 - c], ("out",)).wait_recv()
    eng.copy(dy.at[0], o_gt.at[1 - c], ("gt",)).wait_recv()
    ready("kept", "kept_gt")
    eng.spread_two_finish("down")
    eng.spread_two_finish("in")
    eng.spread_finish("attn")
    eng.drain()
    gcopy(tok_h.at[0], mine, 4, blk, z, 1 - c).wait_send()
    gcopy(dy_h.at[0], dy.at[0], 5, nb, z, 1 - c).wait_send()
    for i in range(1, nb):
        gcopy(segbuf, segall.at[0], 10 + i, nb + 1, z, 1 - c).wait_send()
    for way, dz in ways:

        @pl.when(inside(z + dz))
        def _():
            gcopy(tok_h.at[0], mine, 2 * way, blk, z, 1 - c).wait_send()
            gcopy(tok_h.at[0], mine, 2 * way + 1, blk, z, 1 - c).wait_send()
            eng.copy(buf_b.at[0, 0:tq], rd.at[way], ("d2", way)).wait_send()

        @pl.when(inside(z + 2 * dz))
        def _():
            eng.copy(buf_b.at[0, 0:tq], relay.at[way], ("d1", way)).wait_send()

        @pl.when(inside(z - dz) & inside(z + dz))
        def _():
            for h in range(2):
                gcopy(tok_h.at[0], mine, 6 + 2 * way + h, blk, z, 1 - c).wait_send()


def layer(nz, tok, dy, seg, wq, wk, wv, wout, win, wdown, gains, table):
    _, block, width = tok.shape
    nb = 2 * nz
    length, tq = nb * block, 2 * block
    share = width // nb
    pairs = table.shape[1] // 2
    steps = win.shape[1] // width
    vm = pl.BlockSpec(memory_space=pltpu.VMEM)
    hbm = pl.BlockSpec(memory_space=pl.ANY)
    home = jax.ShapeDtypeStruct((2, block, width), BF)
    quarters = jax.ShapeDtypeStruct((4, share, width), BF)
    one = (share, width)
    small = (24, TILE)

    def bf(*shape):
        return pltpu.VMEM(shape, BF)

    def f32(*shape):
        return pltpu.VMEM(shape, F32)

    sums = [bf(nz, 4, *one), bf(nz, 4, *one)]
    for i, route in enumerate(("xzy", "xyz", "xyz")):
        last = route == "xyz"
        sums += [bf(nz, 2, *one)] if i < 2 else []
        sums += [bf(nz if last else 1, *one), bf(3, *one) if last else bf(3, 2, *one)]
    scratch = [
        bf(nb, block, width), bf(length, width), bf(length, width),
        bf(pairs, 2 * tq, 2 * TILE), bf(pairs, length, 2 * tq), bf(tq, width),
        bf(2, block, width), bf(3, width, width), bf(width, width),
        bf(nb, 4, *one), bf(steps, width, width), bf(nb, 4, *one), bf(nb, 4, *one),
        *sums,
        bf(tq, width), f32(tq, width), bf(tq, width), f32(tq, width),
        f32(length, 2 * tq), bf(length + 2 * TILE, 2 * tq), bf(max(2 * pairs * 3 * TILE, pairs * tq + nz * 2 * tq), TILE), bf(length, TILE),
        f32(3, 16, 2 * TILE), f32(2, 16, tq), f32(pairs, 8, 2 * tq), f32(pairs, 8, 2 * tq),
        bf(2, tq, width), bf(2, tq, width),
        pltpu.VMEM((nb, 8, block), jnp.int32), pltpu.VMEM((8, block), jnp.int32),
        f32(6, *small), f32(5, *small),
        pltpu.SemaphoreType.DMA((140,)), pltpu.SemaphoreType.DMA((140,)), pltpu.SemaphoreType.DMA((32,)),
        pltpu.SemaphoreType.DMA((10 + nb,)), pltpu.SemaphoreType.DMA((2 * nb + 2,)),
        pltpu.SemaphoreType.REGULAR, pltpu.SemaphoreType.REGULAR,
    ]
    return pl.pallas_call(
        functools.partial(layer_kernel, nz),
        out_shape=(home, home, quarters, quarters, quarters, jax.ShapeDtypeStruct(small, F32)),
        in_specs=[hbm, hbm, vm] + [hbm] * 6 + [vm, vm],
        out_specs=(vm,) * 6,
        scratch_shapes=scratch,
        compiler_params=pltpu.CompilerParams(
            collective_id=1, has_side_effects=True, vmem_limit_bytes=64 * 1024 * 1024
        ),
    )(tok, dy, seg, wq, wk, wv, wout, win, wdown, gains, table)


def fast_device(
    nz, tokens, segment_ids, gain_attn, w_query, w_key, w_value, w_out, gain_ffn, w_in, w_down,
    rel_table, cotangent,
):
    rows, block, width = tokens.shape
    nb = 2 * nz
    share = width // nb
    out, grad_tokens, gdown, gin, gattn, small = layer(
        nz, tokens, cotangent, segment_ids, w_query, w_key, w_value, w_out, w_in,
        w_down.reshape(nb, 4, w_down.shape[0] // nb // 4, width),
        jnp.stack([gain_attn, gain_ffn]), rel_table,
    )
    b = lax.axis_index("blk")
    lines = width // TILE
    ga = lax.dynamic_slice_in_dim(small[:lines].reshape(-1), b * share, share)
    gf = lax.dynamic_slice_in_dim(small[lines : 2 * lines].reshape(-1), b * share, share)
    heads = rel_table.shape[1]
    gt = lax.dynamic_slice(small, (2 * lines, b * (32 // nb)), (heads, 32 // nb)).T
    gin = jnp.transpose(gin, (1, 0, 2)).reshape(share, -1).astype(F32)
    gattn = gattn.astype(F32)
    return (
        out, grad_tokens, ga, gattn[0], gattn[1], gattn[2], gattn[3], gf, gin,
        gdown.reshape(-1, width).astype(F32), gt,
    )


def pick(mesh):
    if mesh.shape["dp"] == 4 and mesh.shape["blk"] == 8:
        return functools.partial(fast_device, mesh.shape["blk"] // 2)
    return on_device


def solution(mesh):
    placed = (
        P("dp", "blk", None),
        P("dp", "blk"),
        P(),
        P(),
        P(),
        P(),
        P(),
        P(),
        P(),
        P(),
        P(),
        P("dp", "blk", None),
    )
    return jax.shard_map(
        pick(mesh),
        mesh=mesh,
        in_specs=placed,
        out_specs=(
            P("dp", "blk", None),
            P("dp", "blk", None),
            P("blk"),
            P("blk", None),
            P("blk", None),
            P("blk", None),
            P("blk", None),
            P("blk"),
            P("blk", None),
            P("blk", None),
            P("blk", None),
        ),
        check_vma=False,
    )
```

```python
import functools
import math

import jax
import jax.numpy as jnp
from jax import lax
from jax.experimental import pallas as pl
from jax.experimental.pallas import tpu as pltpu
from jax.sharding import PartitionSpec as P

EPS = 1e-06
NEG = -1e30
EDGES = (12, 16, 23, 32, 46, 64, 91)
ROOT_TWO_PI = 0.7978845608028654
CUBIC = 0.044715


def bucket_of(offset):
    distance = jnp.abs(offset)
    far_part = 8 + sum(((distance >= edge).astype(jnp.int32) for edge in EDGES))
    return jnp.where(offset > 0, 16, 0) + jnp.where(distance < 8, distance, far_part)


def gelu_both(values):
    inner_arg = ROOT_TWO_PI * (values + CUBIC * values * values * values)
    tangent = jnp.tanh(inner_arg)
    result = 0.5 * values * (1.0 + tangent)
    slope = 0.5 * (1.0 + tangent) + 0.5 * values * (1.0 - tangent * tangent) * ROOT_TWO_PI * (
        1.0 + 3.0 * CUBIC * values * values
    )
    return (result, slope)


def rms_forward(values, gain):
    scale = lax.rsqrt(jnp.mean(values * values, axis=-1, keepdims=True) + EPS)
    normed = values * scale
    return (normed, scale, (normed * gain).astype(jnp.bfloat16))


def rms_backward(grad, normed, scale, gain):
    gain_grad = jnp.sum(grad * normed, axis=0)
    inner_grad = grad * gain
    back = scale * (inner_grad - normed * jnp.mean(inner_grad * normed, axis=-1, keepdims=True))
    return (back, gain_grad)


def outer_sum(left, right):
    return jnp.einsum("td,tf->df", left, right, preferred_element_type=jnp.float32)


def times_t(left, right):
    return jnp.einsum("tf,df->td", left, right, preferred_element_type=jnp.float32)


def masked_scores(query, keys, bias, seg_query, seg_keys):
    raw = (
        jnp.einsum("bqhd,bkhd->bhqk", query, keys, preferred_element_type=jnp.float32) + bias[None]
    )
    same = seg_query[:, None, :, None] == seg_keys[:, None, None, :]
    return jnp.where(same, raw, NEG)


def score_grads(q_part, k_part, v_part, bias, sq_part, sk_part, total, d_mixed):
    scores = masked_scores(q_part, k_part, bias, sq_part, sk_part)
    probs = jnp.exp(scores - total[..., None])
    grad_probs = jnp.einsum("bqhd,bkhd->bhqk", d_mixed, v_part, preferred_element_type=jnp.float32)
    return (probs, grad_probs)


def on_device(
    tokens,
    segment_ids,
    gain_attn,
    w_query,
    w_key,
    w_value,
    w_out,
    gain_ffn,
    w_in,
    w_down,
    rel_table,
    cotangent,
):
    rows, block, width = tokens.shape
    buckets, heads = rel_table.shape
    inner = w_query.shape[1]
    head_dim = inner // heads
    length = block * lax.axis_size("blk")
    group = math.gcd(rows, max(1, 512 // block))
    blocks = rows // group
    gain_one = gain_attn.astype(jnp.float32)
    gain_two = gain_ffn.astype(jnp.float32)
    table_f = rel_table.astype(jnp.float32)
    flat = tokens.reshape(rows * block, width).astype(jnp.float32)
    normed_one, scale_one, low_one = rms_forward(flat, gain_one)

    def project(weight):
        return (
            jnp.dot(low_one, weight, preferred_element_type=jnp.float32)
            .astype(jnp.bfloat16)
            .reshape(rows, block, inner)
        )

    query, keys, values = (project(w_query), project(w_key), project(w_value))
    key_all, value_all, seg_all = (
        lax.all_gather(keys, "blk", axis=1, tiled=True),
        lax.all_gather(values, "blk", axis=1, tiled=True),
        lax.all_gather(segment_ids, "blk", axis=1, tiled=True),
    )
    places = lax.axis_index("blk") * block + jnp.arange(block, dtype=jnp.int32)
    offsets = jnp.arange(length, dtype=jnp.int32)[None, :] - places[:, None]
    onehot = (
        bucket_of(offsets)[None] == jnp.arange(buckets, dtype=jnp.int32)[:, None, None]
    ).astype(jnp.float32)
    bias = jnp.einsum("nqk,nh->hqk", onehot, table_f, precision=lax.Precision.HIGHEST)
    q_groups = query.reshape(blocks, group, block, heads, head_dim)
    seg_query = segment_ids.reshape(blocks, group, block)

    def key_groups(key_rows, value_rows, seg_rows):
        return (
            key_rows.reshape(blocks, group, length, heads, head_dim),
            value_rows.reshape(blocks, group, length, heads, head_dim),
            seg_rows.reshape(blocks, group, length),
        )

    k_groups, v_groups, seg_keys = key_groups(key_all, value_all, seg_all)

    def attend(parts):
        q_part, k_part, v_part, sq_part, sk_part = parts
        scores = masked_scores(q_part, k_part, bias, sq_part, sk_part)
        top = jnp.max(scores, axis=-1, keepdims=True)
        total = jnp.log(jnp.sum(jnp.exp(scores - top), axis=-1, keepdims=True)) + top
        probs = jnp.exp(scores - total).astype(jnp.bfloat16)
        mixed = jnp.einsum("bhqk,bkhd->bqhd", probs, v_part, preferred_element_type=jnp.float32)
        return (mixed.astype(jnp.bfloat16), total[..., 0])

    attended, log_totals = lax.map(attend, (q_groups, k_groups, v_groups, seg_query, seg_keys))
    attended_flat = attended.reshape(rows * block, inner)
    hidden = flat + jnp.dot(attended_flat, w_out, preferred_element_type=jnp.float32)
    normed_two, scale_two, low_two = rms_forward(hidden, gain_two)
    pre = jnp.dot(low_two, w_in, preferred_element_type=jnp.float32)
    gelu_value, gelu_slope = gelu_both(pre)
    active = gelu_value.astype(jnp.bfloat16)
    output = (hidden + jnp.dot(active, w_down, preferred_element_type=jnp.float32)).astype(
        jnp.bfloat16
    )
    grad_out = cotangent.reshape(rows * block, width)
    grad_down = outer_sum(active, grad_out)
    grad_pre = (times_t(grad_out, w_down) * gelu_slope).astype(jnp.bfloat16)
    grad_in = outer_sum(low_two, grad_pre)
    back_two, grad_gain_two = rms_backward(times_t(grad_pre, w_in), normed_two, scale_two, gain_two)
    grad_hidden = grad_out.astype(jnp.float32) + back_two
    grad_proj = grad_hidden.astype(jnp.bfloat16)
    grad_wout = outer_sum(attended_flat, grad_proj)
    grad_att = (
        times_t(grad_proj, w_out)
        .astype(jnp.bfloat16)
        .reshape(blocks, group, block, heads, head_dim)
    )
    key_back, value_back, seg_back = (
        lax.all_gather(keys, "blk", axis=1, tiled=True),
        lax.all_gather(values, "blk", axis=1, tiled=True),
        lax.all_gather(segment_ids, "blk", axis=1, tiled=True),
    )
    k_back, v_back, sk_back = key_groups(key_back, value_back, seg_back)
    start = jnp.zeros((heads, block, length), jnp.float32)

    def attend_back(carry, parts):
        q_part, k_part, v_part, sq_part, sk_part, total, d_mixed = parts
        probs, grad_probs = score_grads(
            q_part, k_part, v_part, bias, sq_part, sk_part, total, d_mixed
        )
        center = jnp.sum(probs * grad_probs, axis=-1, keepdims=True)
        grad_scores = (probs * (grad_probs - center)).astype(jnp.bfloat16)
        grad_q = jnp.einsum(
            "bhqk,bkhd->bqhd", grad_scores, k_part, preferred_element_type=jnp.float32
        ).astype(jnp.bfloat16)
        grad_k = jnp.einsum(
            "bhqk,bqhd->bkhd", grad_scores, q_part, preferred_element_type=jnp.float32
        )
        grad_v = jnp.einsum(
            "bhqk,bqhd->bkhd",
            probs.astype(jnp.bfloat16),
            d_mixed,
            preferred_element_type=jnp.float32,
        )
        paired = jnp.stack([grad_k, grad_v], axis=2).reshape(group, length, 2, inner)
        return (carry + jnp.sum(grad_scores.astype(jnp.float32), axis=0), (grad_q, paired))

    bias_grad, (grad_query, paired) = lax.scan(
        attend_back, start, (q_groups, k_back, v_back, seg_query, sk_back, log_totals, grad_att)
    )
    paired = paired.reshape(rows, length, 2, inner)
    kv_grad = lax.psum_scatter(paired, "blk", scatter_dimension=1, tiled=True).astype(jnp.bfloat16)
    grad_key = kv_grad[:, :, 0].reshape(rows * block, inner)
    grad_value = kv_grad[:, :, 1].reshape(rows * block, inner)
    grad_query = grad_query.reshape(rows * block, inner)
    grad_wq = outer_sum(low_one, grad_query)
    grad_wk = outer_sum(low_one, grad_key)
    grad_wv = outer_sum(low_one, grad_value)
    grad_low_one = (
        times_t(grad_query, w_query) + times_t(grad_key, w_key) + times_t(grad_value, w_value)
    )
    back_one, grad_gain_one = rms_backward(grad_low_one, normed_one, scale_one, gain_one)
    grad_tokens = (grad_hidden + back_one).astype(jnp.bfloat16).reshape(rows, block, width)
    grad_table = jnp.einsum("hqk,nqk->nh", bias_grad, onehot, precision=lax.Precision.HIGHEST)
    grads = (
        grad_gain_one,
        grad_wq,
        grad_wk,
        grad_wv,
        grad_wout,
        grad_gain_two,
        grad_in,
        grad_down,
        grad_table,
    )
    pieces = (
        lax.psum_scatter(grads[0], "blk", scatter_dimension=0, tiled=True),
        lax.psum_scatter(grads[1], "blk", scatter_dimension=0, tiled=True),
        lax.psum_scatter(grads[2], "blk", scatter_dimension=0, tiled=True),
        lax.psum_scatter(grads[3], "blk", scatter_dimension=0, tiled=True),
        lax.psum_scatter(grads[4], "blk", scatter_dimension=0, tiled=True),
        lax.psum_scatter(grads[5], "blk", scatter_dimension=0, tiled=True),
        lax.psum_scatter(grads[6], "blk", scatter_dimension=0, tiled=True),
        lax.psum_scatter(grads[7], "blk", scatter_dimension=0, tiled=True),
        lax.psum_scatter(grads[8], "blk", scatter_dimension=0, tiled=True),
    )
    shares = lax.psum(
        (
            pieces[0],
            pieces[1],
            pieces[2],
            pieces[3],
            pieces[4],
            pieces[5],
            pieces[6],
            pieces[7],
            pieces[8],
        ),
        "dp",
    )
    return (
        output.reshape(rows, block, width),
        grad_tokens,
        shares[0],
        shares[1],
        shares[2],
        shares[3],
        shares[4],
        shares[5],
        shares[6],
        shares[7],
        shares[8],
    )


BF = jnp.bfloat16
F32 = jnp.float32
MESH = pl.DeviceIdType.MESH
VLIMIT = 60 * 1024 * 1024
TILE = 128
REACH = 511


def mm(a, b):
    return lax.dot_general(a, b, (((1,), (0,)), ((), ())), preferred_element_type=F32)


def mm_nt(a, b):
    return lax.dot_general(a, b, (((1,), (1,)), ((), ())), preferred_element_type=F32)


def mm_tn(a, b):
    return lax.dot_general(a, b, (((0,), (0,)), ((), ())), preferred_element_type=F32)


def iota(shape, dim):
    return lax.broadcasted_iota(jnp.int32, shape, dim)


def spot():
    blk = lax.axis_index("blk")
    return lax.axis_index("dp"), blk // 2, blk % 2


def norm_rows(x, gain):
    x = x.astype(F32)
    scale = lax.rsqrt(jnp.mean(x * x, axis=-1, keepdims=True) + EPS)
    normed = x * scale
    return normed, scale, (normed * gain).astype(BF)


def flip():
    return (iota((TILE, TILE), 0) + iota((TILE, TILE), 1) == TILE - 1).astype(BF)


def flipped(x):
    turn = flip()
    parts = [mm(turn, x[i : i + TILE, :]).astype(BF) for i in range(0, x.shape[0], TILE)]
    return jnp.concatenate(parts, axis=0)


def near_rows(h, d):
    return pl.ds(pl.multiple_of((3 * h + d) * TILE, TILE), TILE)


def prepare_bias(table_ref, near, heads):
    buckets = table_ref.shape[0]
    turn = flip()
    for d in range(3):
        lane = iota((buckets, 2 * TILE), 1)
        back = jnp.where(lane < TILE, lane, lane - 2 * TILE)
        hot = (bucket_of((d - 1) * TILE - back) == iota((buckets, 2 * TILE), 0)).astype(BF)
        strip = mm_tn(table_ref[...], hot)
        for h in range(heads):
            row = jnp.broadcast_to(strip[h : h + 1, :], (TILE, 2 * TILE))
            line = pltpu.roll(row, 0, 1, stride=1, stride_axis=0)[:, :TILE]
            near[near_rows(h, d), :] = mm(line.astype(BF), turn).astype(BF)


class Sums:
    def __init__(self, nz, bufs, s_sem, r_sem):
        self.nz = nz
        self.dp, self.z, self.c = spot()
        self.bufs, self.s_sem, self.r_sem = bufs, s_sem, r_sem
        self.block = bufs["in"]["pb"].shape[-2:]
        x, y = self.dp % 2, self.dp // 2
        c = self.c
        self.f, self.g = 1 + c, 2 - c
        self.s1 = (1 - c) * x + c * y
        self.s2 = (1 - c) * y + c * x
        self.peer1 = self.dp + self.f * (1 - 2 * self.s1)
        self.peer2 = self.dp + self.g * (1 - 2 * self.s2)
        self.bit, self.high = self.z % 2, self.z // 2
        self.near_z = self.z + 1 - 2 * self.bit
        self.far_z = self.z + 2 - 4 * self.high
        away, here = 2 * (1 - self.high), 2 * self.high
        self.order = (away, away + 1, here, here + 1)
        self.table = {}
        self.pending = []

    def copy(self, src, dst, key, dp=None, z=None, c=None):
        n = self.table.setdefault(key, len(self.table))
        dp = self.dp if dp is None else dp
        z = self.z if z is None else z
        c = self.c if c is None else c
        return pltpu.make_async_remote_copy(
            src, dst, self.s_sem.at[n], self.r_sem.at[n], device_id=(dp, 2 * z + c), device_id_type=MESH
        )

    def start(self, src, dst, key, **to):
        op = self.copy(src, dst, key, **to)
        op.start()
        self.pending.append((key, op))

    def drain(self, *head):
        left = []
        for key, op in self.pending:
            if key[: len(head)] == head:
                op.wait_send()
            else:
                left.append((key, op))
        self.pending = left

    def arrived(self, dst, key):
        self.copy(dst, dst, key).wait_recv()

    def part(self, u, name, *at):
        b = self.bufs[u]
        if name == "r1" and "lent" in b:
            rows, cols = self.block
            zz, i2 = at
            row = pl.multiple_of(i2 * rows, rows) if not isinstance(i2, int) else i2 * rows
            return b["lent"].at[pl.ds(zz, 1), pl.ds(row, rows), b["cols"]]
        return b[name].at[(b["h"], *at)]

    def q(self, i1, i2):
        return i1 * self.f + i2 * self.g

    def add(self, dst, a, b):
        dst[...] = (a[...].astype(F32) + b[...].astype(F32)).astype(BF)

    def a_start(self, u, i, q, zz, k):
        self.start(
            self.part(u, "pb", 2 * zz + 1 - self.c, q), self.part(u, "ra", zz, q), (u, "a", i, k), c=1 - self.c
        )

    def a_finish(self, u, i):
        zz = self.order[i]
        for k in range(4):
            self.arrived(self.part(u, "ra", zz, k), (u, "a", i, k))

        def one(q, carry):
            mine = self.part(u, "ra", zz, q)
            self.add(mine, mine, self.part(u, "pb", 2 * zz + self.c, q))
            return carry

        lax.fori_loop(0, 4, one, 0)

    def first_start(self, u, i):
        zz = self.order[i]
        for i2 in range(2):
            self.start(
                self.part(u, "ra", zz, self.q(1 - self.s1, i2)),
                self.part(u, "r1", zz, i2),
                (u, "1", i, i2),
                dp=self.peer1,
            )

    def first_finish(self, u, i):
        zz = self.order[i]
        for i2 in range(2):
            mine = self.part(u, "r1", zz, i2)
            self.arrived(mine, (u, "1", i, i2))
            self.add(mine, mine, self.part(u, "ra", zz, self.q(self.s1, i2)))

    def second_start(self, u, i):
        zz = self.order[i]
        self.start(
            self.part(u, "r1", zz, 1 - self.s2), self.part(u, "r2", zz), (u, "2", i), dp=self.peer2
        )

    def second_finish(self, u, i):
        zz = self.order[i]
        mine = self.part(u, "r2", zz)
        self.arrived(mine, (u, "2", i))
        self.add(mine, mine, self.part(u, "r1", zz, self.s2))

    def near_start(self, u, name, i):
        zz = self.order[2 * i] + 1 - self.bit
        self.start(self.part(u, name, zz), self.part(u, "rz", i), (u, "z", i), z=self.near_z)

    def near_finish(self, u, name, i):
        mine = self.part(u, "rz", i)
        self.arrived(mine, (u, "z", i))
        self.add(mine, mine, self.part(u, name, self.order[2 * i] + self.bit))
        if i == 0:
            self.start(mine, self.part(u, "rz", 2), (u, "z", 2), z=self.far_z)

    def far_last(self, u):
        last = self.part(u, "rz", 2)
        self.arrived(last, (u, "z", 2))
        self.add(self.part(u, "g", self.dp), last, self.part(u, "rz", 1))

    def far_mid(self, u):
        last = self.part(u, "rz", 2)
        self.arrived(last, (u, "z", 2))
        self.add(last, last, self.part(u, "rz", 1))
        self.start(self.part(u, "rz", 2, 1 - self.s2), self.part(u, "r2", 0), (u, "2", 0), dp=self.peer2)

    def second_last_finish(self, u):
        mine = self.part(u, "r2", 0)
        self.arrived(mine, (u, "2", 0))
        self.add(self.part(u, "g", self.dp), mine, self.part(u, "rz", 2, self.s2))

    def spread_two_start(self, u):
        for dp, key in ((self.peer2, "g0"), (self.peer1, "g1")):
            mine = self.part(u, "g", self.dp)
            self.start(mine, mine, (u, key), dp=dp)

    def spread_two_mid(self, u):
        other = self.part(u, "g", self.peer2)
        self.arrived(other, (u, "g0"))
        self.start(other, other, (u, "g2"), dp=self.peer1)

    def spread_two_finish(self, u):
        self.arrived(self.part(u, "g", self.peer1), (u, "g1"))
        self.arrived(self.part(u, "g", self.peer1 + self.peer2 - self.dp), (u, "g2"))

    def spread_start(self, u):
        mine = self.part(u, "g", self.dp)
        for k in range(1, 4):
            self.start(mine, mine, (u, "g", 3 - k), dp=lax.rem(self.dp + k, 4))

    def spread_finish(self, u):
        for k in range(1, 4):
            self.arrived(self.part(u, "g", lax.rem(self.dp + k, 4)), (u, "g", k - 1))


def table_sums(diag, far, heads):
    rows = diag.shape[1]
    total = jnp.zeros((rows, TILE), F32)
    for d in range(3):
        offset = (d - 1) * TILE + iota((2 * TILE, TILE), 0) - (TILE - 1)
        hot = (bucket_of(offset) == iota((2 * TILE, TILE), 1)).astype(F32)
        total = total + lax.dot_general(
            diag[d], hot, (((1,), (0,)), ((), ())),
            preferred_element_type=F32, precision=lax.Precision.HIGHEST,
        )
    lane = iota((rows, TILE), 1)
    for side, b in ((0, 31), (1, 15)):
        total = total + jnp.where(lane == b, jnp.sum(far[side], axis=1, keepdims=True), 0.0)
    return jnp.where(iota((rows, TILE), 0) < heads, total, 0.0)


def key_masks(segall, kaug, zz, c, nkb):
    for h in range(2):
        b = 2 * zz + h
        row = segall[b, pl.ds(c, 1), :]
        r = iota((TILE, TILE), 0)
        hot = jnp.where((r == row) | (r == 8 + b), 1.0, 0.0).astype(F32)
        kaug[pl.ds(pl.multiple_of(b * TILE, TILE), TILE), :] = hot.T.astype(BF)


def query_side(q, segall, table, qa, z, c, nkb):
    tq = q.shape[0]
    lost, right, left = [], [], []
    for i in range(tq // TILE):
        qb = (tq // TILE) * z + i
        row = segall[qb, pl.ds(c, 1), :]
        r = iota((TILE, TILE), 0)
        one = jnp.where((r < 8) & (r != row), NEG, 0.0).astype(F32)
        lost.append(mm(flip(), one.T.astype(BF)))
        col = iota((TILE, TILE), 1) - 8
        ok = (col >= 0) & (col < nkb)
        right.append(jnp.where(ok & (col >= qb + 2), 1.0, 0.0))
        left.append(jnp.where(ok & (col <= qb - 2), 1.0, 0.0))
    low = iota((tq, TILE), 1) < TILE // 2
    for p in range(qa.shape[0]):
        part = q[:, p * TILE : (p + 1) * TILE]
        for hh in range(2):
            h = 2 * p + hh
            rows = slice(hh * tq, (hh + 1) * tq)
            qa[p, rows, 0:TILE] = jnp.where(low if hh == 0 else jnp.logical_not(low), part, 0.0).astype(BF)
            far_r = table[31:32, h : h + 1].astype(F32)
            far_l = table[15:16, h : h + 1].astype(F32)
            for i in range(tq // TILE):
                at = hh * tq + i * TILE
                qa[p, at : at + TILE, TILE:] = (lost[i] + far_r * right[i] + far_l * left[i]).astype(BF)


def attend_step(i, zz, z, k, v, kaug, qa, near, probs, stat, s, acc, tq):
    rows = pl.ds(pl.multiple_of(zz * tq, tq), tq)
    blocks = tq // TILE

    def pair(p, carry):
        cols = pl.ds(pl.multiple_of(p * TILE, TILE), TILE)
        s[...] = mm_nt(jnp.concatenate([k[rows, cols], kaug[rows, :]], axis=1), qa[p])
        if i == 0:
            for kk in range(blocks):
                for qq in range(blocks):
                    for hh in range(2):
                        at = hh * tq + qq * TILE
                        spot_ = (slice(kk * TILE, (kk + 1) * TILE), slice(at, at + TILE))
                        s[spot_] = s[spot_] + near[near_rows(2 * p + hh, kk - qq + 1), :].astype(F32)
        else:

            @pl.when(jnp.abs(zz - z) == 1)
            def _():
                after = (zz - z + 1) // 2
                kr = pl.ds(pl.multiple_of((1 - after) * (tq - TILE), TILE), TILE)
                for hh in range(2):
                    qc = pl.ds(pl.multiple_of(hh * tq + after * (tq - TILE), TILE), TILE)
                    s[kr, qc] = s[kr, qc] + near[near_rows(2 * p + hh, 2 * after), :].astype(F32)

        top = jnp.max(s[...], axis=0, keepdims=True)
        if i > 0:
            old = stat[p, 0:1, :]
            top = jnp.maximum(old, top)
        e = jnp.exp(s[...] - top)
        probs[p, rows, :] = e.astype(BF)
        total = jnp.sum(e, axis=0, keepdims=True)
        mixed = mm_tn(v[rows, cols], probs[p, rows, :])
        arows = pl.ds(pl.multiple_of(p * TILE, TILE), TILE)
        if i > 0:
            fade = jnp.exp(old - top)
            total = total + stat[p, 1:2, :] * fade
            mixed = mixed + acc[arows, :] * fade
        acc[arows, :] = mixed
        stat[p, 0:1, :] = top
        stat[p, 1:2, :] = total
        stat[p, 2 + i : 3 + i, :] = top
        return carry

    lax.fori_loop(0, probs.shape[0], pair, 0)


def attn_backward_pair(p, z, nz, qa, k, v, kaug, datt, probs, scale, dq, diag, far, dm, dprob, ds):
    tq = dq.shape[0]
    length = k.shape[0]
    nkb = length // TILE
    cols = slice(p * TILE, (p + 1) * TILE)
    part = datt[p * tq : (p + 1) * tq, :].astype(F32)
    low = iota((tq, TILE), 1) < TILE // 2
    both = jnp.concatenate([jnp.where(low, part, 0.0), jnp.where(low, 0.0, part)], axis=0)
    column = scale[p].T
    total = jnp.zeros((8, 2 * tq), F32)
    for b in range(nz):
        rows = slice(b * tq, (b + 1) * tq)
        scaled = (both * column[:, b : b + 1]).astype(BF)
        dm[b * 2 * tq : (b + 1) * 2 * tq, :] = scaled
        dprob[rows, :] = mm_nt(v[rows, cols], scaled)
        mixed = dprob[rows, :] * probs[p, rows, :].astype(F32)
        total = total + jnp.sum(mixed.reshape(tq // 8, 8, 2 * tq), axis=0)
    center = jnp.sum(total, axis=0, keepdims=True)
    for b in range(nz):
        rows = slice(b * tq, (b + 1) * tq)
        v[rows, cols] = mm(probs[p, rows, :], dm[b * 2 * tq : (b + 1) * 2 * tq, :]).astype(BF)
        shift = center * scale[p, b : b + 1, :]
        ds[TILE + b * tq : TILE + (b + 1) * tq, :] = (
            probs[p, rows, :].astype(F32) * (dprob[rows, :] - shift)
        ).astype(BF)
    left = jnp.concatenate([k[:, cols], kaug[...]], axis=1)
    back = mm_tn(left, ds[TILE : TILE + length, :])
    k[:, cols] = mm(ds[TILE : TILE + length, :], qa[p, :, 0:TILE]).astype(BF)
    both = jnp.concatenate([back[: TILE // 2, :tq], back[TILE // 2 : TILE, tq:]], axis=0)
    dq[:, cols] = both.T.astype(BF)
    sums = back[TILE + 8 : TILE + 8 + nkb, :]
    kb = iota((nkb, 2 * tq), 0)
    lane = iota((nkb, 2 * tq), 1)
    qb = (tq // TILE) * z + (lane % tq) // TILE
    right = jnp.sum(jnp.where(kb >= qb + 2, sums, 0.0), axis=0, keepdims=True)
    left = jnp.sum(jnp.where(kb <= qb - 2, sums, 0.0), axis=0, keepdims=True)
    for hh in range(2):
        h = 2 * p + hh
        far[0, h : h + 1, :] = right[:, hh * tq : (hh + 1) * tq]
        far[1, h : h + 1, :] = left[:, hh * tq : (hh + 1) * tq]
        for d in range(3):
            near_sum = jnp.zeros((TILE, TILE), F32)
            for i in range(tq // TILE):
                row = ((tq // TILE) * z + i + d) * TILE
                at = hh * tq + i * TILE
                near_sum = near_sum + ds[pl.ds(pl.multiple_of(row, TILE), TILE), at : at + TILE].astype(F32)
            wide = jnp.concatenate([near_sum, jnp.zeros((TILE, TILE), F32)], axis=1)
            wide = pltpu.roll(wide, 0, 1, stride=1, stride_axis=0)
            diag[d, h : h + 1, :] = jnp.sum(wide, axis=0, keepdims=True)


def layer_kernel(nz, *refs):
    (tok_h, dy_h, seg, wq_h, wk_h, wv_h, wout_h, win_h, wdown_h, gains, table) = refs[:11]
    o_home, o_grads, o_small = refs[11:14]
    o_out, o_gt = o_home.at[0], o_home.at[1]
    g_down, g_in, g_attn = (o_grads.at[0:2, 4 * i : 4 * i + 4] for i in range(3))
    (
        x, k, v, qa, probs, att, dy, wqkv, wout, wdown, buf_b, pdown, pin,
        ra_d, ra_i, r1_d, r2_d, rz_d, r1_i, r2_i, rz_i, r2_a, rz_a,
        n2, dh, dhl, own_dn1, dprob, ds, near, kaug, diag, far, stat, scale,
        rd, relay, segall, segbuf, sm, smr, s_sem, r_sem, l_sem, gs_sem, gr_sem, credit,
    ) = refs[14:]
    both, one, two = pl.ds(0, 2), pl.ds(0, 1), pl.ds(1, 1)
    half = x.shape[2] // 2
    bufs = {
        "down": dict(h=both, pb=pdown, ra=ra_d, r1=r1_d, r2=r2_d, rz=rz_d, g=g_down),
        "in": dict(h=both, pb=pin, ra=ra_i, r1=r1_i, r2=r2_i, rz=rz_i, g=g_in),
        "attn0": dict(h=one, pb=pdown, ra=ra_d, r2=r2_a, rz=rz_a, g=g_attn, lent=wdown, cols=slice(0, half)),
        "attn1": dict(h=two, pb=pdown, ra=ra_d, r2=r2_a, rz=rz_a, g=g_attn, lent=wdown, cols=slice(half, 2 * half)),
    }
    eng = Sums(nz, bufs, s_sem, r_sem)
    dp, z, c = eng.dp, eng.z, eng.c
    blk = 2 * z + c
    nb, block, width = x.shape
    tq = 2 * block
    length = nb * block
    nkb = length // TILE
    share = width // nb
    steps = buf_b.shape[0]
    per = nb // steps
    pairs = probs.shape[0]
    heads = 2 * pairs
    barrier = pltpu.get_barrier_semaphore()
    peers = [(dp, lax.rem(blk + i, nb)) for i in range(1, nb)]
    peers += [(eng.peer1, blk), (eng.peer2, blk), (eng.peer1 + eng.peer2 - dp, blk)]
    for peer in peers:
        pl.semaphore_signal(barrier, inc=1, device_id=peer, device_id_type=MESH)

    loads = {}

    def load(name, src, dst):
        loads[name] = pltpu.make_async_copy(src, dst, l_sem.at[len(loads)])
        loads[name].start()

    def ready(*names):
        for name in names:
            loads[name].wait()

    load("x", tok_h.at[c], x.at[blk])
    load("wk", wk_h, wqkv.at[1])
    load("wv", wv_h, wqkv.at[2])
    load("wq", wq_h, wqkv.at[0])

    def gcopy(src, dst, send, recv, zz, cc):
        return pltpu.make_async_remote_copy(
            src, dst, gs_sem.at[send], gr_sem.at[recv], device_id=(dp, 2 * zz + cc), device_id_type=MESH
        )

    def inside(other):
        return (other >= 0) & (other < nz)

    segbuf[...] = jnp.zeros_like(segbuf)
    segbuf[0:2, :] = seg[...]
    segall[blk] = segbuf[...]
    pl.semaphore_wait(barrier, len(peers))

    ways = ((0, 1), (1, -1))
    mine = x.at[blk]
    gcopy(tok_h.at[1 - c], mine, 4, blk, z, 1 - c).start()
    for i in range(1, nb):
        pltpu.make_async_remote_copy(
            segbuf, segall.at[blk], gs_sem.at[10 + i], gr_sem.at[nb + 1 + blk],
            device_id=(dp, lax.rem(blk + i, nb)), device_id_type=MESH,
        ).start()
    for way, dz in ways:

        @pl.when(inside(z + dz))
        def _():
            gcopy(tok_h.at[1 - c], mine, 2 * way, blk, z + dz, 1 - c).start()
            gcopy(tok_h.at[c], mine, 2 * way + 1, blk, z + dz, c).start()

    gcopy(dy_h.at[1 - c], dy.at[c], 5, nb, z, 1 - c).start()
    load("dy", dy_h.at[c], dy.at[c])
    load("wout", wout_h, wout)
    for j in range(steps):
        jj = eng.order[j]
        load(("win", j), win_h.at[:, pl.ds(pl.multiple_of(jj * width, width), width)], buf_b.at[jj])
        load(("wdown", j), wdown_h.at[jj], wdown.at[jj])

    prepare_bias(table, near, heads)
    reach = -(-REACH // tq)
    for zz in range(nz):

        @pl.when(jnp.abs(zz - z) > reach)
        def _():
            rows = slice(zz * tq, (zz + 1) * tq)
            x[2 * zz : 2 * zz + 2] = jnp.zeros((2, block, width), BF)
            for ref in (k, v):
                ref[rows, :] = jnp.zeros((tq, width), BF)
            kaug[rows, :] = jnp.zeros((tq, TILE), BF)
            for p in range(pairs):
                probs[p, rows, :] = jnp.zeros((tq, 2 * tq), BF)

    ds[0:TILE, :] = jnp.zeros((TILE, ds.shape[1]), BF)
    ds[ds.shape[0] - TILE :, :] = jnp.zeros((TILE, ds.shape[1]), BF)
    diag[...] = jnp.zeros_like(diag)
    far[...] = jnp.zeros_like(far)
    scale[...] = jnp.zeros_like(scale)
    sm[0] = jnp.zeros(sm.shape[1:], F32)
    gain1 = gains[0:1, :].astype(F32)
    gain2 = gains[1:2, :].astype(F32)

    def x_arrived(b):
        gcopy(x.at[b], x.at[b], 0, b, z, 1 - c).wait_recv()

    def seg_arrived(b):
        gcopy(segbuf, segall.at[b], 0, nb + 1 + b, z, 1 - c).wait_recv()

    def keys_of(zz):
        rows = pl.ds(pl.multiple_of(zz * tq, tq), tq)
        key_masks(segall, kaug, zz, c, nkb)
        n1 = norm_rows(x[pl.ds(2 * zz, 2)].reshape(tq, width), gain1)[2]
        k[rows, :] = mm(n1, wqkv[1]).astype(BF)
        v[rows, :] = mm(n1, wqkv[2]).astype(BF)
        return n1

    s_blk, acc = dprob.at[0:tq], dprob.at[tq : tq + pairs * TILE]
    ready("x", "wk", "wv", "wq")
    x_arrived(2 * z + 1 - c)
    seg_arrived(2 * z + 1 - c)
    q_rev = mm(flipped(keys_of(z)), wqkv[0]).astype(BF).astype(F32)
    query_side(q_rev, segall, table, qa, z, c, nkb)
    order = (z, eng.near_z, 2 - eng.high, 3 - 3 * eng.high)
    wide = width // 2
    attend_step(0, order[0], z, k, v, kaug, qa, near, probs, stat, s_blk, acc, tq)
    for way, dz in ways:
        src = z - dz

        @pl.when(inside(src))
        def _():
            for h in range(2):
                x_arrived(2 * src + h)

                @pl.when(inside(z + dz))
                def _():
                    gcopy(
                        x.at[2 * src + h], x.at[2 * src + h], 6 + 2 * way + h, 2 * src + h, z + dz, c
                    ).start()

    for i in range(1, nb):
        other = lax.rem(blk + i, nb)

        @pl.when(other // 2 != z)
        def _():
            seg_arrived(other)

    for i in range(1, 4):
        zz = order[i]

        @pl.when(jnp.abs(zz - z) <= reach)
        def _():
            @pl.when(jnp.abs(zz - z) == 2)
            def _():
                for h in range(2):
                    x_arrived(2 * zz + h)

            keys_of(zz)
            attend_step(i, zz, z, k, v, kaug, qa, near, probs, stat, s_blk, acc, tq)

    for p in range(pairs):
        inverse = 1.0 / stat[p, 1:2, :]
        top = stat[p, 0:1, :]
        for i in range(4):

            @pl.when(jnp.abs(order[i] - z) <= reach)
            def _():
                scale[p, pl.ds(order[i], 1), :] = jnp.exp(stat[p, 2 + i : 3 + i, :] - top) * inverse

        mixed = acc[p * TILE : (p + 1) * TILE, :] * inverse
        both = jnp.concatenate([mixed[: TILE // 2, :tq], mixed[TILE // 2 :, tq:]], axis=0)
        att[:, p * TILE : (p + 1) * TILE] = both.T.astype(BF)
    att[...] = flipped(att[...])

    ready("wout")
    x_own = x.at[pl.ds(2 * z, 2)]
    dh[...] = x_own[...].reshape(tq, width).astype(F32) + mm(att[...], wout[...])
    n2[...] = norm_rows(dh[...], gain2)[2]
    ready("dy")
    gcopy(dy.at[0], dy.at[1 - c], 0, nb, z, 1 - c).wait_recv()
    total = own_dn1
    for j in range(steps):
        jj = eng.order[j]
        ready(("win", j), ("wdown", j))
        value, slant = gelu_both(mm(n2[...], buf_b[jj]))
        act = value.astype(BF)
        d = dy[...].reshape(tq, width)
        grad = mm_tn(act, d).astype(BF)
        for hh in range(2):
            part = grad[:, hh * wide : (hh + 1) * wide]
            pdown[hh, pl.ds(jj * per, per)] = part.reshape(per, 4, share, wide)
        for qq in range(4):
            eng.a_start("down", j, qq, jj, qq)
        dpre = (mm_nt(d, wdown[jj]) * slant).astype(BF)
        grad = mm_tn(n2[...], dpre).astype(BF)
        for hh in range(2):
            part = grad[:, hh * wide : (hh + 1) * wide]
            pin[hh, :, jj] = part.reshape(nb, share, wide)
        for i in range(nz):
            eng.a_start("in", i, jj, eng.order[i], j)
        if j == 0:
            total[...] = mm(act, wdown[jj])
            dn2 = mm_nt(dpre, buf_b[jj])
        else:
            total[...] += mm(act, wdown[jj])
            dn2 = dn2 + mm_nt(dpre, buf_b[jj])
        eng.a_finish("down", j)
        eng.first_start("down", j)
    h = dh[...]
    n2[...] = (h + total[...]).astype(BF)
    normed, r2, _ = norm_rows(h, gain2)
    back, gain_grad = rms_backward(dn2, normed, r2, gain2)
    lines = width // TILE
    for i in range(lines):
        sm[0, lines + i : lines + i + 1, :] = gain_grad[None, i * TILE : (i + 1) * TILE]
    dh[...] = dy[...].reshape(tq, width).astype(F32) + back
    dhl[...] = dh[...].astype(BF)
    back = flipped(mm_nt(dhl[...], wout[...]).astype(BF))
    datt, dm = near.at[0 : pairs * tq], near.at[pairs * tq : pairs * tq + nz * 2 * tq]
    for p in range(pairs):
        datt[p * tq : (p + 1) * tq, :] = back[:, p * TILE : (p + 1) * TILE]
    for i in range(nz):
        eng.a_finish("in", i)
    out_half = [n2.at[pl.ds(pl.multiple_of(i * block, block), block)] for i in (c, 1 - c)]
    eng.start(out_half[1], o_out.at[c], ("out",), c=1 - c)
    load("kept", out_half[0], o_out.at[c])

    def first_near(u, i):
        for ii in (2 * i, 2 * i + 1):
            eng.first_finish(u, ii)
        eng.near_start(u, "r1", i)

    def first_second(u, i):
        for ii in (2 * i, 2 * i + 1):
            eng.first_finish(u, ii)
            eng.second_start(u, ii)

    def second_near(u, i):
        for ii in (2 * i, 2 * i + 1):
            eng.second_finish(u, ii)
        eng.near_start(u, "r2", i)

    first_near("down", 0)
    eng.drain("down", "a")
    for hh in range(2):
        grad = mm_tn(att[...], dhl[:, hh * wide : (hh + 1) * wide]).astype(BF)
        pdown[hh, :, 3] = grad.reshape(nb, share, wide)
    dq = dhl
    for b in range(nz):
        buf_b[b, tq : 2 * tq] = norm_rows(x[2 * b : 2 * b + 2].reshape(tq, width), gain1)[2]

    def weights(part):
        cols = slice(part * wide, (part + 1) * wide)
        dq[:, cols] = flipped(dq[:, cols])
        for i, ref in ((1, k), (2, v)):
            grad = sum(
                mm_tn(buf_b[b, tq : 2 * tq], ref[b * tq : (b + 1) * tq, cols]) for b in range(nz)
            )
            pdown[part, :, i] = grad.astype(BF).reshape(nb, share, wide)
        pdown[part, :, 0] = mm_tn(buf_b[z, tq : 2 * tq], dq[:, cols]).astype(BF).reshape(nb, share, wide)

    def a_start_all(u):
        for i in range(nz):
            for qq in range(4):
                eng.a_start(u, i, qq, eng.order[i], qq)

    for p in range(pairs):
        attn_backward_pair(
            p, z, nz, qa, k, v, kaug, datt, probs, scale, dq, diag, far, dm, dprob, ds
        )
        if p == 0:
            eng.first_start("in", 0)
            eng.first_start("in", 1)
        if p == 2:
            eng.first_start("in", 2)
            eng.first_start("in", 3)
            weights(0)
            first_near("down", 1)
            eng.near_finish("down", "r1", 0)
            eng.drain("down", "1")
            pl.semaphore_signal(credit, inc=1, device_id=(dp, 2 * z + 1 - c), device_id_type=MESH)
        if p == 3:
            pl.semaphore_wait(credit, 1)
            a_start_all("attn0")
        if p == 4:
            first_second("in", 0)
            for i in range(nz):
                eng.a_finish("attn0", i)
                eng.first_start("attn0", i)
    weights(1)
    a_start_all("attn1")
    eng.near_finish("down", "r1", 1)

    for b in range(nz):
        rows = slice(b * tq, (b + 1) * tq)
        part = mm_nt(k[rows, :], wqkv[1]) + mm_nt(v[rows, :], wqkv[2])
        buf_b[b, 0:tq] = part.astype(BF)
    for way, dz in ways:

        @pl.when(inside(z + 2 * dz))
        def _():
            eng.copy(buf_b.at[z + 2 * dz, 0:tq], relay.at[way], ("d1", way), z=z + dz).start()

    for i in range(nz):
        eng.a_finish("attn1", i)
        eng.first_start("attn1", i)
    first_second("in", 1)
    second_near("in", 0)

    own_dn1[...] = mm_nt(dq[...], wqkv[0])
    own_normed = norm_rows(x_own[...].reshape(tq, width), gain1)[0]
    gain_sum = jnp.sum(own_dn1[...] * own_normed, axis=0, keepdims=True)
    for b in range(nz):
        rows = slice(b * tq, (b + 1) * tq)
        part = mm_nt(k[rows, :], wqkv[1]) + mm_nt(v[rows, :], wqkv[2])
        normed = norm_rows(x[2 * b : 2 * b + 2].reshape(tq, width), gain1)[0]
        gain_sum = gain_sum + jnp.sum(part * normed, axis=0, keepdims=True)

        @pl.when(z == b)
        def _():
            own_dn1[...] += part

    for i in range(lines):
        sm[0, i : i + 1, :] = gain_sum[:, i * TILE : (i + 1) * TILE]
    sm[0, 2 * lines :, :] = table_sums(diag, far, heads)[: sm.shape[1] - 2 * lines]
    hops = (
        dict(c=1 - c), dict(dp=dp + 1 - 2 * (dp % 2)), dict(dp=dp + 2 - 4 * (dp // 2)),
        dict(z=eng.near_z), dict(z=eng.far_z),
    )

    def small_start(i):
        eng.start(sm.at[i], smr.at[i], ("s", i), **hops[i])

    def small_finish(i):
        eng.copy(sm.at[i], smr.at[i], ("s", i), **hops[i]).wait_recv()
        sm[i + 1] = sm[i] + smr[i]

    small_start(0)
    eng.far_mid("down")
    first_second("attn0", 0)
    small_finish(0)
    small_start(1)
    for way, dz in ways:

        @pl.when(inside(z - dz) & inside(z + dz))
        def _():
            eng.copy(relay.at[way], relay.at[way], ("d1", way)).wait_recv()
            buf_b[z + dz, 0:tq] = (buf_b[z + dz, 0:tq].astype(F32) + relay[way].astype(F32)).astype(BF)

        @pl.when(inside(z + dz))
        def _():
            eng.copy(buf_b.at[z + dz, 0:tq], rd.at[way], ("d2", way), z=z + dz).start()

    first_second("attn0", 1)
    eng.near_finish("in", "r2", 0)
    first_second("attn1", 0)
    second_near("in", 1)
    second_near("attn0", 0)
    first_second("attn1", 1)
    small_finish(1)
    small_start(2)
    second_near("attn0", 1)
    eng.second_last_finish("down")
    eng.near_finish("in", "r2", 1)
    eng.near_finish("attn0", "r2", 0)
    second_near("attn1", 0)
    eng.spread_two_start("down")
    small_finish(2)
    small_start(3)
    second_near("attn1", 1)
    eng.near_finish("attn0", "r2", 1)
    eng.far_last("in")
    eng.spread_two_start("in")
    eng.near_finish("attn1", "r2", 0)
    eng.spread_two_mid("down")
    eng.near_finish("attn1", "r2", 1)
    small_finish(3)
    small_start(4)
    eng.far_last("attn0")
    eng.spread_two_start("attn0")

    dn1 = own_dn1
    for way, dz in ways:

        @pl.when(inside(z - dz))
        def _():
            eng.copy(rd.at[way], rd.at[way], ("d2", way)).wait_recv()
            dn1[...] += rd[way].astype(F32)

    normed, r1, _ = norm_rows(x_own[...].reshape(tq, width), gain1)
    back, _ = rms_backward(dn1[...], normed, r1, gain1)
    dy[...] = (dh[...] + back).astype(BF).reshape(dy.shape)
    eng.start(dy.at[1 - c], o_gt.at[c], ("gt",), c=1 - c)
    load("kept_gt", dy.at[c], o_gt.at[c])

    eng.spread_two_mid("in")
    eng.far_last("attn1")
    eng.spread_start("attn1")
    eng.spread_two_mid("attn0")
    small_finish(4)
    o_small[...] = sm[5]
    eng.copy(dy.at[0], o_out.at[1 - c], ("out",)).wait_recv()
    eng.copy(dy.at[0], o_gt.at[1 - c], ("gt",)).wait_recv()
    ready("kept", "kept_gt")
    eng.spread_two_finish("down")
    eng.spread_two_finish("in")
    eng.spread_two_finish("attn0")
    eng.spread_finish("attn1")
    eng.drain()
    gcopy(tok_h.at[0], mine, 4, blk, z, 1 - c).wait_send()
    gcopy(dy_h.at[0], dy.at[0], 5, nb, z, 1 - c).wait_send()
    for i in range(1, nb):
        gcopy(segbuf, segall.at[0], 10 + i, nb + 1, z, 1 - c).wait_send()
    for way, dz in ways:

        @pl.when(inside(z + dz))
        def _():
            gcopy(tok_h.at[0], mine, 2 * way, blk, z, 1 - c).wait_send()
            gcopy(tok_h.at[0], mine, 2 * way + 1, blk, z, 1 - c).wait_send()
            eng.copy(buf_b.at[0, 0:tq], rd.at[way], ("d2", way)).wait_send()

        @pl.when(inside(z + 2 * dz))
        def _():
            eng.copy(buf_b.at[0, 0:tq], relay.at[way], ("d1", way)).wait_send()

        @pl.when(inside(z - dz) & inside(z + dz))
        def _():
            for h in range(2):
                gcopy(tok_h.at[0], mine, 6 + 2 * way + h, blk, z, 1 - c).wait_send()


def layer(nz, tok, dy, seg, wq, wk, wv, wout, win, wdown, gains, table):
    _, block, width = tok.shape
    nb = 2 * nz
    length, tq = nb * block, 2 * block
    share = width // nb
    pairs = table.shape[1] // 2
    steps = win.shape[1] // width
    vm = pl.BlockSpec(memory_space=pltpu.VMEM)
    hbm = pl.BlockSpec(memory_space=pl.ANY)
    home = jax.ShapeDtypeStruct((2, 2, block, width), BF)
    grads = jax.ShapeDtypeStruct((2, 12, share, width // 2), BF)
    one = (share, width // 2)
    small = (24, TILE)

    def bf(*shape):
        return pltpu.VMEM(shape, BF)

    def f32(*shape):
        return pltpu.VMEM(shape, F32)

    sums = [bf(2, nz, 4, *one), bf(2, nz, 4, *one)]
    for i, route in enumerate(("xzy", "xyz", "xyz")):
        last = route == "xyz"
        sums += [bf(2, nz, 2, *one)] if i < 2 else []
        sums += [bf(2, nz if last else 1, *one), bf(2, 3, *one) if last else bf(2, 3, 2, *one)]
    scratch = [
        bf(nb, block, width), bf(length, width), bf(length, width),
        bf(pairs, 2 * tq, 2 * TILE), bf(pairs, length, 2 * tq), bf(tq, width),
        bf(2, block, width), bf(3, width, width), bf(width, width),
        bf(steps, width, width), bf(steps, width, width), bf(2, nb, 4, *one), bf(2, nb, 4, *one),
        *sums,
        bf(tq, width), f32(tq, width), bf(tq, width), f32(tq, width),
        f32(length, 2 * tq), bf(length + 2 * TILE, 2 * tq), bf(max(2 * pairs * 3 * TILE, pairs * tq + nz * 2 * tq), TILE), bf(length, TILE),
        f32(3, 16, 2 * TILE), f32(2, 16, tq), f32(pairs, 8, 2 * tq), f32(pairs, 8, 2 * tq),
        bf(2, tq, width), bf(2, tq, width),
        pltpu.VMEM((nb, 8, block), jnp.int32), pltpu.VMEM((8, block), jnp.int32),
        f32(6, *small), f32(5, *small),
        pltpu.SemaphoreType.DMA((180,)), pltpu.SemaphoreType.DMA((180,)), pltpu.SemaphoreType.DMA((32,)),
        pltpu.SemaphoreType.DMA((10 + nb,)), pltpu.SemaphoreType.DMA((2 * nb + 2,)),
        pltpu.SemaphoreType.REGULAR,
    ]
    return pl.pallas_call(
        functools.partial(layer_kernel, nz),
        out_shape=(home, grads, jax.ShapeDtypeStruct(small, F32)),
        in_specs=[hbm, hbm, vm] + [hbm] * 6 + [vm, vm],
        out_specs=(vm,) * 3,
        scratch_shapes=scratch,
        compiler_params=pltpu.CompilerParams(
            collective_id=1, has_side_effects=True, vmem_limit_bytes=64 * 1024 * 1024
        ),
    )(tok, dy, seg, wq, wk, wv, wout, win, wdown, gains, table)


def fast_device(
    nz, tokens, segment_ids, gain_attn, w_query, w_key, w_value, w_out, gain_ffn, w_in, w_down,
    rel_table, cotangent,
):
    rows, block, width = tokens.shape
    nb = 2 * nz
    share = width // nb
    home, grads, small = layer(
        nz, tokens, cotangent, segment_ids, w_query, w_key, w_value, w_out, w_in,
        w_down.reshape(-1, width, width),
        jnp.stack([gain_attn, gain_ffn]), rel_table,
    )
    b = lax.axis_index("blk")
    lines = width // TILE
    ga = lax.dynamic_slice_in_dim(small[:lines].reshape(-1), b * share, share)
    gf = lax.dynamic_slice_in_dim(small[lines : 2 * lines].reshape(-1), b * share, share)
    heads = rel_table.shape[1]
    gt = lax.dynamic_slice(small, (2 * lines, b * (32 // nb)), (heads, 32 // nb)).T
    grads = jnp.concatenate([grads[0], grads[1]], axis=-1).astype(F32)
    gin = jnp.concatenate([grads[4 + j] for j in range(4)], axis=1)
    return (
        home[0], home[1], ga, grads[8], grads[9], grads[10], grads[11], gf, gin,
        grads[:4].reshape(-1, width), gt,
    )


def pick(mesh):
    if mesh.shape["dp"] == 4 and mesh.shape["blk"] == 8:
        return functools.partial(fast_device, mesh.shape["blk"] // 2)
    return on_device


def solution(mesh):
    placed = (
        P("dp", "blk", None),
        P("dp", "blk"),
        P(),
        P(),
        P(),
        P(),
        P(),
        P(),
        P(),
        P(),
        P(),
        P("dp", "blk", None),
    )
    return jax.shard_map(
        pick(mesh),
        mesh=mesh,
        in_specs=placed,
        out_specs=(
            P("dp", "blk", None),
            P("dp", "blk", None),
            P("blk"),
            P("blk", None),
            P("blk", None),
            P("blk", None),
            P("blk", None),
            P("blk"),
            P("blk", None),
            P("blk", None),
            P("blk", None),
        ),
        check_vma=False,
    )
```

```python
import functools
import math

import jax
import jax.numpy as jnp
from jax import lax
from jax.experimental import pallas as pl
from jax.experimental.pallas import tpu as pltpu
from jax.sharding import PartitionSpec as P

EPS = 1e-06
NEG = -1e30
EDGES = (12, 16, 23, 32, 46, 64, 91)
ROOT_TWO_PI = 0.7978845608028654
CUBIC = 0.044715


def bucket_of(offset):
    distance = jnp.abs(offset)
    far_part = 8 + sum(((distance >= edge).astype(jnp.int32) for edge in EDGES))
    return jnp.where(offset > 0, 16, 0) + jnp.where(distance < 8, distance, far_part)


def gelu_both(values):
    inner_arg = ROOT_TWO_PI * (values + CUBIC * values * values * values)
    tangent = jnp.tanh(inner_arg)
    result = 0.5 * values * (1.0 + tangent)
    slope = 0.5 * (1.0 + tangent) + 0.5 * values * (1.0 - tangent * tangent) * ROOT_TWO_PI * (
        1.0 + 3.0 * CUBIC * values * values
    )
    return (result, slope)


def rms_forward(values, gain):
    scale = lax.rsqrt(jnp.mean(values * values, axis=-1, keepdims=True) + EPS)
    normed = values * scale
    return (normed, scale, (normed * gain).astype(jnp.bfloat16))


def rms_backward(grad, normed, scale, gain):
    gain_grad = jnp.sum(grad * normed, axis=0)
    inner_grad = grad * gain
    back = scale * (inner_grad - normed * jnp.mean(inner_grad * normed, axis=-1, keepdims=True))
    return (back, gain_grad)


def outer_sum(left, right):
    return jnp.einsum("td,tf->df", left, right, preferred_element_type=jnp.float32)


def times_t(left, right):
    return jnp.einsum("tf,df->td", left, right, preferred_element_type=jnp.float32)


def masked_scores(query, keys, bias, seg_query, seg_keys):
    raw = (
        jnp.einsum("bqhd,bkhd->bhqk", query, keys, preferred_element_type=jnp.float32) + bias[None]
    )
    same = seg_query[:, None, :, None] == seg_keys[:, None, None, :]
    return jnp.where(same, raw, NEG)


def score_grads(q_part, k_part, v_part, bias, sq_part, sk_part, total, d_mixed):
    scores = masked_scores(q_part, k_part, bias, sq_part, sk_part)
    probs = jnp.exp(scores - total[..., None])
    grad_probs = jnp.einsum("bqhd,bkhd->bhqk", d_mixed, v_part, preferred_element_type=jnp.float32)
    return (probs, grad_probs)


def on_device(
    tokens,
    segment_ids,
    gain_attn,
    w_query,
    w_key,
    w_value,
    w_out,
    gain_ffn,
    w_in,
    w_down,
    rel_table,
    cotangent,
):
    rows, block, width = tokens.shape
    buckets, heads = rel_table.shape
    inner = w_query.shape[1]
    head_dim = inner // heads
    length = block * lax.axis_size("blk")
    group = math.gcd(rows, max(1, 512 // block))
    blocks = rows // group
    gain_one = gain_attn.astype(jnp.float32)
    gain_two = gain_ffn.astype(jnp.float32)
    table_f = rel_table.astype(jnp.float32)
    flat = tokens.reshape(rows * block, width).astype(jnp.float32)
    normed_one, scale_one, low_one = rms_forward(flat, gain_one)

    def project(weight):
        return (
            jnp.dot(low_one, weight, preferred_element_type=jnp.float32)
            .astype(jnp.bfloat16)
            .reshape(rows, block, inner)
        )

    query, keys, values = (project(w_query), project(w_key), project(w_value))
    key_all, value_all, seg_all = (
        lax.all_gather(keys, "blk", axis=1, tiled=True),
        lax.all_gather(values, "blk", axis=1, tiled=True),
        lax.all_gather(segment_ids, "blk", axis=1, tiled=True),
    )
    places = lax.axis_index("blk") * block + jnp.arange(block, dtype=jnp.int32)
    offsets = jnp.arange(length, dtype=jnp.int32)[None, :] - places[:, None]
    onehot = (
        bucket_of(offsets)[None] == jnp.arange(buckets, dtype=jnp.int32)[:, None, None]
    ).astype(jnp.float32)
    bias = jnp.einsum("nqk,nh->hqk", onehot, table_f, precision=lax.Precision.HIGHEST)
    q_groups = query.reshape(blocks, group, block, heads, head_dim)
    seg_query = segment_ids.reshape(blocks, group, block)

    def key_groups(key_rows, value_rows, seg_rows):
        return (
            key_rows.reshape(blocks, group, length, heads, head_dim),
            value_rows.reshape(blocks, group, length, heads, head_dim),
            seg_rows.reshape(blocks, group, length),
        )

    k_groups, v_groups, seg_keys = key_groups(key_all, value_all, seg_all)

    def attend(parts):
        q_part, k_part, v_part, sq_part, sk_part = parts
        scores = masked_scores(q_part, k_part, bias, sq_part, sk_part)
        top = jnp.max(scores, axis=-1, keepdims=True)
        total = jnp.log(jnp.sum(jnp.exp(scores - top), axis=-1, keepdims=True)) + top
        probs = jnp.exp(scores - total).astype(jnp.bfloat16)
        mixed = jnp.einsum("bhqk,bkhd->bqhd", probs, v_part, preferred_element_type=jnp.float32)
        return (mixed.astype(jnp.bfloat16), total[..., 0])

    attended, log_totals = lax.map(attend, (q_groups, k_groups, v_groups, seg_query, seg_keys))
    attended_flat = attended.reshape(rows * block, inner)
    hidden = flat + jnp.dot(attended_flat, w_out, preferred_element_type=jnp.float32)
    normed_two, scale_two, low_two = rms_forward(hidden, gain_two)
    pre = jnp.dot(low_two, w_in, preferred_element_type=jnp.float32)
    gelu_value, gelu_slope = gelu_both(pre)
    active = gelu_value.astype(jnp.bfloat16)
    output = (hidden + jnp.dot(active, w_down, preferred_element_type=jnp.float32)).astype(
        jnp.bfloat16
    )
    grad_out = cotangent.reshape(rows * block, width)
    grad_down = outer_sum(active, grad_out)
    grad_pre = (times_t(grad_out, w_down) * gelu_slope).astype(jnp.bfloat16)
    grad_in = outer_sum(low_two, grad_pre)
    back_two, grad_gain_two = rms_backward(times_t(grad_pre, w_in), normed_two, scale_two, gain_two)
    grad_hidden = grad_out.astype(jnp.float32) + back_two
    grad_proj = grad_hidden.astype(jnp.bfloat16)
    grad_wout = outer_sum(attended_flat, grad_proj)
    grad_att = (
        times_t(grad_proj, w_out)
        .astype(jnp.bfloat16)
        .reshape(blocks, group, block, heads, head_dim)
    )
    key_back, value_back, seg_back = (
        lax.all_gather(keys, "blk", axis=1, tiled=True),
        lax.all_gather(values, "blk", axis=1, tiled=True),
        lax.all_gather(segment_ids, "blk", axis=1, tiled=True),
    )
    k_back, v_back, sk_back = key_groups(key_back, value_back, seg_back)
    start = jnp.zeros((heads, block, length), jnp.float32)

    def attend_back(carry, parts):
        q_part, k_part, v_part, sq_part, sk_part, total, d_mixed = parts
        probs, grad_probs = score_grads(
            q_part, k_part, v_part, bias, sq_part, sk_part, total, d_mixed
        )
        center = jnp.sum(probs * grad_probs, axis=-1, keepdims=True)
        grad_scores = (probs * (grad_probs - center)).astype(jnp.bfloat16)
        grad_q = jnp.einsum(
            "bhqk,bkhd->bqhd", grad_scores, k_part, preferred_element_type=jnp.float32
        ).astype(jnp.bfloat16)
        grad_k = jnp.einsum(
            "bhqk,bqhd->bkhd", grad_scores, q_part, preferred_element_type=jnp.float32
        )
        grad_v = jnp.einsum(
            "bhqk,bqhd->bkhd",
            probs.astype(jnp.bfloat16),
            d_mixed,
            preferred_element_type=jnp.float32,
        )
        paired = jnp.stack([grad_k, grad_v], axis=2).reshape(group, length, 2, inner)
        return (carry + jnp.sum(grad_scores.astype(jnp.float32), axis=0), (grad_q, paired))

    bias_grad, (grad_query, paired) = lax.scan(
        attend_back, start, (q_groups, k_back, v_back, seg_query, sk_back, log_totals, grad_att)
    )
    paired = paired.reshape(rows, length, 2, inner)
    kv_grad = lax.psum_scatter(paired, "blk", scatter_dimension=1, tiled=True).astype(jnp.bfloat16)
    grad_key = kv_grad[:, :, 0].reshape(rows * block, inner)
    grad_value = kv_grad[:, :, 1].reshape(rows * block, inner)
    grad_query = grad_query.reshape(rows * block, inner)
    grad_wq = outer_sum(low_one, grad_query)
    grad_wk = outer_sum(low_one, grad_key)
    grad_wv = outer_sum(low_one, grad_value)
    grad_low_one = (
        times_t(grad_query, w_query) + times_t(grad_key, w_key) + times_t(grad_value, w_value)
    )
    back_one, grad_gain_one = rms_backward(grad_low_one, normed_one, scale_one, gain_one)
    grad_tokens = (grad_hidden + back_one).astype(jnp.bfloat16).reshape(rows, block, width)
    grad_table = jnp.einsum("hqk,nqk->nh", bias_grad, onehot, precision=lax.Precision.HIGHEST)
    grads = (
        grad_gain_one,
        grad_wq,
        grad_wk,
        grad_wv,
        grad_wout,
        grad_gain_two,
        grad_in,
        grad_down,
        grad_table,
    )
    pieces = (
        lax.psum_scatter(grads[0], "blk", scatter_dimension=0, tiled=True),
        lax.psum_scatter(grads[1], "blk", scatter_dimension=0, tiled=True),
        lax.psum_scatter(grads[2], "blk", scatter_dimension=0, tiled=True),
        lax.psum_scatter(grads[3], "blk", scatter_dimension=0, tiled=True),
        lax.psum_scatter(grads[4], "blk", scatter_dimension=0, tiled=True),
        lax.psum_scatter(grads[5], "blk", scatter_dimension=0, tiled=True),
        lax.psum_scatter(grads[6], "blk", scatter_dimension=0, tiled=True),
        lax.psum_scatter(grads[7], "blk", scatter_dimension=0, tiled=True),
        lax.psum_scatter(grads[8], "blk", scatter_dimension=0, tiled=True),
    )
    shares = lax.psum(
        (
            pieces[0],
            pieces[1],
            pieces[2],
            pieces[3],
            pieces[4],
            pieces[5],
            pieces[6],
            pieces[7],
            pieces[8],
        ),
        "dp",
    )
    return (
        output.reshape(rows, block, width),
        grad_tokens,
        shares[0],
        shares[1],
        shares[2],
        shares[3],
        shares[4],
        shares[5],
        shares[6],
        shares[7],
        shares[8],
    )


BF = jnp.bfloat16
F32 = jnp.float32
MESH = pl.DeviceIdType.MESH
VLIMIT = 60 * 1024 * 1024
TILE = 128
REACH = 511


def mm(a, b):
    return lax.dot_general(a, b, (((1,), (0,)), ((), ())), preferred_element_type=F32)


def mm_nt(a, b):
    return lax.dot_general(a, b, (((1,), (1,)), ((), ())), preferred_element_type=F32)


def mm_tn(a, b):
    return lax.dot_general(a, b, (((0,), (0,)), ((), ())), preferred_element_type=F32)


def iota(shape, dim):
    return lax.broadcasted_iota(jnp.int32, shape, dim)


def spot():
    blk = lax.axis_index("blk")
    return lax.axis_index("dp"), blk // 2, blk % 2


def norm_rows(x, gain):
    x = x.astype(F32)
    scale = lax.rsqrt(jnp.mean(x * x, axis=-1, keepdims=True) + EPS)
    normed = x * scale
    return normed, scale, (normed * gain).astype(BF)


def flip():
    return (iota((TILE, TILE), 0) + iota((TILE, TILE), 1) == TILE - 1).astype(BF)


def flipped(x):
    turn = flip()
    parts = [mm(turn, x[i : i + TILE, :]).astype(BF) for i in range(0, x.shape[0], TILE)]
    return jnp.concatenate(parts, axis=0)


def near_rows(h, d):
    return pl.ds(pl.multiple_of((3 * h + d) * TILE, TILE), TILE)


def prepare_bias(table_ref, near, heads):
    buckets = table_ref.shape[1]
    turn = flip()
    for d in range(3):
        lane = iota((buckets, 2 * TILE), 1)
        back = jnp.where(lane < TILE, lane, lane - 2 * TILE)
        hot = (bucket_of((d - 1) * TILE - back) == iota((buckets, 2 * TILE), 0)).astype(BF)
        strip = mm(table_ref[...], hot)
        for h in range(heads):
            row = jnp.broadcast_to(strip[h : h + 1, :], (TILE, 2 * TILE))
            line = pltpu.roll(row, 0, 1, stride=1, stride_axis=0)[:, :TILE]
            near[near_rows(h, d), :] = mm(line.astype(BF), turn).astype(BF)


class Sums:
    def __init__(self, nz, bufs, s_sem, r_sem):
        self.nz = nz
        self.dp, self.z, self.c = spot()
        self.bufs, self.s_sem, self.r_sem = bufs, s_sem, r_sem
        self.block = bufs["in"]["pb"].shape[-2:]
        x, y = self.dp % 2, self.dp // 2
        c = self.c
        self.f, self.g = 1 + c, 2 - c
        self.s1 = (1 - c) * x + c * y
        self.s2 = (1 - c) * y + c * x
        self.peer1 = self.dp + self.f * (1 - 2 * self.s1)
        self.peer2 = self.dp + self.g * (1 - 2 * self.s2)
        self.bit, self.high = self.z % 2, self.z // 2
        self.near_z = self.z + 1 - 2 * self.bit
        self.far_z = self.z + 2 - 4 * self.high
        away, here = 2 * (1 - self.high), 2 * self.high
        self.order = (away, away + 1, here, here + 1)
        self.table = {}
        self.pending = []

    def copy(self, src, dst, key, dp=None, z=None, c=None):
        n = self.table.setdefault(key, len(self.table))
        dp = self.dp if dp is None else dp
        z = self.z if z is None else z
        c = self.c if c is None else c
        return pltpu.make_async_remote_copy(
            src, dst, self.s_sem.at[n], self.r_sem.at[n], device_id=(dp, 2 * z + c), device_id_type=MESH
        )

    def start(self, src, dst, key, **to):
        op = self.copy(src, dst, key, **to)
        op.start()
        self.pending.append((key, op))

    def drain(self, *head):
        left = []
        for key, op in self.pending:
            if key[: len(head)] == head:
                op.wait_send()
            else:
                left.append((key, op))
        self.pending = left

    def arrived(self, dst, key):
        self.copy(dst, dst, key).wait_recv()

    def part(self, u, name, *at):
        b = self.bufs[u]
        if name == "r1" and "lent" in b:
            rows, cols = self.block
            zz, i2 = at
            row = pl.multiple_of(i2 * rows, rows) if not isinstance(i2, int) else i2 * rows
            return b["lent"].at[pl.ds(zz, 1), pl.ds(row, rows), b["cols"]]
        return b[name].at[(b["h"], *at)]

    def q(self, i1, i2):
        return i1 * self.f + i2 * self.g

    def add(self, dst, a, b):
        dst[...] = (a[...].astype(F32) + b[...].astype(F32)).astype(BF)

    def a_start(self, u, i, q, zz, k):
        self.start(
            self.part(u, "pb", 2 * zz + 1 - self.c, q), self.part(u, "ra", zz, q), (u, "a", i, k), c=1 - self.c
        )

    def a_finish(self, u, i):
        zz = self.order[i]
        for k in range(4):
            self.arrived(self.part(u, "ra", zz, k), (u, "a", i, k))

        def one(q, carry):
            mine = self.part(u, "ra", zz, q)
            self.add(mine, mine, self.part(u, "pb", 2 * zz + self.c, q))
            return carry

        lax.fori_loop(0, 4, one, 0)

    def first_start(self, u, i):
        zz = self.order[i]
        for i2 in range(2):
            self.start(
                self.part(u, "ra", zz, self.q(1 - self.s1, i2)),
                self.part(u, "r1", zz, i2),
                (u, "1", i, i2),
                dp=self.peer1,
            )

    def first_finish(self, u, i):
        zz = self.order[i]
        for i2 in range(2):
            mine = self.part(u, "r1", zz, i2)
            self.arrived(mine, (u, "1", i, i2))
            self.add(mine, mine, self.part(u, "ra", zz, self.q(self.s1, i2)))

    def second_start(self, u, i):
        zz = self.order[i]
        self.start(
            self.part(u, "r1", zz, 1 - self.s2), self.part(u, "r2", zz), (u, "2", i), dp=self.peer2
        )

    def second_finish(self, u, i):
        zz = self.order[i]
        mine = self.part(u, "r2", zz)
        self.arrived(mine, (u, "2", i))
        self.add(mine, mine, self.part(u, "r1", zz, self.s2))

    def near_start(self, u, name, i):
        zz = self.order[2 * i] + 1 - self.bit
        self.start(self.part(u, name, zz), self.part(u, "rz", i), (u, "z", i), z=self.near_z)

    def near_finish(self, u, name, i):
        mine = self.part(u, "rz", i)
        self.arrived(mine, (u, "z", i))
        self.add(mine, mine, self.part(u, name, self.order[2 * i] + self.bit))
        if i == 0:
            self.start(mine, self.part(u, "rz", 2), (u, "z", 2), z=self.far_z)

    def far_last(self, u):
        last = self.part(u, "rz", 2)
        self.arrived(last, (u, "z", 2))
        self.add(self.part(u, "g", self.dp), last, self.part(u, "rz", 1))

    def far_mid(self, u):
        last = self.part(u, "rz", 2)
        self.arrived(last, (u, "z", 2))
        self.add(last, last, self.part(u, "rz", 1))
        self.start(self.part(u, "rz", 2, 1 - self.s2), self.part(u, "r2", 0), (u, "2", 0), dp=self.peer2)

    def second_last_finish(self, u):
        mine = self.part(u, "r2", 0)
        self.arrived(mine, (u, "2", 0))
        self.add(self.part(u, "g", self.dp), mine, self.part(u, "rz", 2, self.s2))

    def spread_two_start(self, u):
        for dp, key in ((self.peer2, "g0"), (self.peer1, "g1")):
            mine = self.part(u, "g", self.dp)
            self.start(mine, mine, (u, key), dp=dp)

    def spread_two_mid(self, u):
        other = self.part(u, "g", self.peer2)
        self.arrived(other, (u, "g0"))
        self.start(other, other, (u, "g2"), dp=self.peer1)

    def spread_two_finish(self, u):
        self.arrived(self.part(u, "g", self.peer1), (u, "g1"))
        self.arrived(self.part(u, "g", self.peer1 + self.peer2 - self.dp), (u, "g2"))

    def spread_start(self, u):
        mine = self.part(u, "g", self.dp)
        for k in range(1, 4):
            self.start(mine, mine, (u, "g", 3 - k), dp=lax.rem(self.dp + k, 4))

    def spread_finish(self, u):
        for k in range(1, 4):
            self.arrived(self.part(u, "g", lax.rem(self.dp + k, 4)), (u, "g", k - 1))


def table_sums(diag, far, heads):
    rows = diag.shape[1]
    total = jnp.zeros((rows, TILE), F32)
    for d in range(3):
        offset = (d - 1) * TILE + iota((2 * TILE, TILE), 0) - (TILE - 1)
        hot = (bucket_of(offset) == iota((2 * TILE, TILE), 1)).astype(F32)
        total = total + lax.dot_general(
            diag[d], hot, (((1,), (0,)), ((), ())),
            preferred_element_type=F32, precision=lax.Precision.HIGHEST,
        )
    lane = iota((rows, TILE), 1)
    for side, b in ((0, 31), (1, 15)):
        total = total + jnp.where(lane == b, jnp.sum(far[side], axis=1, keepdims=True), 0.0)
    return jnp.where(iota((rows, TILE), 0) < heads, total, 0.0)


def key_masks(segall, kaug, zz, c, nkb):
    for h in range(2):
        b = 2 * zz + h
        row = segall[b, pl.ds(c, 1), :]
        r = iota((TILE, TILE), 0)
        hot = jnp.where((r == row) | (r == 8 + b), 1.0, 0.0).astype(F32)
        kaug[pl.ds(pl.multiple_of(b * TILE, TILE), TILE), :] = hot.T.astype(BF)


def query_side(q, segall, table, qa, z, c, nkb):
    tq = q.shape[0]
    lost, right, left = [], [], []
    for i in range(tq // TILE):
        qb = (tq // TILE) * z + i
        row = segall[qb, pl.ds(c, 1), :]
        r = iota((TILE, TILE), 0)
        one = jnp.where((r < 8) & (r != row), NEG, 0.0).astype(F32)
        lost.append(mm(flip(), one.T.astype(BF)))
        col = iota((TILE, TILE), 1) - 8
        ok = (col >= 0) & (col < nkb)
        right.append(jnp.where(ok & (col >= qb + 2), 1.0, 0.0))
        left.append(jnp.where(ok & (col <= qb - 2), 1.0, 0.0))
    low = iota((tq, TILE), 1) < TILE // 2
    for p in range(qa.shape[0]):
        part = q[:, p * TILE : (p + 1) * TILE]
        for hh in range(2):
            h = 2 * p + hh
            rows = slice(hh * tq, (hh + 1) * tq)
            qa[p, rows, 0:TILE] = jnp.where(low if hh == 0 else jnp.logical_not(low), part, 0.0).astype(BF)
            far_r = table[h : h + 1, 31:32].astype(F32)
            far_l = table[h : h + 1, 15:16].astype(F32)
            for i in range(tq // TILE):
                at = hh * tq + i * TILE
                qa[p, at : at + TILE, TILE:] = (lost[i] + far_r * right[i] + far_l * left[i]).astype(BF)


def attend_step(i, zz, z, k, v, kaug, qa, near, probs, stat, s, acc, tq):
    rows = pl.ds(pl.multiple_of(zz * tq, tq), tq)
    blocks = tq // TILE

    def pair(p, carry):
        cols = pl.ds(pl.multiple_of(p * TILE, TILE), TILE)
        s[...] = mm_nt(jnp.concatenate([k[rows, cols], kaug[rows, :]], axis=1), qa[p])
        if i == 0:
            for kk in range(blocks):
                for qq in range(blocks):
                    for hh in range(2):
                        at = hh * tq + qq * TILE
                        spot_ = (slice(kk * TILE, (kk + 1) * TILE), slice(at, at + TILE))
                        s[spot_] = s[spot_] + near[near_rows(2 * p + hh, kk - qq + 1), :].astype(F32)
        else:

            @pl.when(jnp.abs(zz - z) == 1)
            def _():
                after = (zz - z + 1) // 2
                kr = pl.ds(pl.multiple_of((1 - after) * (tq - TILE), TILE), TILE)
                for hh in range(2):
                    qc = pl.ds(pl.multiple_of(hh * tq + after * (tq - TILE), TILE), TILE)
                    s[kr, qc] = s[kr, qc] + near[near_rows(2 * p + hh, 2 * after), :].astype(F32)

        top = jnp.max(s[...], axis=0, keepdims=True)
        if i > 0:
            old = stat[p, 0:1, :]
            top = jnp.maximum(old, top)
        e = jnp.exp(s[...] - top)
        probs[p, rows, :] = e.astype(BF)
        total = jnp.sum(e, axis=0, keepdims=True)
        mixed = mm_tn(v[rows, cols], probs[p, rows, :])
        arows = pl.ds(pl.multiple_of(p * TILE, TILE), TILE)
        if i > 0:
            fade = jnp.exp(old - top)
            total = total + stat[p, 1:2, :] * fade
            mixed = mixed + acc[arows, :] * fade
        acc[arows, :] = mixed
        stat[p, 0:1, :] = top
        stat[p, 1:2, :] = total
        stat[p, 2 + i : 3 + i, :] = top
        return carry

    lax.fori_loop(0, probs.shape[0], pair, 0)


def attn_backward_pair(p, z, nz, qa, k, v, kaug, datt, probs, scale, dq, diag, far, dm, dprob, ds):
    tq = dq.shape[0]
    length = k.shape[0]
    nkb = length // TILE
    cols = slice(p * TILE, (p + 1) * TILE)
    part = datt[p * tq : (p + 1) * tq, :].astype(F32)
    low = iota((tq, TILE), 1) < TILE // 2
    both = jnp.concatenate([jnp.where(low, part, 0.0), jnp.where(low, 0.0, part)], axis=0)
    column = scale[p].T
    total = jnp.zeros((8, 2 * tq), F32)
    for b in range(nz):
        rows = slice(b * tq, (b + 1) * tq)
        scaled = (both * column[:, b : b + 1]).astype(BF)
        dm[b * 2 * tq : (b + 1) * 2 * tq, :] = scaled
        dprob[rows, :] = mm_nt(v[rows, cols], scaled)
        mixed = dprob[rows, :] * probs[p, rows, :].astype(F32)
        total = total + jnp.sum(mixed.reshape(tq // 8, 8, 2 * tq), axis=0)
    center = jnp.sum(total, axis=0, keepdims=True)
    for b in range(nz):
        rows = slice(b * tq, (b + 1) * tq)
        v[rows, cols] = mm(probs[p, rows, :], dm[b * 2 * tq : (b + 1) * 2 * tq, :]).astype(BF)
        shift = center * scale[p, b : b + 1, :]
        ds[TILE + b * tq : TILE + (b + 1) * tq, :] = (
            probs[p, rows, :].astype(F32) * (dprob[rows, :] - shift)
        ).astype(BF)
    left = jnp.concatenate([k[:, cols], kaug[...]], axis=1)
    back = mm_tn(left, ds[TILE : TILE + length, :])
    k[:, cols] = mm(ds[TILE : TILE + length, :], qa[p, :, 0:TILE]).astype(BF)
    both = jnp.concatenate([back[: TILE // 2, :tq], back[TILE // 2 : TILE, tq:]], axis=0)
    dq[:, cols] = both.T.astype(BF)
    sums = back[TILE + 8 : TILE + 8 + nkb, :]
    kb = iota((nkb, 2 * tq), 0)
    lane = iota((nkb, 2 * tq), 1)
    qb = (tq // TILE) * z + (lane % tq) // TILE
    right = jnp.sum(jnp.where(kb >= qb + 2, sums, 0.0), axis=0, keepdims=True)
    left = jnp.sum(jnp.where(kb <= qb - 2, sums, 0.0), axis=0, keepdims=True)
    for hh in range(2):
        h = 2 * p + hh
        far[0, h : h + 1, :] = right[:, hh * tq : (hh + 1) * tq]
        far[1, h : h + 1, :] = left[:, hh * tq : (hh + 1) * tq]
        for d in range(3):
            near_sum = jnp.zeros((TILE, TILE), F32)
            for i in range(tq // TILE):
                row = ((tq // TILE) * z + i + d) * TILE
                at = hh * tq + i * TILE
                near_sum = near_sum + ds[pl.ds(pl.multiple_of(row, TILE), TILE), at : at + TILE].astype(F32)
            wide = jnp.concatenate([near_sum, jnp.zeros((TILE, TILE), F32)], axis=1)
            wide = pltpu.roll(wide, 0, 1, stride=1, stride_axis=0)
            diag[d, h : h + 1, :] = jnp.sum(wide, axis=0, keepdims=True)


def layer_kernel(nz, *refs):
    (tok_h, dy_h, seg, wq_h, wk_h, wv_h, wout_h, win_h, wdown_h, gain_a, gain_f, table_h) = refs[:12]
    o_home, o_grads, o_small = refs[12:15]
    o_out, o_gt = o_home.at[0], o_home.at[1]
    g_down, g_in, g_attn = (o_grads.at[0:2, 4 * i : 4 * i + 4] for i in range(3))
    (
        x, k, v, qa, probs, att, dy, wqkv, wout, wdown, buf_b, pdown, pin,
        ra_d, ra_i, r1_d, r2_d, rz_d, r1_i, r2_i, rz_i, r2_a, rz_a,
        n2, dh, dhl, own_dn1, dprob, ds, near, kaug, diag, far, stat, scale,
        rd, relay, segall, segbuf, table, sm, smr, s_sem, r_sem, l_sem, gs_sem, gr_sem, credit,
    ) = refs[15:]
    both, one, two = pl.ds(0, 2), pl.ds(0, 1), pl.ds(1, 1)
    half = x.shape[2] // 2
    bufs = {
        "down": dict(h=both, pb=pdown, ra=ra_d, r1=r1_d, r2=r2_d, rz=rz_d, g=g_down),
        "in": dict(h=both, pb=pin, ra=ra_i, r1=r1_i, r2=r2_i, rz=rz_i, g=g_in),
        "attn0": dict(h=one, pb=pdown, ra=ra_d, r2=r2_a, rz=rz_a, g=g_attn, lent=wdown, cols=slice(0, half)),
        "attn1": dict(h=two, pb=pdown, ra=ra_d, r2=r2_a, rz=rz_a, g=g_attn, lent=wdown, cols=slice(half, 2 * half)),
    }
    eng = Sums(nz, bufs, s_sem, r_sem)
    dp, z, c = eng.dp, eng.z, eng.c
    blk = 2 * z + c
    nb, block, width = x.shape
    tq = 2 * block
    length = nb * block
    nkb = length // TILE
    share = width // nb
    steps = buf_b.shape[0]
    per = nb // steps
    pairs = probs.shape[0]
    heads = 2 * pairs
    barrier = pltpu.get_barrier_semaphore()
    peers = [(dp, lax.rem(blk + i, nb)) for i in range(1, nb)]
    peers += [(eng.peer1, blk), (eng.peer2, blk), (eng.peer1 + eng.peer2 - dp, blk)]
    for peer in peers:
        pl.semaphore_signal(barrier, inc=1, device_id=peer, device_id_type=MESH)

    loads = {}

    def load(name, src, dst):
        loads[name] = pltpu.make_async_copy(src, dst, l_sem.at[len(loads)])
        loads[name].start()

    def ready(*names):
        for name in names:
            loads[name].wait()

    load("x", tok_h.at[c], x.at[blk])
    load("table", table_h, table)
    load("wk", wk_h, wqkv.at[1])
    load("wv", wv_h, wqkv.at[2])
    load("wq", wq_h, wqkv.at[0])

    def gcopy(src, dst, send, recv, zz, cc):
        return pltpu.make_async_remote_copy(
            src, dst, gs_sem.at[send], gr_sem.at[recv], device_id=(dp, 2 * zz + cc), device_id_type=MESH
        )

    def inside(other):
        return (other >= 0) & (other < nz)

    segbuf[...] = jnp.zeros_like(segbuf)
    segbuf[0:2, :] = seg[...]
    segall[blk] = segbuf[...]
    pl.semaphore_wait(barrier, len(peers))

    ways = ((0, 1), (1, -1))
    mine = x.at[blk]
    gcopy(tok_h.at[1 - c], mine, 4, blk, z, 1 - c).start()
    for i in range(1, nb):
        pltpu.make_async_remote_copy(
            segbuf, segall.at[blk], gs_sem.at[10 + i], gr_sem.at[nb + 1 + blk],
            device_id=(dp, lax.rem(blk + i, nb)), device_id_type=MESH,
        ).start()
    for way, dz in ways:

        @pl.when(inside(z + dz))
        def _():
            gcopy(tok_h.at[1 - c], mine, 2 * way, blk, z + dz, 1 - c).start()
            gcopy(tok_h.at[c], mine, 2 * way + 1, blk, z + dz, c).start()

    gcopy(dy_h.at[1 - c], dy.at[c], 5, nb, z, 1 - c).start()
    load("dy", dy_h.at[c], dy.at[c])
    load("wout", wout_h, wout)
    for j in range(steps):
        jj = eng.order[j]
        load(("win", j), win_h.at[:, pl.ds(pl.multiple_of(jj * width, width), width)], buf_b.at[jj])
        load(("wdown", j), wdown_h.at[jj], wdown.at[jj])

    ready("table")
    prepare_bias(table, near, heads)
    reach = -(-REACH // tq)
    for zz in range(nz):

        @pl.when(jnp.abs(zz - z) > reach)
        def _():
            rows = slice(zz * tq, (zz + 1) * tq)
            x[2 * zz : 2 * zz + 2] = jnp.zeros((2, block, width), BF)
            for ref in (k, v):
                ref[rows, :] = jnp.zeros((tq, width), BF)
            kaug[rows, :] = jnp.zeros((tq, TILE), BF)
            for p in range(pairs):
                probs[p, rows, :] = jnp.zeros((tq, 2 * tq), BF)

    ds[0:TILE, :] = jnp.zeros((TILE, ds.shape[1]), BF)
    ds[ds.shape[0] - TILE :, :] = jnp.zeros((TILE, ds.shape[1]), BF)
    diag[...] = jnp.zeros_like(diag)
    far[...] = jnp.zeros_like(far)
    scale[...] = jnp.zeros_like(scale)
    sm[0] = jnp.zeros(sm.shape[1:], F32)
    gain1, gain2 = gain_a[...].reshape(1, width).astype(F32), gain_f[...].reshape(1, width).astype(F32)

    def x_arrived(b):
        gcopy(x.at[b], x.at[b], 0, b, z, 1 - c).wait_recv()

    def seg_arrived(b):
        gcopy(segbuf, segall.at[b], 0, nb + 1 + b, z, 1 - c).wait_recv()

    def keys_of(zz):
        rows = pl.ds(pl.multiple_of(zz * tq, tq), tq)
        key_masks(segall, kaug, zz, c, nkb)
        n1 = norm_rows(x[pl.ds(2 * zz, 2)].reshape(tq, width), gain1)[2]
        k[rows, :] = mm(n1, wqkv[1]).astype(BF)
        v[rows, :] = mm(n1, wqkv[2]).astype(BF)
        return n1

    s_blk, acc = dprob.at[0:tq], dprob.at[tq : tq + pairs * TILE]
    ready("x", "wk", "wv", "wq")
    x_arrived(2 * z + 1 - c)
    seg_arrived(2 * z + 1 - c)
    q_rev = mm(flipped(keys_of(z)), wqkv[0]).astype(BF).astype(F32)
    query_side(q_rev, segall, table, qa, z, c, nkb)
    order = (z, eng.near_z, 2 - eng.high, 3 - 3 * eng.high)
    wide = width // 2
    attend_step(0, order[0], z, k, v, kaug, qa, near, probs, stat, s_blk, acc, tq)
    for way, dz in ways:
        src = z - dz

        @pl.when(inside(src))
        def _():
            for h in range(2):
                x_arrived(2 * src + h)

                @pl.when(inside(z + dz))
                def _():
                    gcopy(
                        x.at[2 * src + h], x.at[2 * src + h], 6 + 2 * way + h, 2 * src + h, z + dz, c
                    ).start()

    for i in range(1, nb):
        other = lax.rem(blk + i, nb)

        @pl.when(other // 2 != z)
        def _():
            seg_arrived(other)

    for i in range(1, 4):
        zz = order[i]

        @pl.when(jnp.abs(zz - z) <= reach)
        def _():
            @pl.when(jnp.abs(zz - z) == 2)
            def _():
                for h in range(2):
                    x_arrived(2 * zz + h)

            keys_of(zz)
            attend_step(i, zz, z, k, v, kaug, qa, near, probs, stat, s_blk, acc, tq)

    for p in range(pairs):
        inverse = 1.0 / stat[p, 1:2, :]
        top = stat[p, 0:1, :]
        for i in range(4):

            @pl.when(jnp.abs(order[i] - z) <= reach)
            def _():
                scale[p, pl.ds(order[i], 1), :] = jnp.exp(stat[p, 2 + i : 3 + i, :] - top) * inverse

        mixed = acc[p * TILE : (p + 1) * TILE, :] * inverse
        both = jnp.concatenate([mixed[: TILE // 2, :tq], mixed[TILE // 2 :, tq:]], axis=0)
        att[:, p * TILE : (p + 1) * TILE] = both.T.astype(BF)
    att[...] = flipped(att[...])

    ready("wout")
    x_own = x.at[pl.ds(2 * z, 2)]
    dh[...] = x_own[...].reshape(tq, width).astype(F32) + mm(att[...], wout[...])
    n2[...] = norm_rows(dh[...], gain2)[2]
    ready("dy")
    gcopy(dy.at[0], dy.at[1 - c], 0, nb, z, 1 - c).wait_recv()
    total = own_dn1
    for j in range(steps):
        jj = eng.order[j]
        ready(("win", j), ("wdown", j))
        value, slant = gelu_both(mm(n2[...], buf_b[jj]))
        act = value.astype(BF)
        d = dy[...].reshape(tq, width)
        grad = mm_tn(act, d).astype(BF)
        for hh in range(2):
            part = grad[:, hh * wide : (hh + 1) * wide]
            pdown[hh, pl.ds(jj * per, per)] = part.reshape(per, 4, share, wide)
        for qq in range(4):
            eng.a_start("down", j, qq, jj, qq)
        dpre = (mm_nt(d, wdown[jj]) * slant).astype(BF)
        grad = mm_tn(n2[...], dpre).astype(BF)
        for hh in range(2):
            part = grad[:, hh * wide : (hh + 1) * wide]
            pin[hh, :, jj] = part.reshape(nb, share, wide)
        for i in range(nz):
            eng.a_start("in", i, jj, eng.order[i], j)
        if j == 0:
            total[...] = mm(act, wdown[jj])
            dn2 = mm_nt(dpre, buf_b[jj])
        else:
            total[...] += mm(act, wdown[jj])
            dn2 = dn2 + mm_nt(dpre, buf_b[jj])
        eng.a_finish("down", j)
        eng.first_start("down", j)
    h = dh[...]
    n2[...] = (h + total[...]).astype(BF)
    normed, r2, _ = norm_rows(h, gain2)
    back, gain_grad = rms_backward(dn2, normed, r2, gain2)
    lines = width // TILE
    for i in range(lines):
        sm[0, lines + i : lines + i + 1, :] = gain_grad[None, i * TILE : (i + 1) * TILE]
    dh[...] = dy[...].reshape(tq, width).astype(F32) + back
    dhl[...] = dh[...].astype(BF)
    back = flipped(mm_nt(dhl[...], wout[...]).astype(BF))
    datt, dm = near.at[0 : pairs * tq], near.at[pairs * tq : pairs * tq + nz * 2 * tq]
    for p in range(pairs):
        datt[p * tq : (p + 1) * tq, :] = back[:, p * TILE : (p + 1) * TILE]
    for i in range(nz):
        eng.a_finish("in", i)
    out_half = [n2.at[pl.ds(pl.multiple_of(i * block, block), block)] for i in (c, 1 - c)]
    eng.start(out_half[1], o_out.at[c], ("out",), c=1 - c)
    load("kept", out_half[0], o_out.at[c])

    def first_near(u, i):
        for ii in (2 * i, 2 * i + 1):
            eng.first_finish(u, ii)
        eng.near_start(u, "r1", i)

    def first_second(u, i):
        for ii in (2 * i, 2 * i + 1):
            eng.first_finish(u, ii)
            eng.second_start(u, ii)

    def second_near(u, i):
        for ii in (2 * i, 2 * i + 1):
            eng.second_finish(u, ii)
        eng.near_start(u, "r2", i)

    first_near("down", 0)
    eng.drain("down", "a")
    for hh in range(2):
        grad = mm_tn(att[...], dhl[:, hh * wide : (hh + 1) * wide]).astype(BF)
        pdown[hh, :, 3] = grad.reshape(nb, share, wide)
    dq = dhl
    for b in range(nz):
        buf_b[b, tq : 2 * tq] = norm_rows(x[2 * b : 2 * b + 2].reshape(tq, width), gain1)[2]

    def weights(part):
        cols = slice(part * wide, (part + 1) * wide)
        dq[:, cols] = flipped(dq[:, cols])
        for i, ref in ((1, k), (2, v)):
            grad = sum(
                mm_tn(buf_b[b, tq : 2 * tq], ref[b * tq : (b + 1) * tq, cols]) for b in range(nz)
            )
            pdown[part, :, i] = grad.astype(BF).reshape(nb, share, wide)
        pdown[part, :, 0] = mm_tn(buf_b[z, tq : 2 * tq], dq[:, cols]).astype(BF).reshape(nb, share, wide)

    def a_start_all(u):
        for i in range(nz):
            for qq in range(4):
                eng.a_start(u, i, qq, eng.order[i], qq)

    for p in range(pairs):
        attn_backward_pair(
            p, z, nz, qa, k, v, kaug, datt, probs, scale, dq, diag, far, dm, dprob, ds
        )
        if p == 0:
            eng.first_start("in", 0)
            eng.first_start("in", 1)
        if p == 2:
            eng.first_start("in", 2)
            eng.first_start("in", 3)
            weights(0)
            first_near("down", 1)
            eng.near_finish("down", "r1", 0)
            eng.drain("down", "1")
            pl.semaphore_signal(credit, inc=1, device_id=(dp, 2 * z + 1 - c), device_id_type=MESH)
        if p == 3:
            pl.semaphore_wait(credit, 1)
            a_start_all("attn0")
        if p == 4:
            first_second("in", 0)
            for i in range(nz):
                eng.a_finish("attn0", i)
                eng.first_start("attn0", i)

    for b in range(nz):
        rows = slice(b * tq, (b + 1) * tq)
        part = mm_nt(k[rows, :], wqkv[1]) + mm_nt(v[rows, :], wqkv[2])
        buf_b[b, 0:tq] = part.astype(BF)
    for way, dz in ways:

        @pl.when(inside(z + 2 * dz))
        def _():
            eng.copy(buf_b.at[z + 2 * dz, 0:tq], relay.at[way], ("d1", way), z=z + dz).start()

    weights(1)
    a_start_all("attn1")
    first_second("in", 1)
    for i in range(nz):
        eng.a_finish("attn1", i)
        eng.first_start("attn1", i)
    eng.near_finish("down", "r1", 1)
    second_near("in", 0)

    own_dn1[...] = mm_nt(dq[...], wqkv[0])
    own_normed = norm_rows(x_own[...].reshape(tq, width), gain1)[0]
    gain_sum = jnp.sum(own_dn1[...] * own_normed, axis=0, keepdims=True)
    for b in range(nz):
        rows = slice(b * tq, (b + 1) * tq)
        part = mm_nt(k[rows, :], wqkv[1]) + mm_nt(v[rows, :], wqkv[2])
        normed = norm_rows(x[2 * b : 2 * b + 2].reshape(tq, width), gain1)[0]
        gain_sum = gain_sum + jnp.sum(part * normed, axis=0, keepdims=True)

        @pl.when(z == b)
        def _():
            own_dn1[...] += part

    for i in range(lines):
        sm[0, i : i + 1, :] = gain_sum[:, i * TILE : (i + 1) * TILE]
    sm[0, 2 * lines :, :] = table_sums(diag, far, heads)[: sm.shape[1] - 2 * lines]
    hops = (
        dict(c=1 - c), dict(dp=dp + 1 - 2 * (dp % 2)), dict(dp=dp + 2 - 4 * (dp // 2)),
        dict(z=eng.near_z), dict(z=eng.far_z),
    )

    def small_start(i):
        eng.start(sm.at[i], smr.at[i], ("s", i), **hops[i])

    def small_finish(i):
        eng.copy(sm.at[i], smr.at[i], ("s", i), **hops[i]).wait_recv()
        sm[i + 1] = sm[i] + smr[i]

    small_start(0)
    eng.far_mid("down")
    first_second("attn0", 0)
    small_finish(0)
    small_start(1)
    for way, dz in ways:

        @pl.when(inside(z - dz) & inside(z + dz))
        def _():
            eng.copy(relay.at[way], relay.at[way], ("d1", way)).wait_recv()
            buf_b[z + dz, 0:tq] = (buf_b[z + dz, 0:tq].astype(F32) + relay[way].astype(F32)).astype(BF)

        @pl.when(inside(z + dz))
        def _():
            eng.copy(buf_b.at[z + dz, 0:tq], rd.at[way], ("d2", way), z=z + dz).start()

    first_second("attn0", 1)
    eng.near_finish("in", "r2", 0)
    first_second("attn1", 0)
    second_near("in", 1)
    second_near("attn0", 0)
    first_second("attn1", 1)
    eng.second_last_finish("down")
    eng.spread_two_start("down")
    small_finish(1)
    small_start(2)
    second_near("attn0", 1)
    eng.near_finish("in", "r2", 1)
    eng.near_finish("attn0", "r2", 0)
    second_near("attn1", 0)
    eng.spread_two_mid("down")
    small_finish(2)
    small_start(3)
    second_near("attn1", 1)
    eng.near_finish("attn0", "r2", 1)
    eng.far_last("in")
    eng.spread_start("in")
    eng.near_finish("attn1", "r2", 0)
    eng.near_finish("attn1", "r2", 1)
    eng.far_last("attn0")
    eng.spread_start("attn0")
    small_finish(3)
    small_start(4)

    dn1 = own_dn1
    for way, dz in ways:

        @pl.when(inside(z - dz))
        def _():
            eng.copy(rd.at[way], rd.at[way], ("d2", way)).wait_recv()
            dn1[...] += rd[way].astype(F32)

    normed, r1, _ = norm_rows(x_own[...].reshape(tq, width), gain1)
    back, _ = rms_backward(dn1[...], normed, r1, gain1)
    dy[...] = (dh[...] + back).astype(BF).reshape(dy.shape)
    eng.start(dy.at[1 - c], o_gt.at[c], ("gt",), c=1 - c)
    load("kept_gt", dy.at[c], o_gt.at[c])

    eng.far_last("attn1")
    eng.spread_start("attn1")
    small_finish(4)
    o_small[...] = sm[5]
    eng.copy(dy.at[0], o_out.at[1 - c], ("out",)).wait_recv()
    eng.copy(dy.at[0], o_gt.at[1 - c], ("gt",)).wait_recv()
    ready("kept", "kept_gt")
    eng.spread_two_finish("down")
    eng.spread_finish("in")
    eng.spread_finish("attn0")
    eng.spread_finish("attn1")
    eng.drain()
    gcopy(tok_h.at[0], mine, 4, blk, z, 1 - c).wait_send()
    gcopy(dy_h.at[0], dy.at[0], 5, nb, z, 1 - c).wait_send()
    for i in range(1, nb):
        gcopy(segbuf, segall.at[0], 10 + i, nb + 1, z, 1 - c).wait_send()
    for way, dz in ways:

        @pl.when(inside(z + dz))
        def _():
            gcopy(tok_h.at[0], mine, 2 * way, blk, z, 1 - c).wait_send()
            gcopy(tok_h.at[0], mine, 2 * way + 1, blk, z, 1 - c).wait_send()
            eng.copy(buf_b.at[0, 0:tq], rd.at[way], ("d2", way)).wait_send()

        @pl.when(inside(z + 2 * dz))
        def _():
            eng.copy(buf_b.at[0, 0:tq], relay.at[way], ("d1", way)).wait_send()

        @pl.when(inside(z - dz) & inside(z + dz))
        def _():
            for h in range(2):
                gcopy(tok_h.at[0], mine, 6 + 2 * way + h, blk, z, 1 - c).wait_send()


def layer(nz, tok, dy, seg, wq, wk, wv, wout, win, wdown, gain_a, gain_f, table):
    _, block, width = tok.shape
    nb = 2 * nz
    length, tq = nb * block, 2 * block
    share = width // nb
    pairs = table.shape[0] // 2
    steps = win.shape[1] // width
    vm = pl.BlockSpec(memory_space=pltpu.VMEM)
    hbm = pl.BlockSpec(memory_space=pl.ANY)
    home = jax.ShapeDtypeStruct((2, 2, block, width), BF)
    grads = jax.ShapeDtypeStruct((2, 12, share, width // 2), BF)
    one = (share, width // 2)
    small = (24, TILE)

    def bf(*shape):
        return pltpu.VMEM(shape, BF)

    def f32(*shape):
        return pltpu.VMEM(shape, F32)

    sums = [bf(2, nz, 4, *one), bf(2, nz, 4, *one)]
    for i, route in enumerate(("xzy", "xyz", "xyz")):
        last = route == "xyz"
        sums += [bf(2, nz, 2, *one)] if i < 2 else []
        sums += [bf(2, nz if last else 1, *one), bf(2, 3, *one) if last else bf(2, 3, 2, *one)]
    scratch = [
        bf(nb, block, width), bf(length, width), bf(length, width),
        bf(pairs, 2 * tq, 2 * TILE), bf(pairs, length, 2 * tq), bf(tq, width),
        bf(2, block, width), bf(3, width, width), bf(width, width),
        bf(steps, width, width), bf(steps, width, width), bf(2, nb, 4, *one), bf(2, nb, 4, *one),
        *sums,
        bf(tq, width), f32(tq, width), bf(tq, width), f32(tq, width),
        f32(length, 2 * tq), bf(length + 2 * TILE, 2 * tq), bf(max(2 * pairs * 3 * TILE, pairs * tq + nz * 2 * tq), TILE), bf(length, TILE),
        f32(3, 16, 2 * TILE), f32(2, 16, tq), f32(pairs, 8, 2 * tq), f32(pairs, 8, 2 * tq),
        bf(2, tq, width), bf(2, tq, width),
        pltpu.VMEM((nb, 8, block), jnp.int32), pltpu.VMEM((8, block), jnp.int32), bf(*table.shape),
        f32(6, *small), f32(5, *small),
        pltpu.SemaphoreType.DMA((180,)), pltpu.SemaphoreType.DMA((180,)), pltpu.SemaphoreType.DMA((32,)),
        pltpu.SemaphoreType.DMA((10 + nb,)), pltpu.SemaphoreType.DMA((2 * nb + 2,)),
        pltpu.SemaphoreType.REGULAR,
    ]
    return pl.pallas_call(
        functools.partial(layer_kernel, nz),
        out_shape=(home, grads, jax.ShapeDtypeStruct(small, F32)),
        in_specs=[hbm, hbm, vm] + [hbm] * 6 + [vm, vm, hbm],
        out_specs=(vm,) * 3,
        scratch_shapes=scratch,
        compiler_params=pltpu.CompilerParams(
            collective_id=1, has_side_effects=True, vmem_limit_bytes=64 * 1024 * 1024
        ),
    )(tok, dy, seg, wq, wk, wv, wout, win, wdown, gain_a, gain_f, table)


def finish_kernel(home, grads, small, o_out, o_gt, o_ga, o_q, o_k, o_v, o_o, o_gf, o_in, o_down, o_gt_table):
    share, wide = grads.shape[2:]
    width = 2 * wide
    lines = width // TILE
    blk = lax.axis_index("blk")
    o_out[...] = home[0]
    o_gt[...] = home[1]
    for hh in range(2):
        cols = slice(hh * wide, (hh + 1) * wide)
        for i in range(4):
            o_down[i * share : (i + 1) * share, cols] = grads[hh, i].astype(F32)
            at = i * width + hh * wide
            o_in[:, at : at + wide] = grads[hh, 4 + i].astype(F32)
        for i, ref in enumerate((o_q, o_k, o_v, o_o)):
            ref[:, cols] = grads[hh, 8 + i].astype(F32)

    def mine(first, count, each):
        flat = jnp.concatenate([small[first + i : first + i + 1, :] for i in range(count)], axis=1)
        flat = jnp.broadcast_to(flat, (8, count * TILE))
        return pltpu.roll(flat, lax.rem(count * TILE - blk * each, count * TILE), 1)[0:1, :each]

    o_ga[...] = mine(0, lines, share).reshape(share)
    o_gf[...] = mine(lines, lines, share).reshape(share)
    per, heads = o_gt_table.shape
    table = small[2 * lines : 2 * lines + 16, :] if small.shape[0] >= 2 * lines + 16 else jnp.concatenate(
        [small[2 * lines :, :], jnp.zeros((16 - (small.shape[0] - 2 * lines), TILE), F32)], axis=0
    )
    turned = pltpu.roll(table, lax.rem(TILE - blk * per, TILE), 1).T
    o_gt_table[...] = turned[:per, :heads]


def finish(home, grads, small, heads, nb):
    _, _, block, width = home.shape
    share = width // nb
    vm = pl.BlockSpec(memory_space=pltpu.VMEM)
    one = jax.ShapeDtypeStruct((share, width), F32)
    gain = jax.ShapeDtypeStruct((share,), F32)
    own = jax.ShapeDtypeStruct((2, block, width), BF)
    return pl.pallas_call(
        finish_kernel,
        out_shape=(
            own, own, gain, one, one, one, one, gain,
            jax.ShapeDtypeStruct((share, 4 * width), F32),
            jax.ShapeDtypeStruct((4 * share, width), F32),
            jax.ShapeDtypeStruct((32 // nb, heads), F32),
        ),
        in_specs=[vm] * 3,
        out_specs=(vm,) * 11,
    )(home, grads, small)


def fast_device(
    nz, tokens, segment_ids, gain_attn, w_query, w_key, w_value, w_out, gain_ffn, w_in, w_down,
    rel_table, cotangent,
):
    width = tokens.shape[2]
    home, grads, small = layer(
        nz, tokens, cotangent, segment_ids, w_query, w_key, w_value, w_out, w_in,
        w_down.reshape(-1, width, width), gain_attn, gain_ffn, rel_table.T,
    )
    return finish(home, grads, small, rel_table.shape[1], 2 * nz)


def pick(mesh):
    if mesh.shape["dp"] == 4 and mesh.shape["blk"] == 8:
        return functools.partial(fast_device, mesh.shape["blk"] // 2)
    return on_device


def solution(mesh):
    placed = (
        P("dp", "blk", None),
        P("dp", "blk"),
        P(),
        P(),
        P(),
        P(),
        P(),
        P(),
        P(),
        P(),
        P(),
        P("dp", "blk", None),
    )
    return jax.shard_map(
        pick(mesh),
        mesh=mesh,
        in_specs=placed,
        out_specs=(
            P("dp", "blk", None),
            P("dp", "blk", None),
            P("blk"),
            P("blk", None),
            P("blk", None),
            P("blk", None),
            P("blk", None),
            P("blk"),
            P("blk", None),
            P("blk", None),
            P("blk", None),
        ),
        check_vma=False,
    )
```

```python
import functools
import math

import jax
import jax.numpy as jnp
from jax import lax
from jax.experimental import pallas as pl
from jax.experimental.pallas import tpu as pltpu
from jax.sharding import PartitionSpec as P

EPS = 1e-06
NEG = -1e30
EDGES = (12, 16, 23, 32, 46, 64, 91)
ROOT_TWO_PI = 0.7978845608028654
CUBIC = 0.044715


def bucket_of(offset):
    distance = jnp.abs(offset)
    far_part = 8 + sum(((distance >= edge).astype(jnp.int32) for edge in EDGES))
    return jnp.where(offset > 0, 16, 0) + jnp.where(distance < 8, distance, far_part)


def gelu_both(values):
    inner_arg = ROOT_TWO_PI * (values + CUBIC * values * values * values)
    tangent = jnp.tanh(inner_arg)
    result = 0.5 * values * (1.0 + tangent)
    slope = 0.5 * (1.0 + tangent) + 0.5 * values * (1.0 - tangent * tangent) * ROOT_TWO_PI * (
        1.0 + 3.0 * CUBIC * values * values
    )
    return (result, slope)


def rms_forward(values, gain):
    scale = lax.rsqrt(jnp.mean(values * values, axis=-1, keepdims=True) + EPS)
    normed = values * scale
    return (normed, scale, (normed * gain).astype(jnp.bfloat16))


def rms_backward(grad, normed, scale, gain):
    gain_grad = jnp.sum(grad * normed, axis=0)
    inner_grad = grad * gain
    back = scale * (inner_grad - normed * jnp.mean(inner_grad * normed, axis=-1, keepdims=True))
    return (back, gain_grad)


def outer_sum(left, right):
    return jnp.einsum("td,tf->df", left, right, preferred_element_type=jnp.float32)


def times_t(left, right):
    return jnp.einsum("tf,df->td", left, right, preferred_element_type=jnp.float32)


def masked_scores(query, keys, bias, seg_query, seg_keys):
    raw = (
        jnp.einsum("bqhd,bkhd->bhqk", query, keys, preferred_element_type=jnp.float32) + bias[None]
    )
    same = seg_query[:, None, :, None] == seg_keys[:, None, None, :]
    return jnp.where(same, raw, NEG)


def score_grads(q_part, k_part, v_part, bias, sq_part, sk_part, total, d_mixed):
    scores = masked_scores(q_part, k_part, bias, sq_part, sk_part)
    probs = jnp.exp(scores - total[..., None])
    grad_probs = jnp.einsum("bqhd,bkhd->bhqk", d_mixed, v_part, preferred_element_type=jnp.float32)
    return (probs, grad_probs)


def on_device(
    tokens,
    segment_ids,
    gain_attn,
    w_query,
    w_key,
    w_value,
    w_out,
    gain_ffn,
    w_in,
    w_down,
    rel_table,
    cotangent,
):
    rows, block, width = tokens.shape
    buckets, heads = rel_table.shape
    inner = w_query.shape[1]
    head_dim = inner // heads
    length = block * lax.axis_size("blk")
    group = math.gcd(rows, max(1, 512 // block))
    blocks = rows // group
    gain_one = gain_attn.astype(jnp.float32)
    gain_two = gain_ffn.astype(jnp.float32)
    table_f = rel_table.astype(jnp.float32)
    flat = tokens.reshape(rows * block, width).astype(jnp.float32)
    normed_one, scale_one, low_one = rms_forward(flat, gain_one)

    def project(weight):
        return (
            jnp.dot(low_one, weight, preferred_element_type=jnp.float32)
            .astype(jnp.bfloat16)
            .reshape(rows, block, inner)
        )

    query, keys, values = (project(w_query), project(w_key), project(w_value))
    key_all, value_all, seg_all = (
        lax.all_gather(keys, "blk", axis=1, tiled=True),
        lax.all_gather(values, "blk", axis=1, tiled=True),
        lax.all_gather(segment_ids, "blk", axis=1, tiled=True),
    )
    places = lax.axis_index("blk") * block + jnp.arange(block, dtype=jnp.int32)
    offsets = jnp.arange(length, dtype=jnp.int32)[None, :] - places[:, None]
    onehot = (
        bucket_of(offsets)[None] == jnp.arange(buckets, dtype=jnp.int32)[:, None, None]
    ).astype(jnp.float32)
    bias = jnp.einsum("nqk,nh->hqk", onehot, table_f, precision=lax.Precision.HIGHEST)
    q_groups = query.reshape(blocks, group, block, heads, head_dim)
    seg_query = segment_ids.reshape(blocks, group, block)

    def key_groups(key_rows, value_rows, seg_rows):
        return (
            key_rows.reshape(blocks, group, length, heads, head_dim),
            value_rows.reshape(blocks, group, length, heads, head_dim),
            seg_rows.reshape(blocks, group, length),
        )

    k_groups, v_groups, seg_keys = key_groups(key_all, value_all, seg_all)

    def attend(parts):
        q_part, k_part, v_part, sq_part, sk_part = parts
        scores = masked_scores(q_part, k_part, bias, sq_part, sk_part)
        top = jnp.max(scores, axis=-1, keepdims=True)
        total = jnp.log(jnp.sum(jnp.exp(scores - top), axis=-1, keepdims=True)) + top
        probs = jnp.exp(scores - total).astype(jnp.bfloat16)
        mixed = jnp.einsum("bhqk,bkhd->bqhd", probs, v_part, preferred_element_type=jnp.float32)
        return (mixed.astype(jnp.bfloat16), total[..., 0])

    attended, log_totals = lax.map(attend, (q_groups, k_groups, v_groups, seg_query, seg_keys))
    attended_flat = attended.reshape(rows * block, inner)
    hidden = flat + jnp.dot(attended_flat, w_out, preferred_element_type=jnp.float32)
    normed_two, scale_two, low_two = rms_forward(hidden, gain_two)
    pre = jnp.dot(low_two, w_in, preferred_element_type=jnp.float32)
    gelu_value, gelu_slope = gelu_both(pre)
    active = gelu_value.astype(jnp.bfloat16)
    output = (hidden + jnp.dot(active, w_down, preferred_element_type=jnp.float32)).astype(
        jnp.bfloat16
    )
    grad_out = cotangent.reshape(rows * block, width)
    grad_down = outer_sum(active, grad_out)
    grad_pre = (times_t(grad_out, w_down) * gelu_slope).astype(jnp.bfloat16)
    grad_in = outer_sum(low_two, grad_pre)
    back_two, grad_gain_two = rms_backward(times_t(grad_pre, w_in), normed_two, scale_two, gain_two)
    grad_hidden = grad_out.astype(jnp.float32) + back_two
    grad_proj = grad_hidden.astype(jnp.bfloat16)
    grad_wout = outer_sum(attended_flat, grad_proj)
    grad_att = (
        times_t(grad_proj, w_out)
        .astype(jnp.bfloat16)
        .reshape(blocks, group, block, heads, head_dim)
    )
    key_back, value_back, seg_back = (
        lax.all_gather(keys, "blk", axis=1, tiled=True),
        lax.all_gather(values, "blk", axis=1, tiled=True),
        lax.all_gather(segment_ids, "blk", axis=1, tiled=True),
    )
    k_back, v_back, sk_back = key_groups(key_back, value_back, seg_back)
    start = jnp.zeros((heads, block, length), jnp.float32)

    def attend_back(carry, parts):
        q_part, k_part, v_part, sq_part, sk_part, total, d_mixed = parts
        probs, grad_probs = score_grads(
            q_part, k_part, v_part, bias, sq_part, sk_part, total, d_mixed
        )
        center = jnp.sum(probs * grad_probs, axis=-1, keepdims=True)
        grad_scores = (probs * (grad_probs - center)).astype(jnp.bfloat16)
        grad_q = jnp.einsum(
            "bhqk,bkhd->bqhd", grad_scores, k_part, preferred_element_type=jnp.float32
        ).astype(jnp.bfloat16)
        grad_k = jnp.einsum(
            "bhqk,bqhd->bkhd", grad_scores, q_part, preferred_element_type=jnp.float32
        )
        grad_v = jnp.einsum(
            "bhqk,bqhd->bkhd",
            probs.astype(jnp.bfloat16),
            d_mixed,
            preferred_element_type=jnp.float32,
        )
        paired = jnp.stack([grad_k, grad_v], axis=2).reshape(group, length, 2, inner)
        return (carry + jnp.sum(grad_scores.astype(jnp.float32), axis=0), (grad_q, paired))

    bias_grad, (grad_query, paired) = lax.scan(
        attend_back, start, (q_groups, k_back, v_back, seg_query, sk_back, log_totals, grad_att)
    )
    paired = paired.reshape(rows, length, 2, inner)
    kv_grad = lax.psum_scatter(paired, "blk", scatter_dimension=1, tiled=True).astype(jnp.bfloat16)
    grad_key = kv_grad[:, :, 0].reshape(rows * block, inner)
    grad_value = kv_grad[:, :, 1].reshape(rows * block, inner)
    grad_query = grad_query.reshape(rows * block, inner)
    grad_wq = outer_sum(low_one, grad_query)
    grad_wk = outer_sum(low_one, grad_key)
    grad_wv = outer_sum(low_one, grad_value)
    grad_low_one = (
        times_t(grad_query, w_query) + times_t(grad_key, w_key) + times_t(grad_value, w_value)
    )
    back_one, grad_gain_one = rms_backward(grad_low_one, normed_one, scale_one, gain_one)
    grad_tokens = (grad_hidden + back_one).astype(jnp.bfloat16).reshape(rows, block, width)
    grad_table = jnp.einsum("hqk,nqk->nh", bias_grad, onehot, precision=lax.Precision.HIGHEST)
    grads = (
        grad_gain_one,
        grad_wq,
        grad_wk,
        grad_wv,
        grad_wout,
        grad_gain_two,
        grad_in,
        grad_down,
        grad_table,
    )
    pieces = (
        lax.psum_scatter(grads[0], "blk", scatter_dimension=0, tiled=True),
        lax.psum_scatter(grads[1], "blk", scatter_dimension=0, tiled=True),
        lax.psum_scatter(grads[2], "blk", scatter_dimension=0, tiled=True),
        lax.psum_scatter(grads[3], "blk", scatter_dimension=0, tiled=True),
        lax.psum_scatter(grads[4], "blk", scatter_dimension=0, tiled=True),
        lax.psum_scatter(grads[5], "blk", scatter_dimension=0, tiled=True),
        lax.psum_scatter(grads[6], "blk", scatter_dimension=0, tiled=True),
        lax.psum_scatter(grads[7], "blk", scatter_dimension=0, tiled=True),
        lax.psum_scatter(grads[8], "blk", scatter_dimension=0, tiled=True),
    )
    shares = lax.psum(
        (
            pieces[0],
            pieces[1],
            pieces[2],
            pieces[3],
            pieces[4],
            pieces[5],
            pieces[6],
            pieces[7],
            pieces[8],
        ),
        "dp",
    )
    return (
        output.reshape(rows, block, width),
        grad_tokens,
        shares[0],
        shares[1],
        shares[2],
        shares[3],
        shares[4],
        shares[5],
        shares[6],
        shares[7],
        shares[8],
    )


BF = jnp.bfloat16
F32 = jnp.float32
MESH = pl.DeviceIdType.MESH
VLIMIT = 60 * 1024 * 1024
TILE = 128
REACH = 511


def mm(a, b):
    return lax.dot_general(a, b, (((1,), (0,)), ((), ())), preferred_element_type=F32)


def mm_nt(a, b):
    return lax.dot_general(a, b, (((1,), (1,)), ((), ())), preferred_element_type=F32)


def mm_tn(a, b):
    return lax.dot_general(a, b, (((0,), (0,)), ((), ())), preferred_element_type=F32)


def iota(shape, dim):
    return lax.broadcasted_iota(jnp.int32, shape, dim)


def spot():
    blk = lax.axis_index("blk")
    return lax.axis_index("dp"), blk // 2, blk % 2


def norm_rows(x, gain):
    x = x.astype(F32)
    scale = lax.rsqrt(jnp.mean(x * x, axis=-1, keepdims=True) + EPS)
    normed = x * scale
    return normed, scale, (normed * gain).astype(BF)


def flip():
    return (iota((TILE, TILE), 0) + iota((TILE, TILE), 1) == TILE - 1).astype(BF)


def flipped(x):
    turn = flip()
    parts = [mm(turn, x[i : i + TILE, :]).astype(BF) for i in range(0, x.shape[0], TILE)]
    return jnp.concatenate(parts, axis=0)


def near_rows(h, d):
    return pl.ds(pl.multiple_of((3 * h + d) * TILE, TILE), TILE)


def prepare_bias(table_ref, near, heads):
    buckets = table_ref.shape[1]
    turn = flip()
    for d in range(3):
        lane = iota((buckets, 2 * TILE), 1)
        back = jnp.where(lane < TILE, lane, lane - 2 * TILE)
        hot = (bucket_of((d - 1) * TILE - back) == iota((buckets, 2 * TILE), 0)).astype(BF)
        strip = mm(table_ref[...], hot)
        for h in range(heads):
            row = jnp.broadcast_to(strip[h : h + 1, :], (TILE, 2 * TILE))
            line = pltpu.roll(row, 0, 1, stride=1, stride_axis=0)[:, :TILE]
            near[near_rows(h, d), :] = mm(line.astype(BF), turn).astype(BF)


class Sums:
    def __init__(self, nz, bufs, s_sem, r_sem):
        self.nz = nz
        self.dp, self.z, self.c = spot()
        self.bufs, self.s_sem, self.r_sem = bufs, s_sem, r_sem
        self.block = bufs["in"]["pb"].shape[-2:]
        x, y = self.dp % 2, self.dp // 2
        c = self.c
        self.f, self.g = 1 + c, 2 - c
        self.s1 = (1 - c) * x + c * y
        self.s2 = (1 - c) * y + c * x
        self.peer1 = self.dp + self.f * (1 - 2 * self.s1)
        self.peer2 = self.dp + self.g * (1 - 2 * self.s2)
        self.bit, self.high = self.z % 2, self.z // 2
        self.near_z = self.z + 1 - 2 * self.bit
        self.far_z = self.z + 2 - 4 * self.high
        away, here = 2 * (1 - self.high), 2 * self.high
        self.order = (away, away + 1, here, here + 1)
        self.table = {}
        self.pending = []

    def copy(self, src, dst, key, dp=None, z=None, c=None):
        n = self.table.setdefault(key, len(self.table))
        dp = self.dp if dp is None else dp
        z = self.z if z is None else z
        c = self.c if c is None else c
        return pltpu.make_async_remote_copy(
            src, dst, self.s_sem.at[n], self.r_sem.at[n], device_id=(dp, 2 * z + c), device_id_type=MESH
        )

    def start(self, src, dst, key, **to):
        op = self.copy(src, dst, key, **to)
        op.start()
        self.pending.append((key, op))

    def drain(self, *head):
        left = []
        for key, op in self.pending:
            if key[: len(head)] == head:
                op.wait_send()
            else:
                left.append((key, op))
        self.pending = left

    def arrived(self, dst, key):
        self.copy(dst, dst, key).wait_recv()

    def part(self, u, name, *at):
        b = self.bufs[u]
        if name == "r1" and "lent" in b:
            rows, cols = self.block
            zz, i2 = at
            row = pl.multiple_of(i2 * rows, rows) if not isinstance(i2, int) else i2 * rows
            return b["lent"].at[pl.ds(zz, 1), pl.ds(row, rows), b["cols"]]
        return b[name].at[(b["h"], *at)]

    def q(self, i1, i2):
        return i1 * self.f + i2 * self.g

    def add(self, dst, a, b):
        dst[...] = (a[...].astype(F32) + b[...].astype(F32)).astype(BF)

    def a_start(self, u, i, q, zz, k):
        self.start(
            self.part(u, "pb", 2 * zz + 1 - self.c, q), self.part(u, "ra", zz, q), (u, "a", i, k), c=1 - self.c
        )

    def a_finish(self, u, i):
        zz = self.order[i]
        for k in range(4):
            self.arrived(self.part(u, "ra", zz, k), (u, "a", i, k))

        def one(q, carry):
            mine = self.part(u, "ra", zz, q)
            self.add(mine, mine, self.part(u, "pb", 2 * zz + self.c, q))
            return carry

        lax.fori_loop(0, 4, one, 0)

    def first_start(self, u, i):
        zz = self.order[i]
        for i2 in range(2):
            self.start(
                self.part(u, "ra", zz, self.q(1 - self.s1, i2)),
                self.part(u, "r1", zz, i2),
                (u, "1", i, i2),
                dp=self.peer1,
            )

    def first_finish(self, u, i):
        zz = self.order[i]
        for i2 in range(2):
            mine = self.part(u, "r1", zz, i2)
            self.arrived(mine, (u, "1", i, i2))
            self.add(mine, mine, self.part(u, "ra", zz, self.q(self.s1, i2)))

    def second_start(self, u, i):
        zz = self.order[i]
        self.start(
            self.part(u, "r1", zz, 1 - self.s2), self.part(u, "r2", zz), (u, "2", i), dp=self.peer2
        )

    def second_finish(self, u, i):
        zz = self.order[i]
        mine = self.part(u, "r2", zz)
        self.arrived(mine, (u, "2", i))
        self.add(mine, mine, self.part(u, "r1", zz, self.s2))

    def near_start(self, u, name, i):
        zz = self.order[2 * i] + 1 - self.bit
        self.start(self.part(u, name, zz), self.part(u, "rz", i), (u, "z", i), z=self.near_z)

    def near_finish(self, u, name, i):
        mine = self.part(u, "rz", i)
        self.arrived(mine, (u, "z", i))
        self.add(mine, mine, self.part(u, name, self.order[2 * i] + self.bit))
        if i == 0:
            self.start(mine, self.part(u, "rz", 2), (u, "z", 2), z=self.far_z)

    def far_last(self, u):
        last = self.part(u, "rz", 2)
        self.arrived(last, (u, "z", 2))
        self.add(self.part(u, "g", self.dp), last, self.part(u, "rz", 1))

    def far_mid(self, u):
        last = self.part(u, "rz", 2)
        self.arrived(last, (u, "z", 2))
        self.add(last, last, self.part(u, "rz", 1))
        self.start(self.part(u, "rz", 2, 1 - self.s2), self.part(u, "r2", 0), (u, "2", 0), dp=self.peer2)

    def second_last_finish(self, u):
        mine = self.part(u, "r2", 0)
        self.arrived(mine, (u, "2", 0))
        self.add(self.part(u, "g", self.dp), mine, self.part(u, "rz", 2, self.s2))

    def spread_two_start(self, u):
        for dp, key in ((self.peer2, "g0"), (self.peer1, "g1")):
            mine = self.part(u, "g", self.dp)
            self.start(mine, mine, (u, key), dp=dp)

    def spread_two_mid(self, u):
        other = self.part(u, "g", self.peer2)
        self.arrived(other, (u, "g0"))
        self.start(other, other, (u, "g2"), dp=self.peer1)

    def spread_two_finish(self, u):
        self.arrived(self.part(u, "g", self.peer1), (u, "g1"))
        self.arrived(self.part(u, "g", self.peer1 + self.peer2 - self.dp), (u, "g2"))

    def spread_start(self, u):
        mine = self.part(u, "g", self.dp)
        for k in range(1, 4):
            self.start(mine, mine, (u, "g", 3 - k), dp=lax.rem(self.dp + k, 4))

    def spread_finish(self, u):
        for k in range(1, 4):
            self.arrived(self.part(u, "g", lax.rem(self.dp + k, 4)), (u, "g", k - 1))


def table_sums(diag, far, heads):
    rows = diag.shape[1]
    total = jnp.zeros((rows, TILE), F32)
    for d in range(3):
        offset = (d - 1) * TILE + iota((2 * TILE, TILE), 0) - (TILE - 1)
        hot = (bucket_of(offset) == iota((2 * TILE, TILE), 1)).astype(F32)
        total = total + lax.dot_general(
            diag[d], hot, (((1,), (0,)), ((), ())),
            preferred_element_type=F32, precision=lax.Precision.HIGHEST,
        )
    lane = iota((rows, TILE), 1)
    for side, b in ((0, 31), (1, 15)):
        total = total + jnp.where(lane == b, jnp.sum(far[side], axis=1, keepdims=True), 0.0)
    return jnp.where(iota((rows, TILE), 0) < heads, total, 0.0)


def key_masks(segall, kaug, zz, c, nkb):
    for h in range(2):
        b = 2 * zz + h
        row = segall[b, pl.ds(c, 1), :]
        r = iota((TILE, TILE), 0)
        hot = jnp.where((r == row) | (r == 8 + b), 1.0, 0.0).astype(F32)
        kaug[pl.ds(pl.multiple_of(b * TILE, TILE), TILE), :] = hot.T.astype(BF)


def query_side(q, segall, table, qa, z, c, nkb):
    tq = q.shape[0]
    lost, right, left = [], [], []
    for i in range(tq // TILE):
        qb = (tq // TILE) * z + i
        row = segall[qb, pl.ds(c, 1), :]
        r = iota((TILE, TILE), 0)
        one = jnp.where((r < 8) & (r != row), NEG, 0.0).astype(F32)
        lost.append(mm(flip(), one.T.astype(BF)))
        col = iota((TILE, TILE), 1) - 8
        ok = (col >= 0) & (col < nkb)
        right.append(jnp.where(ok & (col >= qb + 2), 1.0, 0.0))
        left.append(jnp.where(ok & (col <= qb - 2), 1.0, 0.0))
    low = iota((tq, TILE), 1) < TILE // 2
    for p in range(qa.shape[0]):
        part = q[:, p * TILE : (p + 1) * TILE]
        for hh in range(2):
            h = 2 * p + hh
            rows = slice(hh * tq, (hh + 1) * tq)
            qa[p, rows, 0:TILE] = jnp.where(low if hh == 0 else jnp.logical_not(low), part, 0.0).astype(BF)
            far_r = table[h : h + 1, 31:32].astype(F32)
            far_l = table[h : h + 1, 15:16].astype(F32)
            for i in range(tq // TILE):
                at = hh * tq + i * TILE
                qa[p, at : at + TILE, TILE:] = (lost[i] + far_r * right[i] + far_l * left[i]).astype(BF)


def attend_step(i, zz, z, k, v, kaug, qa, near, probs, stat, s, acc, tq):
    rows = pl.ds(pl.multiple_of(zz * tq, tq), tq)
    blocks = tq // TILE

    def pair(p, carry):
        cols = pl.ds(pl.multiple_of(p * TILE, TILE), TILE)
        s[...] = mm_nt(jnp.concatenate([k[rows, cols], kaug[rows, :]], axis=1), qa[p])
        if i == 0:
            for kk in range(blocks):
                for qq in range(blocks):
                    for hh in range(2):
                        at = hh * tq + qq * TILE
                        spot_ = (slice(kk * TILE, (kk + 1) * TILE), slice(at, at + TILE))
                        s[spot_] = s[spot_] + near[near_rows(2 * p + hh, kk - qq + 1), :].astype(F32)
        else:

            @pl.when(jnp.abs(zz - z) == 1)
            def _():
                after = (zz - z + 1) // 2
                kr = pl.ds(pl.multiple_of((1 - after) * (tq - TILE), TILE), TILE)
                for hh in range(2):
                    qc = pl.ds(pl.multiple_of(hh * tq + after * (tq - TILE), TILE), TILE)
                    s[kr, qc] = s[kr, qc] + near[near_rows(2 * p + hh, 2 * after), :].astype(F32)

        top = jnp.max(s[...], axis=0, keepdims=True)
        if i > 0:
            old = stat[p, 0:1, :]
            top = jnp.maximum(old, top)
        e = jnp.exp(s[...] - top)
        probs[p, rows, :] = e.astype(BF)
        total = jnp.sum(e, axis=0, keepdims=True)
        mixed = mm_tn(v[rows, cols], probs[p, rows, :])
        arows = pl.ds(pl.multiple_of(p * TILE, TILE), TILE)
        if i > 0:
            fade = jnp.exp(old - top)
            total = total + stat[p, 1:2, :] * fade
            mixed = mixed + acc[arows, :] * fade
        acc[arows, :] = mixed
        stat[p, 0:1, :] = top
        stat[p, 1:2, :] = total
        stat[p, 2 + i : 3 + i, :] = top
        return carry

    lax.fori_loop(0, probs.shape[0], pair, 0)


def attn_backward_pair(p, z, nz, qa, k, v, kaug, datt, probs, scale, dq, diag, far, dm, dprob, ds):
    tq = dq.shape[0]
    length = k.shape[0]
    nkb = length // TILE
    cols = slice(p * TILE, (p + 1) * TILE)
    part = datt[p * tq : (p + 1) * tq, :].astype(F32)
    low = iota((tq, TILE), 1) < TILE // 2
    both = jnp.concatenate([jnp.where(low, part, 0.0), jnp.where(low, 0.0, part)], axis=0)
    column = scale[p].T
    total = jnp.zeros((8, 2 * tq), F32)
    for b in range(nz):
        rows = slice(b * tq, (b + 1) * tq)
        scaled = (both * column[:, b : b + 1]).astype(BF)
        dm[b * 2 * tq : (b + 1) * 2 * tq, :] = scaled
        dprob[rows, :] = mm_nt(v[rows, cols], scaled)
        mixed = dprob[rows, :] * probs[p, rows, :].astype(F32)
        total = total + jnp.sum(mixed.reshape(tq // 8, 8, 2 * tq), axis=0)
    center = jnp.sum(total, axis=0, keepdims=True)
    for b in range(nz):
        rows = slice(b * tq, (b + 1) * tq)
        v[rows, cols] = mm(probs[p, rows, :], dm[b * 2 * tq : (b + 1) * 2 * tq, :]).astype(BF)
        shift = center * scale[p, b : b + 1, :]
        ds[TILE + b * tq : TILE + (b + 1) * tq, :] = (
            probs[p, rows, :].astype(F32) * (dprob[rows, :] - shift)
        ).astype(BF)
    left = jnp.concatenate([k[:, cols], kaug[...]], axis=1)
    back = mm_tn(left, ds[TILE : TILE + length, :])
    k[:, cols] = mm(ds[TILE : TILE + length, :], qa[p, :, 0:TILE]).astype(BF)
    both = jnp.concatenate([back[: TILE // 2, :tq], back[TILE // 2 : TILE, tq:]], axis=0)
    dq[:, cols] = both.T.astype(BF)
    sums = back[TILE + 8 : TILE + 8 + nkb, :]
    kb = iota((nkb, 2 * tq), 0)
    lane = iota((nkb, 2 * tq), 1)
    qb = (tq // TILE) * z + (lane % tq) // TILE
    right = jnp.sum(jnp.where(kb >= qb + 2, sums, 0.0), axis=0, keepdims=True)
    left = jnp.sum(jnp.where(kb <= qb - 2, sums, 0.0), axis=0, keepdims=True)
    for hh in range(2):
        h = 2 * p + hh
        far[0, h : h + 1, :] = right[:, hh * tq : (hh + 1) * tq]
        far[1, h : h + 1, :] = left[:, hh * tq : (hh + 1) * tq]
        for d in range(3):
            near_sum = jnp.zeros((TILE, TILE), F32)
            for i in range(tq // TILE):
                row = ((tq // TILE) * z + i + d) * TILE
                at = hh * tq + i * TILE
                near_sum = near_sum + ds[pl.ds(pl.multiple_of(row, TILE), TILE), at : at + TILE].astype(F32)
            wide = jnp.concatenate([near_sum, jnp.zeros((TILE, TILE), F32)], axis=1)
            wide = pltpu.roll(wide, 0, 1, stride=1, stride_axis=0)
            diag[d, h : h + 1, :] = jnp.sum(wide, axis=0, keepdims=True)


def layer_kernel(nz, *refs):
    (tok_h, dy_h, seg, wq_h, wk_h, wv_h, wout_h, win_h, wdown_h, gain_a, gain_f, table_h) = refs[:12]
    o_home, o_grads, o_small = refs[12:15]
    o_out, o_gt = o_home.at[0], o_home.at[1]
    g_down, g_in, g_attn = (o_grads.at[0:2, 4 * i : 4 * i + 4] for i in range(3))
    (
        x, k, v, qa, probs, att, dy, wqkv, wout, wdown, buf_b, pdown, pin,
        ra_d, ra_i, r1_d, r2_d, rz_d, r1_i, r2_i, rz_i, r2_a, rz_a,
        n2, dh, dhl, own_dn1, dprob, ds, near, kaug, diag, far, stat, scale,
        rd, relay, segall, segbuf, table, sm, smr, s_sem, r_sem, l_sem, gs_sem, gr_sem, credit,
    ) = refs[15:]
    both, one, two = pl.ds(0, 2), pl.ds(0, 1), pl.ds(1, 1)
    half = x.shape[2] // 2
    bufs = {
        "down": dict(h=both, pb=pdown, ra=ra_d, r1=r1_d, r2=r2_d, rz=rz_d, g=g_down),
        "in": dict(h=both, pb=pin, ra=ra_i, r1=r1_i, r2=r2_i, rz=rz_i, g=g_in),
        "attn0": dict(h=one, pb=pdown, ra=ra_d, r2=r2_a, rz=rz_a, g=g_attn, lent=wdown, cols=slice(0, half)),
        "attn1": dict(h=two, pb=pdown, ra=ra_d, r2=r2_a, rz=rz_a, g=g_attn, lent=wdown, cols=slice(half, 2 * half)),
    }
    eng = Sums(nz, bufs, s_sem, r_sem)
    dp, z, c = eng.dp, eng.z, eng.c
    blk = 2 * z + c
    nb, block, width = x.shape
    tq = 2 * block
    length = nb * block
    nkb = length // TILE
    share = width // nb
    steps = buf_b.shape[0]
    per = nb // steps
    pairs = probs.shape[0]
    heads = 2 * pairs
    barrier = pltpu.get_barrier_semaphore()
    peers = [(dp, lax.rem(blk + i, nb)) for i in range(1, nb)]
    peers += [(eng.peer1, blk), (eng.peer2, blk), (eng.peer1 + eng.peer2 - dp, blk)]
    for peer in peers:
        pl.semaphore_signal(barrier, inc=1, device_id=peer, device_id_type=MESH)

    loads = {}

    def load(name, src, dst):
        loads[name] = pltpu.make_async_copy(src, dst, l_sem.at[len(loads)])
        loads[name].start()

    def ready(*names):
        for name in names:
            loads[name].wait()

    load("x", tok_h.at[c], x.at[blk])
    load("table", table_h, table)
    load("wk", wk_h, wqkv.at[1])
    load("wv", wv_h, wqkv.at[2])
    load("wq", wq_h, wqkv.at[0])

    def gcopy(src, dst, send, recv, zz, cc):
        return pltpu.make_async_remote_copy(
            src, dst, gs_sem.at[send], gr_sem.at[recv], device_id=(dp, 2 * zz + cc), device_id_type=MESH
        )

    def inside(other):
        return (other >= 0) & (other < nz)

    segbuf[...] = jnp.zeros_like(segbuf)
    segbuf[0:2, :] = seg[...]
    segall[blk] = segbuf[...]
    pl.semaphore_wait(barrier, len(peers))

    ways = ((0, 1), (1, -1))
    mine = x.at[blk]
    gcopy(tok_h.at[1 - c], mine, 4, blk, z, 1 - c).start()
    for i in range(1, nb):
        pltpu.make_async_remote_copy(
            segbuf, segall.at[blk], gs_sem.at[10 + i], gr_sem.at[nb + 1 + blk],
            device_id=(dp, lax.rem(blk + i, nb)), device_id_type=MESH,
        ).start()
    for way, dz in ways:

        @pl.when(inside(z + dz))
        def _():
            gcopy(tok_h.at[1 - c], mine, 2 * way, blk, z + dz, 1 - c).start()
            gcopy(tok_h.at[c], mine, 2 * way + 1, blk, z + dz, c).start()

    gcopy(dy_h.at[1 - c], dy.at[c], 5, nb, z, 1 - c).start()
    load("dy", dy_h.at[c], dy.at[c])
    load("wout", wout_h, wout)
    for j in range(steps):
        jj = eng.order[j]
        load(("win", j), win_h.at[:, pl.ds(pl.multiple_of(jj * width, width), width)], buf_b.at[jj])
        load(("wdown", j), wdown_h.at[jj], wdown.at[jj])

    ready("table")
    prepare_bias(table, near, heads)
    reach = -(-REACH // tq)
    for zz in range(nz):

        @pl.when(jnp.abs(zz - z) > reach)
        def _():
            rows = slice(zz * tq, (zz + 1) * tq)
            x[2 * zz : 2 * zz + 2] = jnp.zeros((2, block, width), BF)
            for ref in (k, v):
                ref[rows, :] = jnp.zeros((tq, width), BF)
            kaug[rows, :] = jnp.zeros((tq, TILE), BF)
            for p in range(pairs):
                probs[p, rows, :] = jnp.zeros((tq, 2 * tq), BF)

    ds[0:TILE, :] = jnp.zeros((TILE, ds.shape[1]), BF)
    ds[ds.shape[0] - TILE :, :] = jnp.zeros((TILE, ds.shape[1]), BF)
    diag[...] = jnp.zeros_like(diag)
    far[...] = jnp.zeros_like(far)
    scale[...] = jnp.zeros_like(scale)
    sm[0] = jnp.zeros(sm.shape[1:], F32)
    gain1, gain2 = gain_a[...].reshape(1, width).astype(F32), gain_f[...].reshape(1, width).astype(F32)

    def x_arrived(b):
        gcopy(x.at[b], x.at[b], 0, b, z, 1 - c).wait_recv()

    def seg_arrived(b):
        gcopy(segbuf, segall.at[b], 0, nb + 1 + b, z, 1 - c).wait_recv()

    def keys_of(zz):
        rows = pl.ds(pl.multiple_of(zz * tq, tq), tq)
        key_masks(segall, kaug, zz, c, nkb)
        n1 = norm_rows(x[pl.ds(2 * zz, 2)].reshape(tq, width), gain1)[2]
        k[rows, :] = mm(n1, wqkv[1]).astype(BF)
        v[rows, :] = mm(n1, wqkv[2]).astype(BF)
        return n1

    s_blk, acc = dprob.at[0:tq], dprob.at[tq : tq + pairs * TILE]
    ready("x", "wk", "wv", "wq")
    x_arrived(2 * z + 1 - c)
    seg_arrived(2 * z + 1 - c)
    q_rev = mm(flipped(keys_of(z)), wqkv[0]).astype(BF).astype(F32)
    query_side(q_rev, segall, table, qa, z, c, nkb)
    order = (z, eng.near_z, 2 - eng.high, 3 - 3 * eng.high)
    wide = width // 2
    attend_step(0, order[0], z, k, v, kaug, qa, near, probs, stat, s_blk, acc, tq)
    for way, dz in ways:
        src = z - dz

        @pl.when(inside(src))
        def _():
            for h in range(2):
                x_arrived(2 * src + h)

                @pl.when(inside(z + dz))
                def _():
                    gcopy(
                        x.at[2 * src + h], x.at[2 * src + h], 6 + 2 * way + h, 2 * src + h, z + dz, c
                    ).start()

    for i in range(1, nb):
        other = lax.rem(blk + i, nb)

        @pl.when(other // 2 != z)
        def _():
            seg_arrived(other)

    for i in range(1, 4):
        zz = order[i]

        @pl.when(jnp.abs(zz - z) <= reach)
        def _():
            @pl.when(jnp.abs(zz - z) == 2)
            def _():
                for h in range(2):
                    x_arrived(2 * zz + h)

            keys_of(zz)
            attend_step(i, zz, z, k, v, kaug, qa, near, probs, stat, s_blk, acc, tq)

    for p in range(pairs):
        inverse = 1.0 / stat[p, 1:2, :]
        top = stat[p, 0:1, :]
        for i in range(4):

            @pl.when(jnp.abs(order[i] - z) <= reach)
            def _():
                scale[p, pl.ds(order[i], 1), :] = jnp.exp(stat[p, 2 + i : 3 + i, :] - top) * inverse

        mixed = acc[p * TILE : (p + 1) * TILE, :] * inverse
        both = jnp.concatenate([mixed[: TILE // 2, :tq], mixed[TILE // 2 :, tq:]], axis=0)
        att[:, p * TILE : (p + 1) * TILE] = both.T.astype(BF)
    att[...] = flipped(att[...])

    ready("wout")
    x_own = x.at[pl.ds(2 * z, 2)]
    dh[...] = x_own[...].reshape(tq, width).astype(F32) + mm(att[...], wout[...])
    n2[...] = norm_rows(dh[...], gain2)[2]
    ready("dy")
    gcopy(dy.at[0], dy.at[1 - c], 0, nb, z, 1 - c).wait_recv()
    total = own_dn1
    for j in range(steps):
        jj = eng.order[j]
        ready(("win", j), ("wdown", j))
        value, slant = gelu_both(mm(n2[...], buf_b[jj]))
        act = value.astype(BF)
        d = dy[...].reshape(tq, width)
        grad = mm_tn(act, d).astype(BF)
        for hh in range(2):
            part = grad[:, hh * wide : (hh + 1) * wide]
            pdown[hh, pl.ds(jj * per, per)] = part.reshape(per, 4, share, wide)
        for qq in range(4):
            eng.a_start("down", j, qq, jj, qq)
        if j > 1:
            eng.a_finish("down", j - 1)
            eng.first_start("down", j - 1)
        dpre = (mm_nt(d, wdown[jj]) * slant).astype(BF)
        grad = mm_tn(n2[...], dpre).astype(BF)
        for hh in range(2):
            part = grad[:, hh * wide : (hh + 1) * wide]
            pin[hh, :, jj] = part.reshape(nb, share, wide)
        for i in range(nz):
            eng.a_start("in", i, jj, eng.order[i], j)
        if j == 0:
            total[...] = mm(act, wdown[jj])
            dn2 = mm_nt(dpre, buf_b[jj])
        else:
            total[...] += mm(act, wdown[jj])
            dn2 = dn2 + mm_nt(dpre, buf_b[jj])
        if j == 0:
            eng.a_finish("down", 0)
            eng.first_start("down", 0)
    eng.a_finish("down", steps - 1)
    eng.first_start("down", steps - 1)
    h = dh[...]
    n2[...] = (h + total[...]).astype(BF)
    normed, r2, _ = norm_rows(h, gain2)
    back, gain_grad = rms_backward(dn2, normed, r2, gain2)
    lines = width // TILE
    for i in range(lines):
        sm[0, lines + i : lines + i + 1, :] = gain_grad[None, i * TILE : (i + 1) * TILE]
    dh[...] = dy[...].reshape(tq, width).astype(F32) + back
    dhl[...] = dh[...].astype(BF)
    back = flipped(mm_nt(dhl[...], wout[...]).astype(BF))
    datt, dm = near.at[0 : pairs * tq], near.at[pairs * tq : pairs * tq + nz * 2 * tq]
    for p in range(pairs):
        datt[p * tq : (p + 1) * tq, :] = back[:, p * TILE : (p + 1) * TILE]
    for i in range(nz):
        eng.a_finish("in", i)
    out_half = [n2.at[pl.ds(pl.multiple_of(i * block, block), block)] for i in (c, 1 - c)]
    eng.start(out_half[1], o_out.at[c], ("out",), c=1 - c)
    load("kept", out_half[0], o_out.at[c])

    def first_near(u, i):
        for ii in (2 * i, 2 * i + 1):
            eng.first_finish(u, ii)
        eng.near_start(u, "r1", i)

    def first_second(u, i):
        for ii in (2 * i, 2 * i + 1):
            eng.first_finish(u, ii)
            eng.second_start(u, ii)

    def second_near(u, i):
        for ii in (2 * i, 2 * i + 1):
            eng.second_finish(u, ii)
        eng.near_start(u, "r2", i)

    first_near("down", 0)
    eng.drain("down", "a")
    for hh in range(2):
        grad = mm_tn(att[...], dhl[:, hh * wide : (hh + 1) * wide]).astype(BF)
        pdown[hh, :, 3] = grad.reshape(nb, share, wide)
    dq = dhl
    for b in range(nz):
        buf_b[b, tq : 2 * tq] = norm_rows(x[2 * b : 2 * b + 2].reshape(tq, width), gain1)[2]

    def weights(part):
        cols = slice(part * wide, (part + 1) * wide)
        dq[:, cols] = flipped(dq[:, cols])
        for i, ref in ((1, k), (2, v)):
            grad = sum(
                mm_tn(buf_b[b, tq : 2 * tq], ref[b * tq : (b + 1) * tq, cols]) for b in range(nz)
            )
            pdown[part, :, i] = grad.astype(BF).reshape(nb, share, wide)
        pdown[part, :, 0] = mm_tn(buf_b[z, tq : 2 * tq], dq[:, cols]).astype(BF).reshape(nb, share, wide)

    def a_start_all(u):
        for i in range(nz):
            for qq in range(4):
                eng.a_start(u, i, qq, eng.order[i], qq)

    for p in range(pairs):
        attn_backward_pair(
            p, z, nz, qa, k, v, kaug, datt, probs, scale, dq, diag, far, dm, dprob, ds
        )
        if p == 0:
            eng.first_start("in", 0)
            eng.first_start("in", 1)
        if p == 2:
            eng.first_start("in", 2)
            eng.first_start("in", 3)
            weights(0)
            first_near("down", 1)
            eng.near_finish("down", "r1", 0)
            eng.drain("down", "1")
            pl.semaphore_signal(credit, inc=1, device_id=(dp, 2 * z + 1 - c), device_id_type=MESH)
        if p == 3:
            pl.semaphore_wait(credit, 1)
            a_start_all("attn0")
        if p == 4:
            first_second("in", 0)
            for i in range(nz):
                eng.a_finish("attn0", i)
                eng.first_start("attn0", i)

    for b in range(nz):
        rows = slice(b * tq, (b + 1) * tq)
        part = mm_nt(k[rows, :], wqkv[1]) + mm_nt(v[rows, :], wqkv[2])
        buf_b[b, 0:tq] = part.astype(BF)
    for way, dz in ways:

        @pl.when(inside(z + 2 * dz))
        def _():
            eng.copy(buf_b.at[z + 2 * dz, 0:tq], relay.at[way], ("d1", way), z=z + dz).start()

    weights(1)
    a_start_all("attn1")
    first_second("in", 1)
    for i in range(nz):
        eng.a_finish("attn1", i)
        eng.first_start("attn1", i)
    eng.near_finish("down", "r1", 1)
    second_near("in", 0)

    hops = (
        dict(c=1 - c), dict(dp=dp + 1 - 2 * (dp % 2)), dict(dp=dp + 2 - 4 * (dp // 2)),
        dict(z=eng.near_z), dict(z=eng.far_z),
    )

    def small_start(i):
        eng.start(sm.at[i], smr.at[i], ("s", i), **hops[i])

    def small_finish(i):
        eng.copy(sm.at[i], smr.at[i], ("s", i), **hops[i]).wait_recv()
        sm[i + 1] = sm[i] + smr[i]

    first_second("attn0", 0)
    first_second("attn0", 1)
    eng.far_mid("down")
    for way, dz in ways:

        @pl.when(inside(z - dz) & inside(z + dz))
        def _():
            eng.copy(relay.at[way], relay.at[way], ("d1", way)).wait_recv()
            buf_b[z + dz, 0:tq] = (buf_b[z + dz, 0:tq].astype(F32) + relay[way].astype(F32)).astype(BF)

        @pl.when(inside(z + dz))
        def _():
            eng.copy(buf_b.at[z + dz, 0:tq], rd.at[way], ("d2", way), z=z + dz).start()

    own_dn1[...] = mm_nt(dq[...], wqkv[0])
    own_normed = norm_rows(x_own[...].reshape(tq, width), gain1)[0]
    gain_sum = jnp.sum(own_dn1[...] * own_normed, axis=0, keepdims=True)
    for b in range(nz):
        rows = slice(b * tq, (b + 1) * tq)
        part = mm_nt(k[rows, :], wqkv[1]) + mm_nt(v[rows, :], wqkv[2])
        normed = norm_rows(x[2 * b : 2 * b + 2].reshape(tq, width), gain1)[0]
        gain_sum = gain_sum + jnp.sum(part * normed, axis=0, keepdims=True)

        @pl.when(z == b)
        def _():
            own_dn1[...] += part

    for i in range(lines):
        sm[0, i : i + 1, :] = gain_sum[:, i * TILE : (i + 1) * TILE]
    sm[0, 2 * lines :, :] = table_sums(diag, far, heads)[: sm.shape[1] - 2 * lines]
    small_start(0)
    eng.near_finish("in", "r2", 0)
    second_near("in", 1)
    small_finish(0)
    small_start(1)
    first_second("attn1", 0)
    second_near("attn0", 0)
    first_second("attn1", 1)
    eng.second_last_finish("down")
    eng.spread_two_start("down")
    small_finish(1)
    small_start(2)
    second_near("attn0", 1)
    eng.near_finish("in", "r2", 1)
    eng.near_finish("attn0", "r2", 0)
    eng.far_last("in")
    eng.spread_two_start("in")
    second_near("attn1", 0)
    eng.spread_two_mid("down")
    small_finish(2)
    small_start(3)
    second_near("attn1", 1)
    eng.near_finish("attn0", "r2", 1)
    eng.near_finish("attn1", "r2", 0)
    eng.far_last("attn0")
    eng.spread_start("attn0")
    eng.spread_two_mid("in")
    eng.near_finish("attn1", "r2", 1)
    small_finish(3)
    small_start(4)

    dn1 = own_dn1
    for way, dz in ways:

        @pl.when(inside(z - dz))
        def _():
            eng.copy(rd.at[way], rd.at[way], ("d2", way)).wait_recv()
            dn1[...] += rd[way].astype(F32)

    normed, r1, _ = norm_rows(x_own[...].reshape(tq, width), gain1)
    back, _ = rms_backward(dn1[...], normed, r1, gain1)
    dy[...] = (dh[...] + back).astype(BF).reshape(dy.shape)
    eng.start(dy.at[1 - c], o_gt.at[c], ("gt",), c=1 - c)
    load("kept_gt", dy.at[c], o_gt.at[c])

    eng.far_last("attn1")
    eng.spread_start("attn1")
    small_finish(4)
    o_small[...] = sm[5]
    eng.copy(dy.at[0], o_out.at[1 - c], ("out",)).wait_recv()
    eng.copy(dy.at[0], o_gt.at[1 - c], ("gt",)).wait_recv()
    ready("kept", "kept_gt")
    eng.spread_two_finish("down")
    eng.spread_two_finish("in")
    eng.spread_finish("attn0")
    eng.spread_finish("attn1")
    eng.drain()
    gcopy(tok_h.at[0], mine, 4, blk, z, 1 - c).wait_send()
    gcopy(dy_h.at[0], dy.at[0], 5, nb, z, 1 - c).wait_send()
    for i in range(1, nb):
        gcopy(segbuf, segall.at[0], 10 + i, nb + 1, z, 1 - c).wait_send()
    for way, dz in ways:

        @pl.when(inside(z + dz))
        def _():
            gcopy(tok_h.at[0], mine, 2 * way, blk, z, 1 - c).wait_send()
            gcopy(tok_h.at[0], mine, 2 * way + 1, blk, z, 1 - c).wait_send()
            eng.copy(buf_b.at[0, 0:tq], rd.at[way], ("d2", way)).wait_send()

        @pl.when(inside(z + 2 * dz))
        def _():
            eng.copy(buf_b.at[0, 0:tq], relay.at[way], ("d1", way)).wait_send()

        @pl.when(inside(z - dz) & inside(z + dz))
        def _():
            for h in range(2):
                gcopy(tok_h.at[0], mine, 6 + 2 * way + h, blk, z, 1 - c).wait_send()


def layer(nz, tok, dy, seg, wq, wk, wv, wout, win, wdown, gain_a, gain_f, table):
    _, block, width = tok.shape
    nb = 2 * nz
    length, tq = nb * block, 2 * block
    share = width // nb
    pairs = table.shape[0] // 2
    steps = win.shape[1] // width
    vm = pl.BlockSpec(memory_space=pltpu.VMEM)
    hbm = pl.BlockSpec(memory_space=pl.ANY)
    home = jax.ShapeDtypeStruct((2, 2, block, width), BF)
    grads = jax.ShapeDtypeStruct((2, 12, share, width // 2), BF)
    one = (share, width // 2)
    small = (24, TILE)

    def bf(*shape):
        return pltpu.VMEM(shape, BF)

    def f32(*shape):
        return pltpu.VMEM(shape, F32)

    sums = [bf(2, nz, 4, *one), bf(2, nz, 4, *one)]
    for i, route in enumerate(("xzy", "xyz", "xyz")):
        last = route == "xyz"
        sums += [bf(2, nz, 2, *one)] if i < 2 else []
        sums += [bf(2, nz if last else 1, *one), bf(2, 3, *one) if last else bf(2, 3, 2, *one)]
    scratch = [
        bf(nb, block, width), bf(length, width), bf(length, width),
        bf(pairs, 2 * tq, 2 * TILE), bf(pairs, length, 2 * tq), bf(tq, width),
        bf(2, block, width), bf(3, width, width), bf(width, width),
        bf(steps, width, width), bf(steps, width, width), bf(2, nb, 4, *one), bf(2, nb, 4, *one),
        *sums,
        bf(tq, width), f32(tq, width), bf(tq, width), f32(tq, width),
        f32(length, 2 * tq), bf(length + 2 * TILE, 2 * tq), bf(max(2 * pairs * 3 * TILE, pairs * tq + nz * 2 * tq), TILE), bf(length, TILE),
        f32(3, 16, 2 * TILE), f32(2, 16, tq), f32(pairs, 8, 2 * tq), f32(pairs, 8, 2 * tq),
        bf(2, tq, width), bf(2, tq, width),
        pltpu.VMEM((nb, 8, block), jnp.int32), pltpu.VMEM((8, block), jnp.int32), bf(*table.shape),
        f32(6, *small), f32(5, *small),
        pltpu.SemaphoreType.DMA((180,)), pltpu.SemaphoreType.DMA((180,)), pltpu.SemaphoreType.DMA((32,)),
        pltpu.SemaphoreType.DMA((10 + nb,)), pltpu.SemaphoreType.DMA((2 * nb + 2,)),
        pltpu.SemaphoreType.REGULAR,
    ]
    return pl.pallas_call(
        functools.partial(layer_kernel, nz),
        out_shape=(home, grads, jax.ShapeDtypeStruct(small, F32)),
        in_specs=[hbm, hbm, vm] + [hbm] * 6 + [vm, vm, hbm],
        out_specs=(vm,) * 3,
        scratch_shapes=scratch,
        compiler_params=pltpu.CompilerParams(
            collective_id=1, has_side_effects=True, vmem_limit_bytes=64 * 1024 * 1024
        ),
    )(tok, dy, seg, wq, wk, wv, wout, win, wdown, gain_a, gain_f, table)


def finish_kernel(home, grads, small, o_out, o_gt, o_ga, o_q, o_k, o_v, o_o, o_gf, o_in, o_down, o_gt_table):
    share, wide = grads.shape[2:]
    width = 2 * wide
    lines = width // TILE
    blk = lax.axis_index("blk")
    o_out[...] = home[0]
    o_gt[...] = home[1]
    for hh in range(2):
        cols = slice(hh * wide, (hh + 1) * wide)
        for i in range(4):
            o_down[i * share : (i + 1) * share, cols] = grads[hh, i].astype(F32)
            at = i * width + hh * wide
            o_in[:, at : at + wide] = grads[hh, 4 + i].astype(F32)
        for i, ref in enumerate((o_q, o_k, o_v, o_o)):
            ref[:, cols] = grads[hh, 8 + i].astype(F32)

    def mine(first, count, each):
        flat = jnp.concatenate([small[first + i : first + i + 1, :] for i in range(count)], axis=1)
        flat = jnp.broadcast_to(flat, (8, count * TILE))
        return pltpu.roll(flat, lax.rem(count * TILE - blk * each, count * TILE), 1)[0:1, :each]

    o_ga[...] = mine(0, lines, share).reshape(share)
    o_gf[...] = mine(lines, lines, share).reshape(share)
    per, heads = o_gt_table.shape
    table = small[2 * lines : 2 * lines + 16, :] if small.shape[0] >= 2 * lines + 16 else jnp.concatenate(
        [small[2 * lines :, :], jnp.zeros((16 - (small.shape[0] - 2 * lines), TILE), F32)], axis=0
    )
    turned = pltpu.roll(table, lax.rem(TILE - blk * per, TILE), 1).T
    o_gt_table[...] = turned[:per, :heads]


def finish(home, grads, small, heads, nb):
    _, _, block, width = home.shape
    share = width // nb
    vm = pl.BlockSpec(memory_space=pltpu.VMEM)
    one = jax.ShapeDtypeStruct((share, width), F32)
    gain = jax.ShapeDtypeStruct((share,), F32)
    own = jax.ShapeDtypeStruct((2, block, width), BF)
    return pl.pallas_call(
        finish_kernel,
        out_shape=(
            own, own, gain, one, one, one, one, gain,
            jax.ShapeDtypeStruct((share, 4 * width), F32),
            jax.ShapeDtypeStruct((4 * share, width), F32),
            jax.ShapeDtypeStruct((32 // nb, heads), F32),
        ),
        in_specs=[vm] * 3,
        out_specs=(vm,) * 11,
    )(home, grads, small)


def fast_device(
    nz, tokens, segment_ids, gain_attn, w_query, w_key, w_value, w_out, gain_ffn, w_in, w_down,
    rel_table, cotangent,
):
    width = tokens.shape[2]
    home, grads, small = layer(
        nz, tokens, cotangent, segment_ids, w_query, w_key, w_value, w_out, w_in,
        w_down.reshape(-1, width, width), gain_attn, gain_ffn, rel_table.T,
    )
    return finish(home, grads, small, rel_table.shape[1], 2 * nz)


def pick(mesh):
    if mesh.shape["dp"] == 4 and mesh.shape["blk"] == 8:
        return functools.partial(fast_device, mesh.shape["blk"] // 2)
    return on_device


def solution(mesh):
    placed = (
        P("dp", "blk", None),
        P("dp", "blk"),
        P(),
        P(),
        P(),
        P(),
        P(),
        P(),
        P(),
        P(),
        P(),
        P("dp", "blk", None),
    )
    return jax.shard_map(
        pick(mesh),
        mesh=mesh,
        in_specs=placed,
        out_specs=(
            P("dp", "blk", None),
            P("dp", "blk", None),
            P("blk"),
            P("blk", None),
            P("blk", None),
            P("blk", None),
            P("blk", None),
            P("blk"),
            P("blk", None),
            P("blk", None),
            P("blk", None),
        ),
        check_vma=False,
    )
```

```python
import functools
import math

import jax
import jax.numpy as jnp
from jax import lax
from jax.experimental import pallas as pl
from jax.experimental.pallas import tpu as pltpu
from jax.sharding import PartitionSpec as P

EPS = 1e-06
NEG = -1e30
EDGES = (12, 16, 23, 32, 46, 64, 91)
ROOT_TWO_PI = 0.7978845608028654
CUBIC = 0.044715


def bucket_of(offset):
    distance = jnp.abs(offset)
    far_part = 8 + sum(((distance >= edge).astype(jnp.int32) for edge in EDGES))
    return jnp.where(offset > 0, 16, 0) + jnp.where(distance < 8, distance, far_part)


def gelu_both(values):
    inner_arg = ROOT_TWO_PI * (values + CUBIC * values * values * values)
    tangent = jnp.tanh(inner_arg)
    result = 0.5 * values * (1.0 + tangent)
    slope = 0.5 * (1.0 + tangent) + 0.5 * values * (1.0 - tangent * tangent) * ROOT_TWO_PI * (
        1.0 + 3.0 * CUBIC * values * values
    )
    return (result, slope)


def rms_forward(values, gain):
    scale = lax.rsqrt(jnp.mean(values * values, axis=-1, keepdims=True) + EPS)
    normed = values * scale
    return (normed, scale, (normed * gain).astype(jnp.bfloat16))


def rms_backward(grad, normed, scale, gain):
    gain_grad = jnp.sum(grad * normed, axis=0)
    inner_grad = grad * gain
    back = scale * (inner_grad - normed * jnp.mean(inner_grad * normed, axis=-1, keepdims=True))
    return (back, gain_grad)


def outer_sum(left, right):
    return jnp.einsum("td,tf->df", left, right, preferred_element_type=jnp.float32)


def times_t(left, right):
    return jnp.einsum("tf,df->td", left, right, preferred_element_type=jnp.float32)


def masked_scores(query, keys, bias, seg_query, seg_keys):
    raw = (
        jnp.einsum("bqhd,bkhd->bhqk", query, keys, preferred_element_type=jnp.float32) + bias[None]
    )
    same = seg_query[:, None, :, None] == seg_keys[:, None, None, :]
    return jnp.where(same, raw, NEG)


def score_grads(q_part, k_part, v_part, bias, sq_part, sk_part, total, d_mixed):
    scores = masked_scores(q_part, k_part, bias, sq_part, sk_part)
    probs = jnp.exp(scores - total[..., None])
    grad_probs = jnp.einsum("bqhd,bkhd->bhqk", d_mixed, v_part, preferred_element_type=jnp.float32)
    return (probs, grad_probs)


def on_device(
    tokens,
    segment_ids,
    gain_attn,
    w_query,
    w_key,
    w_value,
    w_out,
    gain_ffn,
    w_in,
    w_down,
    rel_table,
    cotangent,
):
    rows, block, width = tokens.shape
    buckets, heads = rel_table.shape
    inner = w_query.shape[1]
    head_dim = inner // heads
    length = block * lax.axis_size("blk")
    group = math.gcd(rows, max(1, 512 // block))
    blocks = rows // group
    gain_one = gain_attn.astype(jnp.float32)
    gain_two = gain_ffn.astype(jnp.float32)
    table_f = rel_table.astype(jnp.float32)
    flat = tokens.reshape(rows * block, width).astype(jnp.float32)
    normed_one, scale_one, low_one = rms_forward(flat, gain_one)

    def project(weight):
        return (
            jnp.dot(low_one, weight, preferred_element_type=jnp.float32)
            .astype(jnp.bfloat16)
            .reshape(rows, block, inner)
        )

    query, keys, values = (project(w_query), project(w_key), project(w_value))
    key_all, value_all, seg_all = (
        lax.all_gather(keys, "blk", axis=1, tiled=True),
        lax.all_gather(values, "blk", axis=1, tiled=True),
        lax.all_gather(segment_ids, "blk", axis=1, tiled=True),
    )
    places = lax.axis_index("blk") * block + jnp.arange(block, dtype=jnp.int32)
    offsets = jnp.arange(length, dtype=jnp.int32)[None, :] - places[:, None]
    onehot = (
        bucket_of(offsets)[None] == jnp.arange(buckets, dtype=jnp.int32)[:, None, None]
    ).astype(jnp.float32)
    bias = jnp.einsum("nqk,nh->hqk", onehot, table_f, precision=lax.Precision.HIGHEST)
    q_groups = query.reshape(blocks, group, block, heads, head_dim)
    seg_query = segment_ids.reshape(blocks, group, block)

    def key_groups(key_rows, value_rows, seg_rows):
        return (
            key_rows.reshape(blocks, group, length, heads, head_dim),
            value_rows.reshape(blocks, group, length, heads, head_dim),
            seg_rows.reshape(blocks, group, length),
        )

    k_groups, v_groups, seg_keys = key_groups(key_all, value_all, seg_all)

    def attend(parts):
        q_part, k_part, v_part, sq_part, sk_part = parts
        scores = masked_scores(q_part, k_part, bias, sq_part, sk_part)
        top = jnp.max(scores, axis=-1, keepdims=True)
        total = jnp.log(jnp.sum(jnp.exp(scores - top), axis=-1, keepdims=True)) + top
        probs = jnp.exp(scores - total).astype(jnp.bfloat16)
        mixed = jnp.einsum("bhqk,bkhd->bqhd", probs, v_part, preferred_element_type=jnp.float32)
        return (mixed.astype(jnp.bfloat16), total[..., 0])

    attended, log_totals = lax.map(attend, (q_groups, k_groups, v_groups, seg_query, seg_keys))
    attended_flat = attended.reshape(rows * block, inner)
    hidden = flat + jnp.dot(attended_flat, w_out, preferred_element_type=jnp.float32)
    normed_two, scale_two, low_two = rms_forward(hidden, gain_two)
    pre = jnp.dot(low_two, w_in, preferred_element_type=jnp.float32)
    gelu_value, gelu_slope = gelu_both(pre)
    active = gelu_value.astype(jnp.bfloat16)
    output = (hidden + jnp.dot(active, w_down, preferred_element_type=jnp.float32)).astype(
        jnp.bfloat16
    )
    grad_out = cotangent.reshape(rows * block, width)
    grad_down = outer_sum(active, grad_out)
    grad_pre = (times_t(grad_out, w_down) * gelu_slope).astype(jnp.bfloat16)
    grad_in = outer_sum(low_two, grad_pre)
    back_two, grad_gain_two = rms_backward(times_t(grad_pre, w_in), normed_two, scale_two, gain_two)
    grad_hidden = grad_out.astype(jnp.float32) + back_two
    grad_proj = grad_hidden.astype(jnp.bfloat16)
    grad_wout = outer_sum(attended_flat, grad_proj)
    grad_att = (
        times_t(grad_proj, w_out)
        .astype(jnp.bfloat16)
        .reshape(blocks, group, block, heads, head_dim)
    )
    key_back, value_back, seg_back = (
        lax.all_gather(keys, "blk", axis=1, tiled=True),
        lax.all_gather(values, "blk", axis=1, tiled=True),
        lax.all_gather(segment_ids, "blk", axis=1, tiled=True),
    )
    k_back, v_back, sk_back = key_groups(key_back, value_back, seg_back)
    start = jnp.zeros((heads, block, length), jnp.float32)

    def attend_back(carry, parts):
        q_part, k_part, v_part, sq_part, sk_part, total, d_mixed = parts
        probs, grad_probs = score_grads(
            q_part, k_part, v_part, bias, sq_part, sk_part, total, d_mixed
        )
        center = jnp.sum(probs * grad_probs, axis=-1, keepdims=True)
        grad_scores = (probs * (grad_probs - center)).astype(jnp.bfloat16)
        grad_q = jnp.einsum(
            "bhqk,bkhd->bqhd", grad_scores, k_part, preferred_element_type=jnp.float32
        ).astype(jnp.bfloat16)
        grad_k = jnp.einsum(
            "bhqk,bqhd->bkhd", grad_scores, q_part, preferred_element_type=jnp.float32
        )
        grad_v = jnp.einsum(
            "bhqk,bqhd->bkhd",
            probs.astype(jnp.bfloat16),
            d_mixed,
            preferred_element_type=jnp.float32,
        )
        paired = jnp.stack([grad_k, grad_v], axis=2).reshape(group, length, 2, inner)
        return (carry + jnp.sum(grad_scores.astype(jnp.float32), axis=0), (grad_q, paired))

    bias_grad, (grad_query, paired) = lax.scan(
        attend_back, start, (q_groups, k_back, v_back, seg_query, sk_back, log_totals, grad_att)
    )
    paired = paired.reshape(rows, length, 2, inner)
    kv_grad = lax.psum_scatter(paired, "blk", scatter_dimension=1, tiled=True).astype(jnp.bfloat16)
    grad_key = kv_grad[:, :, 0].reshape(rows * block, inner)
    grad_value = kv_grad[:, :, 1].reshape(rows * block, inner)
    grad_query = grad_query.reshape(rows * block, inner)
    grad_wq = outer_sum(low_one, grad_query)
    grad_wk = outer_sum(low_one, grad_key)
    grad_wv = outer_sum(low_one, grad_value)
    grad_low_one = (
        times_t(grad_query, w_query) + times_t(grad_key, w_key) + times_t(grad_value, w_value)
    )
    back_one, grad_gain_one = rms_backward(grad_low_one, normed_one, scale_one, gain_one)
    grad_tokens = (grad_hidden + back_one).astype(jnp.bfloat16).reshape(rows, block, width)
    grad_table = jnp.einsum("hqk,nqk->nh", bias_grad, onehot, precision=lax.Precision.HIGHEST)
    grads = (
        grad_gain_one,
        grad_wq,
        grad_wk,
        grad_wv,
        grad_wout,
        grad_gain_two,
        grad_in,
        grad_down,
        grad_table,
    )
    pieces = (
        lax.psum_scatter(grads[0], "blk", scatter_dimension=0, tiled=True),
        lax.psum_scatter(grads[1], "blk", scatter_dimension=0, tiled=True),
        lax.psum_scatter(grads[2], "blk", scatter_dimension=0, tiled=True),
        lax.psum_scatter(grads[3], "blk", scatter_dimension=0, tiled=True),
        lax.psum_scatter(grads[4], "blk", scatter_dimension=0, tiled=True),
        lax.psum_scatter(grads[5], "blk", scatter_dimension=0, tiled=True),
        lax.psum_scatter(grads[6], "blk", scatter_dimension=0, tiled=True),
        lax.psum_scatter(grads[7], "blk", scatter_dimension=0, tiled=True),
        lax.psum_scatter(grads[8], "blk", scatter_dimension=0, tiled=True),
    )
    shares = lax.psum(
        (
            pieces[0],
            pieces[1],
            pieces[2],
            pieces[3],
            pieces[4],
            pieces[5],
            pieces[6],
            pieces[7],
            pieces[8],
        ),
        "dp",
    )
    return (
        output.reshape(rows, block, width),
        grad_tokens,
        shares[0],
        shares[1],
        shares[2],
        shares[3],
        shares[4],
        shares[5],
        shares[6],
        shares[7],
        shares[8],
    )


BF = jnp.bfloat16
F32 = jnp.float32
MESH = pl.DeviceIdType.MESH
VLIMIT = 60 * 1024 * 1024
TILE = 128
REACH = 511


def mm(a, b):
    return lax.dot_general(a, b, (((1,), (0,)), ((), ())), preferred_element_type=F32)


def mm_nt(a, b):
    return lax.dot_general(a, b, (((1,), (1,)), ((), ())), preferred_element_type=F32)


def mm_tn(a, b):
    return lax.dot_general(a, b, (((0,), (0,)), ((), ())), preferred_element_type=F32)


def iota(shape, dim):
    return lax.broadcasted_iota(jnp.int32, shape, dim)


def spot():
    blk = lax.axis_index("blk")
    return lax.axis_index("dp"), blk // 2, blk % 2


def norm_rows(x, gain):
    x = x.astype(F32)
    scale = lax.rsqrt(jnp.mean(x * x, axis=-1, keepdims=True) + EPS)
    normed = x * scale
    return normed, scale, (normed * gain).astype(BF)


def flip():
    return (iota((TILE, TILE), 0) + iota((TILE, TILE), 1) == TILE - 1).astype(BF)


def flipped(x):
    turn = flip()
    parts = [mm(turn, x[i : i + TILE, :]).astype(BF) for i in range(0, x.shape[0], TILE)]
    return jnp.concatenate(parts, axis=0)


def near_rows(h, d):
    return pl.ds(pl.multiple_of((3 * h + d) * TILE, TILE), TILE)


def prepare_bias(table_ref, near, heads):
    buckets = table_ref.shape[1]
    turn = flip()
    for d in range(3):
        lane = iota((buckets, 2 * TILE), 1)
        back = jnp.where(lane < TILE, lane, lane - 2 * TILE)
        hot = (bucket_of((d - 1) * TILE - back) == iota((buckets, 2 * TILE), 0)).astype(BF)
        strip = mm(table_ref[...], hot)
        for h in range(heads):
            row = jnp.broadcast_to(strip[h : h + 1, :], (TILE, 2 * TILE))
            line = pltpu.roll(row, 0, 1, stride=1, stride_axis=0)[:, :TILE]
            near[near_rows(h, d), :] = mm(line.astype(BF), turn).astype(BF)


class Sums:
    def __init__(self, nz, bufs, s_sem, r_sem):
        self.nz = nz
        self.dp, self.z, self.c = spot()
        self.bufs, self.s_sem, self.r_sem = bufs, s_sem, r_sem
        self.block = bufs["in"]["pb"].shape[-2:]
        x, y = self.dp % 2, self.dp // 2
        c = self.c
        self.f, self.g = 1 + c, 2 - c
        self.s1 = (1 - c) * x + c * y
        self.s2 = (1 - c) * y + c * x
        self.peer1 = self.dp + self.f * (1 - 2 * self.s1)
        self.peer2 = self.dp + self.g * (1 - 2 * self.s2)
        self.bit, self.high = self.z % 2, self.z // 2
        self.near_z = self.z + 1 - 2 * self.bit
        self.far_z = self.z + 2 - 4 * self.high
        away, here = 2 * (1 - self.high), 2 * self.high
        self.order = (away, away + 1, here, here + 1)
        self.table = {}
        self.pending = []

    def copy(self, src, dst, key, dp=None, z=None, c=None):
        n = self.table.setdefault(key, len(self.table))
        dp = self.dp if dp is None else dp
        z = self.z if z is None else z
        c = self.c if c is None else c
        return pltpu.make_async_remote_copy(
            src, dst, self.s_sem.at[n], self.r_sem.at[n], device_id=(dp, 2 * z + c), device_id_type=MESH
        )

    def start(self, src, dst, key, **to):
        op = self.copy(src, dst, key, **to)
        op.start()
        self.pending.append((key, op))

    def drain(self, *head):
        left = []
        for key, op in self.pending:
            if key[: len(head)] == head:
                op.wait_send()
            else:
                left.append((key, op))
        self.pending = left

    def arrived(self, dst, key):
        self.copy(dst, dst, key).wait_recv()

    def part(self, u, name, *at):
        b = self.bufs[u]
        if name == "r1" and "lent" in b:
            rows, cols = self.block
            zz, i2 = at
            row = pl.multiple_of(i2 * rows, rows) if not isinstance(i2, int) else i2 * rows
            return b["lent"].at[pl.ds(zz, 1), pl.ds(row, rows), b["cols"]]
        return b[name].at[(b["h"], *at)]

    def q(self, i1, i2):
        return i1 * self.f + i2 * self.g

    def add(self, dst, a, b):
        dst[...] = (a[...].astype(F32) + b[...].astype(F32)).astype(BF)

    def a_start(self, u, i, q, zz, k):
        self.start(
            self.part(u, "pb", 2 * zz + 1 - self.c, q), self.part(u, "ra", zz, q), (u, "a", i, k), c=1 - self.c
        )

    def a_finish(self, u, i):
        zz = self.order[i]
        for k in range(4):
            self.arrived(self.part(u, "ra", zz, k), (u, "a", i, k))

        def one(q, carry):
            mine = self.part(u, "ra", zz, q)
            self.add(mine, mine, self.part(u, "pb", 2 * zz + self.c, q))
            return carry

        lax.fori_loop(0, 4, one, 0)

    def first_start(self, u, i):
        zz = self.order[i]
        for i2 in range(2):
            self.start(
                self.part(u, "ra", zz, self.q(1 - self.s1, i2)),
                self.part(u, "r1", zz, i2),
                (u, "1", i, i2),
                dp=self.peer1,
            )

    def first_finish(self, u, i):
        zz = self.order[i]
        for i2 in range(2):
            mine = self.part(u, "r1", zz, i2)
            self.arrived(mine, (u, "1", i, i2))
            self.add(mine, mine, self.part(u, "ra", zz, self.q(self.s1, i2)))

    def second_start(self, u, i):
        zz = self.order[i]
        self.start(
            self.part(u, "r1", zz, 1 - self.s2), self.part(u, "r2", zz), (u, "2", i), dp=self.peer2
        )

    def second_finish(self, u, i):
        zz = self.order[i]
        mine = self.part(u, "r2", zz)
        self.arrived(mine, (u, "2", i))
        self.add(mine, mine, self.part(u, "r1", zz, self.s2))

    def near_start(self, u, name, i):
        zz = self.order[2 * i] + 1 - self.bit
        self.start(self.part(u, name, zz), self.part(u, "rz", i), (u, "z", i), z=self.near_z)

    def near_finish(self, u, name, i):
        mine = self.part(u, "rz", i)
        self.arrived(mine, (u, "z", i))
        self.add(mine, mine, self.part(u, name, self.order[2 * i] + self.bit))
        if i == 0:
            self.start(mine, self.part(u, "rz", 2), (u, "z", 2), z=self.far_z)

    def far_last(self, u):
        last = self.part(u, "rz", 2)
        self.arrived(last, (u, "z", 2))
        self.add(self.part(u, "g", self.dp), last, self.part(u, "rz", 1))

    def far_mid(self, u):
        last = self.part(u, "rz", 2)
        self.arrived(last, (u, "z", 2))
        self.add(last, last, self.part(u, "rz", 1))
        self.start(self.part(u, "rz", 2, 1 - self.s2), self.part(u, "r2", 0), (u, "2", 0), dp=self.peer2)

    def second_last_finish(self, u):
        mine = self.part(u, "r2", 0)
        self.arrived(mine, (u, "2", 0))
        self.add(self.part(u, "g", self.dp), mine, self.part(u, "rz", 2, self.s2))

    def spread_two_start(self, u):
        for dp, key in ((self.peer2, "g0"), (self.peer1, "g1")):
            mine = self.part(u, "g", self.dp)
            self.start(mine, mine, (u, key), dp=dp)

    def spread_two_mid(self, u):
        other = self.part(u, "g", self.peer2)
        self.arrived(other, (u, "g0"))
        self.start(other, other, (u, "g2"), dp=self.peer1)

    def spread_two_finish(self, u):
        self.arrived(self.part(u, "g", self.peer1), (u, "g1"))
        self.arrived(self.part(u, "g", self.peer1 + self.peer2 - self.dp), (u, "g2"))

    def spread_start(self, u):
        mine = self.part(u, "g", self.dp)
        for k in range(1, 4):
            self.start(mine, mine, (u, "g", 3 - k), dp=lax.rem(self.dp + k, 4))

    def spread_finish(self, u):
        for k in range(1, 4):
            self.arrived(self.part(u, "g", lax.rem(self.dp + k, 4)), (u, "g", k - 1))


def table_sums(diag, far, heads):
    rows = diag.shape[1]
    total = jnp.zeros((rows, TILE), F32)
    for d in range(3):
        offset = (d - 1) * TILE + iota((2 * TILE, TILE), 0) - (TILE - 1)
        hot = (bucket_of(offset) == iota((2 * TILE, TILE), 1)).astype(F32)
        total = total + lax.dot_general(
            diag[d], hot, (((1,), (0,)), ((), ())),
            preferred_element_type=F32, precision=lax.Precision.HIGHEST,
        )
    lane = iota((rows, TILE), 1)
    for side, b in ((0, 31), (1, 15)):
        total = total + jnp.where(lane == b, jnp.sum(far[side], axis=1, keepdims=True), 0.0)
    return jnp.where(iota((rows, TILE), 0) < heads, total, 0.0)


def key_masks(segall, kaug, zz, c, nkb):
    for h in range(2):
        b = 2 * zz + h
        row = segall[b, pl.ds(c, 1), :]
        r = iota((TILE, TILE), 0)
        hot = jnp.where((r == row) | (r == 8 + b), 1.0, 0.0).astype(F32)
        kaug[pl.ds(pl.multiple_of(b * TILE, TILE), TILE), :] = hot.T.astype(BF)


def query_side(q, segall, table, qa, z, c, nkb):
    tq = q.shape[0]
    lost, right, left = [], [], []
    for i in range(tq // TILE):
        qb = (tq // TILE) * z + i
        row = segall[qb, pl.ds(c, 1), :]
        r = iota((TILE, TILE), 0)
        one = jnp.where((r < 8) & (r != row), NEG, 0.0).astype(F32)
        lost.append(mm(flip(), one.T.astype(BF)))
        col = iota((TILE, TILE), 1) - 8
        ok = (col >= 0) & (col < nkb)
        right.append(jnp.where(ok & (col >= qb + 2), 1.0, 0.0))
        left.append(jnp.where(ok & (col <= qb - 2), 1.0, 0.0))
    low = iota((tq, TILE), 1) < TILE // 2
    for p in range(qa.shape[0]):
        part = q[:, p * TILE : (p + 1) * TILE]
        for hh in range(2):
            h = 2 * p + hh
            rows = slice(hh * tq, (hh + 1) * tq)
            qa[p, rows, 0:TILE] = jnp.where(low if hh == 0 else jnp.logical_not(low), part, 0.0).astype(BF)
            far_r = table[h : h + 1, 31:32].astype(F32)
            far_l = table[h : h + 1, 15:16].astype(F32)
            for i in range(tq // TILE):
                at = hh * tq + i * TILE
                qa[p, at : at + TILE, TILE:] = (lost[i] + far_r * right[i] + far_l * left[i]).astype(BF)


def attend_step(i, zz, z, k, v, kaug, qa, near, probs, stat, s, acc, tq):
    rows = pl.ds(pl.multiple_of(zz * tq, tq), tq)
    blocks = tq // TILE

    def pair(p, carry):
        cols = pl.ds(pl.multiple_of(p * TILE, TILE), TILE)
        s[...] = mm_nt(jnp.concatenate([k[rows, cols], kaug[rows, :]], axis=1), qa[p])
        if i == 0:
            for kk in range(blocks):
                for qq in range(blocks):
                    for hh in range(2):
                        at = hh * tq + qq * TILE
                        spot_ = (slice(kk * TILE, (kk + 1) * TILE), slice(at, at + TILE))
                        s[spot_] = s[spot_] + near[near_rows(2 * p + hh, kk - qq + 1), :].astype(F32)
        else:

            @pl.when(jnp.abs(zz - z) == 1)
            def _():
                after = (zz - z + 1) // 2
                kr = pl.ds(pl.multiple_of((1 - after) * (tq - TILE), TILE), TILE)
                for hh in range(2):
                    qc = pl.ds(pl.multiple_of(hh * tq + after * (tq - TILE), TILE), TILE)
                    s[kr, qc] = s[kr, qc] + near[near_rows(2 * p + hh, 2 * after), :].astype(F32)

        top = jnp.max(s[...], axis=0, keepdims=True)
        if i > 0:
            old = stat[p, 0:1, :]
            top = jnp.maximum(old, top)
        e = jnp.exp(s[...] - top)
        probs[p, rows, :] = e.astype(BF)
        total = jnp.sum(e, axis=0, keepdims=True)
        mixed = mm_tn(v[rows, cols], probs[p, rows, :])
        arows = pl.ds(pl.multiple_of(p * TILE, TILE), TILE)
        if i > 0:
            fade = jnp.exp(old - top)
            total = total + stat[p, 1:2, :] * fade
            mixed = mixed + acc[arows, :] * fade
        acc[arows, :] = mixed
        stat[p, 0:1, :] = top
        stat[p, 1:2, :] = total
        stat[p, 2 + i : 3 + i, :] = top
        return carry

    lax.fori_loop(0, probs.shape[0], pair, 0)


def attn_backward_pair(p, z, nz, qa, k, v, kaug, datt, probs, scale, dq, diag, far, dm, dprob, ds):
    tq = dq.shape[0]
    length = k.shape[0]
    nkb = length // TILE
    cols = slice(p * TILE, (p + 1) * TILE)
    part = datt[p * tq : (p + 1) * tq, :].astype(F32)
    low = iota((tq, TILE), 1) < TILE // 2
    both = jnp.concatenate([jnp.where(low, part, 0.0), jnp.where(low, 0.0, part)], axis=0)
    column = scale[p].T
    total = jnp.zeros((8, 2 * tq), F32)
    for b in range(nz):
        rows = slice(b * tq, (b + 1) * tq)
        scaled = (both * column[:, b : b + 1]).astype(BF)
        dm[b * 2 * tq : (b + 1) * 2 * tq, :] = scaled
        dprob[rows, :] = mm_nt(v[rows, cols], scaled)
        mixed = dprob[rows, :] * probs[p, rows, :].astype(F32)
        total = total + jnp.sum(mixed.reshape(tq // 8, 8, 2 * tq), axis=0)
    center = jnp.sum(total, axis=0, keepdims=True)
    for b in range(nz):
        rows = slice(b * tq, (b + 1) * tq)
        v[rows, cols] = mm(probs[p, rows, :], dm[b * 2 * tq : (b + 1) * 2 * tq, :]).astype(BF)
        shift = center * scale[p, b : b + 1, :]
        ds[TILE + b * tq : TILE + (b + 1) * tq, :] = (
            probs[p, rows, :].astype(F32) * (dprob[rows, :] - shift)
        ).astype(BF)
    left = jnp.concatenate([k[:, cols], kaug[...]], axis=1)
    back = mm_tn(left, ds[TILE : TILE + length, :])
    k[:, cols] = mm(ds[TILE : TILE + length, :], qa[p, :, 0:TILE]).astype(BF)
    both = jnp.concatenate([back[: TILE // 2, :tq], back[TILE // 2 : TILE, tq:]], axis=0)
    dq[:, cols] = both.T.astype(BF)
    sums = back[TILE + 8 : TILE + 8 + nkb, :]
    kb = iota((nkb, 2 * tq), 0)
    lane = iota((nkb, 2 * tq), 1)
    qb = (tq // TILE) * z + (lane % tq) // TILE
    right = jnp.sum(jnp.where(kb >= qb + 2, sums, 0.0), axis=0, keepdims=True)
    left = jnp.sum(jnp.where(kb <= qb - 2, sums, 0.0), axis=0, keepdims=True)
    for hh in range(2):
        h = 2 * p + hh
        far[0, h : h + 1, :] = right[:, hh * tq : (hh + 1) * tq]
        far[1, h : h + 1, :] = left[:, hh * tq : (hh + 1) * tq]
        for d in range(3):
            near_sum = jnp.zeros((TILE, TILE), F32)
            for i in range(tq // TILE):
                row = ((tq // TILE) * z + i + d) * TILE
                at = hh * tq + i * TILE
                near_sum = near_sum + ds[pl.ds(pl.multiple_of(row, TILE), TILE), at : at + TILE].astype(F32)
            wide = jnp.concatenate([near_sum, jnp.zeros((TILE, TILE), F32)], axis=1)
            wide = pltpu.roll(wide, 0, 1, stride=1, stride_axis=0)
            diag[d, h : h + 1, :] = jnp.sum(wide, axis=0, keepdims=True)


def layer_kernel(nz, *refs):
    (tok_h, dy_h, seg, wq_h, wk_h, wv_h, wout_h, win_h, wdown_h, gain_a, gain_f, table_h) = refs[:12]
    o_home, o_grads, o_small = refs[12:15]
    o_out, o_gt = o_home.at[0], o_home.at[1]
    g_down, g_in, g_attn = (o_grads.at[0:2, 4 * i : 4 * i + 4] for i in range(3))
    (
        x, k, v, qa, probs, att, dy, wqkv, wout, wdown, buf_b, pdown, pin,
        ra_d, ra_i, r1_d, r2_d, rz_d, r1_i, r2_i, rz_i, r2_a, rz_a,
        n2, dh, dhl, own_dn1, dprob, ds, near, kaug, diag, far, stat, scale,
        rd, relay, segall, segbuf, table, sm, smr, s_sem, r_sem, l_sem, gs_sem, gr_sem, credit,
    ) = refs[15:]
    both, one, two = pl.ds(0, 2), pl.ds(0, 1), pl.ds(1, 1)
    half = x.shape[2] // 2
    bufs = {
        "down": dict(h=both, pb=pdown, ra=ra_d, r1=r1_d, r2=r2_d, rz=rz_d, g=g_down),
        "in": dict(h=both, pb=pin, ra=ra_i, r1=r1_i, r2=r2_i, rz=rz_i, g=g_in),
        "attn0": dict(h=one, pb=pdown, ra=ra_d, r2=r2_a, rz=rz_a, g=g_attn, lent=wdown, cols=slice(0, half)),
        "attn1": dict(h=two, pb=pdown, ra=ra_d, r2=r2_a, rz=rz_a, g=g_attn, lent=wdown, cols=slice(half, 2 * half)),
    }
    eng = Sums(nz, bufs, s_sem, r_sem)
    dp, z, c = eng.dp, eng.z, eng.c
    blk = 2 * z + c
    nb, block, width = x.shape
    tq = 2 * block
    length = nb * block
    nkb = length // TILE
    share = width // nb
    steps = buf_b.shape[0]
    per = nb // steps
    pairs = probs.shape[0]
    heads = 2 * pairs
    barrier = pltpu.get_barrier_semaphore()
    peers = [(dp, lax.rem(blk + i, nb)) for i in range(1, nb)]
    peers += [(eng.peer1, blk), (eng.peer2, blk), (eng.peer1 + eng.peer2 - dp, blk)]
    for peer in peers:
        pl.semaphore_signal(barrier, inc=1, device_id=peer, device_id_type=MESH)

    loads = {}

    def load(name, src, dst):
        loads[name] = pltpu.make_async_copy(src, dst, l_sem.at[len(loads)])
        loads[name].start()

    def ready(*names):
        for name in names:
            loads[name].wait()

    load("x", tok_h.at[c], x.at[blk])
    load("table", table_h, table)
    load("wk", wk_h, wqkv.at[1])
    load("wv", wv_h, wqkv.at[2])
    load("wq", wq_h, wqkv.at[0])

    def gcopy(src, dst, send, recv, zz, cc):
        return pltpu.make_async_remote_copy(
            src, dst, gs_sem.at[send], gr_sem.at[recv], device_id=(dp, 2 * zz + cc), device_id_type=MESH
        )

    def inside(other):
        return (other >= 0) & (other < nz)

    segbuf[...] = jnp.zeros_like(segbuf)
    segbuf[0:2, :] = seg[...]
    segall[blk] = segbuf[...]
    pl.semaphore_wait(barrier, len(peers))

    ways = ((0, 1), (1, -1))
    mine = x.at[blk]
    gcopy(tok_h.at[1 - c], mine, 4, blk, z, 1 - c).start()
    for i in range(1, nb):
        pltpu.make_async_remote_copy(
            segbuf, segall.at[blk], gs_sem.at[10 + i], gr_sem.at[nb + 1 + blk],
            device_id=(dp, lax.rem(blk + i, nb)), device_id_type=MESH,
        ).start()
    for way, dz in ways:

        @pl.when(inside(z + dz))
        def _():
            gcopy(tok_h.at[1 - c], mine, 2 * way, blk, z + dz, 1 - c).start()
            gcopy(tok_h.at[c], mine, 2 * way + 1, blk, z + dz, c).start()

    gcopy(dy_h.at[1 - c], dy.at[c], 5, nb, z, 1 - c).start()
    load("dy", dy_h.at[c], dy.at[c])
    load("wout", wout_h, wout)
    for j in range(steps):
        jj = eng.order[j]
        load(("win", j), win_h.at[:, pl.ds(pl.multiple_of(jj * width, width), width)], buf_b.at[jj])
        load(("wdown", j), wdown_h.at[jj], wdown.at[jj])

    ready("table")
    prepare_bias(table, near, heads)
    reach = -(-REACH // tq)
    for zz in range(nz):

        @pl.when(jnp.abs(zz - z) > reach)
        def _():
            rows = slice(zz * tq, (zz + 1) * tq)
            x[2 * zz : 2 * zz + 2] = jnp.zeros((2, block, width), BF)
            for ref in (k, v):
                ref[rows, :] = jnp.zeros((tq, width), BF)
            kaug[rows, :] = jnp.zeros((tq, TILE), BF)
            for p in range(pairs):
                probs[p, rows, :] = jnp.zeros((tq, 2 * tq), BF)

    ds[0:TILE, :] = jnp.zeros((TILE, ds.shape[1]), BF)
    ds[ds.shape[0] - TILE :, :] = jnp.zeros((TILE, ds.shape[1]), BF)
    diag[...] = jnp.zeros_like(diag)
    far[...] = jnp.zeros_like(far)
    scale[...] = jnp.zeros_like(scale)
    sm[0] = jnp.zeros(sm.shape[1:], F32)
    gain1, gain2 = gain_a[...].reshape(1, width).astype(F32), gain_f[...].reshape(1, width).astype(F32)

    def x_arrived(b):
        gcopy(x.at[b], x.at[b], 0, b, z, 1 - c).wait_recv()

    def seg_arrived(b):
        gcopy(segbuf, segall.at[b], 0, nb + 1 + b, z, 1 - c).wait_recv()

    def keys_of(zz):
        rows = pl.ds(pl.multiple_of(zz * tq, tq), tq)
        key_masks(segall, kaug, zz, c, nkb)
        n1 = norm_rows(x[pl.ds(2 * zz, 2)].reshape(tq, width), gain1)[2]
        k[rows, :] = mm(n1, wqkv[1]).astype(BF)
        v[rows, :] = mm(n1, wqkv[2]).astype(BF)
        return n1

    s_blk, acc = dprob.at[0:tq], dprob.at[tq : tq + pairs * TILE]
    ready("x", "wk", "wv", "wq")
    x_arrived(2 * z + 1 - c)
    seg_arrived(2 * z + 1 - c)
    q_rev = mm(flipped(keys_of(z)), wqkv[0]).astype(BF).astype(F32)
    query_side(q_rev, segall, table, qa, z, c, nkb)
    order = (z, eng.near_z, 2 - eng.high, 3 - 3 * eng.high)
    wide = width // 2
    attend_step(0, order[0], z, k, v, kaug, qa, near, probs, stat, s_blk, acc, tq)
    for way, dz in ways:
        src = z - dz

        @pl.when(inside(src))
        def _():
            for h in range(2):
                x_arrived(2 * src + h)

                @pl.when(inside(z + dz))
                def _():
                    gcopy(
                        x.at[2 * src + h], x.at[2 * src + h], 6 + 2 * way + h, 2 * src + h, z + dz, c
                    ).start()

    for i in range(1, nb):
        other = lax.rem(blk + i, nb)

        @pl.when(other // 2 != z)
        def _():
            seg_arrived(other)

    for i in range(1, 4):
        zz = order[i]

        @pl.when(jnp.abs(zz - z) <= reach)
        def _():
            @pl.when(jnp.abs(zz - z) == 2)
            def _():
                for h in range(2):
                    x_arrived(2 * zz + h)

            keys_of(zz)
            attend_step(i, zz, z, k, v, kaug, qa, near, probs, stat, s_blk, acc, tq)

    for p in range(pairs):
        inverse = 1.0 / stat[p, 1:2, :]
        top = stat[p, 0:1, :]
        for i in range(4):

            @pl.when(jnp.abs(order[i] - z) <= reach)
            def _():
                scale[p, pl.ds(order[i], 1), :] = jnp.exp(stat[p, 2 + i : 3 + i, :] - top) * inverse

        mixed = acc[p * TILE : (p + 1) * TILE, :] * inverse
        both = jnp.concatenate([mixed[: TILE // 2, :tq], mixed[TILE // 2 :, tq:]], axis=0)
        att[:, p * TILE : (p + 1) * TILE] = both.T.astype(BF)
    att[...] = flipped(att[...])

    ready("wout")
    x_own = x.at[pl.ds(2 * z, 2)]
    dh[...] = x_own[...].reshape(tq, width).astype(F32) + mm(att[...], wout[...])
    n2[...] = norm_rows(dh[...], gain2)[2]
    ready("dy")
    gcopy(dy.at[0], dy.at[1 - c], 0, nb, z, 1 - c).wait_recv()
    total = own_dn1
    for j in range(steps):
        jj = eng.order[j]
        ready(("win", j), ("wdown", j))
        value, slant = gelu_both(mm(n2[...], buf_b[jj]))
        act = value.astype(BF)
        d = dy[...].reshape(tq, width)
        grad = mm_tn(act, d).astype(BF)
        for hh in range(2):
            part = grad[:, hh * wide : (hh + 1) * wide]
            pdown[hh, pl.ds(jj * per, per)] = part.reshape(per, 4, share, wide)
        for qq in range(4):
            eng.a_start("down", j, qq, jj, qq)
        if j > 1:
            eng.a_finish("down", j - 1)
            eng.first_start("down", j - 1)
        dpre = (mm_nt(d, wdown[jj]) * slant).astype(BF)
        grad = mm_tn(n2[...], dpre).astype(BF)
        for hh in range(2):
            part = grad[:, hh * wide : (hh + 1) * wide]
            pin[hh, :, jj] = part.reshape(nb, share, wide)
        for i in range(nz):
            eng.a_start("in", i, jj, eng.order[i], j)
        if j == 0:
            total[...] = mm(act, wdown[jj])
            dn2 = mm_nt(dpre, buf_b[jj])
        else:
            total[...] += mm(act, wdown[jj])
            dn2 = dn2 + mm_nt(dpre, buf_b[jj])
        if j == 0:
            eng.a_finish("down", 0)
            eng.first_start("down", 0)
    eng.a_finish("down", steps - 1)
    eng.first_start("down", steps - 1)
    h = dh[...]
    n2[...] = (h + total[...]).astype(BF)
    normed, r2, _ = norm_rows(h, gain2)
    back, gain_grad = rms_backward(dn2, normed, r2, gain2)
    lines = width // TILE
    for i in range(lines):
        sm[0, lines + i : lines + i + 1, :] = gain_grad[None, i * TILE : (i + 1) * TILE]
    dh[...] = dy[...].reshape(tq, width).astype(F32) + back
    dhl[...] = dh[...].astype(BF)
    back = flipped(mm_nt(dhl[...], wout[...]).astype(BF))
    datt, dm = near.at[0 : pairs * tq], near.at[pairs * tq : pairs * tq + nz * 2 * tq]
    for p in range(pairs):
        datt[p * tq : (p + 1) * tq, :] = back[:, p * TILE : (p + 1) * TILE]
    for i in range(nz):
        eng.a_finish("in", i)
    out_half = [n2.at[pl.ds(pl.multiple_of(i * block, block), block)] for i in (c, 1 - c)]
    eng.start(out_half[1], o_out.at[c], ("out",), c=1 - c)
    load("kept", out_half[0], o_out.at[c])

    def first_near(u, i):
        for ii in (2 * i, 2 * i + 1):
            eng.first_finish(u, ii)
        eng.near_start(u, "r1", i)

    def first_second(u, i):
        for ii in (2 * i, 2 * i + 1):
            eng.first_finish(u, ii)
            eng.second_start(u, ii)

    def second_near(u, i):
        for ii in (2 * i, 2 * i + 1):
            eng.second_finish(u, ii)
        eng.near_start(u, "r2", i)

    first_near("down", 0)
    eng.drain("down", "a")
    for hh in range(2):
        grad = mm_tn(att[...], dhl[:, hh * wide : (hh + 1) * wide]).astype(BF)
        pdown[hh, :, 3] = grad.reshape(nb, share, wide)
    dq = dhl
    for b in range(nz):
        buf_b[b, tq : 2 * tq] = norm_rows(x[2 * b : 2 * b + 2].reshape(tq, width), gain1)[2]

    def weights(part):
        cols = slice(part * wide, (part + 1) * wide)
        dq[:, cols] = flipped(dq[:, cols])
        for i, ref in ((1, k), (2, v)):
            grad = sum(
                mm_tn(buf_b[b, tq : 2 * tq], ref[b * tq : (b + 1) * tq, cols]) for b in range(nz)
            )
            pdown[part, :, i] = grad.astype(BF).reshape(nb, share, wide)
        pdown[part, :, 0] = mm_tn(buf_b[z, tq : 2 * tq], dq[:, cols]).astype(BF).reshape(nb, share, wide)

    def a_start_all(u):
        for i in range(nz):
            for qq in range(4):
                eng.a_start(u, i, qq, eng.order[i], qq)

    for p in range(pairs):
        attn_backward_pair(
            p, z, nz, qa, k, v, kaug, datt, probs, scale, dq, diag, far, dm, dprob, ds
        )
        if p == 0:
            eng.first_start("in", 0)
            eng.first_start("in", 1)
        if p == 2:
            eng.first_start("in", 2)
            eng.first_start("in", 3)
            weights(0)
            first_near("down", 1)
            eng.near_finish("down", "r1", 0)
            eng.drain("down", "1")
            pl.semaphore_signal(credit, inc=1, device_id=(dp, 2 * z + 1 - c), device_id_type=MESH)
        if p == 3:
            pl.semaphore_wait(credit, 1)
            a_start_all("attn0")
        if p == 4:
            first_second("in", 0)
            for i in range(nz):
                eng.a_finish("attn0", i)
                eng.first_start("attn0", i)

    for b in range(nz):
        rows = slice(b * tq, (b + 1) * tq)
        part = mm_nt(k[rows, :], wqkv[1]) + mm_nt(v[rows, :], wqkv[2])
        buf_b[b, 0:tq] = part.astype(BF)
    for way, dz in ways:

        @pl.when(inside(z + 2 * dz))
        def _():
            eng.copy(buf_b.at[z + 2 * dz, 0:tq], relay.at[way], ("d1", way), z=z + dz).start()

    weights(1)
    a_start_all("attn1")
    first_second("in", 1)
    for i in range(nz):
        eng.a_finish("attn1", i)
        eng.first_start("attn1", i)
    eng.near_finish("down", "r1", 1)
    second_near("in", 0)

    hops = (
        dict(c=1 - c), dict(dp=dp + 1 - 2 * (dp % 2)), dict(dp=dp + 2 - 4 * (dp // 2)),
        dict(z=eng.near_z), dict(z=eng.far_z),
    )

    def small_start(i):
        eng.start(sm.at[i], smr.at[i], ("s", i), **hops[i])

    def small_finish(i):
        eng.copy(sm.at[i], smr.at[i], ("s", i), **hops[i]).wait_recv()
        sm[i + 1] = sm[i] + smr[i]

    first_second("attn0", 0)
    first_second("attn0", 1)
    eng.far_mid("down")
    for way, dz in ways:

        @pl.when(inside(z - dz) & inside(z + dz))
        def _():
            eng.copy(relay.at[way], relay.at[way], ("d1", way)).wait_recv()
            buf_b[z + dz, 0:tq] = (buf_b[z + dz, 0:tq].astype(F32) + relay[way].astype(F32)).astype(BF)

        @pl.when(inside(z + dz))
        def _():
            eng.copy(buf_b.at[z + dz, 0:tq], rd.at[way], ("d2", way), z=z + dz).start()

    own_dn1[...] = mm_nt(dq[...], wqkv[0])
    own_normed = norm_rows(x_own[...].reshape(tq, width), gain1)[0]
    gain_sum = jnp.sum(own_dn1[...] * own_normed, axis=0, keepdims=True)
    for b in range(nz):
        rows = slice(b * tq, (b + 1) * tq)
        part = mm_nt(k[rows, :], wqkv[1]) + mm_nt(v[rows, :], wqkv[2])
        normed = norm_rows(x[2 * b : 2 * b + 2].reshape(tq, width), gain1)[0]
        gain_sum = gain_sum + jnp.sum(part * normed, axis=0, keepdims=True)

        @pl.when(z == b)
        def _():
            own_dn1[...] += part

    for i in range(lines):
        sm[0, i : i + 1, :] = gain_sum[:, i * TILE : (i + 1) * TILE]
    sm[0, 2 * lines :, :] = table_sums(diag, far, heads)[: sm.shape[1] - 2 * lines]
    small_start(0)
    eng.near_finish("in", "r2", 0)
    second_near("in", 1)
    small_finish(0)
    small_start(1)
    first_second("attn1", 0)
    second_near("attn0", 0)
    first_second("attn1", 1)
    eng.second_last_finish("down")
    eng.spread_two_start("down")
    small_finish(1)
    small_start(2)
    second_near("attn0", 1)
    eng.near_finish("in", "r2", 1)
    eng.near_finish("attn0", "r2", 0)
    eng.far_last("in")
    eng.spread_two_start("in")
    second_near("attn1", 0)
    eng.spread_two_mid("down")
    small_finish(2)
    small_start(3)
    second_near("attn1", 1)
    eng.near_finish("attn0", "r2", 1)
    eng.near_finish("attn1", "r2", 0)
    eng.far_last("attn0")
    eng.spread_start("attn0")
    eng.spread_two_mid("in")
    eng.near_finish("attn1", "r2", 1)
    small_finish(3)
    small_start(4)

    dn1 = own_dn1
    for way, dz in ways:

        @pl.when(inside(z - dz))
        def _():
            eng.copy(rd.at[way], rd.at[way], ("d2", way)).wait_recv()
            dn1[...] += rd[way].astype(F32)

    normed, r1, _ = norm_rows(x_own[...].reshape(tq, width), gain1)
    back, _ = rms_backward(dn1[...], normed, r1, gain1)
    dy[...] = (dh[...] + back).astype(BF).reshape(dy.shape)
    eng.start(dy.at[1 - c], o_gt.at[c], ("gt",), c=1 - c)
    load("kept_gt", dy.at[c], o_gt.at[c])

    eng.far_last("attn1")
    eng.spread_start("attn1")
    small_finish(4)
    o_small[...] = sm[5]
    eng.copy(dy.at[0], o_out.at[1 - c], ("out",)).wait_recv()
    eng.copy(dy.at[0], o_gt.at[1 - c], ("gt",)).wait_recv()
    ready("kept", "kept_gt")
    eng.spread_two_finish("down")
    eng.spread_two_finish("in")
    eng.spread_finish("attn0")
    eng.spread_finish("attn1")
    eng.drain()
    gcopy(tok_h.at[0], mine, 4, blk, z, 1 - c).wait_send()
    gcopy(dy_h.at[0], dy.at[0], 5, nb, z, 1 - c).wait_send()
    for i in range(1, nb):
        gcopy(segbuf, segall.at[0], 10 + i, nb + 1, z, 1 - c).wait_send()
    for way, dz in ways:

        @pl.when(inside(z + dz))
        def _():
            gcopy(tok_h.at[0], mine, 2 * way, blk, z, 1 - c).wait_send()
            gcopy(tok_h.at[0], mine, 2 * way + 1, blk, z, 1 - c).wait_send()
            eng.copy(buf_b.at[0, 0:tq], rd.at[way], ("d2", way)).wait_send()

        @pl.when(inside(z + 2 * dz))
        def _():
            eng.copy(buf_b.at[0, 0:tq], relay.at[way], ("d1", way)).wait_send()

        @pl.when(inside(z - dz) & inside(z + dz))
        def _():
            for h in range(2):
                gcopy(tok_h.at[0], mine, 6 + 2 * way + h, blk, z, 1 - c).wait_send()


def layer(nz, tok, dy, seg, wq, wk, wv, wout, win, wdown, gain_a, gain_f, table):
    _, block, width = tok.shape
    nb = 2 * nz
    length, tq = nb * block, 2 * block
    share = width // nb
    pairs = table.shape[0] // 2
    steps = win.shape[1] // width
    vm = pl.BlockSpec(memory_space=pltpu.VMEM)
    hbm = pl.BlockSpec(memory_space=pl.ANY)
    home = jax.ShapeDtypeStruct((2, 2, block, width), BF)
    grads = jax.ShapeDtypeStruct((2, 12, share, width // 2), BF)
    one = (share, width // 2)
    small = (24, TILE)

    def bf(*shape):
        return pltpu.VMEM(shape, BF)

    def f32(*shape):
        return pltpu.VMEM(shape, F32)

    sums = [bf(2, nz, 4, *one), bf(2, nz, 4, *one)]
    for i, route in enumerate(("xzy", "xyz", "xyz")):
        last = route == "xyz"
        sums += [bf(2, nz, 2, *one)] if i < 2 else []
        sums += [bf(2, nz if last else 1, *one), bf(2, 3, *one) if last else bf(2, 3, 2, *one)]
    scratch = [
        bf(nb, block, width), bf(length, width), bf(length, width),
        bf(pairs, 2 * tq, 2 * TILE), bf(pairs, length, 2 * tq), bf(tq, width),
        bf(2, block, width), bf(3, width, width), bf(width, width),
        bf(steps, width, width), bf(steps, width, width), bf(2, nb, 4, *one), bf(2, nb, 4, *one),
        *sums,
        bf(tq, width), f32(tq, width), bf(tq, width), f32(tq, width),
        f32(length, 2 * tq), bf(length + 2 * TILE, 2 * tq), bf(max(2 * pairs * 3 * TILE, pairs * tq + nz * 2 * tq), TILE), bf(length, TILE),
        f32(3, 16, 2 * TILE), f32(2, 16, tq), f32(pairs, 8, 2 * tq), f32(pairs, 8, 2 * tq),
        bf(2, tq, width), bf(2, tq, width),
        pltpu.VMEM((nb, 8, block), jnp.int32), pltpu.VMEM((8, block), jnp.int32), bf(*table.shape),
        f32(6, *small), f32(5, *small),
        pltpu.SemaphoreType.DMA((180,)), pltpu.SemaphoreType.DMA((180,)), pltpu.SemaphoreType.DMA((32,)),
        pltpu.SemaphoreType.DMA((10 + nb,)), pltpu.SemaphoreType.DMA((2 * nb + 2,)),
        pltpu.SemaphoreType.REGULAR,
    ]
    return pl.pallas_call(
        functools.partial(layer_kernel, nz),
        out_shape=(home, grads, jax.ShapeDtypeStruct(small, F32)),
        in_specs=[hbm, hbm, vm] + [hbm] * 6 + [vm, vm, hbm],
        out_specs=(vm,) * 3,
        scratch_shapes=scratch,
        compiler_params=pltpu.CompilerParams(
            collective_id=1, has_side_effects=True, vmem_limit_bytes=64 * 1024 * 1024
        ),
    )(tok, dy, seg, wq, wk, wv, wout, win, wdown, gain_a, gain_f, table)


def finish_kernel(
    home, grads_h, small, o_out, o_gt, o_ga, o_q, o_k, o_v, o_o, o_gf, o_in, o_down, o_table,
    grads, f_down, f_in, f_attn, sem,
):
    share, wide = grads.shape[2:]
    width = 2 * wide
    lines = width // TILE
    blk = lax.axis_index("blk")
    units = (2, 1, 0)
    ins = [
        pltpu.make_async_copy(grads_h.at[:, 4 * i : 4 * i + 4], grads.at[:, 4 * i : 4 * i + 4], sem.at[i])
        for i in units
    ]
    outs = [pltpu.make_async_copy(home.at[i], ref, sem.at[3 + i]) for i, ref in enumerate((o_out, o_gt))]
    for op in ins + outs:
        op.start()

    def send(src, dst):
        op = pltpu.make_async_copy(src, dst, sem.at[3 + len(outs)])
        op.start()
        outs.append(op)

    def mine(first, count, each):
        flat = jnp.concatenate([small[first + i : first + i + 1, :] for i in range(count)], axis=1)
        flat = jnp.broadcast_to(flat, (8, count * TILE))
        return pltpu.roll(flat, lax.rem(count * TILE - blk * each, count * TILE), 1)[0:1, :each]

    o_ga[...] = mine(0, lines, share).reshape(share)
    o_gf[...] = mine(lines, lines, share).reshape(share)
    per, heads = o_table.shape
    left = small.shape[0] - 2 * lines
    table = jnp.concatenate([small[2 * lines :, :], jnp.zeros((16 - left, TILE), F32)], axis=0)
    turned = pltpu.roll(table, lax.rem(TILE - blk * per, TILE), 1).T
    o_table[...] = turned[:per, :heads]

    cols = [slice(hh * wide, (hh + 1) * wide) for hh in range(2)]
    ins[0].wait()
    for i, ref in enumerate((o_q, o_k, o_v, o_o)):
        for hh in range(2):
            f_attn[i, :, cols[hh]] = grads[hh, 8 + i].astype(F32)
        send(f_attn.at[i], ref)
    ins[1].wait()
    for i in range(4):
        for hh in range(2):
            f_in[:, i * width + hh * wide : i * width + (hh + 1) * wide] = grads[hh, 4 + i].astype(F32)
    send(f_in, o_in)
    ins[2].wait()
    for i in range(4):
        for hh in range(2):
            f_down[i * share : (i + 1) * share, cols[hh]] = grads[hh, i].astype(F32)
    send(f_down, o_down)
    for op in outs:
        op.wait()


def finish(home, grads, small, heads, nb):
    _, _, block, width = home.shape
    share = width // nb
    vm = pl.BlockSpec(memory_space=pltpu.VMEM)
    hbm = pl.BlockSpec(memory_space=pl.ANY)
    one = jax.ShapeDtypeStruct((share, width), F32)
    gain = jax.ShapeDtypeStruct((share,), F32)
    own = jax.ShapeDtypeStruct((2, block, width), BF)
    return pl.pallas_call(
        finish_kernel,
        out_shape=(
            own, own, gain, one, one, one, one, gain,
            jax.ShapeDtypeStruct((share, 4 * width), F32),
            jax.ShapeDtypeStruct((4 * share, width), F32),
            jax.ShapeDtypeStruct((32 // nb, heads), F32),
        ),
        in_specs=[hbm, hbm, vm],
        out_specs=(hbm, hbm, vm, hbm, hbm, hbm, hbm, vm, hbm, hbm, vm),
        scratch_shapes=[
            pltpu.VMEM(grads.shape, BF),
            pltpu.VMEM((4 * share, width), F32),
            pltpu.VMEM((share, 4 * width), F32),
            pltpu.VMEM((4, share, width), F32),
            pltpu.SemaphoreType.DMA((12,)),
        ],
        compiler_params=pltpu.CompilerParams(vmem_limit_bytes=VLIMIT),
    )(home, grads, small)


def fast_device(
    nz, tokens, segment_ids, gain_attn, w_query, w_key, w_value, w_out, gain_ffn, w_in, w_down,
    rel_table, cotangent,
):
    width = tokens.shape[2]
    home, grads, small = layer(
        nz, tokens, cotangent, segment_ids, w_query, w_key, w_value, w_out, w_in,
        w_down.reshape(-1, width, width), gain_attn, gain_ffn, rel_table.T,
    )
    return finish(home, grads, small, rel_table.shape[1], 2 * nz)


def pick(mesh):
    if mesh.shape["dp"] == 4 and mesh.shape["blk"] == 8:
        return functools.partial(fast_device, mesh.shape["blk"] // 2)
    return on_device


def solution(mesh):
    placed = (
        P("dp", "blk", None),
        P("dp", "blk"),
        P(),
        P(),
        P(),
        P(),
        P(),
        P(),
        P(),
        P(),
        P(),
        P("dp", "blk", None),
    )
    return jax.shard_map(
        pick(mesh),
        mesh=mesh,
        in_specs=placed,
        out_specs=(
            P("dp", "blk", None),
            P("dp", "blk", None),
            P("blk"),
            P("blk", None),
            P("blk", None),
            P("blk", None),
            P("blk", None),
            P("blk"),
            P("blk", None),
            P("blk", None),
            P("blk", None),
        ),
        check_vma=False,
    )
```
